256 devices in a mesh: gx: 8 (over x, core), gy: 32 (over y, z).
Axes of the slice: x: 4, y: 4, z: 8, core: 2. Of those that a mesh axis runs over, the one named last changes fastest.
Arguments:
- features: bfloat16 [2048, 64, 128], P(('gx', 'gy')), may hold values from -6 to 6
- weights: bfloat16 [27, 128, 128], replicated, may hold values from -0.109375 to 0.109375
- cotangent: bfloat16 [2048, 64, 128], P(('gx', 'gy')), may hold values from -6 to 6
- dst_index: int32 [27, 2048], P(None, ('gx', 'gy')), may hold values from 0 to 48, as said below
- recv_slot: int32 [10240], P(('gx', 'gy')), may hold values from 0 to 8, as said below
Outputs:
- outputs: bfloat16 [2048, 64, 128], P(('gx', 'gy'))
- input_grad: bfloat16 [2048, 64, 128], P(('gx', 'gy'))
- weight_grad: float32 [27, 128, 128], replicated
The draws below stay inside these ranges and needn't reach their ends.
Inputs may be any that keep to these rules, and one draw needn't show every extreme that they name: `dst_index`: A value below 8 is an occupied slot of the same device; from 8 to 47 an occupied brick of the tile beside it; 48 means no occupied neighbour. Occupied slots of a device come first; an unoccupied slot has 48 for every offset. Some device has all 8 slots occupied. `recv_slot`: 8 marks a halo layer position with no occupied brick.
All inputs are finite; a program needn't handle non-finite values.
Results may differ from the reference program's by a relative error of at most 0.003.
Values may be sent and summed in bfloat16 or wider, within the bound.
No kernel may reach another device: no remote copies, remote signals or barrier semaphores. Data moves between devices by JAX's collectives and lax.ppermute only.
A program may use at most 64 MiB of HBM per device.

```python
import math
import jax
import jax.numpy as jnp
import numpy as np
from jax import lax

C = 128
BRICK = 4
VOX = 64
TILE = 4
BZ = 2
NB = 8
HALO = 40
BRICKS = 2048
N_GX = 8
N_GY = 32


DIRECTIONS = ((1, 0), (-1, 0), (0, 1), (0, -1), (1, 1), (1, -1), (-1, 1), (-1, -1))


def occupancy(key):
    devices = N_GX * N_GY
    cell_count = TILE * TILE * BZ
    key_count, key_score, key_busy = jax.random.split(key, 3)
    counts = jax.random.randint(key_count, (devices,), NB // 2, NB + 1)
    busiest = jax.random.randint(key_busy, (), 0, devices)
    counts = jnp.where(jnp.arange(devices) == busiest, NB, counts)
    scores = jax.random.randint(key_score, (devices, cell_count), 0, 1 << 20) * cell_count
    scores = scores + jnp.arange(cell_count, dtype=jnp.int32)[None, :]
    ranking = jnp.argsort(jnp.argsort(scores, axis=1), axis=1).astype(jnp.int32)
    return jnp.where(ranking < counts[:, None], ranking, NB).astype(jnp.int32)


def draw_dst_index(key, part):
    slot_of = occupancy(key)
    key = jax.random.fold_in(key, 7)
    devices = N_GX * N_GY
    cell_count = TILE * TILE * BZ
    dump_index = NB + HALO
    face_cells = TILE * BZ
    cell_ids = np.arange(cell_count)
    cell_x = cell_ids // (TILE * BZ)
    cell_y = cell_ids // BZ % TILE
    cell_z = cell_ids % BZ
    offsets = np.array([(a, b, c) for a in (-1, 0, 1) for b in (-1, 0, 1) for c in (-1, 0, 1)])
    reach_x = cell_x[:, None] + offsets[None, :, 0]
    reach_y = cell_y[:, None] + offsets[None, :, 1]
    reach_z = cell_z[:, None] + offsets[None, :, 2]
    cross_x = (reach_x >= TILE).astype(np.int64) - (reach_x < 0).astype(np.int64)
    cross_y = (reach_y >= TILE).astype(np.int64) - (reach_y < 0).astype(np.int64)
    inside_z = (reach_z >= 0) & (reach_z < BZ)
    clip_z = np.clip(reach_z, 0, BZ - 1)
    target_cell = (reach_x % TILE * TILE + reach_y % TILE) * BZ + clip_z
    start_table = np.zeros(9, np.int64)
    begin_at = 0
    for number, heading in enumerate(DIRECTIONS):
        start_table[(heading[0] + 1) * 3 + heading[1] + 1] = begin_at
        begin_at += face_cells if number < 4 else BZ
    heading_code = (cross_x + 1) * 3 + cross_y + 1
    position = np.where(cross_y == 0, reach_y % TILE * BZ + clip_z, np.where(cross_x == 0, reach_x % TILE * BZ + clip_z, clip_z))
    halo_index = NB + start_table[heading_code] + position
    is_local = (cross_x == 0) & (cross_y == 0)
    device_ids = jnp.arange(devices, dtype=jnp.int32)
    grid_x = device_ids // N_GY
    grid_y = device_ids % N_GY
    owner_x = grid_x[:, None, None] + jnp.asarray(cross_x, jnp.int32)[None]
    owner_y = grid_y[:, None, None] + jnp.asarray(cross_y, jnp.int32)[None]
    in_grid = (owner_x >= 0) & (owner_x < N_GX) & (owner_y >= 0) & (owner_y < N_GY)
    in_grid = in_grid & jnp.asarray(inside_z)[None]
    owner_dev = jnp.clip(owner_x, 0, N_GX - 1) * N_GY + jnp.clip(owner_y, 0, N_GY - 1)
    target_slot = slot_of[owner_dev, jnp.asarray(target_cell, jnp.int32)[None]]
    occupied = in_grid & (target_slot < NB)
    entries = jnp.where(occupied, jnp.where(jnp.asarray(is_local)[None], target_slot, jnp.asarray(halo_index, jnp.int32)[None]), dump_index).astype(jnp.int32)
    slot_table = jnp.full((devices, NB + 1, 27), dump_index, jnp.int32)
    slot_table = slot_table.at[device_ids[:, None], slot_of].set(entries)
    return slot_table[:, :NB].reshape(devices * NB, 27).T


def draw_recv_slot(key, part):
    slot_of = occupancy(key)
    key = jax.random.fold_in(key, 11)
    layer_cells = []
    for heading in DIRECTIONS:
        edge_x = 0 if heading[0] == 1 else TILE - 1
        edge_y = 0 if heading[1] == 1 else TILE - 1
        if heading[1] == 0:
            for across in range(TILE):
                for height in range(BZ):
                    layer_cells.append((edge_x * TILE + across) * BZ + height)
        elif heading[0] == 0:
            for across in range(TILE):
                for height in range(BZ):
                    layer_cells.append((across * TILE + edge_y) * BZ + height)
        else:
            for height in range(BZ):
                layer_cells.append((edge_x * TILE + edge_y) * BZ + height)
    return slot_of[:, jnp.asarray(np.array(layer_cells), jnp.int32)].reshape(-1).astype(jnp.int32)


def level_of(rng, dims, shards, low, largest):
    def one(dim, parts):
        heights = jax.random.uniform(jax.random.fold_in(jax.random.fold_in(rng, 6), dim), (parts,), jnp.float32, low / len(shards), largest / len(shards))
        return jnp.repeat(jnp.exp(heights), dims[dim] // parts).reshape((-1,) + (1,) * (len(dims) - dim - 1))

    factor_of = one(*shards[0])
    for cut in shards[1:]:
        factor_of = factor_of * one(*cut)
    return factor_of


def normal_values(own_key, shape, deviation, limit, shards=(), held_as=jnp.bfloat16):
    factor_of = level_of(own_key, shape, shards, -0.22, 0.18) if shards else 1.0
    values = jax.random.normal(own_key, shape, jnp.float32) * deviation * factor_of
    return jnp.minimum(jnp.maximum(values, -limit), limit).astype(held_as)


def setup_inputs(seed: int = 0) -> dict:
    streams_of = jax.random.split(jax.random.key(seed), 6)
    return {
        "features": normal_values(streams_of[0], (BRICKS, VOX, C), 1.0, 6.0, ((0, 256),)),
        "weights": normal_values(streams_of[1], (27, C, C), (27 * C) ** -0.5, 0.109375),
        "cotangent": normal_values(streams_of[2], (BRICKS, VOX, C), 1.0, 6.0, ((0, 256),)),
        "dst_index": draw_dst_index(jax.random.fold_in(streams_of[5], 71), 0),
        "recv_slot": draw_recv_slot(jax.random.fold_in(streams_of[5], 71), 0),
    }


DIRECTIONS = ((1, 0), (-1, 0), (0, 1), (0, -1), (1, 1), (1, -1), (-1, 1), (-1, -1))
OFFSETS = tuple((a, b, c) for a in (-1, 0, 1) for b in (-1, 0, 1) for c in (-1, 0, 1))


def halo_headings():
    heading_x = []
    heading_y = []
    for number, heading in enumerate(DIRECTIONS):
        length = TILE * BZ if number < 4 else BZ
        heading_x += [heading[0]] * length
        heading_y += [heading[1]] * length
    return np.array(heading_x, np.int32), np.array(heading_y, np.int32)


def neighbour_table(dst_index, recv_slot):
    bricks = dst_index.shape[1]
    heading_x, heading_y = halo_headings()
    brick_ids = jnp.arange(bricks, dtype=jnp.int32)
    device = brick_ids // NB
    grid_x = device // N_GY
    grid_y = device % N_GY
    targets = dst_index.T.astype(jnp.int32)
    halo_pos = jnp.clip(targets - NB, 0, HALO - 1)
    owner_x = jnp.clip(grid_x[:, None] + jnp.asarray(heading_x, jnp.int32)[halo_pos], 0, N_GX - 1)
    owner_y = jnp.clip(grid_y[:, None] + jnp.asarray(heading_y, jnp.int32)[halo_pos], 0, N_GY - 1)
    owner_dev = owner_x * N_GY + owner_y
    remote_slot = recv_slot[owner_dev * HALO + halo_pos]
    remote = jnp.where(remote_slot < NB, owner_dev * NB + remote_slot, bricks)
    own_ids = device[:, None] * NB + targets
    result = jnp.where(targets < NB, own_ids, jnp.where(targets < NB + HALO, remote, bricks))
    return result.astype(jnp.int32)


def brick_taps(gathered, orient):
    group_size = gathered.shape[0]
    channels = gathered.shape[-1]
    edge = BRICK
    volume = gathered.reshape(group_size, 3, 3, 3, edge, edge, edge, channels)
    volume = jnp.transpose(volume, (0, 1, 4, 2, 5, 3, 6, 7)).reshape(group_size, 3 * edge, 3 * edge, 3 * edge, channels)
    tap_list = []
    for shift_x, shift_y, shift_z in OFFSETS:
        begin_x = edge + orient * shift_x
        begin_y = edge + orient * shift_y
        begin_z = edge + orient * shift_z
        window = volume[:, begin_x:begin_x + edge, begin_y:begin_y + edge, begin_z:begin_z + edge]
        tap_list.append(window.reshape(group_size, edge * edge * edge, channels))
    return jnp.concatenate(tap_list, axis=-1)


def reference(features, weights, cotangent, dst_index, recv_slot):
    bricks, voxels, channels = features.shape
    neighbours = neighbour_table(dst_index, recv_slot)
    zero_rows = jnp.zeros((1, voxels, channels), jnp.bfloat16)
    feat_ext = jnp.concatenate((features, zero_rows), axis=0)
    grad_ext = jnp.concatenate((cotangent, zero_rows), axis=0)
    w_taps = weights.reshape(27 * channels, channels)
    w_back = jnp.transpose(weights, (0, 2, 1)).reshape(27 * channels, channels)
    group_size = NB * math.gcd(N_GX * N_GY, 8)
    group_count = bricks // group_size

    def visit_group(running, inputs):
        brick_rows, neighbour_ids = inputs
        forward = brick_taps(feat_ext[neighbour_ids], 1)
        outputs = jnp.dot(forward, w_taps, preferred_element_type=jnp.float32).astype(jnp.bfloat16)
        backward = brick_taps(grad_ext[neighbour_ids], -1)
        input_grad = jnp.dot(backward, w_back, preferred_element_type=jnp.float32).astype(jnp.bfloat16)
        running = running + lax.dot_general(
            brick_rows.reshape(-1, channels), backward.reshape(-1, 27 * channels),
            (((0,), (0,)), ((), ())), preferred_element_type=jnp.float32)
        return running, (outputs, input_grad)

    grad_start = jnp.zeros((channels, 27 * channels), jnp.float32)
    grad_total, (outputs, input_grad) = lax.scan(
        visit_group, grad_start,
        (features.reshape(group_count, group_size, voxels, channels),
         neighbours.reshape(group_count, group_size, 27)))
    weight_grad = jnp.transpose(grad_total.reshape(channels, 27, channels), (1, 0, 2)) / float(VOX * NB)
    return (outputs.reshape(bricks, voxels, channels),
            input_grad.reshape(bricks, voxels, channels),
            weight_grad)
```

```python
import functools

import jax
import jax.numpy as jnp
import numpy as np
from jax import lax
from jax.experimental import pallas as pl
from jax.experimental.pallas import tpu as pltpu
from jax.sharding import Mesh, PartitionSpec as P

BRICK = 4
TILE = 4
BZ = 2
HALO = 40
SLOTS = 8
VOXELS = 64
CHANNELS = 128
PLANE = BRICK * BRICK
PLANES = BRICK + 2
WIDE = 9 * CHANNELS
ROWS_M = 28

DIRECTIONS = ((1, 0), (-1, 0), (0, 1), (0, -1), (1, 1), (1, -1), (-1, 1), (-1, -1))
LENGTHS = (TILE * BZ,) * 4 + (BZ,) * 4
AXES = ("x", "c", "y", "z")
VMEM_LIMIT = 48 * 1024 * 1024


def shift_matrix():
    picked = np.zeros((9 * PLANE, 9 * PLANE), np.float32)
    for number in range(9):
        for voxel in range(PLANE):
            y = voxel // BRICK + number // 3 - 1 + BRICK
            z = voxel % BRICK + number % 3 - 1 + BRICK
            source = (y // BRICK * 3 + z // BRICK) * PLANE + y % BRICK * BRICK + z % BRICK
            picked[number * PLANE + voxel, source] = 1.0
    return picked


def pack_kernel(slot_ref, features_ref, cotangent_ref, *packets):
    begin_at = 0
    for packet in packets:
        for position in range(packet.shape[0]):
            slot = slot_ref[begin_at + position]
            row = jnp.clip(slot, 0, SLOTS - 1)

            @pl.when(slot < SLOTS)
            def _():
                packet[position, :, :CHANNELS] = features_ref[row]
                packet[position, :, CHANNELS:] = cotangent_ref[row]

            @pl.when(slot >= SLOTS)
            def _():
                packet[position] = jnp.zeros((VOXELS, 2 * CHANNELS), jnp.bfloat16)

        begin_at += packet.shape[0]


def pack(recv_slot, features, cotangent):
    vmem = pl.BlockSpec(memory_space=pltpu.VMEM)
    return pl.pallas_call(
        pack_kernel,
        in_specs=[pl.BlockSpec(memory_space=pltpu.SMEM), vmem, vmem],
        out_specs=[vmem] * 8,
        out_shape=[
            jax.ShapeDtypeStruct((length, VOXELS, 2 * CHANNELS), jnp.bfloat16) for length in LENGTHS
        ],
        compiler_params=pltpu.CompilerParams(vmem_limit_bytes=VMEM_LIMIT),
    )(recv_slot, features, cotangent)


def conv_kernel(
    core_ref, dst_ref, features_ref, cotangent_ref, *rest
):
    halos = rest[:8]
    (flipped_ref, shift_ref, weights_ref, w_back_ref, outputs_ref, grad_ref, send_ref, keep_ref,
     bricks, taps_f, taps_c) = rest[8:]
    bricks[:SLOTS, :, :CHANNELS] = features_ref[...]
    bricks[:SLOTS, :, CHANNELS:] = cotangent_ref[...]
    begin_at = SLOTS
    for halo in halos:
        bricks[begin_at : begin_at + halo.shape[0]] = halo[...]
        begin_at += halo.shape[0]
    bricks[begin_at] = jnp.zeros((VOXELS, 2 * CHANNELS), jnp.bfloat16)

    def one_slot(slot, carry):
        for plane in range(PLANES):
            side = 0 if plane == 0 else 2 if plane == PLANES - 1 else 1
            local = (plane - 1) % BRICK * PLANE
            around = [
                bricks[jnp.clip(dst_ref[side * 9 + number, slot], 0, SLOTS + HALO), local : local + PLANE]
                for number in range(9)
            ]
            moved = jnp.dot(
                shift_ref[...], jnp.concatenate(around, axis=0), preferred_element_type=jnp.float32
            ).astype(jnp.bfloat16)
            for number in range(9):
                rows = moved[number * PLANE : (number + 1) * PLANE]
                lanes = slice(number * CHANNELS, (number + 1) * CHANNELS)
                taps_f[slot, plane, :, lanes] = rows[:, :CHANNELS]
                taps_c[slot, plane, :, lanes] = rows[:, CHANNELS:]
        return carry

    lax.fori_loop(0, SLOTS, one_slot, 0)

    core = core_ref[0]
    flipped = jnp.concatenate((flipped_ref[1 - core], flipped_ref[core]), axis=0)
    half = CHANNELS // 2
    for side in range(3):
        tap = taps_c[:, side : side + BRICK].reshape(SLOTS * VOXELS, WIDE)
        part = jnp.dot(flipped, tap, preferred_element_type=jnp.float32)
        for number in range(9):
            block = part[:, number * CHANNELS : (number + 1) * CHANNELS]
            m = side * 9 + number
            for quarter in range(4):
                rows = slice(quarter * 16, quarter * 16 + 16)
                send_ref[quarter, m] = block[:half][rows].astype(jnp.bfloat16)
                keep_ref[quarter, m] = block[half:][rows]
    for quarter in range(4):
        send_ref[quarter, 27] = jnp.zeros((16, CHANNELS), jnp.bfloat16)
        keep_ref[quarter, 27] = jnp.zeros((16, CHANNELS), jnp.float32)

    for source, kernel, target in (
        (taps_f, weights_ref, outputs_ref), (taps_c, w_back_ref, grad_ref)
    ):
        total = None
        for side in range(3):
            tap = source[:, side : side + BRICK].reshape(SLOTS * VOXELS, WIDE)
            matrix = kernel[side * 9 : side * 9 + 9].reshape(WIDE, CHANNELS)
            part = jnp.dot(tap, matrix, preferred_element_type=jnp.float32)
            total = part if total is None else total + part
        target[...] = total.astype(jnp.bfloat16).reshape(SLOTS, VOXELS, CHANNELS)


def convolve(core, dst_index, features, cotangent, halos, flipped, shift, weights, w_back):
    vmem = pl.BlockSpec(memory_space=pltpu.VMEM)
    smem = pl.BlockSpec(memory_space=pltpu.SMEM)
    return pl.pallas_call(
        conv_kernel,
        in_specs=[smem, smem] + [vmem] * 14,
        out_specs=[vmem] * 4,
        out_shape=[
            jax.ShapeDtypeStruct((SLOTS, VOXELS, CHANNELS), jnp.bfloat16),
            jax.ShapeDtypeStruct((SLOTS, VOXELS, CHANNELS), jnp.bfloat16),
            jax.ShapeDtypeStruct((4, ROWS_M, 16, CHANNELS), jnp.bfloat16),
            jax.ShapeDtypeStruct((4, ROWS_M, 16, CHANNELS), jnp.float32),
        ],
        scratch_shapes=[
            pltpu.VMEM((SLOTS + HALO + 1, VOXELS, 2 * CHANNELS), jnp.bfloat16),
            pltpu.VMEM((SLOTS, PLANES, PLANE, WIDE), jnp.bfloat16),
            pltpu.VMEM((SLOTS, PLANES, PLANE, WIDE), jnp.bfloat16),
        ],
        compiler_params=pltpu.CompilerParams(vmem_limit_bytes=VMEM_LIMIT),
    )(core, dst_index, features, cotangent, *halos, flipped, shift, weights, w_back)


def pass_to(value, step_x, step_y):
    pairs = []
    for gx in range(8):
        for gy in range(32):
            if 0 <= gx + step_x < 8 and 0 <= gy + step_y < 32:
                pairs.append((gx * 32 + gy, (gx + step_x) * 32 + gy + step_y))
    return lax.ppermute(value, AXES, pairs)


def local(features, weights, cotangent, dst_index, recv_slot):
    packets = pack(recv_slot, features, cotangent)
    halos = [None] * 8
    for number in (2, 3, 0, 1, 4, 5, 6, 7):
        step_x, step_y = DIRECTIONS[number]
        halos[number] = pass_to(packets[number], -step_x, -step_y)
    core = lax.axis_index("c").astype(jnp.int32).reshape(1)
    flipped = jnp.transpose(features.reshape(SLOTS * VOXELS, CHANNELS)).reshape(2, CHANNELS // 2, SLOTS * VOXELS)
    w_back = jnp.transpose(weights[::-1], (0, 2, 1))
    shift = jnp.asarray(shift_matrix(), jnp.bfloat16)
    outputs, input_grad, send, keep = convolve(
        core, dst_index, features, cotangent, halos, flipped, shift, weights, w_back
    )
    arrived = lax.ppermute(send, "c", [(0, 1), (1, 0)])
    chip_sum = (keep + arrived.astype(jnp.float32)).astype(jnp.bfloat16)
    parts = chip_sum.reshape(16, 7, 16, CHANNELS)
    parts = lax.all_to_all(parts, ("x", "y"), 0, 0)
    share = jnp.sum(parts.astype(jnp.float32), axis=0)
    column = jnp.broadcast_to(share[None], (8,) + share.shape)
    column = lax.all_to_all(column, "z", 0, 0)
    share = (jnp.sum(column, axis=0) * (1.0 / (VOXELS * SLOTS))).astype(jnp.bfloat16)
    whole = jnp.broadcast_to(share[None], (16,) + share.shape)
    whole = lax.all_to_all(whole, ("x", "y"), 0, 0)
    whole = lax.all_gather(whole, "c")
    whole = whole.reshape(2, 4, ROWS_M, 16, CHANNELS)[:, :, :27]
    whole = jnp.transpose(whole, (2, 0, 1, 3, 4)).reshape(27, CHANNELS, CHANNELS)[::-1]
    return outputs, input_grad, whole.astype(jnp.float32)


def solution(mesh):
    fine = Mesh(mesh.devices.reshape(4, 2, 4, 8), AXES)
    bricks = P(AXES, None, None)
    return jax.shard_map(
        local,
        mesh=fine,
        in_specs=(bricks, P(), bricks, P(None, AXES), P(AXES)),
        out_specs=(bricks, bricks, P()),
        check_vma=False,
    )
```

```python
import functools

import jax
import jax.numpy as jnp
import numpy as np
from jax import lax
from jax.experimental import pallas as pl
from jax.experimental.pallas import tpu as pltpu
from jax.sharding import Mesh, PartitionSpec as P

BRICK = 4
TILE = 4
BZ = 2
HALO = 40
SLOTS = 8
VOXELS = 64
CHANNELS = 128
PLANE = BRICK * BRICK
PLANES = BRICK + 2
WIDE = 9 * CHANNELS
ROWS_M = 28

DIRECTIONS = ((1, 0), (-1, 0), (0, 1), (0, -1), (1, 1), (1, -1), (-1, 1), (-1, -1))
LENGTHS = (TILE * BZ,) * 4 + (BZ,) * 4
STARTS = tuple(int(start) for start in np.cumsum((0,) + LENGTHS[:-1]))
AXES = ("x", "c", "y", "z")
VMEM_LIMIT = 48 * 1024 * 1024


def shift_matrix():
    picked = np.zeros((9 * PLANE, 9 * PLANE), np.float32)
    for number in range(9):
        for voxel in range(PLANE):
            y = voxel // BRICK + number // 3 - 1 + BRICK
            z = voxel % BRICK + number % 3 - 1 + BRICK
            source = (y // BRICK * 3 + z // BRICK) * PLANE + y % BRICK * BRICK + z % BRICK
            picked[number * PLANE + voxel, source] = 1.0
    return picked


def layer_matrix():
    picked = np.zeros((2 * PLANE, VOXELS), np.float32)
    for side, vy in enumerate((0, BRICK - 1)):
        for vx in range(BRICK):
            for vz in range(BRICK):
                picked[side * PLANE + vx * BRICK + vz, vx * PLANE + vy * BRICK + vz] = 1.0
    return picked


def pack_layers_kernel(slot_ref, layer_ref, features_ref, cotangent_ref, to_y_down, to_y_up, to_x_down, to_x_up,
                       bricks, sides, sems):
    copies = [
        pltpu.make_async_copy(ref, bricks.at[number], sems.at[number])
        for number, ref in enumerate((features_ref, cotangent_ref))
    ]
    for copy in copies:
        copy.start()
    for copy in copies:
        copy.wait()
    layer = layer_ref[...]
    for kind in range(2):
        for slot in range(SLOTS):
            sides[kind, slot] = jnp.dot(
                layer, bricks[kind, slot], preferred_element_type=jnp.float32
            ).astype(jnp.bfloat16)
    zero = jnp.zeros((PLANE, 2 * CHANNELS), jnp.bfloat16)

    def put(packet, position, halo, from_sides, begin):
        slot = slot_ref[halo]
        row = jnp.clip(slot, 0, SLOTS - 1)
        source = sides if from_sides else bricks

        @pl.when(slot < SLOTS)
        def _():
            packet[position, :, :CHANNELS] = source[0, row, begin : begin + PLANE]
            packet[position, :, CHANNELS:] = source[1, row, begin : begin + PLANE]

        @pl.when(slot >= SLOTS)
        def _():
            packet[position] = zero

    for packet, numbers, begin in (
        (to_y_down, (2, 4, 6), 0),
        (to_y_up, (3, 5, 7), PLANE),
    ):
        position = 0
        for number in numbers:
            for halo in range(STARTS[number], STARTS[number] + LENGTHS[number]):
                put(packet, position, halo, True, begin)
                position += 1
    for packet, number, begin in ((to_x_down, 0, 0), (to_x_up, 1, VOXELS - PLANE)):
        for position in range(LENGTHS[number]):
            put(packet, position, STARTS[number] + position, False, begin)


def pack_layers(recv_slot, layer, features, cotangent):
    vmem = pl.BlockSpec(memory_space=pltpu.VMEM)
    smem = pl.BlockSpec(memory_space=pltpu.SMEM)
    hbm = pl.BlockSpec(memory_space=pl.ANY)
    return pl.pallas_call(
        pack_layers_kernel,
        in_specs=[smem, vmem, hbm, hbm],
        out_specs=[vmem] * 4,
        out_shape=[
            jax.ShapeDtypeStruct((length, PLANE, 2 * CHANNELS), jnp.bfloat16) for length in (12, 12, 8, 8)
        ],
        scratch_shapes=[
            pltpu.VMEM((2, SLOTS, VOXELS, CHANNELS), jnp.bfloat16),
            pltpu.VMEM((2, SLOTS, 2 * PLANE, CHANNELS), jnp.bfloat16),
            pltpu.SemaphoreType.DMA((2,)),
        ],
        compiler_params=pltpu.CompilerParams(vmem_limit_bytes=VMEM_LIMIT),
    )(recv_slot, layer, features, cotangent)


def fill_bricks(halos, bricks):
    begin_at = SLOTS
    for halo in halos:
        bricks[begin_at : begin_at + halo.shape[0]] = halo[...]
        begin_at += halo.shape[0]


def fill_layers(halos, bricks):
    expand_ref, y_above, y_below, x_above, x_below = halos
    for position in range(SLOTS):
        bricks[SLOTS + STARTS[0] + position, :PLANE] = x_above[position]
        bricks[SLOTS + STARTS[1] + position, VOXELS - PLANE :] = x_below[position]
    for side, faces, number in ((0, y_above, 2), (1, y_below, 3)):
        corner = SLOTS + 2 * side
        tiles = [faces[position] for position in range(SLOTS)]
        tiles += [x_above[corner + position] for position in range(BZ)]
        tiles += [x_below[corner + position] for position in range(BZ)]
        targets = list(range(STARTS[number], STARTS[number] + SLOTS))
        targets += list(range(STARTS[4 + side], STARTS[4 + side] + BZ))
        targets += list(range(STARTS[6 + side], STARTS[6 + side] + BZ))
        whole = jnp.dot(
            expand_ref[side], jnp.concatenate(tiles, axis=1), preferred_element_type=jnp.float32
        ).astype(jnp.bfloat16)
        for position, target in enumerate(targets):
            bricks[SLOTS + target] = whole[:, position * 2 * CHANNELS : (position + 1) * 2 * CHANNELS]


def pack_bricks_kernel(slot_ref, features_ref, cotangent_ref, *packets):
    begin_at = 0
    for packet in packets:
        for position in range(packet.shape[0]):
            slot = slot_ref[begin_at + position]
            row = jnp.clip(slot, 0, SLOTS - 1)

            @pl.when(slot < SLOTS)
            def _():
                packet[position, :, :CHANNELS] = features_ref[row]
                packet[position, :, CHANNELS:] = cotangent_ref[row]

            @pl.when(slot >= SLOTS)
            def _():
                packet[position] = jnp.zeros((VOXELS, 2 * CHANNELS), jnp.bfloat16)

        begin_at += packet.shape[0]


def pack_bricks(recv_slot, features, cotangent):
    vmem = pl.BlockSpec(memory_space=pltpu.VMEM)
    return pl.pallas_call(
        pack_bricks_kernel,
        in_specs=[pl.BlockSpec(memory_space=pltpu.SMEM), vmem, vmem],
        out_specs=[vmem] * 8,
        out_shape=[
            jax.ShapeDtypeStruct((length, VOXELS, 2 * CHANNELS), jnp.bfloat16) for length in LENGTHS
        ],
        compiler_params=pltpu.CompilerParams(vmem_limit_bytes=VMEM_LIMIT),
    )(recv_slot, features, cotangent)


def conv_kernel(fill, count, core_ref, flag_ref, dst_ref, features_ref, cotangent_ref, *rest):
    halos = rest[:count]
    (flipped_ref, shift_ref, weights_ref, w_back_ref, outputs_ref, grad_ref, send_ref, keep_ref,
     bricks, taps_f, taps_c) = rest[count:]
    bricks[:SLOTS, :, :CHANNELS] = features_ref[...]
    bricks[:SLOTS, :, CHANNELS:] = cotangent_ref[...]
    fill(halos, bricks)
    bricks[SLOTS + HALO] = jnp.zeros((VOXELS, 2 * CHANNELS), jnp.bfloat16)

    def one_slot(slot, carry):
        for plane in range(PLANES):
            side = 0 if plane == 0 else 2 if plane == PLANES - 1 else 1
            local = (plane - 1) % BRICK * PLANE
            around = [
                bricks[jnp.clip(dst_ref[side * 9 + number, slot], 0, SLOTS + HALO), local : local + PLANE]
                for number in range(9)
            ]
            moved = jnp.dot(
                shift_ref[...], jnp.concatenate(around, axis=0), preferred_element_type=jnp.float32
            ).astype(jnp.bfloat16)
            for number in range(9):
                rows = moved[number * PLANE : (number + 1) * PLANE]
                lanes = slice(number * CHANNELS, (number + 1) * CHANNELS)
                taps_f[slot, plane, :, lanes] = rows[:, :CHANNELS]
                taps_c[slot, plane, :, lanes] = rows[:, CHANNELS:]
        return carry

    lax.fori_loop(0, SLOTS, one_slot, 0)

    core = core_ref[0]
    flipped = jnp.concatenate((flipped_ref[1 - core], flipped_ref[core]), axis=0)
    half = CHANNELS // 2
    for side in range(3):
        tap = taps_c[:, side : side + BRICK].reshape(SLOTS * VOXELS, WIDE)
        part = jnp.dot(flipped, tap, preferred_element_type=jnp.float32)
        for number in range(9):
            block = part[:, number * CHANNELS : (number + 1) * CHANNELS]
            m = side * 9 + number
            for quarter in range(4):
                rows = slice(quarter * 16, quarter * 16 + 16)
                send_ref[quarter, m] = block[:half][rows].astype(jnp.bfloat16)
                keep_ref[quarter, m] = block[half:][rows]
    for quarter in range(4):
        spread = jnp.full((16, CHANNELS), flag_ref[0], jnp.float32)
        send_ref[quarter, 27] = spread.astype(jnp.bfloat16)
        keep_ref[quarter, 27] = spread

    for source, kernel, target in (
        (taps_f, weights_ref, outputs_ref), (taps_c, w_back_ref, grad_ref)
    ):
        total = None
        for side in range(3):
            tap = source[:, side : side + BRICK].reshape(SLOTS * VOXELS, WIDE)
            matrix = kernel[side * 9 : side * 9 + 9].reshape(WIDE, CHANNELS)
            part = jnp.dot(tap, matrix, preferred_element_type=jnp.float32)
            total = part if total is None else total + part
        target[...] = total.astype(jnp.bfloat16).reshape(SLOTS, VOXELS, CHANNELS)


def convolve(fill, core, flag, dst_index, features, cotangent, halos, flipped, shift, weights, w_back):
    vmem = pl.BlockSpec(memory_space=pltpu.VMEM)
    smem = pl.BlockSpec(memory_space=pltpu.SMEM)
    return pl.pallas_call(
        functools.partial(conv_kernel, fill, len(halos)),
        in_specs=[smem] * 3 + [vmem] * (6 + len(halos)),
        out_specs=[vmem] * 4,
        out_shape=[
            jax.ShapeDtypeStruct((SLOTS, VOXELS, CHANNELS), jnp.bfloat16),
            jax.ShapeDtypeStruct((SLOTS, VOXELS, CHANNELS), jnp.bfloat16),
            jax.ShapeDtypeStruct((4, ROWS_M, 16, CHANNELS), jnp.bfloat16),
            jax.ShapeDtypeStruct((4, ROWS_M, 16, CHANNELS), jnp.float32),
        ],
        scratch_shapes=[
            pltpu.VMEM((SLOTS + HALO + 1, VOXELS, 2 * CHANNELS), jnp.bfloat16),
            pltpu.VMEM((SLOTS, PLANES, PLANE, WIDE), jnp.bfloat16),
            pltpu.VMEM((SLOTS, PLANES, PLANE, WIDE), jnp.bfloat16),
        ],
        compiler_params=pltpu.CompilerParams(vmem_limit_bytes=VMEM_LIMIT),
    )(core, flag, dst_index, features, cotangent, *halos, flipped, shift, weights, w_back)


def pass_to(value, step_x, step_y):
    pairs = []
    for gx in range(8):
        for gy in range(32):
            if 0 <= gx + step_x < 8 and 0 <= gy + step_y < 32:
                pairs.append((gx * 32 + gy, (gx + step_x) * 32 + gy + step_y))
    return lax.ppermute(value, AXES, pairs)


def out_of_place(dst_index):
    offsets = np.array([(a, b, c) for a in (-1, 0, 1) for b in (-1, 0, 1) for c in (-1, 0, 1)], np.int32)
    allowed = np.zeros((27, 8), bool)
    for k in range(27):
        for number, heading in enumerate(DIRECTIONS):
            allowed[k, number] = all(heading[d] in (0, offsets[k, d]) for d in range(2))
    wrong = jnp.zeros(dst_index.shape, bool)
    for number in range(8):
        start = SLOTS + STARTS[number]
        inside = (dst_index >= start) & (dst_index < start + LENGTHS[number])
        wrong = wrong | (inside & jnp.asarray(~allowed[:, number : number + 1]))
    return jnp.max(wrong.astype(jnp.float32)).reshape(1)


def sum_everywhere(send, keep):
    arrived = lax.ppermute(send, "c", [(0, 1), (1, 0)])
    chip_sum = (keep + arrived.astype(jnp.float32)).astype(jnp.bfloat16)
    parts = chip_sum.reshape(16, 7, 16, CHANNELS)
    parts = lax.all_to_all(parts, ("x", "y"), 0, 0)
    share = jnp.sum(parts.astype(jnp.float32), axis=0)
    column = jnp.broadcast_to(share[None], (8,) + share.shape)
    column = lax.all_to_all(column, "z", 0, 0)
    share = (jnp.sum(column, axis=0) * (1.0 / (VOXELS * SLOTS))).astype(jnp.bfloat16)
    whole = jnp.broadcast_to(share[None], (16,) + share.shape)
    own = lax.all_to_all(whole, ("x", "y"), 0, 0).reshape(4, ROWS_M, 16, CHANNELS)
    return own, lax.ppermute(own, "c", [(0, 1), (1, 0)])


def spread_kernel(core_ref, own_ref, other_ref, out_ref):
    half = CHANNELS // 2
    core = core_ref[0]
    for number in range(out_ref.shape[0]):
        for quarter in range(4):
            target = out_ref.shape[0] - 1 - number
            for ref, side in ((own_ref, core), (other_ref, 1 - core)):
                begin = pl.multiple_of(side * half + quarter * 16, 16)
                out_ref[target, pl.ds(begin, 16)] = ref[quarter, number].astype(jnp.float32)


def spread_out(core, own, other):
    block = pl.BlockSpec((4, 3, 16, CHANNELS), lambda step: (0, step, 0, 0))
    return pl.pallas_call(
        spread_kernel,
        grid=(9,),
        in_specs=[pl.BlockSpec(memory_space=pltpu.SMEM), block, block],
        out_specs=pl.BlockSpec((3, CHANNELS, CHANNELS), lambda step: (8 - step, 0, 0)),
        out_shape=jax.ShapeDtypeStruct((27, CHANNELS, CHANNELS), jnp.float32),
    )(core, own, other)


def local(features, weights, cotangent, dst_index, recv_slot):
    core = lax.axis_index("c").astype(jnp.int32).reshape(1)
    flag = out_of_place(dst_index)
    layer = layer_matrix()
    expand = jnp.asarray(np.stack((layer[:PLANE].T, layer[PLANE:].T)), jnp.bfloat16)
    layer = jnp.asarray(layer, jnp.bfloat16)
    shift = jnp.asarray(shift_matrix(), jnp.bfloat16)
    flipped = jnp.transpose(features.reshape(SLOTS * VOXELS, CHANNELS)).reshape(2, CHANNELS // 2, SLOTS * VOXELS)
    w_back = jnp.transpose(weights[::-1], (0, 2, 1))

    to_y_down, to_y_up, to_x_down, to_x_up = pack_layers(recv_slot, layer, features, cotangent)
    y_above = pass_to(to_y_down, 0, -1)
    y_below = pass_to(to_y_up, 0, 1)
    x_above = pass_to(jnp.concatenate((to_x_down, y_above[8:10], y_below[8:10]), axis=0), -1, 0)
    x_below = pass_to(jnp.concatenate((to_x_up, y_above[10:], y_below[10:]), axis=0), 1, 0)
    outputs, input_grad, send, keep = convolve(
        fill_layers, core, flag, dst_index, features, cotangent,
        (expand, y_above, y_below, x_above, x_below), flipped, shift, weights, w_back,
    )
    own, other = sum_everywhere(send, keep)

    def with_whole_bricks(results):
        packets = pack_bricks(recv_slot, features, cotangent)
        halos = [pass_to(packet, -heading[0], -heading[1]) for packet, heading in zip(packets, DIRECTIONS)]
        outputs, input_grad, send, keep = convolve(
            fill_bricks, core, flag, dst_index, features, cotangent, halos, flipped, shift, weights, w_back
        )
        return outputs, input_grad, *sum_everywhere(send, keep)

    outputs, input_grad, own, other = lax.cond(
        own[0, 27, 0, 0] > 0, with_whole_bricks, lambda results: results, (outputs, input_grad, own, other)
    )
    return outputs, input_grad, spread_out(core, own, other)


def solution(mesh):
    fine = Mesh(mesh.devices.reshape(4, 2, 4, 8), AXES)
    bricks = P(AXES, None, None)
    return jax.shard_map(
        local,
        mesh=fine,
        in_specs=(bricks, P(), bricks, P(None, AXES), P(AXES)),
        out_specs=(bricks, bricks, P()),
        check_vma=False,
    )
```

```python
import functools

import jax
import jax.numpy as jnp
import numpy as np
from jax import lax
from jax.experimental import pallas as pl
from jax.experimental.pallas import tpu as pltpu
from jax.sharding import Mesh, PartitionSpec as P

BRICK = 4
TILE = 4
BZ = 2
HALO = 40
SLOTS = 8
VOXELS = 64
CHANNELS = 128
PLANE = BRICK * BRICK
PLANES = BRICK + 2
WIDE = 9 * CHANNELS
ROWS_M = 28

DIRECTIONS = ((1, 0), (-1, 0), (0, 1), (0, -1), (1, 1), (1, -1), (-1, 1), (-1, -1))
LENGTHS = (TILE * BZ,) * 4 + (BZ,) * 4
STARTS = tuple(int(start) for start in np.cumsum((0,) + LENGTHS[:-1]))
AXES = ("x", "c", "y", "z")
VMEM_LIMIT = 48 * 1024 * 1024


def shift_matrix():
    picked = np.zeros((9 * PLANE, 9 * PLANE), np.float32)
    for number in range(9):
        for voxel in range(PLANE):
            y = voxel // BRICK + number // 3 - 1 + BRICK
            z = voxel % BRICK + number % 3 - 1 + BRICK
            source = (y // BRICK * 3 + z // BRICK) * PLANE + y % BRICK * BRICK + z % BRICK
            picked[number * PLANE + voxel, source] = 1.0
    return picked


def layer_matrix():
    picked = np.zeros((2 * PLANE, VOXELS), np.float32)
    for side, vy in enumerate((0, BRICK - 1)):
        for vx in range(BRICK):
            for vz in range(BRICK):
                picked[side * PLANE + vx * BRICK + vz, vx * PLANE + vy * BRICK + vz] = 1.0
    return picked


def pack_layers_kernel(slot_ref, layer_ref, features_ref, cotangent_ref, to_y_down, to_y_up, to_x_down, to_x_up,
                       bricks, sides, sems):
    copies = [
        pltpu.make_async_copy(ref, bricks.at[number, pl.ds(0, SLOTS)], sems.at[number])
        for number, ref in enumerate((features_ref, cotangent_ref))
    ]
    for copy in copies:
        copy.start()
    bricks[:, SLOTS] = jnp.zeros((2, VOXELS, CHANNELS), jnp.bfloat16)
    sides[:, SLOTS] = jnp.zeros((2, 2 * PLANE, CHANNELS), jnp.bfloat16)
    for copy in copies:
        copy.wait()
    layer = layer_ref[...]
    for kind in range(2):
        beside = jnp.concatenate([bricks[kind, slot] for slot in range(SLOTS)], axis=1)
        picked = jnp.dot(layer, beside, preferred_element_type=jnp.float32).astype(jnp.bfloat16)
        for slot in range(SLOTS):
            sides[kind, slot] = picked[:, slot * CHANNELS : (slot + 1) * CHANNELS]

    def put(packet, position, halo, source, begin):
        slot = jnp.clip(slot_ref[halo], 0, SLOTS)
        packet[position, :, :CHANNELS] = source[0, slot, begin : begin + PLANE]
        packet[position, :, CHANNELS:] = source[1, slot, begin : begin + PLANE]

    for packet, numbers, begin in (
        (to_y_down, (2, 4, 6), 0),
        (to_y_up, (3, 5, 7), PLANE),
    ):
        position = 0
        for number in numbers:
            for halo in range(STARTS[number], STARTS[number] + LENGTHS[number]):
                put(packet, position, halo, sides, begin)
                position += 1
    for packet, number, begin in ((to_x_down, 0, 0), (to_x_up, 1, VOXELS - PLANE)):
        for position in range(LENGTHS[number]):
            put(packet, position, STARTS[number] + position, bricks, begin)


def pack_layers(recv_slot, layer, features, cotangent):
    vmem = pl.BlockSpec(memory_space=pltpu.VMEM)
    smem = pl.BlockSpec(memory_space=pltpu.SMEM)
    hbm = pl.BlockSpec(memory_space=pltpu.HBM)
    return pl.pallas_call(
        pack_layers_kernel,
        in_specs=[smem, vmem, hbm, hbm],
        out_specs=[vmem] * 4,
        out_shape=[
            jax.ShapeDtypeStruct((length, PLANE, 2 * CHANNELS), jnp.bfloat16) for length in (12, 12, 8, 8)
        ],
        scratch_shapes=[
            pltpu.VMEM((2, SLOTS + 1, VOXELS, CHANNELS), jnp.bfloat16),
            pltpu.VMEM((2, SLOTS + 1, 2 * PLANE, CHANNELS), jnp.bfloat16),
            pltpu.SemaphoreType.DMA((2,)),
        ],
        compiler_params=pltpu.CompilerParams(vmem_limit_bytes=VMEM_LIMIT),
    )(recv_slot, layer, features, cotangent)


def fill_bricks(halos, lanes, bricks):
    begin_at = SLOTS
    for halo in halos:
        bricks[begin_at : begin_at + halo.shape[0]] = halo[:, :, lanes]
        begin_at += halo.shape[0]


def fill_layers(halos, lanes, bricks):
    expand_ref, y_above, y_below, x_above, x_below = halos
    for position in range(SLOTS):
        bricks[SLOTS + STARTS[0] + position, :PLANE] = x_above[position, :, lanes]
        bricks[SLOTS + STARTS[1] + position, VOXELS - PLANE :] = x_below[position, :, lanes]
    for side, faces, number in ((0, y_above, 2), (1, y_below, 3)):
        corner = SLOTS + 2 * side
        tiles = [faces[position, :, lanes] for position in range(SLOTS)]
        tiles += [x_above[corner + position, :, lanes] for position in range(BZ)]
        tiles += [x_below[corner + position, :, lanes] for position in range(BZ)]
        targets = list(range(STARTS[number], STARTS[number] + SLOTS))
        targets += list(range(STARTS[4 + side], STARTS[4 + side] + BZ))
        targets += list(range(STARTS[6 + side], STARTS[6 + side] + BZ))
        whole = jnp.dot(
            expand_ref[side], jnp.concatenate(tiles, axis=1), preferred_element_type=jnp.float32
        ).astype(jnp.bfloat16)
        for position, target in enumerate(targets):
            bricks[SLOTS + target] = whole[:, position * CHANNELS : (position + 1) * CHANNELS]


def build_taps(fill, halos, lanes, own_ref, dst_ref, shift_ref, bricks, taps):
    bricks[:SLOTS] = own_ref[...]
    fill(halos, lanes, bricks)
    bricks[SLOTS + HALO] = jnp.zeros((VOXELS, CHANNELS), jnp.bfloat16)

    def around(slot, plane):
        side = 0 if plane == 0 else 2 if plane == PLANES - 1 else 1
        local = (plane - 1) % BRICK * PLANE
        return jnp.concatenate(
            [
                bricks[jnp.clip(dst_ref[slot, side * 9 + number], 0, SLOTS + HALO), local : local + PLANE]
                for number in range(9)
            ],
            axis=0,
        )

    def one_slot(slot, carry):
        for plane in range(0, PLANES, 2):
            pair = jnp.concatenate((around(slot, plane), around(slot, plane + 1)), axis=1)
            moved = jnp.dot(shift_ref[...], pair, preferred_element_type=jnp.float32).astype(jnp.bfloat16)
            for number in range(9):
                rows = moved[number * PLANE : (number + 1) * PLANE]
                target = slice(number * CHANNELS, (number + 1) * CHANNELS)
                taps[slot, plane, :, target] = rows[:, :CHANNELS]
                taps[slot, plane + 1, :, target] = rows[:, CHANNELS:]
        return carry

    lax.fori_loop(0, SLOTS, one_slot, 0)


def weight_kernel(fill, count, core_ref, flag_ref, dst_ref, cotangent_ref, *rest):
    halos = rest[:count]
    flipped_ref, shift_ref, send_ref, keep_ref, taps, bricks = rest[count:]
    build_taps(fill, halos, slice(CHANNELS, 2 * CHANNELS), cotangent_ref, dst_ref, shift_ref, bricks, taps)
    core = core_ref[0]
    flipped = jnp.concatenate((flipped_ref[1 - core], flipped_ref[core]), axis=0)
    half = CHANNELS // 2
    for side in range(3):
        tap = taps[:, side : side + BRICK].reshape(SLOTS * VOXELS, WIDE)
        part = jnp.dot(flipped, tap, preferred_element_type=jnp.float32)
        for number in range(9):
            block = part[:, number * CHANNELS : (number + 1) * CHANNELS]
            m = side * 9 + number
            for quarter in range(4):
                rows = slice(quarter * 16, quarter * 16 + 16)
                send_ref[quarter, m] = block[:half][rows].astype(jnp.bfloat16)
                keep_ref[quarter, m] = block[half:][rows]
    for quarter in range(4):
        spread = jnp.full((16, CHANNELS), flag_ref[0], jnp.float32)
        send_ref[quarter, 27] = spread.astype(jnp.bfloat16)
        keep_ref[quarter, 27] = spread


def output_kernel(fill, count, dst_ref, features_ref, *rest):
    halos = rest[:count]
    shift_ref, weights_ref, taps_c, outputs_ref, grad_ref, bricks, taps_f = rest[count:]
    build_taps(fill, halos, slice(0, CHANNELS), features_ref, dst_ref, shift_ref, bricks, taps_f)
    outputs = None
    grad = None
    for side in range(3):
        tap = taps_f[:, side : side + BRICK].reshape(SLOTS * VOXELS, WIDE)
        matrix = weights_ref[side * 9 : side * 9 + 9].reshape(WIDE, CHANNELS)
        part = jnp.dot(tap, matrix, preferred_element_type=jnp.float32)
        outputs = part if outputs is None else outputs + part
    outputs_ref[...] = outputs.astype(jnp.bfloat16).reshape(SLOTS, VOXELS, CHANNELS)
    for side in range(3):
        tap = taps_c[:, side : side + BRICK].reshape(SLOTS * VOXELS, WIDE)
        matrix = jnp.concatenate([weights_ref[26 - side * 9 - number] for number in range(9)], axis=1)
        part = lax.dot_general(tap, matrix, (((1,), (1,)), ((), ())), preferred_element_type=jnp.float32)
        grad = part if grad is None else grad + part
    grad_ref[...] = grad.astype(jnp.bfloat16).reshape(SLOTS, VOXELS, CHANNELS)


def weight_sums(fill, core, flag, dst, cotangent, halos, flipped, shift):
    vmem = pl.BlockSpec(memory_space=pltpu.VMEM)
    smem = pl.BlockSpec(memory_space=pltpu.SMEM)
    return pl.pallas_call(
        functools.partial(weight_kernel, fill, len(halos)),
        in_specs=[smem] * 3 + [vmem] * (3 + len(halos)),
        out_specs=[vmem] * 3,
        out_shape=[
            jax.ShapeDtypeStruct((4, ROWS_M, 16, CHANNELS), jnp.bfloat16),
            jax.ShapeDtypeStruct((4, ROWS_M, 16, CHANNELS), jnp.float32),
            jax.ShapeDtypeStruct((SLOTS, PLANES, PLANE, WIDE), jnp.bfloat16),
        ],
        scratch_shapes=[pltpu.VMEM((SLOTS + HALO + 1, VOXELS, CHANNELS), jnp.bfloat16)],
        compiler_params=pltpu.CompilerParams(vmem_limit_bytes=VMEM_LIMIT),
        cost_estimate=pl.CostEstimate(flops=2 * 512 * 3456 * 128 * 2, bytes_accessed=4_000_000, transcendentals=0),
    )(core, flag, dst, cotangent, *halos, flipped, shift)


def both_outputs(fill, dst, features, halos, shift, weights, taps):
    vmem = pl.BlockSpec(memory_space=pltpu.VMEM)
    smem = pl.BlockSpec(memory_space=pltpu.SMEM)
    return pl.pallas_call(
        functools.partial(output_kernel, fill, len(halos)),
        in_specs=[smem] + [vmem] * (4 + len(halos)),
        out_specs=[vmem] * 2,
        out_shape=[jax.ShapeDtypeStruct((SLOTS, VOXELS, CHANNELS), jnp.bfloat16)] * 2,
        scratch_shapes=[
            pltpu.VMEM((SLOTS + HALO + 1, VOXELS, CHANNELS), jnp.bfloat16),
            pltpu.VMEM((SLOTS, PLANES, PLANE, WIDE), jnp.bfloat16),
        ],
        compiler_params=pltpu.CompilerParams(vmem_limit_bytes=VMEM_LIMIT),
        cost_estimate=pl.CostEstimate(flops=2 * 512 * 3456 * 128 * 3, bytes_accessed=4_000_000, transcendentals=0),
    )(dst, features, *halos, shift, weights, taps)


def pack_bricks_kernel(slot_ref, features_ref, cotangent_ref, *packets):
    begin_at = 0
    for packet in packets:
        for position in range(packet.shape[0]):
            slot = slot_ref[begin_at + position]
            row = jnp.clip(slot, 0, SLOTS - 1)

            @pl.when(slot < SLOTS)
            def _():
                packet[position, :, :CHANNELS] = features_ref[row]
                packet[position, :, CHANNELS:] = cotangent_ref[row]

            @pl.when(slot >= SLOTS)
            def _():
                packet[position] = jnp.zeros((VOXELS, 2 * CHANNELS), jnp.bfloat16)

        begin_at += packet.shape[0]


def pack_bricks(recv_slot, features, cotangent):
    vmem = pl.BlockSpec(memory_space=pltpu.VMEM)
    return pl.pallas_call(
        pack_bricks_kernel,
        in_specs=[pl.BlockSpec(memory_space=pltpu.SMEM), vmem, vmem],
        out_specs=[vmem] * 8,
        out_shape=[
            jax.ShapeDtypeStruct((length, VOXELS, 2 * CHANNELS), jnp.bfloat16) for length in LENGTHS
        ],
        compiler_params=pltpu.CompilerParams(vmem_limit_bytes=VMEM_LIMIT),
    )(recv_slot, features, cotangent)


def pass_to(value, step_x, step_y):
    pairs = []
    for gx in range(8):
        for gy in range(32):
            if 0 <= gx + step_x < 8 and 0 <= gy + step_y < 32:
                pairs.append((gx * 32 + gy, (gx + step_x) * 32 + gy + step_y))
    return lax.ppermute(value, AXES, pairs)


def out_of_place(dst_index):
    offsets = np.array([(a, b, c) for a in (-1, 0, 1) for b in (-1, 0, 1) for c in (-1, 0, 1)], np.int32)
    allowed = np.zeros((27, 8), bool)
    for k in range(27):
        for number, heading in enumerate(DIRECTIONS):
            allowed[k, number] = all(heading[d] in (0, offsets[k, d]) for d in range(2))
    wrong = jnp.zeros(dst_index.shape, bool)
    for number in range(8):
        start = SLOTS + STARTS[number]
        inside = (dst_index >= start) & (dst_index < start + LENGTHS[number])
        wrong = wrong | (inside & jnp.asarray(~allowed[:, number][None]))
    return jnp.max(wrong.astype(jnp.float32)).reshape(1)


def sum_everywhere(send, keep):
    arrived = lax.ppermute(send, "c", [(0, 1), (1, 0)])
    chip_sum = (keep + arrived.astype(jnp.float32)).astype(jnp.bfloat16)
    parts = chip_sum.reshape(16, 7, 16, CHANNELS)
    parts = lax.all_to_all(parts, ("x", "y"), 0, 0)
    share = jnp.sum(parts.astype(jnp.float32), axis=0)
    column = jnp.broadcast_to(share[None], (8,) + share.shape)
    column = lax.all_to_all(column, "z", 0, 0)
    share = (jnp.sum(column, axis=0) * (1.0 / (VOXELS * SLOTS))).astype(jnp.bfloat16)
    whole = jnp.broadcast_to(share[None], (16,) + share.shape)
    own = lax.all_to_all(whole, ("x", "y"), 0, 0).reshape(4, ROWS_M, 16, CHANNELS)
    return own, lax.ppermute(own, "c", [(0, 1), (1, 0)])


def spread_kernel(core_ref, own_ref, other_ref, out_ref, whole, sems):
    half = CHANNELS // 2
    core = core_ref[0]
    copies = []
    for chunk in range(9):
        for m in range(3 * chunk, 3 * chunk + 3):
            for quarter in range(4):
                for ref, side in ((own_ref, core), (other_ref, 1 - core)):
                    begin = pl.multiple_of(side * half + quarter * 16, 16)
                    whole[26 - m, pl.ds(begin, 16)] = ref[quarter, m].astype(jnp.float32)
        rows = pl.ds(24 - 3 * chunk, 3)
        copies.append(pltpu.make_async_copy(whole.at[rows], out_ref.at[rows], sems.at[chunk]))
        copies[-1].start()
    for copy in copies:
        copy.wait()


def spread_out(core, own, other):
    vmem = pl.BlockSpec(memory_space=pltpu.VMEM)
    return pl.pallas_call(
        spread_kernel,
        in_specs=[pl.BlockSpec(memory_space=pltpu.SMEM), vmem, vmem],
        out_specs=pl.BlockSpec(memory_space=pltpu.HBM),
        out_shape=jax.ShapeDtypeStruct((27, CHANNELS, CHANNELS), jnp.float32),
        scratch_shapes=[
            pltpu.VMEM((27, CHANNELS, CHANNELS), jnp.float32),
            pltpu.SemaphoreType.DMA((9,)),
        ],
        compiler_params=pltpu.CompilerParams(vmem_limit_bytes=VMEM_LIMIT),
    )(core, own, other)


def local(features, weights, cotangent, dst_index, recv_slot):
    core = lax.axis_index("c").astype(jnp.int32).reshape(1)
    dst = dst_index.T
    flag = out_of_place(dst)
    layer = layer_matrix()
    expand = jnp.asarray(np.stack((layer[:PLANE].T, layer[PLANE:].T)), jnp.bfloat16)
    layer = jnp.asarray(layer, jnp.bfloat16)
    shift = jnp.asarray(shift_matrix(), jnp.bfloat16)
    flipped = jnp.transpose(features.reshape(SLOTS * VOXELS, CHANNELS)).reshape(2, CHANNELS // 2, SLOTS * VOXELS)

    to_y_down, to_y_up, to_x_down, to_x_up = pack_layers(recv_slot, layer, features, cotangent)
    y_above = pass_to(to_y_down, 0, -1)
    y_below = pass_to(to_y_up, 0, 1)
    x_above = pass_to(jnp.concatenate((to_x_down, y_above[8:10], y_below[8:10]), axis=0), -1, 0)
    x_below = pass_to(jnp.concatenate((to_x_up, y_above[10:], y_below[10:]), axis=0), 1, 0)
    halos = (expand, y_above, y_below, x_above, x_below)
    send, keep, taps = weight_sums(fill_layers, core, flag, dst, cotangent, halos, flipped, shift)
    outputs, input_grad = both_outputs(fill_layers, dst, features, halos, shift, weights, taps)
    own, other = sum_everywhere(send, keep)

    def with_whole_bricks(results):
        packets = pack_bricks(recv_slot, features, cotangent)
        halos = [pass_to(packet, -heading[0], -heading[1]) for packet, heading in zip(packets, DIRECTIONS)]
        send, keep, taps = weight_sums(fill_bricks, core, flag, dst, cotangent, halos, flipped, shift)
        outputs, input_grad = both_outputs(fill_bricks, dst, features, halos, shift, weights, taps)
        return outputs, input_grad, *sum_everywhere(send, keep)

    outputs, input_grad, own, other = lax.cond(
        own[0, 27, 0, 0] > 0, with_whole_bricks, lambda results: results, (outputs, input_grad, own, other)
    )
    return outputs, input_grad, spread_out(core, own, other)


def solution(mesh):
    fine = Mesh(mesh.devices.reshape(4, 2, 4, 8), AXES)
    bricks = P(AXES, None, None)
    return jax.shard_map(
        local,
        mesh=fine,
        in_specs=(bricks, P(), bricks, P(None, AXES), P(AXES)),
        out_specs=(bricks, bricks, P()),
        check_vma=False,
    )
```

```python
import functools

import jax
import jax.numpy as jnp
import numpy as np
from jax import lax
from jax.experimental import pallas as pl
from jax.experimental.pallas import tpu as pltpu
from jax.sharding import Mesh, PartitionSpec as P

BRICK = 4
TILE = 4
BZ = 2
HALO = 40
SLOTS = 8
VOXELS = 64
CHANNELS = 128
PLANE = BRICK * BRICK
PLANES = BRICK + 2
WIDE = 9 * CHANNELS
ROWS_M = 28

DIRECTIONS = ((1, 0), (-1, 0), (0, 1), (0, -1), (1, 1), (1, -1), (-1, 1), (-1, -1))
LENGTHS = (TILE * BZ,) * 4 + (BZ,) * 4
STARTS = tuple(int(start) for start in np.cumsum((0,) + LENGTHS[:-1]))
AXES = ("x", "c", "y", "z")
VMEM_LIMIT = 48 * 1024 * 1024


def where_equal(left, right):
    return jnp.where(left == right, 1.0, 0.0).astype(jnp.bfloat16)


def shift_matrix():
    row = lax.broadcasted_iota(jnp.int32, (9 * PLANE, 9 * PLANE), 0)
    column = lax.broadcasted_iota(jnp.int32, (9 * PLANE, 9 * PLANE), 1)
    number = row >> 4
    third = (number * 11) >> 5
    y = ((row >> 2) & 3) + third + 3
    z = (row & 3) + number - 3 * third + 3
    return where_equal(column, ((y >> 2) * 3 + (z >> 2)) * PLANE + (y & 3) * BRICK + (z & 3))


def layer_matrix():
    row = lax.broadcasted_iota(jnp.int32, (2 * PLANE, VOXELS), 0)
    column = lax.broadcasted_iota(jnp.int32, (2 * PLANE, VOXELS), 1)
    return where_equal(column, ((row >> 2) & 3) * PLANE + (row >> 4) * 12 + (row & 3))


def expand_matrix(side):
    row = lax.broadcasted_iota(jnp.int32, (VOXELS, PLANE), 0)
    column = lax.broadcasted_iota(jnp.int32, (VOXELS, PLANE), 1)
    return where_equal(row, (column >> 2) * PLANE + side * 12 + (column & 3))


def pack_layers_kernel(place_ref, slot_ref, features_ref, cotangent_ref, to_first, to_second, to_sibling, to_outer,
                       bricks, sides, sems):
    copies = [
        pltpu.make_async_copy(ref, bricks.at[number, pl.ds(0, SLOTS)], sems.at[number])
        for number, ref in enumerate((features_ref, cotangent_ref))
    ]
    for copy in copies:
        copy.start()
    bricks[:, SLOTS] = jnp.zeros((2, VOXELS, CHANNELS), jnp.bfloat16)
    sides[:, SLOTS] = jnp.zeros((2, 2 * PLANE, CHANNELS), jnp.bfloat16)
    core = place_ref[0]
    odd = place_ref[1]
    layer = layer_matrix()
    for copy in copies:
        copy.wait()
    for kind in range(2):
        beside = jnp.concatenate([bricks[kind, slot] for slot in range(SLOTS)], axis=1)
        picked = jnp.dot(layer, beside, preferred_element_type=jnp.float32).astype(jnp.bfloat16)
        for slot in range(SLOTS):
            sides[kind, slot] = picked[:, slot * CHANNELS : (slot + 1) * CHANNELS]

    def put(packet, position, halo, source, begin):
        slot = jnp.clip(slot_ref[halo], 0, SLOTS)
        rows = pl.ds(begin, PLANE)
        packet[position, :, :CHANNELS] = source[0, slot, rows]
        packet[position, :, CHANNELS:] = source[1, slot, rows]

    for packet, up in ((to_first, 1 - odd), (to_second, odd)):
        begin = pl.multiple_of(up * PLANE, PLANE)
        position = 0
        for number in (2, 4, 6):
            for halo in range(LENGTHS[number]):
                put(packet, position, STARTS[number] + up * LENGTHS[number] + halo, sides, begin)
                position += 1
    for packet, up in ((to_sibling, 1 - core), (to_outer, core)):
        begin = pl.multiple_of(up * (VOXELS - PLANE), PLANE)
        for position in range(LENGTHS[0]):
            put(packet, position, up * LENGTHS[0] + position, bricks, begin)


def pack_layers(place, recv_slot, features, cotangent):
    vmem = pl.BlockSpec(memory_space=pltpu.VMEM)
    smem = pl.BlockSpec(memory_space=pltpu.SMEM)
    hbm = pl.BlockSpec(memory_space=pltpu.HBM)
    return pl.pallas_call(
        pack_layers_kernel,
        in_specs=[smem, smem, hbm, hbm],
        out_specs=[vmem] * 4,
        out_shape=[
            jax.ShapeDtypeStruct((length, PLANE, 2 * CHANNELS), jnp.bfloat16) for length in (12, 12, 8, 8)
        ],
        scratch_shapes=[
            pltpu.VMEM((2, SLOTS + 1, VOXELS, CHANNELS), jnp.bfloat16),
            pltpu.VMEM((2, SLOTS + 1, 2 * PLANE, CHANNELS), jnp.bfloat16),
            pltpu.SemaphoreType.DMA((2,)),
        ],
        compiler_params=pltpu.CompilerParams(vmem_limit_bytes=VMEM_LIMIT),
    )(place, recv_slot, features, cotangent)


def fill_bricks(core, odd, halos, bricks):
    begin_at = SLOTS
    for halo in halos:
        bricks[begin_at : begin_at + halo.shape[0]] = halo[...]
        begin_at += halo.shape[0]


def fill_layers(core, odd, halos, bricks):
    y_first, y_second, x_sibling, x_outer = halos
    both = ((x_sibling, core), (x_outer, 1 - core))
    for packet, below in both:
        for position in range(SLOTS):
            tile = packet[position]
            target = SLOTS + below * LENGTHS[0] + position
            bricks[target, :PLANE] = tile
            bricks[target, VOXELS - PLANE :] = tile
    for order, (faces, side) in enumerate(((y_first, odd), (y_second, 1 - odd))):
        tiles = [faces[position] for position in range(SLOTS)]
        targets = [STARTS[2] + side * LENGTHS[2] + position for position in range(SLOTS)]
        for packet, below in both:
            for position in range(BZ):
                tiles.append(packet[SLOTS + BZ * order + position])
                targets.append(STARTS[4] + side * BZ + below * 2 * BZ + position)
        whole = jnp.dot(
            expand_matrix(side), jnp.concatenate(tiles, axis=1), preferred_element_type=jnp.float32
        ).astype(jnp.bfloat16)
        for position, target in enumerate(targets):
            bricks[SLOTS + target] = whole[:, position * 2 * CHANNELS : (position + 1) * 2 * CHANNELS]


def out_of_place(dst):
    k = lax.broadcasted_iota(jnp.int32, dst.shape, 1)
    ninth = jnp.where(k >= 18, 2, jnp.where(k >= 9, 1, 0))
    rest = k - 9 * ninth
    offset = (ninth - 1, jnp.where(rest >= 6, 2, jnp.where(rest >= 3, 1, 0)) - 1)
    wrong = jnp.zeros(dst.shape, jnp.float32)
    for number, heading in enumerate(DIRECTIONS):
        start = SLOTS + STARTS[number]
        here = (dst >= start) & (dst < start + LENGTHS[number])
        for axis in range(2):
            if heading[axis]:
                wrong = jnp.where(here & (offset[axis] != heading[axis]), 1.0, wrong)
    return jnp.max(jnp.max(wrong, axis=1, keepdims=True), axis=0, keepdims=True)


def conv_kernel(fill, unroll, count, place_ref, dst_ref, table_ref, features_ref, cotangent_ref, *rest):
    halos = rest[:count]
    (flipped_ref, weights_ref, outputs_ref, grad_ref, send_ref, keep_ref, bricks, taps_f, taps_c) = rest[count:]
    core = place_ref[0]
    bricks[:SLOTS, :, :CHANNELS] = features_ref[...]
    bricks[:SLOTS, :, CHANNELS:] = cotangent_ref[...]
    fill(core, place_ref[1], halos, bricks)
    bricks[SLOTS + HALO] = jnp.zeros((VOXELS, 2 * CHANNELS), jnp.bfloat16)
    shift = shift_matrix()

    def one_slot(slot, carry):
        for plane in range(PLANES):
            side = 0 if plane == 0 else 2 if plane == PLANES - 1 else 1
            local = (plane - 1) % BRICK * PLANE
            around = [
                bricks[jnp.clip(dst_ref[slot, side * 9 + number], 0, SLOTS + HALO), local : local + PLANE]
                for number in range(9)
            ]
            moved = jnp.dot(
                shift, jnp.concatenate(around, axis=0), preferred_element_type=jnp.float32
            ).astype(jnp.bfloat16)
            for number in range(9):
                rows = moved[number * PLANE : (number + 1) * PLANE]
                lanes = slice(number * CHANNELS, (number + 1) * CHANNELS)
                taps_f[slot, plane, :, lanes] = rows[:, :CHANNELS]
                taps_c[slot, plane, :, lanes] = rows[:, CHANNELS:]
        return carry

    lax.fori_loop(0, SLOTS, one_slot, 0, unroll=unroll)

    flipped = jnp.concatenate((flipped_ref[1 - core], flipped_ref[core]), axis=0)
    half = CHANNELS // 2
    for side in range(3):
        tap = taps_c[:, side : side + BRICK].reshape(SLOTS * VOXELS, WIDE)
        part = jnp.dot(flipped, tap, preferred_element_type=jnp.float32)
        for number in range(9):
            block = part[:, number * CHANNELS : (number + 1) * CHANNELS]
            m = side * 9 + number
            for quarter in range(4):
                rows = slice(quarter * 16, quarter * 16 + 16)
                send_ref[quarter, m] = block[:half][rows].astype(jnp.bfloat16)
                keep_ref[quarter, m] = block[half:][rows]
    flag = jnp.broadcast_to(out_of_place(table_ref[...]), (16, CHANNELS))
    for quarter in range(4):
        send_ref[quarter, 27] = flag.astype(jnp.bfloat16)
        keep_ref[quarter, 27] = flag

    outputs = None
    grad = None
    for side in range(3):
        tap = taps_f[:, side : side + BRICK].reshape(SLOTS * VOXELS, WIDE)
        matrix = weights_ref[side * 9 : side * 9 + 9].reshape(WIDE, CHANNELS)
        part = jnp.dot(tap, matrix, preferred_element_type=jnp.float32)
        outputs = part if outputs is None else outputs + part
    outputs_ref[...] = outputs.astype(jnp.bfloat16).reshape(SLOTS, VOXELS, CHANNELS)
    for side in range(3):
        tap = taps_c[:, side : side + BRICK].reshape(SLOTS * VOXELS, WIDE)
        matrix = jnp.concatenate([weights_ref[26 - side * 9 - number] for number in range(9)], axis=1)
        part = lax.dot_general(tap, matrix, (((1,), (1,)), ((), ())), preferred_element_type=jnp.float32)
        grad = part if grad is None else grad + part
    grad_ref[...] = grad.astype(jnp.bfloat16).reshape(SLOTS, VOXELS, CHANNELS)


def convolve(fill, unroll, place, dst, features, cotangent, halos, flipped, weights):
    vmem = pl.BlockSpec(memory_space=pltpu.VMEM)
    smem = pl.BlockSpec(memory_space=pltpu.SMEM)
    return pl.pallas_call(
        functools.partial(conv_kernel, fill, unroll, len(halos)),
        in_specs=[smem, smem] + [vmem] * (5 + len(halos)),
        out_specs=[vmem] * 4,
        out_shape=[
            jax.ShapeDtypeStruct((SLOTS, VOXELS, CHANNELS), jnp.bfloat16),
            jax.ShapeDtypeStruct((SLOTS, VOXELS, CHANNELS), jnp.bfloat16),
            jax.ShapeDtypeStruct((4, ROWS_M, 16, CHANNELS), jnp.bfloat16),
            jax.ShapeDtypeStruct((4, ROWS_M, 16, CHANNELS), jnp.float32),
        ],
        scratch_shapes=[
            pltpu.VMEM((SLOTS + HALO + 1, VOXELS, 2 * CHANNELS), jnp.bfloat16),
            pltpu.VMEM((SLOTS, PLANES, PLANE, WIDE), jnp.bfloat16),
            pltpu.VMEM((SLOTS, PLANES, PLANE, WIDE), jnp.bfloat16),
        ],
        compiler_params=pltpu.CompilerParams(vmem_limit_bytes=VMEM_LIMIT),
    )(place, dst, dst, features, cotangent, *halos, flipped, weights)


def pack_bricks_kernel(slot_ref, features_ref, cotangent_ref, *packets):
    begin_at = 0
    for packet in packets:
        for position in range(packet.shape[0]):
            slot = slot_ref[begin_at + position]
            row = jnp.clip(slot, 0, SLOTS - 1)

            @pl.when(slot < SLOTS)
            def _():
                packet[position, :, :CHANNELS] = features_ref[row]
                packet[position, :, CHANNELS:] = cotangent_ref[row]

            @pl.when(slot >= SLOTS)
            def _():
                packet[position] = jnp.zeros((VOXELS, 2 * CHANNELS), jnp.bfloat16)

        begin_at += packet.shape[0]


def pack_bricks(recv_slot, features, cotangent):
    vmem = pl.BlockSpec(memory_space=pltpu.VMEM)
    return pl.pallas_call(
        pack_bricks_kernel,
        in_specs=[pl.BlockSpec(memory_space=pltpu.SMEM), vmem, vmem],
        out_specs=[vmem] * 8,
        out_shape=[
            jax.ShapeDtypeStruct((length, VOXELS, 2 * CHANNELS), jnp.bfloat16) for length in LENGTHS
        ],
        compiler_params=pltpu.CompilerParams(vmem_limit_bytes=VMEM_LIMIT),
    )(recv_slot, features, cotangent)


def pass_to(value, step_x, step_y):
    pairs = []
    for gx in range(8):
        for gy in range(32):
            if 0 <= gx + step_x < 8 and 0 <= gy + step_y < 32:
                pairs.append((gx * 32 + gy, (gx + step_x) * 32 + gy + step_y))
    return lax.ppermute(value, AXES, pairs)


def sum_everywhere(send, keep):
    arrived = lax.ppermute(send, "c", [(0, 1), (1, 0)])
    chip_sum = (keep + arrived.astype(jnp.float32)).astype(jnp.bfloat16)
    parts = chip_sum.reshape(16, 7, 16, CHANNELS)
    parts = lax.all_to_all(parts, ("x", "y"), 0, 0)
    share = jnp.sum(parts.astype(jnp.float32), axis=0)
    column = jnp.broadcast_to(share[None], (8,) + share.shape)
    column = lax.all_to_all(column, "z", 0, 0)
    share = (jnp.sum(column, axis=0) * (1.0 / (VOXELS * SLOTS))).astype(jnp.bfloat16)
    whole = jnp.broadcast_to(share[None], (16,) + share.shape)
    own = lax.all_to_all(whole, ("x", "y"), 0, 0).reshape(4, ROWS_M, 16, CHANNELS)
    return own, lax.ppermute(own, "c", [(0, 1), (1, 0)])


def spread_kernel(core_ref, own_ref, other_ref, out_ref, whole, sems):
    half = CHANNELS // 2
    core = core_ref[0]
    copies = []
    for chunk in range(9):
        for m in range(3 * chunk, 3 * chunk + 3):
            for quarter in range(4):
                for ref, side in ((own_ref, core), (other_ref, 1 - core)):
                    begin = pl.multiple_of(side * half + quarter * 16, 16)
                    whole[26 - m, pl.ds(begin, 16)] = ref[quarter, m].astype(jnp.float32)
        rows = pl.ds(24 - 3 * chunk, 3)
        copies.append(pltpu.make_async_copy(whole.at[rows], out_ref.at[rows], sems.at[chunk]))
        copies[-1].start()
    for copy in copies:
        copy.wait()


def spread_out(core, own, other):
    vmem = pl.BlockSpec(memory_space=pltpu.VMEM)
    return pl.pallas_call(
        spread_kernel,
        in_specs=[pl.BlockSpec(memory_space=pltpu.SMEM), vmem, vmem],
        out_specs=pl.BlockSpec(memory_space=pltpu.HBM),
        out_shape=jax.ShapeDtypeStruct((27, CHANNELS, CHANNELS), jnp.float32),
        scratch_shapes=[
            pltpu.VMEM((27, CHANNELS, CHANNELS), jnp.float32),
            pltpu.SemaphoreType.DMA((9,)),
        ],
        compiler_params=pltpu.CompilerParams(vmem_limit_bytes=VMEM_LIMIT),
    )(core, own, other)


def local(features, weights, cotangent, dst_index, recv_slot):
    core = lax.axis_index("c").astype(jnp.int32)
    first = core.reshape(1)
    place = jnp.stack((core, (lax.axis_index("z") % 2).astype(jnp.int32)))
    dst = dst_index.T
    flipped = jnp.transpose(features.reshape(SLOTS * VOXELS, CHANNELS)).reshape(2, CHANNELS // 2, SLOTS * VOXELS)

    to_first, to_second, to_sibling, to_outer = pack_layers(place, recv_slot, features, cotangent)
    y_first = lax.ppermute(to_first, ("y", "z"), [(gy, gy ^ 1) for gy in range(32)])
    y_second = lax.ppermute(to_second, ("y", "z"), [(gy, ((gy + 1) ^ 1) - 1) for gy in range(1, 31)])

    def relayed(packet, up):
        corners = [lax.dynamic_slice_in_dim(value, SLOTS + BZ * up, BZ, axis=0) for value in (y_first, y_second)]
        return jnp.concatenate((packet, *corners), axis=0)

    x_outer = lax.ppermute(relayed(to_outer, core), ("x", "c"), [(2 * x + 1, 2 * x + 2) for x in range(3)]
                           + [(2 * x + 2, 2 * x + 1) for x in range(3)])
    x_sibling = lax.ppermute(relayed(to_sibling, 1 - core), "c", [(0, 1), (1, 0)])
    halos = (y_first, y_second, x_sibling, x_outer)
    outputs, input_grad, send, keep = convolve(
        fill_layers, SLOTS, place, dst, features, cotangent, halos, flipped, weights
    )
    own, other = sum_everywhere(send, keep)

    def with_whole_bricks(results):
        packets = pack_bricks(recv_slot, features, cotangent)
        halos = [pass_to(packet, -heading[0], -heading[1]) for packet, heading in zip(packets, DIRECTIONS)]
        outputs, input_grad, send, keep = convolve(
            fill_bricks, 1, place, dst, features, cotangent, halos, flipped, weights
        )
        return outputs, input_grad, spread_out(first, *sum_everywhere(send, keep))

    def as_they_are(results):
        outputs, input_grad, own, other = results
        return outputs, input_grad, spread_out(first, own, other)

    return lax.cond(
        own[0, 27, 0, 0] > 0, with_whole_bricks, as_they_are, (outputs, input_grad, own, other)
    )


def solution(mesh):
    fine = Mesh(mesh.devices.reshape(4, 2, 4, 8), AXES)
    bricks = P(AXES, None, None)
    return jax.shard_map(
        local,
        mesh=fine,
        in_specs=(bricks, P(), bricks, P(None, AXES), P(AXES)),
        out_specs=(bricks, bricks, P()),
        check_vma=False,
    )
```

```python
import functools

import jax
import jax.numpy as jnp
import numpy as np
from jax import lax
from jax.experimental import pallas as pl
from jax.experimental.pallas import tpu as pltpu
from jax.sharding import Mesh, PartitionSpec as P

BRICK = 4
TILE = 4
BZ = 2
HALO = 40
SLOTS = 8
VOXELS = 64
CHANNELS = 128
PLANE = BRICK * BRICK
PLANES = BRICK + 2
WIDE = 9 * CHANNELS
ROWS_M = 28

DIRECTIONS = ((1, 0), (-1, 0), (0, 1), (0, -1), (1, 1), (1, -1), (-1, 1), (-1, -1))
LENGTHS = (TILE * BZ,) * 4 + (BZ,) * 4
STARTS = tuple(int(start) for start in np.cumsum((0,) + LENGTHS[:-1]))
AXES = ("x", "c", "y", "z")
VMEM_LIMIT = 48 * 1024 * 1024


def where_equal(left, right):
    return jnp.where(left == right, 1.0, 0.0).astype(jnp.bfloat16)


def shift_matrix():
    row = lax.broadcasted_iota(jnp.int32, (9 * PLANE, 9 * PLANE), 0)
    column = lax.broadcasted_iota(jnp.int32, (9 * PLANE, 9 * PLANE), 1)
    number = row >> 4
    third = (number * 11) >> 5
    y = ((row >> 2) & 3) + third + 3
    z = (row & 3) + number - 3 * third + 3
    return where_equal(column, ((y >> 2) * 3 + (z >> 2)) * PLANE + (y & 3) * BRICK + (z & 3))


def layer_matrix():
    row = lax.broadcasted_iota(jnp.int32, (2 * PLANE, VOXELS), 0)
    column = lax.broadcasted_iota(jnp.int32, (2 * PLANE, VOXELS), 1)
    return where_equal(column, ((row >> 2) & 3) * PLANE + (row >> 4) * 12 + (row & 3))


def expand_matrix(side):
    row = lax.broadcasted_iota(jnp.int32, (VOXELS, PLANE), 0)
    column = lax.broadcasted_iota(jnp.int32, (VOXELS, PLANE), 1)
    return where_equal(row, (column >> 2) * PLANE + side * 12 + (column & 3))


def pack_layers_kernel(place_ref, slot_ref, features_ref, cotangent_ref, to_first, to_second, to_sibling, to_outer,
                       bricks, sides, sems):
    copies = [
        pltpu.make_async_copy(ref, bricks.at[number, pl.ds(0, SLOTS)], sems.at[number])
        for number, ref in enumerate((features_ref, cotangent_ref))
    ]
    for copy in copies:
        copy.start()
    bricks[:, SLOTS] = jnp.zeros((2, VOXELS, CHANNELS), jnp.bfloat16)
    sides[:, SLOTS] = jnp.zeros((2, 2 * PLANE, CHANNELS), jnp.bfloat16)
    core = place_ref[0]
    odd = place_ref[1]
    layer = layer_matrix()
    for copy in copies:
        copy.wait()
    for kind in range(2):
        beside = jnp.concatenate([bricks[kind, slot] for slot in range(SLOTS)], axis=1)
        picked = jnp.dot(layer, beside, preferred_element_type=jnp.float32).astype(jnp.bfloat16)
        for slot in range(SLOTS):
            sides[kind, slot] = picked[:, slot * CHANNELS : (slot + 1) * CHANNELS]

    def put(packet, position, halo, source, begin):
        slot = jnp.clip(slot_ref[halo], 0, SLOTS)
        rows = pl.ds(begin, PLANE)
        packet[position, :, :CHANNELS] = source[0, slot, rows]
        packet[position, :, CHANNELS:] = source[1, slot, rows]

    for packet, up in ((to_first, 1 - odd), (to_second, odd)):
        begin = pl.multiple_of(up * PLANE, PLANE)
        position = 0
        for number in (2, 4, 6):
            for halo in range(LENGTHS[number]):
                put(packet, position, STARTS[number] + up * LENGTHS[number] + halo, sides, begin)
                position += 1
    for packet, up in ((to_sibling, 1 - core), (to_outer, core)):
        begin = pl.multiple_of(up * (VOXELS - PLANE), PLANE)
        for position in range(LENGTHS[0]):
            put(packet, position, up * LENGTHS[0] + position, bricks, begin)


def pack_layers(place, recv_slot, features, cotangent):
    vmem = pl.BlockSpec(memory_space=pltpu.VMEM)
    smem = pl.BlockSpec(memory_space=pltpu.SMEM)
    hbm = pl.BlockSpec(memory_space=pltpu.HBM)
    return pl.pallas_call(
        pack_layers_kernel,
        in_specs=[smem, smem, hbm, hbm],
        out_specs=[vmem] * 4,
        out_shape=[
            jax.ShapeDtypeStruct((length, PLANE, 2 * CHANNELS), jnp.bfloat16) for length in (12, 12, 8, 8)
        ],
        scratch_shapes=[
            pltpu.VMEM((2, SLOTS + 1, VOXELS, CHANNELS), jnp.bfloat16),
            pltpu.VMEM((2, SLOTS + 1, 2 * PLANE, CHANNELS), jnp.bfloat16),
            pltpu.SemaphoreType.DMA((2,)),
        ],
        compiler_params=pltpu.CompilerParams(vmem_limit_bytes=VMEM_LIMIT),
    )(place, recv_slot, features, cotangent)


def fill_bricks(core, odd, halos, bricks):
    begin_at = SLOTS
    for halo in halos:
        bricks[begin_at : begin_at + halo.shape[0]] = halo[...]
        begin_at += halo.shape[0]


def fill_layers(core, odd, halos, bricks):
    y_first, y_second, x_sibling, x_outer = halos
    both = ((x_sibling, core), (x_outer, 1 - core))
    for packet, below in both:
        for position in range(SLOTS):
            tile = packet[position]
            target = SLOTS + below * LENGTHS[0] + position
            for begin in range(0, VOXELS, PLANE):
                bricks[target, begin : begin + PLANE] = tile
    for order, (faces, side) in enumerate(((y_first, odd), (y_second, 1 - odd))):
        tiles = [faces[position] for position in range(SLOTS)]
        targets = [STARTS[2] + side * LENGTHS[2] + position for position in range(SLOTS)]
        for packet, below in both:
            for position in range(BZ):
                tiles.append(packet[SLOTS + BZ * order + position])
                targets.append(STARTS[4] + side * BZ + below * 2 * BZ + position)
        whole = jnp.dot(
            expand_matrix(side), jnp.concatenate(tiles, axis=1), preferred_element_type=jnp.float32
        ).astype(jnp.bfloat16)
        for position, target in enumerate(targets):
            bricks[SLOTS + target] = whole[:, position * 2 * CHANNELS : (position + 1) * 2 * CHANNELS]


def out_of_place(dst):
    k = lax.broadcasted_iota(jnp.int32, dst.shape, 1)
    ninth = jnp.where(k >= 18, 2, jnp.where(k >= 9, 1, 0))
    rest = k - 9 * ninth
    offset = (ninth - 1, jnp.where(rest >= 6, 2, jnp.where(rest >= 3, 1, 0)) - 1)
    wrong = jnp.zeros(dst.shape, jnp.float32)
    for number, heading in enumerate(DIRECTIONS):
        start = SLOTS + STARTS[number]
        here = (dst >= start) & (dst < start + LENGTHS[number])
        for axis in range(2):
            if heading[axis]:
                wrong = jnp.where(here & (offset[axis] != heading[axis]), 1.0, wrong)
    return jnp.max(jnp.max(wrong, axis=1, keepdims=True), axis=0, keepdims=True)


def conv_kernel(fill, unroll, count, place_ref, dst_ref, table_ref, features_ref, cotangent_ref, *rest):
    halos = rest[:count]
    (flipped_ref, weights_ref, outputs_ref, grad_ref, send_ref, keep_ref, bricks, taps_f, taps_c) = rest[count:]
    core = place_ref[0]
    bricks[:SLOTS, :, :CHANNELS] = features_ref[...]
    bricks[:SLOTS, :, CHANNELS:] = cotangent_ref[...]
    fill(core, place_ref[1], halos, bricks)
    bricks[SLOTS + HALO] = jnp.zeros((VOXELS, 2 * CHANNELS), jnp.bfloat16)
    shift = shift_matrix()

    def one_slot(slot, carry):
        for plane in range(PLANES):
            side = 0 if plane == 0 else 2 if plane == PLANES - 1 else 1
            local = (plane - 1) % BRICK * PLANE
            around = [
                bricks[jnp.clip(dst_ref[slot, side * 9 + number], 0, SLOTS + HALO), local : local + PLANE]
                for number in range(9)
            ]
            moved = jnp.dot(
                shift, jnp.concatenate(around, axis=0), preferred_element_type=jnp.float32
            ).astype(jnp.bfloat16)
            for number in range(9):
                rows = moved[number * PLANE : (number + 1) * PLANE]
                lanes = slice(number * CHANNELS, (number + 1) * CHANNELS)
                taps_f[slot, plane, :, lanes] = rows[:, :CHANNELS]
                taps_c[slot, plane, :, lanes] = rows[:, CHANNELS:]
        return carry

    lax.fori_loop(0, SLOTS, one_slot, 0, unroll=unroll)

    flipped = jnp.concatenate((flipped_ref[1 - core], flipped_ref[core]), axis=0)
    half = CHANNELS // 2
    for side in range(3):
        tap = taps_c[:, side : side + BRICK].reshape(SLOTS * VOXELS, WIDE)
        part = jnp.dot(flipped, tap, preferred_element_type=jnp.float32)
        for number in range(9):
            block = part[:, number * CHANNELS : (number + 1) * CHANNELS]
            m = side * 9 + number
            for quarter in range(4):
                rows = slice(quarter * 16, quarter * 16 + 16)
                send_ref[quarter, m] = block[:half][rows].astype(jnp.bfloat16)
                keep_ref[quarter, m] = block[half:][rows]
    flag = jnp.broadcast_to(out_of_place(table_ref[...]), (16, CHANNELS))
    for quarter in range(4):
        send_ref[quarter, 27] = flag.astype(jnp.bfloat16)
        keep_ref[quarter, 27] = flag

    outputs = None
    grad = None
    for side in range(3):
        tap = taps_f[:, side : side + BRICK].reshape(SLOTS * VOXELS, WIDE)
        matrix = weights_ref[side * 9 : side * 9 + 9].reshape(WIDE, CHANNELS)
        part = jnp.dot(tap, matrix, preferred_element_type=jnp.float32)
        outputs = part if outputs is None else outputs + part
    outputs_ref[...] = outputs.astype(jnp.bfloat16).reshape(SLOTS, VOXELS, CHANNELS)
    for side in range(3):
        tap = taps_c[:, side : side + BRICK].reshape(SLOTS * VOXELS, WIDE)
        matrix = jnp.concatenate([weights_ref[26 - side * 9 - number] for number in range(9)], axis=1)
        part = lax.dot_general(tap, matrix, (((1,), (1,)), ((), ())), preferred_element_type=jnp.float32)
        grad = part if grad is None else grad + part
    grad_ref[...] = grad.astype(jnp.bfloat16).reshape(SLOTS, VOXELS, CHANNELS)


def convolve(fill, unroll, place, dst, features, cotangent, halos, flipped, weights):
    vmem = pl.BlockSpec(memory_space=pltpu.VMEM)
    smem = pl.BlockSpec(memory_space=pltpu.SMEM)
    return pl.pallas_call(
        functools.partial(conv_kernel, fill, unroll, len(halos)),
        in_specs=[smem, smem] + [vmem] * (5 + len(halos)),
        out_specs=[vmem] * 4,
        out_shape=[
            jax.ShapeDtypeStruct((SLOTS, VOXELS, CHANNELS), jnp.bfloat16),
            jax.ShapeDtypeStruct((SLOTS, VOXELS, CHANNELS), jnp.bfloat16),
            jax.ShapeDtypeStruct((4, ROWS_M, 16, CHANNELS), jnp.bfloat16),
            jax.ShapeDtypeStruct((4, ROWS_M, 16, CHANNELS), jnp.float32),
        ],
        scratch_shapes=[
            pltpu.VMEM((SLOTS + HALO + 1, VOXELS, 2 * CHANNELS), jnp.bfloat16),
            pltpu.VMEM((SLOTS, PLANES, PLANE, WIDE), jnp.bfloat16),
            pltpu.VMEM((SLOTS, PLANES, PLANE, WIDE), jnp.bfloat16),
        ],
        compiler_params=pltpu.CompilerParams(vmem_limit_bytes=VMEM_LIMIT),
    )(place, dst, dst, features, cotangent, *halos, flipped, weights)


def pack_bricks_kernel(slot_ref, features_ref, cotangent_ref, *packets):
    begin_at = 0
    for packet in packets:
        for position in range(packet.shape[0]):
            slot = slot_ref[begin_at + position]
            row = jnp.clip(slot, 0, SLOTS - 1)

            @pl.when(slot < SLOTS)
            def _():
                packet[position, :, :CHANNELS] = features_ref[row]
                packet[position, :, CHANNELS:] = cotangent_ref[row]

            @pl.when(slot >= SLOTS)
            def _():
                packet[position] = jnp.zeros((VOXELS, 2 * CHANNELS), jnp.bfloat16)

        begin_at += packet.shape[0]


def pack_bricks(recv_slot, features, cotangent):
    vmem = pl.BlockSpec(memory_space=pltpu.VMEM)
    return pl.pallas_call(
        pack_bricks_kernel,
        in_specs=[pl.BlockSpec(memory_space=pltpu.SMEM), vmem, vmem],
        out_specs=[vmem] * 8,
        out_shape=[
            jax.ShapeDtypeStruct((length, VOXELS, 2 * CHANNELS), jnp.bfloat16) for length in LENGTHS
        ],
        compiler_params=pltpu.CompilerParams(vmem_limit_bytes=VMEM_LIMIT),
    )(recv_slot, features, cotangent)


def pass_to(value, step_x, step_y):
    pairs = []
    for gx in range(8):
        for gy in range(32):
            if 0 <= gx + step_x < 8 and 0 <= gy + step_y < 32:
                pairs.append((gx * 32 + gy, (gx + step_x) * 32 + gy + step_y))
    return lax.ppermute(value, AXES, pairs)


def share_kernel(parts_ref, scaled_ref):
    count = parts_ref.shape[1]
    total = parts_ref[0].astype(jnp.float32)
    for number in range(1, parts_ref.shape[0]):
        total = total + parts_ref[number].astype(jnp.float32)
    largest = jnp.max(jnp.abs(total), axis=0)
    largest = jnp.max(jnp.max(largest, axis=1, keepdims=True), axis=0, keepdims=True)
    power = jnp.clip(jnp.ceil(jnp.log2(jnp.maximum(largest, 1e-37))), -100.0, 100.0)
    power = jnp.broadcast_to(power, (16, CHANNELS))
    scale = jnp.exp2(14.0 - power)
    for number in range(count):
        scaled_ref[number] = total[number] * scale
    scaled_ref[count] = power


def column_kernel(column_ref, whole_ref):
    count = whole_ref.shape[1]
    scales = [jnp.exp2(column_ref[z, count] - 14.0) for z in range(column_ref.shape[0])]
    for number in range(count):
        total = column_ref[0, number] * scales[0]
        for z in range(1, column_ref.shape[0]):
            total = total + column_ref[z, number] * scales[z]
        total = (total * (1.0 / (VOXELS * SLOTS))).astype(jnp.bfloat16)
        for target in range(whole_ref.shape[0]):
            whole_ref[target, number] = total


def sum_everywhere(send, keep):
    vmem = pl.BlockSpec(memory_space=pltpu.VMEM)
    arrived = lax.ppermute(send, "c", [(0, 1), (1, 0)])
    chip_sum = (keep + arrived.astype(jnp.float32)).astype(jnp.bfloat16)
    parts = chip_sum.reshape(16, 7, 16, CHANNELS)
    parts = lax.all_to_all(parts, ("x", "y"), 0, 0)
    share = pl.pallas_call(
        share_kernel, in_specs=[vmem], out_specs=vmem, out_shape=jax.ShapeDtypeStruct((8, 16, CHANNELS), jnp.float32)
    )(parts)
    column = jnp.broadcast_to(share.astype(jnp.float16)[None], (8,) + share.shape)
    column = lax.all_to_all(column, "z", 0, 0).astype(jnp.float32)
    whole = pl.pallas_call(
        column_kernel, in_specs=[vmem], out_specs=vmem, out_shape=jax.ShapeDtypeStruct((16, 7, 16, CHANNELS), jnp.bfloat16)
    )(column)
    own = lax.all_to_all(whole, ("x", "y"), 0, 0).reshape(4, ROWS_M, 16, CHANNELS)
    return own, lax.ppermute(own, "c", [(0, 1), (1, 0)])


def spread_kernel(core_ref, own_ref, other_ref, out_ref, whole, sems):
    half = CHANNELS // 2
    core = core_ref[0]
    copies = []
    for chunk in range(9):
        for m in range(3 * chunk, 3 * chunk + 3):
            for quarter in range(4):
                for ref, side in ((own_ref, core), (other_ref, 1 - core)):
                    begin = pl.multiple_of(side * half + quarter * 16, 16)
                    whole[26 - m, pl.ds(begin, 16)] = ref[quarter, m].astype(jnp.float32)
        rows = pl.ds(24 - 3 * chunk, 3)
        copies.append(pltpu.make_async_copy(whole.at[rows], out_ref.at[rows], sems.at[chunk]))
        copies[-1].start()
    for copy in copies:
        copy.wait()


def spread_out(core, own, other):
    vmem = pl.BlockSpec(memory_space=pltpu.VMEM)
    return pl.pallas_call(
        spread_kernel,
        in_specs=[pl.BlockSpec(memory_space=pltpu.SMEM), vmem, vmem],
        out_specs=pl.BlockSpec(memory_space=pltpu.HBM),
        out_shape=jax.ShapeDtypeStruct((27, CHANNELS, CHANNELS), jnp.float32),
        scratch_shapes=[
            pltpu.VMEM((27, CHANNELS, CHANNELS), jnp.float32),
            pltpu.SemaphoreType.DMA((9,)),
        ],
        compiler_params=pltpu.CompilerParams(vmem_limit_bytes=VMEM_LIMIT),
    )(core, own, other)


def local(features, weights, cotangent, dst_index, recv_slot):
    core = lax.axis_index("c").astype(jnp.int32)
    first = core.reshape(1)
    place = jnp.stack((core, (lax.axis_index("z") % 2).astype(jnp.int32)))
    dst = dst_index.T
    flipped = jnp.transpose(features.reshape(SLOTS * VOXELS, CHANNELS)).reshape(2, CHANNELS // 2, SLOTS * VOXELS)

    to_first, to_second, to_sibling, to_outer = pack_layers(place, recv_slot, features, cotangent)
    y_first = lax.ppermute(to_first, ("y", "z"), [(gy, gy ^ 1) for gy in range(32)])
    y_second = lax.ppermute(to_second, ("y", "z"), [(gy, ((gy + 1) ^ 1) - 1) for gy in range(1, 31)])

    def relayed(packet, up):
        corners = [lax.dynamic_slice_in_dim(value, SLOTS + BZ * up, BZ, axis=0) for value in (y_first, y_second)]
        return jnp.concatenate((packet, *corners), axis=0)

    x_outer = lax.ppermute(relayed(to_outer, core), ("x", "c"), [(2 * x + 1, 2 * x + 2) for x in range(3)]
                           + [(2 * x + 2, 2 * x + 1) for x in range(3)])
    x_sibling = lax.ppermute(relayed(to_sibling, 1 - core), "c", [(0, 1), (1, 0)])
    halos = (y_first, y_second, x_sibling, x_outer)
    outputs, input_grad, send, keep = convolve(
        fill_layers, SLOTS, place, dst, features, cotangent, halos, flipped, weights
    )
    own, other = sum_everywhere(send, keep)

    def with_whole_bricks(results):
        packets = pack_bricks(recv_slot, features, cotangent)
        halos = [pass_to(packet, -heading[0], -heading[1]) for packet, heading in zip(packets, DIRECTIONS)]
        outputs, input_grad, send, keep = convolve(
            fill_bricks, 1, place, dst, features, cotangent, halos, flipped, weights
        )
        return outputs, input_grad, spread_out(first, *sum_everywhere(send, keep))

    def as_they_are(results):
        outputs, input_grad, own, other = results
        return outputs, input_grad, spread_out(first, own, other)

    return lax.cond(
        own[0, 27, 0, 0] != 0, with_whole_bricks, as_they_are, (outputs, input_grad, own, other)
    )


def solution(mesh):
    fine = Mesh(mesh.devices.reshape(4, 2, 4, 8), AXES)
    bricks = P(AXES, None, None)
    return jax.shard_map(
        local,
        mesh=fine,
        in_specs=(bricks, P(), bricks, P(None, AXES), P(AXES)),
        out_specs=(bricks, bricks, P()),
        check_vma=False,
    )
```

```python
import functools

import jax
import jax.numpy as jnp
import numpy as np
from jax import lax
from jax.experimental import pallas as pl
from jax.experimental.pallas import tpu as pltpu
from jax.sharding import Mesh, PartitionSpec as P

BRICK = 4
TILE = 4
BZ = 2
HALO = 40
SLOTS = 8
VOXELS = 64
CHANNELS = 128
PLANE = BRICK * BRICK
PLANES = BRICK + 2
WIDE = 9 * CHANNELS
ROWS_M = 28

DIRECTIONS = ((1, 0), (-1, 0), (0, 1), (0, -1), (1, 1), (1, -1), (-1, 1), (-1, -1))
LENGTHS = (TILE * BZ,) * 4 + (BZ,) * 4
STARTS = tuple(int(start) for start in np.cumsum((0,) + LENGTHS[:-1]))
AXES = ("x", "c", "y", "z")
VMEM_LIMIT = 48 * 1024 * 1024


def where_equal(left, right):
    return jnp.where(left == right, 1.0, 0.0).astype(jnp.bfloat16)


def shift_matrix():
    row = lax.broadcasted_iota(jnp.int32, (9 * PLANE, 9 * PLANE), 0)
    column = lax.broadcasted_iota(jnp.int32, (9 * PLANE, 9 * PLANE), 1)
    number = row >> 4
    third = (number * 11) >> 5
    y = ((row >> 2) & 3) + third + 3
    z = (row & 3) + number - 3 * third + 3
    return where_equal(column, ((y >> 2) * 3 + (z >> 2)) * PLANE + (y & 3) * BRICK + (z & 3))


def layer_matrix():
    row = lax.broadcasted_iota(jnp.int32, (2 * PLANE, VOXELS), 0)
    column = lax.broadcasted_iota(jnp.int32, (2 * PLANE, VOXELS), 1)
    return where_equal(column, ((row >> 2) & 3) * PLANE + (row >> 4) * 12 + (row & 3))


def expand_matrix(side):
    row = lax.broadcasted_iota(jnp.int32, (VOXELS, PLANE), 0)
    column = lax.broadcasted_iota(jnp.int32, (VOXELS, PLANE), 1)
    return where_equal(row, (column >> 2) * PLANE + side * 12 + (column & 3))


def pack_layers_kernel(place_ref, slot_ref, features_ref, cotangent_ref, to_first, to_second, to_sibling, to_outer,
                       bricks, sides, sems):
    copies = [
        pltpu.make_async_copy(ref, bricks.at[number, pl.ds(0, SLOTS)], sems.at[number])
        for number, ref in enumerate((features_ref, cotangent_ref))
    ]
    for copy in copies:
        copy.start()
    bricks[:, SLOTS] = jnp.zeros((2, VOXELS, CHANNELS), jnp.bfloat16)
    sides[:, SLOTS] = jnp.zeros((2, 2 * PLANE, CHANNELS), jnp.bfloat16)
    core = place_ref[0]
    odd = place_ref[1]
    layer = layer_matrix()
    for copy in copies:
        copy.wait()
    for kind in range(2):
        beside = jnp.concatenate([bricks[kind, slot] for slot in range(SLOTS)], axis=1)
        picked = jnp.dot(layer, beside, preferred_element_type=jnp.float32).astype(jnp.bfloat16)
        for slot in range(SLOTS):
            sides[kind, slot] = picked[:, slot * CHANNELS : (slot + 1) * CHANNELS]

    def put(packet, position, halo, source, begin):
        slot = jnp.clip(slot_ref[halo], 0, SLOTS)
        rows = pl.ds(begin, PLANE)
        packet[position, :, :CHANNELS] = source[0, slot, rows]
        packet[position, :, CHANNELS:] = source[1, slot, rows]

    for packet, up in ((to_first, 1 - odd), (to_second, odd)):
        begin = pl.multiple_of(up * PLANE, PLANE)
        position = 0
        for number in (2, 4, 6):
            for halo in range(LENGTHS[number]):
                put(packet, position, STARTS[number] + up * LENGTHS[number] + halo, sides, begin)
                position += 1
    for packet, up in ((to_sibling, 1 - core), (to_outer, core)):
        begin = pl.multiple_of(up * (VOXELS - PLANE), PLANE)
        for position in range(LENGTHS[0]):
            put(packet, position, up * LENGTHS[0] + position, bricks, begin)


def pack_layers(place, recv_slot, features, cotangent):
    vmem = pl.BlockSpec(memory_space=pltpu.VMEM)
    smem = pl.BlockSpec(memory_space=pltpu.SMEM)
    hbm = pl.BlockSpec(memory_space=pltpu.HBM)
    return pl.pallas_call(
        pack_layers_kernel,
        in_specs=[smem, smem, hbm, hbm],
        out_specs=[vmem] * 4,
        out_shape=[
            jax.ShapeDtypeStruct((length, PLANE, 2 * CHANNELS), jnp.bfloat16) for length in (12, 12, 8, 8)
        ],
        scratch_shapes=[
            pltpu.VMEM((2, SLOTS + 1, VOXELS, CHANNELS), jnp.bfloat16),
            pltpu.VMEM((2, SLOTS + 1, 2 * PLANE, CHANNELS), jnp.bfloat16),
            pltpu.SemaphoreType.DMA((2,)),
        ],
        compiler_params=pltpu.CompilerParams(vmem_limit_bytes=VMEM_LIMIT),
    )(place, recv_slot, features, cotangent)


def fill_bricks(core, odd, halos, bricks):
    begin_at = SLOTS
    for halo in halos:
        bricks[begin_at : begin_at + halo.shape[0]] = halo[...]
        begin_at += halo.shape[0]


def fill_layers(core, odd, halos, bricks):
    y_first, y_second, x_sibling, x_outer = halos
    both = ((x_sibling, core), (x_outer, 1 - core))
    for packet, below in both:
        for position in range(SLOTS):
            tile = packet[position]
            target = SLOTS + below * LENGTHS[0] + position
            for begin in range(0, VOXELS, PLANE):
                bricks[target, begin : begin + PLANE] = tile
    for order, (faces, side) in enumerate(((y_first, odd), (y_second, 1 - odd))):
        tiles = [faces[position] for position in range(SLOTS)]
        targets = [STARTS[2] + side * LENGTHS[2] + position for position in range(SLOTS)]
        for packet, below in both:
            for position in range(BZ):
                tiles.append(packet[SLOTS + BZ * order + position])
                targets.append(STARTS[4] + side * BZ + below * 2 * BZ + position)
        whole = jnp.dot(
            expand_matrix(side), jnp.concatenate(tiles, axis=1), preferred_element_type=jnp.float32
        ).astype(jnp.bfloat16)
        for position, target in enumerate(targets):
            bricks[SLOTS + target] = whole[:, position * 2 * CHANNELS : (position + 1) * 2 * CHANNELS]


def out_of_place(dst):
    k = lax.broadcasted_iota(jnp.int32, dst.shape, 1)
    ninth = jnp.where(k >= 18, 2, jnp.where(k >= 9, 1, 0))
    rest = k - 9 * ninth
    offset = (ninth - 1, jnp.where(rest >= 6, 2, jnp.where(rest >= 3, 1, 0)) - 1)
    wrong = jnp.zeros(dst.shape, jnp.float32)
    for number, heading in enumerate(DIRECTIONS):
        start = SLOTS + STARTS[number]
        here = (dst >= start) & (dst < start + LENGTHS[number])
        for axis in range(2):
            if heading[axis]:
                wrong = jnp.where(here & (offset[axis] != heading[axis]), 1.0, wrong)
    return jnp.max(jnp.max(wrong, axis=1, keepdims=True), axis=0, keepdims=True)


def conv_kernel(fill, unroll, count, place_ref, dst_ref, table_ref, features_ref, cotangent_ref, *rest):
    halos = rest[:count]
    (flipped_ref, weights_ref, outputs_ref, grad_ref, send_ref, keep_ref, bricks, taps_f, taps_c) = rest[count:]
    core = place_ref[0]
    bricks[:SLOTS, :, :CHANNELS] = features_ref[...]
    bricks[:SLOTS, :, CHANNELS:] = cotangent_ref[...]
    fill(core, place_ref[1], halos, bricks)
    bricks[SLOTS + HALO] = jnp.zeros((VOXELS, 2 * CHANNELS), jnp.bfloat16)
    shift = shift_matrix()

    def one_slot(slot, carry):
        for plane in range(PLANES):
            side = 0 if plane == 0 else 2 if plane == PLANES - 1 else 1
            local = (plane - 1) % BRICK * PLANE
            around = [
                bricks[jnp.clip(dst_ref[slot, side * 9 + number], 0, SLOTS + HALO), local : local + PLANE]
                for number in range(9)
            ]
            moved = jnp.dot(
                shift, jnp.concatenate(around, axis=0), preferred_element_type=jnp.float32
            ).astype(jnp.bfloat16)
            for number in range(9):
                rows = moved[number * PLANE : (number + 1) * PLANE]
                lanes = slice(number * CHANNELS, (number + 1) * CHANNELS)
                taps_f[slot, plane, :, lanes] = rows[:, :CHANNELS]
                taps_c[slot, plane, :, lanes] = rows[:, CHANNELS:]
        return carry

    lax.fori_loop(0, SLOTS, one_slot, 0, unroll=unroll)

    flipped = jnp.concatenate((flipped_ref[1 - core], flipped_ref[core]), axis=0)
    half = CHANNELS // 2
    for side in range(3):
        tap = taps_c[:, side : side + BRICK].reshape(SLOTS * VOXELS, WIDE)
        part = jnp.dot(flipped, tap, preferred_element_type=jnp.float32)
        for number in range(9):
            block = part[:, number * CHANNELS : (number + 1) * CHANNELS]
            m = side * 9 + number
            for quarter in range(4):
                rows = slice(quarter * 16, quarter * 16 + 16)
                send_ref[quarter, m] = block[:half][rows].astype(jnp.bfloat16)
                keep_ref[quarter, m] = block[half:][rows]
    flag = jnp.broadcast_to(out_of_place(table_ref[...]), (16, CHANNELS))
    for quarter in range(4):
        send_ref[quarter, 27] = flag.astype(jnp.bfloat16)
        keep_ref[quarter, 27] = flag

    outputs = None
    grad = None
    for side in range(3):
        tap = taps_f[:, side : side + BRICK].reshape(SLOTS * VOXELS, WIDE)
        matrix = weights_ref[side * 9 : side * 9 + 9].reshape(WIDE, CHANNELS)
        part = jnp.dot(tap, matrix, preferred_element_type=jnp.float32)
        outputs = part if outputs is None else outputs + part
    outputs_ref[...] = outputs.astype(jnp.bfloat16).reshape(SLOTS, VOXELS, CHANNELS)
    for side in range(3):
        tap = taps_c[:, side : side + BRICK].reshape(SLOTS * VOXELS, WIDE)
        matrix = jnp.concatenate([weights_ref[26 - side * 9 - number] for number in range(9)], axis=1)
        part = lax.dot_general(tap, matrix, (((1,), (1,)), ((), ())), preferred_element_type=jnp.float32)
        grad = part if grad is None else grad + part
    grad_ref[...] = grad.astype(jnp.bfloat16).reshape(SLOTS, VOXELS, CHANNELS)


def convolve(fill, unroll, place, dst, features, cotangent, halos, flipped, weights):
    vmem = pl.BlockSpec(memory_space=pltpu.VMEM)
    smem = pl.BlockSpec(memory_space=pltpu.SMEM)
    return pl.pallas_call(
        functools.partial(conv_kernel, fill, unroll, len(halos)),
        in_specs=[smem, smem] + [vmem] * (5 + len(halos)),
        out_specs=[vmem] * 4,
        out_shape=[
            jax.ShapeDtypeStruct((SLOTS, VOXELS, CHANNELS), jnp.bfloat16),
            jax.ShapeDtypeStruct((SLOTS, VOXELS, CHANNELS), jnp.bfloat16),
            jax.ShapeDtypeStruct((4, ROWS_M, 16, CHANNELS), jnp.bfloat16),
            jax.ShapeDtypeStruct((4, ROWS_M, 16, CHANNELS), jnp.float32),
        ],
        scratch_shapes=[
            pltpu.VMEM((SLOTS + HALO + 1, VOXELS, 2 * CHANNELS), jnp.bfloat16),
            pltpu.VMEM((SLOTS, PLANES, PLANE, WIDE), jnp.bfloat16),
            pltpu.VMEM((SLOTS, PLANES, PLANE, WIDE), jnp.bfloat16),
        ],
        compiler_params=pltpu.CompilerParams(vmem_limit_bytes=VMEM_LIMIT),
    )(place, dst, dst, features, cotangent, *halos, flipped, weights)


def pack_bricks_kernel(slot_ref, features_ref, cotangent_ref, *packets):
    begin_at = 0
    for packet in packets:
        for position in range(packet.shape[0]):
            slot = slot_ref[begin_at + position]
            row = jnp.clip(slot, 0, SLOTS - 1)

            @pl.when(slot < SLOTS)
            def _():
                packet[position, :, :CHANNELS] = features_ref[row]
                packet[position, :, CHANNELS:] = cotangent_ref[row]

            @pl.when(slot >= SLOTS)
            def _():
                packet[position] = jnp.zeros((VOXELS, 2 * CHANNELS), jnp.bfloat16)

        begin_at += packet.shape[0]


def pack_bricks(recv_slot, features, cotangent):
    vmem = pl.BlockSpec(memory_space=pltpu.VMEM)
    return pl.pallas_call(
        pack_bricks_kernel,
        in_specs=[pl.BlockSpec(memory_space=pltpu.SMEM), vmem, vmem],
        out_specs=[vmem] * 8,
        out_shape=[
            jax.ShapeDtypeStruct((length, VOXELS, 2 * CHANNELS), jnp.bfloat16) for length in LENGTHS
        ],
        compiler_params=pltpu.CompilerParams(vmem_limit_bytes=VMEM_LIMIT),
    )(recv_slot, features, cotangent)


def pass_to(value, step_x, step_y):
    pairs = []
    for gx in range(8):
        for gy in range(32):
            if 0 <= gx + step_x < 8 and 0 <= gy + step_y < 32:
                pairs.append((gx * 32 + gy, (gx + step_x) * 32 + gy + step_y))
    return lax.ppermute(value, AXES, pairs)


def sum_everywhere(send, keep):
    arrived = lax.ppermute(send, "c", [(0, 1), (1, 0)])
    chip_sum = (keep + arrived.astype(jnp.float32)).astype(jnp.bfloat16)
    parts = chip_sum.reshape(16, 7, 16, CHANNELS)
    parts = lax.all_to_all(parts, ("x", "y"), 0, 0)
    total = jnp.sum(parts.astype(jnp.float32), axis=0)
    largest = jnp.max(jnp.abs(total), axis=(0, 1))
    power = jnp.clip(jnp.ceil(jnp.log2(jnp.maximum(largest, 1e-37))), -100.0, 100.0)
    power = jnp.broadcast_to(power, (1, 16, CHANNELS))
    share = jnp.concatenate((total * jnp.exp2(14.0 - power), power), axis=0).astype(jnp.float16)
    column = lax.all_to_all(jnp.broadcast_to(share[None], (8,) + share.shape), "z", 0, 0).astype(jnp.float32)
    total = jnp.sum(column[:, :7] * jnp.exp2(column[:, 7:] - 14.0), axis=0)
    share = (total * (1.0 / (VOXELS * SLOTS))).astype(jnp.bfloat16)
    whole = jnp.broadcast_to(share[None], (16,) + share.shape)
    own = lax.all_to_all(whole, ("x", "y"), 0, 0).reshape(4, ROWS_M, 16, CHANNELS)
    return own, lax.ppermute(own, "c", [(0, 1), (1, 0)])


def spread_kernel(core_ref, own_ref, other_ref, out_ref, whole, sems):
    half = CHANNELS // 2
    core = core_ref[0]
    copies = []
    for chunk in range(9):
        for m in range(3 * chunk, 3 * chunk + 3):
            for quarter in range(4):
                for ref, side in ((own_ref, core), (other_ref, 1 - core)):
                    begin = pl.multiple_of(side * half + quarter * 16, 16)
                    whole[26 - m, pl.ds(begin, 16)] = ref[quarter, m].astype(jnp.float32)
        rows = pl.ds(24 - 3 * chunk, 3)
        copies.append(pltpu.make_async_copy(whole.at[rows], out_ref.at[rows], sems.at[chunk]))
        copies[-1].start()
    for copy in copies:
        copy.wait()


def spread_out(core, own, other):
    vmem = pl.BlockSpec(memory_space=pltpu.VMEM)
    return pl.pallas_call(
        spread_kernel,
        in_specs=[pl.BlockSpec(memory_space=pltpu.SMEM), vmem, vmem],
        out_specs=pl.BlockSpec(memory_space=pltpu.HBM),
        out_shape=jax.ShapeDtypeStruct((27, CHANNELS, CHANNELS), jnp.float32),
        scratch_shapes=[
            pltpu.VMEM((27, CHANNELS, CHANNELS), jnp.float32),
            pltpu.SemaphoreType.DMA((9,)),
        ],
        compiler_params=pltpu.CompilerParams(vmem_limit_bytes=VMEM_LIMIT),
    )(core, own, other)


def local(features, weights, cotangent, dst_index, recv_slot):
    core = lax.axis_index("c").astype(jnp.int32)
    first = core.reshape(1)
    place = jnp.stack((core, (lax.axis_index("z") % 2).astype(jnp.int32)))
    dst = dst_index.T
    flipped = jnp.transpose(features.reshape(SLOTS * VOXELS, CHANNELS)).reshape(2, CHANNELS // 2, SLOTS * VOXELS)

    to_first, to_second, to_sibling, to_outer = pack_layers(place, recv_slot, features, cotangent)
    y_first = lax.ppermute(to_first, ("y", "z"), [(gy, gy ^ 1) for gy in range(32)])
    y_second = lax.ppermute(to_second, ("y", "z"), [(gy, ((gy + 1) ^ 1) - 1) for gy in range(1, 31)])

    def relayed(packet, up):
        corners = [lax.dynamic_slice_in_dim(value, SLOTS + BZ * up, BZ, axis=0) for value in (y_first, y_second)]
        return jnp.concatenate((packet, *corners), axis=0)

    x_outer = lax.ppermute(relayed(to_outer, core), ("x", "c"), [(2 * x + 1, 2 * x + 2) for x in range(3)]
                           + [(2 * x + 2, 2 * x + 1) for x in range(3)])
    x_sibling = lax.ppermute(relayed(to_sibling, 1 - core), "c", [(0, 1), (1, 0)])
    halos = (y_first, y_second, x_sibling, x_outer)
    outputs, input_grad, send, keep = convolve(
        fill_layers, SLOTS, place, dst, features, cotangent, halos, flipped, weights
    )
    own, other = sum_everywhere(send, keep)

    def with_whole_bricks(results):
        packets = pack_bricks(recv_slot, features, cotangent)
        halos = [pass_to(packet, -heading[0], -heading[1]) for packet, heading in zip(packets, DIRECTIONS)]
        outputs, input_grad, send, keep = convolve(
            fill_bricks, 1, place, dst, features, cotangent, halos, flipped, weights
        )
        return outputs, input_grad, spread_out(first, *sum_everywhere(send, keep))

    def as_they_are(results):
        outputs, input_grad, own, other = results
        return outputs, input_grad, spread_out(first, own, other)

    return lax.cond(
        own[0, 27, 0, 0] != 0, with_whole_bricks, as_they_are, (outputs, input_grad, own, other)
    )


def solution(mesh):
    fine = Mesh(mesh.devices.reshape(4, 2, 4, 8), AXES)
    bricks = P(AXES, None, None)
    return jax.shard_map(
        local,
        mesh=fine,
        in_specs=(bricks, P(), bricks, P(None, AXES), P(AXES)),
        out_specs=(bricks, bricks, P()),
        check_vma=False,
    )
```

```python
import functools

import jax
import jax.numpy as jnp
import numpy as np
from jax import lax
from jax.experimental import pallas as pl
from jax.experimental.pallas import tpu as pltpu
from jax.sharding import Mesh, PartitionSpec as P

BRICK = 4
TILE = 4
BZ = 2
HALO = 40
SLOTS = 8
VOXELS = 64
CHANNELS = 128
PLANE = BRICK * BRICK
PLANES = BRICK + 2
WIDE = 9 * CHANNELS
ROWS_M = 28

DIRECTIONS = ((1, 0), (-1, 0), (0, 1), (0, -1), (1, 1), (1, -1), (-1, 1), (-1, -1))
LENGTHS = (TILE * BZ,) * 4 + (BZ,) * 4
STARTS = tuple(int(start) for start in np.cumsum((0,) + LENGTHS[:-1]))
AXES = ("x", "c", "y", "z")
VMEM_LIMIT = 24 * 1024 * 1024


def where_equal(left, right):
    return jnp.where(left == right, 1.0, 0.0).astype(jnp.bfloat16)


def shift_matrix():
    row = lax.broadcasted_iota(jnp.int32, (9 * PLANE, 9 * PLANE), 0)
    column = lax.broadcasted_iota(jnp.int32, (9 * PLANE, 9 * PLANE), 1)
    number = row >> 4
    third = (number * 11) >> 5
    y = ((row >> 2) & 3) + third + 3
    z = (row & 3) + number - 3 * third + 3
    return where_equal(column, ((y >> 2) * 3 + (z >> 2)) * PLANE + (y & 3) * BRICK + (z & 3))


def layer_matrix():
    row = lax.broadcasted_iota(jnp.int32, (2 * PLANE, VOXELS), 0)
    column = lax.broadcasted_iota(jnp.int32, (2 * PLANE, VOXELS), 1)
    return where_equal(column, ((row >> 2) & 3) * PLANE + (row >> 4) * 12 + (row & 3))


def expand_matrix(side):
    row = lax.broadcasted_iota(jnp.int32, (VOXELS, PLANE), 0)
    column = lax.broadcasted_iota(jnp.int32, (VOXELS, PLANE), 1)
    return where_equal(row, (column >> 2) * PLANE + side * 12 + (column & 3))


def pack_layers_kernel(place_ref, recv_slot_ref, features_ref, cotangent_ref, to_first, to_second, to_sibling, to_outer,
                       own_f, own_c, sides, slot_ref, sems):
    bricks = (own_f, own_c)
    copies = [
        pltpu.make_async_copy(ref, target, sems.at[number])
        for number, (ref, target) in enumerate((
            (features_ref, own_f.at[pl.ds(0, SLOTS)]),
            (cotangent_ref, own_c.at[pl.ds(0, SLOTS)]),
            (recv_slot_ref, slot_ref),
        ))
    ]
    for copy in copies:
        copy.start()
    for own in bricks:
        own[SLOTS] = jnp.zeros((VOXELS, CHANNELS), jnp.bfloat16)
    sides[:, SLOTS] = jnp.zeros((2, 2 * PLANE, CHANNELS), jnp.bfloat16)
    core = place_ref[0]
    odd = place_ref[1]
    layer = layer_matrix()
    for copy in copies:
        copy.wait()
    for kind in range(2):
        beside = jnp.concatenate([bricks[kind][slot] for slot in range(SLOTS)], axis=1)
        picked = jnp.dot(layer, beside, preferred_element_type=jnp.float32).astype(jnp.bfloat16)
        for slot in range(SLOTS):
            sides[kind, slot] = picked[:, slot * CHANNELS : (slot + 1) * CHANNELS]

    def put(packet, position, halo, source, begin):
        slot = jnp.clip(slot_ref[halo], 0, SLOTS)
        rows = pl.ds(begin, PLANE)
        packet[position, :, :CHANNELS] = source[0][slot, rows]
        packet[position, :, CHANNELS:] = source[1][slot, rows]

    for packet, up in ((to_first, 1 - odd), (to_second, odd)):
        begin = pl.multiple_of(up * PLANE, PLANE)
        position = 0
        for number in (2, 4, 6):
            for halo in range(LENGTHS[number]):
                put(packet, position, STARTS[number] + up * LENGTHS[number] + halo, (sides.at[0], sides.at[1]), begin)
                position += 1
    for packet, up in ((to_sibling, 1 - core), (to_outer, core)):
        begin = pl.multiple_of(up * (VOXELS - PLANE), PLANE)
        for position in range(LENGTHS[0]):
            put(packet, position, up * LENGTHS[0] + position, bricks, begin)


def pack_layers(place, recv_slot, features, cotangent):
    vmem = pl.BlockSpec(memory_space=pltpu.VMEM)
    smem = pl.BlockSpec(memory_space=pltpu.SMEM)
    hbm = pl.BlockSpec(memory_space=pltpu.HBM)
    return pl.pallas_call(
        pack_layers_kernel,
        in_specs=[smem, hbm, hbm, hbm],
        out_specs=[vmem] * 6,
        out_shape=[
            jax.ShapeDtypeStruct((length, PLANE, 2 * CHANNELS), jnp.bfloat16) for length in (12, 12, 8, 8)
        ] + [jax.ShapeDtypeStruct((SLOTS + 1, VOXELS, CHANNELS), jnp.bfloat16)] * 2,
        scratch_shapes=[
            pltpu.VMEM((2, SLOTS + 1, 2 * PLANE, CHANNELS), jnp.bfloat16),
            pltpu.SMEM((HALO,), jnp.int32),
            pltpu.SemaphoreType.DMA((3,)),
        ],
        compiler_params=pltpu.CompilerParams(vmem_limit_bytes=VMEM_LIMIT),
    )(place, recv_slot, features, cotangent)


def fill_bricks(core, odd, halos, lanes, bricks):
    begin_at = SLOTS
    for halo in halos:
        bricks[begin_at : begin_at + halo.shape[0]] = halo[:, :, lanes]
        begin_at += halo.shape[0]


def fill_layers(core, odd, halos, lanes, bricks):
    y_first, y_second, x_sibling, x_outer = halos
    both = ((x_sibling, core), (x_outer, 1 - core))
    for packet, below in both:
        for position in range(SLOTS):
            tile = packet[position, :, lanes]
            target = SLOTS + below * LENGTHS[0] + position
            for begin in range(0, VOXELS, PLANE):
                bricks[target, begin : begin + PLANE] = tile
    for order, (faces, side) in enumerate(((y_first, odd), (y_second, 1 - odd))):
        tiles = [faces[position, :, lanes] for position in range(SLOTS)]
        targets = [STARTS[2] + side * LENGTHS[2] + position for position in range(SLOTS)]
        for packet, below in both:
            for position in range(BZ):
                tiles.append(packet[SLOTS + BZ * order + position, :, lanes])
                targets.append(STARTS[4] + side * BZ + below * 2 * BZ + position)
        whole = jnp.dot(
            expand_matrix(side), jnp.concatenate(tiles, axis=1), preferred_element_type=jnp.float32
        ).astype(jnp.bfloat16)
        for position, target in enumerate(targets):
            bricks[SLOTS + target] = whole[:, position * CHANNELS : (position + 1) * CHANNELS]


def out_of_place(dst):
    k = lax.broadcasted_iota(jnp.int32, dst.shape, 1)
    ninth = jnp.where(k >= 18, 2, jnp.where(k >= 9, 1, 0))
    rest = k - 9 * ninth
    offset = (ninth - 1, jnp.where(rest >= 6, 2, jnp.where(rest >= 3, 1, 0)) - 1)
    wrong = jnp.zeros(dst.shape, jnp.float32)
    for number, heading in enumerate(DIRECTIONS):
        start = SLOTS + STARTS[number]
        here = (dst >= start) & (dst < start + LENGTHS[number])
        for axis in range(2):
            if heading[axis]:
                wrong = jnp.where(here & (offset[axis] != heading[axis]), 1.0, wrong)
    return jnp.max(jnp.max(wrong, axis=1, keepdims=True), axis=0, keepdims=True)


def build_taps(fill, unroll, place_ref, dst_ref, own_ref, halos, lanes, bricks, taps):
    bricks[:SLOTS] = own_ref[:SLOTS]
    fill(place_ref[0], place_ref[1], halos, lanes, bricks)
    bricks[SLOTS + HALO] = jnp.zeros((VOXELS, CHANNELS), jnp.bfloat16)
    shift = shift_matrix()

    def around(slot, plane):
        side = 0 if plane == 0 else 2 if plane == PLANES - 1 else 1
        local = (plane - 1) % BRICK * PLANE
        return jnp.concatenate(
            [bricks[dst_ref[slot, side * 9 + number], local : local + PLANE] for number in range(9)], axis=0
        )

    def one_slot(slot, carry):
        for plane in range(0, PLANES, 2):
            pair = jnp.concatenate((around(slot, plane), around(slot, plane + 1)), axis=1)
            moved = jnp.dot(shift, pair, preferred_element_type=jnp.float32).astype(jnp.bfloat16)
            for number in range(9):
                rows = moved[number * PLANE : (number + 1) * PLANE]
                target = slice(number * CHANNELS, (number + 1) * CHANNELS)
                taps[slot, plane, :, target] = rows[:, :CHANNELS]
                taps[slot, plane + 1, :, target] = rows[:, CHANNELS:]
        return carry

    lax.fori_loop(0, SLOTS, one_slot, 0, unroll=unroll)


def weight_kernel(fill, unroll, count, place_ref, dst_ref, table_ref, cotangent_ref, *rest):
    halos = rest[:count]
    flipped_ref, send_ref, keep_ref, taps, bricks = rest[count:]
    build_taps(fill, unroll, place_ref, dst_ref, cotangent_ref, halos, slice(CHANNELS, 2 * CHANNELS), bricks, taps)
    core = place_ref[0]
    flipped = jnp.concatenate((flipped_ref[1 - core], flipped_ref[core]), axis=0)
    half = CHANNELS // 2
    for side in range(3):
        tap = taps[:, side : side + BRICK].reshape(SLOTS * VOXELS, WIDE)
        part = jnp.dot(flipped, tap, preferred_element_type=jnp.float32)
        for number in range(9):
            block = part[:, number * CHANNELS : (number + 1) * CHANNELS]
            m = side * 9 + number
            for quarter in range(4):
                rows = slice(quarter * 16, quarter * 16 + 16)
                send_ref[quarter, m] = block[:half][rows].astype(jnp.bfloat16)
                keep_ref[quarter, m] = block[half:][rows]
    flag = jnp.broadcast_to(out_of_place(table_ref[...]), (16, CHANNELS))
    for quarter in range(4):
        send_ref[quarter, 27] = flag.astype(jnp.bfloat16)
        keep_ref[quarter, 27] = flag


def grad_kernel(taps, weights_ref, grad_ref):
    grad = None
    for side in range(3):
        tap = taps[:, side : side + BRICK].reshape(SLOTS * VOXELS, WIDE)
        matrix = jnp.concatenate([weights_ref[26 - side * 9 - number] for number in range(9)], axis=1)
        part = lax.dot_general(tap, matrix, (((1,), (1,)), ((), ())), preferred_element_type=jnp.float32)
        grad = part if grad is None else grad + part
    grad_ref[...] = grad.astype(jnp.bfloat16).reshape(SLOTS, VOXELS, CHANNELS)


def output_kernel(fill, unroll, count, place_ref, dst_ref, features_ref, *rest):
    halos = rest[:count]
    weights_ref, outputs_ref, bricks, taps = rest[count:]
    build_taps(fill, unroll, place_ref, dst_ref, features_ref, halos, slice(0, CHANNELS), bricks, taps)
    outputs = None
    for side in range(3):
        tap = taps[:, side : side + BRICK].reshape(SLOTS * VOXELS, WIDE)
        matrix = weights_ref[side * 9 : side * 9 + 9].reshape(WIDE, CHANNELS)
        part = jnp.dot(tap, matrix, preferred_element_type=jnp.float32)
        outputs = part if outputs is None else outputs + part
    outputs_ref[...] = outputs.astype(jnp.bfloat16).reshape(SLOTS, VOXELS, CHANNELS)


def convolve(fill, unroll, place, dst, own_f, own_c, halos, flipped, weights):
    vmem = pl.BlockSpec(memory_space=pltpu.VMEM)
    smem = pl.BlockSpec(memory_space=pltpu.SMEM)
    brick = jax.ShapeDtypeStruct((SLOTS, VOXELS, CHANNELS), jnp.bfloat16)
    taps = (SLOTS, PLANES, PLANE, WIDE)
    bricks = pltpu.VMEM((SLOTS + HALO + 1, VOXELS, CHANNELS), jnp.bfloat16)
    params = pltpu.CompilerParams(vmem_limit_bytes=VMEM_LIMIT)
    flops = 2 * SLOTS * VOXELS * 27 * CHANNELS * CHANNELS
    cost = pl.CostEstimate(flops=2 * flops, bytes_accessed=4_000_000, transcendentals=0)
    send, keep, taps_c = pl.pallas_call(
        functools.partial(weight_kernel, fill, unroll, len(halos)),
        in_specs=[smem, smem] + [vmem] * (3 + len(halos)),
        out_specs=[vmem] * 3,
        out_shape=[
            jax.ShapeDtypeStruct((4, ROWS_M, 16, CHANNELS), jnp.bfloat16),
            jax.ShapeDtypeStruct((4, ROWS_M, 16, CHANNELS), jnp.float32),
            jax.ShapeDtypeStruct(taps, jnp.bfloat16),
        ],
        scratch_shapes=[bricks],
        compiler_params=params,
        cost_estimate=cost,
    )(place, dst, dst, own_c, *halos, flipped)
    grad = pl.pallas_call(
        grad_kernel,
        in_specs=[vmem, vmem],
        out_specs=vmem,
        out_shape=brick,
        compiler_params=params,
        cost_estimate=cost,
    )(taps_c, weights)
    outputs = pl.pallas_call(
        functools.partial(output_kernel, fill, unroll, len(halos)),
        in_specs=[smem, smem] + [vmem] * (2 + len(halos)),
        out_specs=vmem,
        out_shape=brick,
        scratch_shapes=[bricks, pltpu.VMEM(taps, jnp.bfloat16)],
        compiler_params=params,
        cost_estimate=cost,
    )(place, dst, own_f, *halos, weights)
    return outputs, grad, send, keep


def pack_bricks_kernel(slot_ref, features_ref, cotangent_ref, *packets):
    begin_at = 0
    for packet in packets:
        for position in range(packet.shape[0]):
            slot = slot_ref[begin_at + position]
            row = jnp.clip(slot, 0, SLOTS - 1)

            @pl.when(slot < SLOTS)
            def _():
                packet[position, :, :CHANNELS] = features_ref[row]
                packet[position, :, CHANNELS:] = cotangent_ref[row]

            @pl.when(slot >= SLOTS)
            def _():
                packet[position] = jnp.zeros((VOXELS, 2 * CHANNELS), jnp.bfloat16)

        begin_at += packet.shape[0]


def pack_bricks(recv_slot, features, cotangent):
    vmem = pl.BlockSpec(memory_space=pltpu.VMEM)
    return pl.pallas_call(
        pack_bricks_kernel,
        in_specs=[pl.BlockSpec(memory_space=pltpu.SMEM), vmem, vmem],
        out_specs=[vmem] * 8,
        out_shape=[
            jax.ShapeDtypeStruct((length, VOXELS, 2 * CHANNELS), jnp.bfloat16) for length in LENGTHS
        ],
        compiler_params=pltpu.CompilerParams(vmem_limit_bytes=VMEM_LIMIT),
    )(recv_slot, features, cotangent)


def pass_to(value, step_x, step_y):
    pairs = []
    for gx in range(8):
        for gy in range(32):
            if 0 <= gx + step_x < 8 and 0 <= gy + step_y < 32:
                pairs.append((gx * 32 + gy, (gx + step_x) * 32 + gy + step_y))
    return lax.ppermute(value, AXES, pairs)


def sum_everywhere(send, keep, grad):
    arrived = lax.ppermute(send, "c", [(0, 1), (1, 0)])
    arrived, grad = lax.optimization_barrier((arrived, grad))
    chip_sum = (keep + arrived.astype(jnp.float32)).astype(jnp.bfloat16)
    parts = chip_sum.reshape(16, 7, 16, CHANNELS)
    parts = lax.all_to_all(parts, ("x", "y"), 0, 0)
    total = jnp.sum(parts.astype(jnp.float32), axis=0)
    largest = jnp.max(jnp.abs(total), axis=(0, 1))
    power = jnp.clip(jnp.ceil(jnp.log2(jnp.maximum(largest, 1e-37))), -100.0, 100.0)
    power = jnp.broadcast_to(power, (1, 16, CHANNELS))
    share = jnp.concatenate((total * jnp.exp2(14.0 - power), power), axis=0).astype(jnp.float16)
    column = lax.all_to_all(jnp.broadcast_to(share[None], (8,) + share.shape), "z", 0, 0).astype(jnp.float32)
    total = jnp.sum(column[:, :7] * jnp.exp2(column[:, 7:] - 14.0), axis=0)
    share = (total * (1.0 / (VOXELS * SLOTS))).astype(jnp.bfloat16)
    whole = jnp.broadcast_to(share[None], (16,) + share.shape)
    own = lax.all_to_all(whole, ("x", "y"), 0, 0).reshape(4, ROWS_M, 16, CHANNELS)
    return own, lax.ppermute(own, "c", [(0, 1), (1, 0)]), grad


def spread_kernel(core_ref, own_ref, other_ref, out_ref, whole, sems):
    half = CHANNELS // 2
    core = core_ref[0]
    copies = []
    for chunk in range(9):
        for m in range(3 * chunk, 3 * chunk + 3):
            for quarter in range(4):
                for ref, side in ((own_ref, core), (other_ref, 1 - core)):
                    begin = pl.multiple_of(side * half + quarter * 16, 16)
                    whole[26 - m, pl.ds(begin, 16)] = ref[quarter, m].astype(jnp.float32)
        rows = pl.ds(24 - 3 * chunk, 3)
        copies.append(pltpu.make_async_copy(whole.at[rows], out_ref.at[rows], sems.at[chunk]))
        copies[-1].start()
    for copy in copies:
        copy.wait()


def spread_out(core, own, other):
    vmem = pl.BlockSpec(memory_space=pltpu.VMEM)
    return pl.pallas_call(
        spread_kernel,
        in_specs=[pl.BlockSpec(memory_space=pltpu.SMEM), vmem, vmem],
        out_specs=pl.BlockSpec(memory_space=pltpu.HBM),
        out_shape=jax.ShapeDtypeStruct((27, CHANNELS, CHANNELS), jnp.float32),
        scratch_shapes=[
            pltpu.VMEM((27, CHANNELS, CHANNELS), jnp.float32),
            pltpu.SemaphoreType.DMA((9,)),
        ],
        compiler_params=pltpu.CompilerParams(vmem_limit_bytes=VMEM_LIMIT),
    )(core, own, other)


def local(features, weights, cotangent, dst_index, recv_slot):
    core = lax.axis_index("c").astype(jnp.int32)
    first = core.reshape(1)
    place = jnp.stack((core, (lax.axis_index("z") % 2).astype(jnp.int32)))
    dst = jnp.clip(dst_index.T, 0, SLOTS + HALO)
    to_first, to_second, to_sibling, to_outer, own_f, own_c = pack_layers(place, recv_slot, features, cotangent)
    flipped = jnp.transpose(own_f[:SLOTS].reshape(SLOTS * VOXELS, CHANNELS))
    flipped = flipped.reshape(2, CHANNELS // 2, SLOTS * VOXELS)
    y_first = lax.ppermute(to_first, ("y", "z"), [(gy, gy ^ 1) for gy in range(32)])
    y_second = lax.ppermute(to_second, ("y", "z"), [(gy, ((gy + 1) ^ 1) - 1) for gy in range(1, 31)])

    def relayed(packet, up):
        corners = [lax.dynamic_slice_in_dim(value, SLOTS + BZ * up, BZ, axis=0) for value in (y_first, y_second)]
        return jnp.concatenate((packet, *corners), axis=0)

    x_outer = lax.ppermute(relayed(to_outer, core), ("x", "c"), [(2 * x + 1, 2 * x + 2) for x in range(3)]
                           + [(2 * x + 2, 2 * x + 1) for x in range(3)])
    x_sibling = lax.ppermute(relayed(to_sibling, 1 - core), "c", [(0, 1), (1, 0)])
    halos = (y_first, y_second, x_sibling, x_outer)
    outputs, input_grad, send, keep = convolve(
        fill_layers, SLOTS, place, dst, own_f, own_c, halos, flipped, weights
    )
    own, other, input_grad = sum_everywhere(send, keep, input_grad)

    def with_whole_bricks(results):
        packets = pack_bricks(recv_slot, features, cotangent)
        halos = [pass_to(packet, -heading[0], -heading[1]) for packet, heading in zip(packets, DIRECTIONS)]
        outputs, input_grad, send, keep = convolve(
            fill_bricks, 1, place, dst, own_f, own_c, halos, flipped, weights
        )
        own, other, input_grad = sum_everywhere(send, keep, input_grad)
        return outputs, input_grad, spread_out(first, own, other)

    def as_they_are(results):
        outputs, input_grad, own, other = results
        return outputs, input_grad, spread_out(first, own, other)

    return lax.cond(
        own[0, 27, 0, 0] != 0, with_whole_bricks, as_they_are, (outputs, input_grad, own, other)
    )


def solution(mesh):
    fine = Mesh(mesh.devices.reshape(4, 2, 4, 8), AXES)
    bricks = P(AXES, None, None)
    return jax.shard_map(
        local,
        mesh=fine,
        in_specs=(bricks, P(), bricks, P(None, AXES), P(AXES)),
        out_specs=(bricks, bricks, P()),
        check_vma=False,
    )
```

```python
import functools

import jax
import jax.numpy as jnp
import numpy as np
from jax import lax
from jax.experimental import pallas as pl
from jax.experimental.pallas import tpu as pltpu
from jax.sharding import Mesh, PartitionSpec as P

BRICK = 4
TILE = 4
BZ = 2
HALO = 40
SLOTS = 8
VOXELS = 64
CHANNELS = 128
PLANE = BRICK * BRICK
PLANES = BRICK + 2
WIDE = 9 * CHANNELS
ROWS_M = 28

DIRECTIONS = ((1, 0), (-1, 0), (0, 1), (0, -1), (1, 1), (1, -1), (-1, 1), (-1, -1))
LENGTHS = (TILE * BZ,) * 4 + (BZ,) * 4
STARTS = tuple(int(start) for start in np.cumsum((0,) + LENGTHS[:-1]))
AXES = ("x", "c", "y", "z")
VMEM_LIMIT = 24 * 1024 * 1024


def where_equal(left, right):
    return jnp.where(left == right, 1.0, 0.0).astype(jnp.bfloat16)


def shift_matrix():
    row = lax.broadcasted_iota(jnp.int32, (9 * PLANE, 9 * PLANE), 0)
    column = lax.broadcasted_iota(jnp.int32, (9 * PLANE, 9 * PLANE), 1)
    number = row >> 4
    third = (number * 11) >> 5
    y = ((row >> 2) & 3) + third + 3
    z = (row & 3) + number - 3 * third + 3
    return where_equal(column, ((y >> 2) * 3 + (z >> 2)) * PLANE + (y & 3) * BRICK + (z & 3))


def layer_matrix():
    row = lax.broadcasted_iota(jnp.int32, (2 * PLANE, VOXELS), 0)
    column = lax.broadcasted_iota(jnp.int32, (2 * PLANE, VOXELS), 1)
    return where_equal(column, ((row >> 2) & 3) * PLANE + (row >> 4) * 12 + (row & 3))


def expand_matrix(side):
    row = lax.broadcasted_iota(jnp.int32, (VOXELS, PLANE), 0)
    column = lax.broadcasted_iota(jnp.int32, (VOXELS, PLANE), 1)
    return where_equal(row, (column >> 2) * PLANE + side * 12 + (column & 3))


def pack_layers_kernel(recv_slot_ref, features_ref, cotangent_ref, to_first, to_second, to_sibling, to_outer,
                       own_f, own_c, sides, slot_ref, sems):
    bricks = (own_f, own_c)
    copies = [
        pltpu.make_async_copy(ref, target, sems.at[number])
        for number, (ref, target) in enumerate((
            (features_ref, own_f.at[pl.ds(0, SLOTS)]),
            (cotangent_ref, own_c.at[pl.ds(0, SLOTS)]),
            (recv_slot_ref, slot_ref),
        ))
    ]
    for copy in copies:
        copy.start()
    for own in bricks:
        own[SLOTS] = jnp.zeros((VOXELS, CHANNELS), jnp.bfloat16)
    sides[:, SLOTS] = jnp.zeros((2, 2 * PLANE, CHANNELS), jnp.bfloat16)
    core = lax.axis_index("c")
    odd = lax.axis_index("z") & 1
    layer = layer_matrix()
    for copy in copies:
        copy.wait()
    for kind in range(2):
        beside = jnp.concatenate([bricks[kind][slot] for slot in range(SLOTS)], axis=1)
        picked = jnp.dot(layer, beside, preferred_element_type=jnp.float32).astype(jnp.bfloat16)
        for slot in range(SLOTS):
            sides[kind, slot] = picked[:, slot * CHANNELS : (slot + 1) * CHANNELS]

    def put(packet, position, halo, source, begin):
        slot = jnp.clip(slot_ref[halo], 0, SLOTS)
        rows = pl.ds(begin, PLANE)
        packet[position, :, :CHANNELS] = source[0][slot, rows]
        packet[position, :, CHANNELS:] = source[1][slot, rows]

    for packet, up in ((to_first, 1 - odd), (to_second, odd)):
        begin = pl.multiple_of(up * PLANE, PLANE)
        position = 0
        for number in (2, 4, 6):
            for halo in range(LENGTHS[number]):
                put(packet, position, STARTS[number] + up * LENGTHS[number] + halo, (sides.at[0], sides.at[1]), begin)
                position += 1
    for packet, up in ((to_sibling, 1 - core), (to_outer, core)):
        begin = pl.multiple_of(up * (VOXELS - PLANE), PLANE)
        for position in range(LENGTHS[0]):
            put(packet, position, up * LENGTHS[0] + position, bricks, begin)


def pack_layers(recv_slot, features, cotangent):
    vmem = pl.BlockSpec(memory_space=pltpu.VMEM)
    hbm = pl.BlockSpec(memory_space=pltpu.HBM)
    return pl.pallas_call(
        pack_layers_kernel,
        in_specs=[hbm, hbm, hbm],
        out_specs=[vmem] * 6,
        out_shape=[
            jax.ShapeDtypeStruct((length, PLANE, 2 * CHANNELS), jnp.bfloat16) for length in (12, 12, 8, 8)
        ] + [jax.ShapeDtypeStruct((SLOTS + 1, VOXELS, CHANNELS), jnp.bfloat16)] * 2,
        scratch_shapes=[
            pltpu.VMEM((2, SLOTS + 1, 2 * PLANE, CHANNELS), jnp.bfloat16),
            pltpu.SMEM((HALO,), jnp.int32),
            pltpu.SemaphoreType.DMA((3,)),
        ],
        compiler_params=pltpu.CompilerParams(vmem_limit_bytes=VMEM_LIMIT),
    )(recv_slot, features, cotangent)


def fill_bricks(core, odd, halos, lanes, bricks):
    begin_at = SLOTS
    for halo in halos:
        bricks[begin_at : begin_at + halo.shape[0]] = halo[:, :, lanes]
        begin_at += halo.shape[0]


def fill_layers(core, odd, halos, lanes, bricks):
    y_first, y_second, x_sibling, x_outer = halos
    both = ((x_sibling, core), (x_outer, 1 - core))
    for packet, below in both:
        for position in range(SLOTS):
            tile = packet[position, :, lanes]
            target = SLOTS + below * LENGTHS[0] + position
            for begin in range(0, VOXELS, PLANE):
                bricks[target, begin : begin + PLANE] = tile
    for order, (faces, side) in enumerate(((y_first, odd), (y_second, 1 - odd))):
        tiles = [faces[position, :, lanes] for position in range(SLOTS)]
        targets = [STARTS[2] + side * LENGTHS[2] + position for position in range(SLOTS)]
        for packet, below in both:
            for position in range(BZ):
                tiles.append(packet[SLOTS + BZ * order + position, :, lanes])
                targets.append(STARTS[4] + side * BZ + below * 2 * BZ + position)
        whole = jnp.dot(
            expand_matrix(side), jnp.concatenate(tiles, axis=1), preferred_element_type=jnp.float32
        ).astype(jnp.bfloat16)
        for position, target in enumerate(targets):
            bricks[SLOTS + target] = whole[:, position * CHANNELS : (position + 1) * CHANNELS]


def out_of_place(dst):
    k = lax.broadcasted_iota(jnp.int32, dst.shape, 1)
    ninth = jnp.where(k >= 18, 2, jnp.where(k >= 9, 1, 0))
    rest = k - 9 * ninth
    offset = (ninth - 1, jnp.where(rest >= 6, 2, jnp.where(rest >= 3, 1, 0)) - 1)
    wrong = jnp.zeros(dst.shape, jnp.float32)
    for number, heading in enumerate(DIRECTIONS):
        start = SLOTS + STARTS[number]
        here = (dst >= start) & (dst < start + LENGTHS[number])
        for axis in range(2):
            if heading[axis]:
                wrong = jnp.where(here & (offset[axis] != heading[axis]), 1.0, wrong)
    return jnp.max(jnp.max(wrong, axis=1, keepdims=True), axis=0, keepdims=True)


def build_taps(fill, unroll, dst_ref, own_ref, halos, lanes, bricks, taps):
    bricks[:SLOTS] = own_ref[:SLOTS]
    fill(lax.axis_index("c"), lax.axis_index("z") & 1, halos, lanes, bricks)
    bricks[SLOTS + HALO] = jnp.zeros((VOXELS, CHANNELS), jnp.bfloat16)
    shift = shift_matrix()

    def around(slot, plane):
        side = 0 if plane == 0 else 2 if plane == PLANES - 1 else 1
        local = (plane - 1) % BRICK * PLANE
        return jnp.concatenate(
            [bricks[dst_ref[slot, side * 9 + number], local : local + PLANE] for number in range(9)], axis=0
        )

    def one_slot(slot, carry):
        for plane in range(0, PLANES, 2):
            pair = jnp.concatenate((around(slot, plane), around(slot, plane + 1)), axis=1)
            moved = jnp.dot(shift, pair, preferred_element_type=jnp.float32).astype(jnp.bfloat16)
            for number in range(9):
                rows = moved[number * PLANE : (number + 1) * PLANE]
                target = slice(number * CHANNELS, (number + 1) * CHANNELS)
                taps[slot, plane, :, target] = rows[:, :CHANNELS]
                taps[slot, plane + 1, :, target] = rows[:, CHANNELS:]
        return carry

    lax.fori_loop(0, SLOTS, one_slot, 0, unroll=unroll)


def weight_kernel(fill, unroll, count, dst_ref, table_ref, cotangent_ref, *rest):
    halos = rest[:count]
    flipped_ref, send_ref, keep_ref, taps, bricks = rest[count:]
    build_taps(fill, unroll, dst_ref, cotangent_ref, halos, slice(CHANNELS, 2 * CHANNELS), bricks, taps)
    core = lax.axis_index("c")
    flipped = jnp.concatenate((flipped_ref[1 - core], flipped_ref[core]), axis=0)
    half = CHANNELS // 2
    for side in range(3):
        tap = taps[:, side : side + BRICK].reshape(SLOTS * VOXELS, WIDE)
        part = jnp.dot(flipped, tap, preferred_element_type=jnp.float32)
        for number in range(9):
            block = part[:, number * CHANNELS : (number + 1) * CHANNELS]
            m = side * 9 + number
            for quarter in range(4):
                rows = slice(quarter * 16, quarter * 16 + 16)
                send_ref[quarter, m] = block[:half][rows].astype(jnp.bfloat16)
                keep_ref[quarter, m] = block[half:][rows]
    flag = jnp.broadcast_to(out_of_place(table_ref[...]), (16, CHANNELS))
    for quarter in range(4):
        send_ref[quarter, 27] = flag.astype(jnp.bfloat16)
        keep_ref[quarter, 27] = flag


def grad_kernel(taps, weights_ref, grad_ref):
    grad = None
    for side in range(3):
        tap = taps[:, side : side + BRICK].reshape(SLOTS * VOXELS, WIDE)
        matrix = jnp.concatenate([weights_ref[26 - side * 9 - number] for number in range(9)], axis=1)
        part = lax.dot_general(tap, matrix, (((1,), (1,)), ((), ())), preferred_element_type=jnp.float32)
        grad = part if grad is None else grad + part
    grad_ref[...] = grad.astype(jnp.bfloat16).reshape(SLOTS, VOXELS, CHANNELS)


def taps_kernel(fill, unroll, count, dst_ref, features_ref, *rest):
    taps, bricks = rest[count:]
    build_taps(fill, unroll, dst_ref, features_ref, rest[:count], slice(0, CHANNELS), bricks, taps)


def output_kernel(taps, weights_ref, outputs_ref):
    outputs = None
    for side in range(3):
        tap = taps[:, side : side + BRICK].reshape(SLOTS * VOXELS, WIDE)
        matrix = weights_ref[side * 9 : side * 9 + 9].reshape(WIDE, CHANNELS)
        part = jnp.dot(tap, matrix, preferred_element_type=jnp.float32)
        outputs = part if outputs is None else outputs + part
    outputs_ref[...] = outputs.astype(jnp.bfloat16).reshape(SLOTS, VOXELS, CHANNELS)


VMEM_SPEC = pl.BlockSpec(memory_space=pltpu.VMEM)
SMEM_SPEC = pl.BlockSpec(memory_space=pltpu.SMEM)
BRICK_SHAPE = jax.ShapeDtypeStruct((SLOTS, VOXELS, CHANNELS), jnp.bfloat16)
TAPS_SHAPE = jax.ShapeDtypeStruct((SLOTS, PLANES, PLANE, WIDE), jnp.bfloat16)
ALL_BRICKS = pltpu.VMEM((SLOTS + HALO + 1, VOXELS, CHANNELS), jnp.bfloat16)
PARAMS = pltpu.CompilerParams(vmem_limit_bytes=VMEM_LIMIT)
COST = pl.CostEstimate(flops=4 * SLOTS * VOXELS * 27 * CHANNELS * CHANNELS, bytes_accessed=4_000_000, transcendentals=0)


def weight_sums(fill, unroll, dst, own_c, halos, flipped):
    return pl.pallas_call(
        functools.partial(weight_kernel, fill, unroll, len(halos)),
        in_specs=[SMEM_SPEC] + [VMEM_SPEC] * (3 + len(halos)),
        out_specs=[VMEM_SPEC] * 3,
        out_shape=[
            jax.ShapeDtypeStruct((4, ROWS_M, 16, CHANNELS), jnp.bfloat16),
            jax.ShapeDtypeStruct((4, ROWS_M, 16, CHANNELS), jnp.float32),
            TAPS_SHAPE,
        ],
        scratch_shapes=[ALL_BRICKS],
        compiler_params=PARAMS,
        cost_estimate=COST,
    )(dst, dst, own_c, *halos, flipped)


def feature_taps(fill, unroll, dst, own_f, halos):
    return pl.pallas_call(
        functools.partial(taps_kernel, fill, unroll, len(halos)),
        in_specs=[SMEM_SPEC] + [VMEM_SPEC] * (1 + len(halos)),
        out_specs=VMEM_SPEC,
        out_shape=TAPS_SHAPE,
        scratch_shapes=[ALL_BRICKS],
        compiler_params=PARAMS,
        cost_estimate=COST,
    )(dst, own_f, *halos)


def product(kernel, taps, weights):
    return pl.pallas_call(
        kernel,
        in_specs=[VMEM_SPEC] * 2,
        out_specs=VMEM_SPEC,
        out_shape=BRICK_SHAPE,
        compiler_params=PARAMS,
        cost_estimate=COST,
    )(taps, weights)


def convolve(fill, unroll, dst, own_f, own_c, halos, flipped, weights):
    send, keep, taps_c = weight_sums(fill, unroll, dst, own_c, halos, flipped)
    arrived = lax.ppermute(send, "c", [(0, 1), (1, 0)])
    input_grad = product(grad_kernel, taps_c, weights)
    taps_f = feature_taps(fill, unroll, dst, own_f, halos)
    arrived, input_grad, taps_f = lax.optimization_barrier((arrived, input_grad, taps_f))
    own = sum_everywhere(arrived, keep)
    other = lax.ppermute(own, "c", [(0, 1), (1, 0)])
    outputs = product(output_kernel, taps_f, weights)
    return outputs, input_grad, own, other


def pack_bricks_kernel(slot_ref, features_ref, cotangent_ref, *packets):
    begin_at = 0
    for packet in packets:
        for position in range(packet.shape[0]):
            slot = slot_ref[begin_at + position]
            row = jnp.clip(slot, 0, SLOTS - 1)

            @pl.when(slot < SLOTS)
            def _():
                packet[position, :, :CHANNELS] = features_ref[row]
                packet[position, :, CHANNELS:] = cotangent_ref[row]

            @pl.when(slot >= SLOTS)
            def _():
                packet[position] = jnp.zeros((VOXELS, 2 * CHANNELS), jnp.bfloat16)

        begin_at += packet.shape[0]


def pack_bricks(recv_slot, features, cotangent):
    vmem = pl.BlockSpec(memory_space=pltpu.VMEM)
    return pl.pallas_call(
        pack_bricks_kernel,
        in_specs=[pl.BlockSpec(memory_space=pltpu.SMEM), vmem, vmem],
        out_specs=[vmem] * 8,
        out_shape=[
            jax.ShapeDtypeStruct((length, VOXELS, 2 * CHANNELS), jnp.bfloat16) for length in LENGTHS
        ],
        compiler_params=pltpu.CompilerParams(vmem_limit_bytes=VMEM_LIMIT),
    )(recv_slot, features, cotangent)


def pass_to(value, step_x, step_y):
    pairs = []
    for gx in range(8):
        for gy in range(32):
            if 0 <= gx + step_x < 8 and 0 <= gy + step_y < 32:
                pairs.append((gx * 32 + gy, (gx + step_x) * 32 + gy + step_y))
    return lax.ppermute(value, AXES, pairs)


def sum_everywhere(arrived, keep):
    chip_sum = (keep + arrived.astype(jnp.float32)).astype(jnp.bfloat16)
    parts = chip_sum.reshape(16, 7, 16, CHANNELS)
    parts = lax.all_to_all(parts, ("x", "y"), 0, 0)
    total = jnp.sum(parts.astype(jnp.float32), axis=0)
    largest = jnp.max(jnp.abs(total), axis=(0, 1))
    power = jnp.clip(jnp.ceil(jnp.log2(jnp.maximum(largest, 1e-37))), -100.0, 100.0)
    power = jnp.broadcast_to(power, (1, 16, CHANNELS))
    share = jnp.concatenate((total * jnp.exp2(14.0 - power), power), axis=0).astype(jnp.float16)
    column = lax.all_to_all(jnp.broadcast_to(share[None], (8,) + share.shape), "z", 0, 0).astype(jnp.float32)
    total = jnp.sum(column[:, :7] * jnp.exp2(column[:, 7:] - 14.0), axis=0)
    share = (total * (1.0 / (VOXELS * SLOTS))).astype(jnp.bfloat16)
    whole = jnp.broadcast_to(share[None], (16,) + share.shape)
    return lax.all_to_all(whole, ("x", "y"), 0, 0).reshape(4, ROWS_M, 16, CHANNELS)


def spread_kernel(own_ref, other_ref, outputs_ref, grad_ref, outputs_out, grad_out, out_ref, whole, sems):
    half = CHANNELS // 2
    core = lax.axis_index("c")
    copies = [
        pltpu.make_async_copy(outputs_ref, outputs_out, sems.at[9]),
        pltpu.make_async_copy(grad_ref, grad_out, sems.at[10]),
    ]
    for copy in copies:
        copy.start()
    for chunk in range(9):
        for m in range(3 * chunk, 3 * chunk + 3):
            for quarter in range(4):
                for ref, side in ((own_ref, core), (other_ref, 1 - core)):
                    begin = pl.multiple_of(side * half + quarter * 16, 16)
                    whole[26 - m, pl.ds(begin, 16)] = ref[quarter, m].astype(jnp.float32)
        rows = pl.ds(24 - 3 * chunk, 3)
        copies.append(pltpu.make_async_copy(whole.at[rows], out_ref.at[rows], sems.at[chunk]))
        copies[-1].start()
    for copy in copies:
        copy.wait()


def spread_out(outputs, input_grad, own, other):
    return pl.pallas_call(
        spread_kernel,
        in_specs=[VMEM_SPEC] * 4,
        out_specs=[pl.BlockSpec(memory_space=pltpu.HBM)] * 3,
        out_shape=[BRICK_SHAPE, BRICK_SHAPE, jax.ShapeDtypeStruct((27, CHANNELS, CHANNELS), jnp.float32)],
        scratch_shapes=[
            pltpu.VMEM((27, CHANNELS, CHANNELS), jnp.float32),
            pltpu.SemaphoreType.DMA((11,)),
        ],
        compiler_params=PARAMS,
    )(own, other, outputs, input_grad)


def local(features, weights, cotangent, dst_index, recv_slot):
    core = lax.axis_index("c")
    dst = jnp.clip(dst_index.T, 0, SLOTS + HALO)

    to_first, to_second, to_sibling, to_outer, own_f, own_c = pack_layers(recv_slot, features, cotangent)
    flipped = jnp.transpose(own_f[:SLOTS].reshape(SLOTS * VOXELS, CHANNELS))
    flipped = flipped.reshape(2, CHANNELS // 2, SLOTS * VOXELS)
    y_first = lax.ppermute(to_first, ("y", "z"), [(gy, gy ^ 1) for gy in range(32)])
    y_second = lax.ppermute(to_second, ("y", "z"), [(gy, ((gy + 1) ^ 1) - 1) for gy in range(1, 31)])

    def relayed(packet, up):
        corners = [lax.dynamic_slice_in_dim(value, SLOTS + BZ * up, BZ, axis=0) for value in (y_first, y_second)]
        return jnp.concatenate((packet, *corners), axis=0)

    x_outer = lax.ppermute(relayed(to_outer, core), ("x", "c"), [(2 * x + 1, 2 * x + 2) for x in range(3)]
                           + [(2 * x + 2, 2 * x + 1) for x in range(3)])
    x_sibling = lax.ppermute(relayed(to_sibling, 1 - core), "c", [(0, 1), (1, 0)])
    halos = (y_first, y_second, x_sibling, x_outer)
    results = convolve(fill_layers, SLOTS, dst, own_f, own_c, halos, flipped, weights)

    def with_whole_bricks(results):
        packets = pack_bricks(recv_slot, features, cotangent)
        halos = [pass_to(packet, -heading[0], -heading[1]) for packet, heading in zip(packets, DIRECTIONS)]
        return spread_out(*convolve(fill_bricks, 1, dst, own_f, own_c, halos, flipped, weights))

    def as_they_are(results):
        return spread_out(*results)

    own = results[2]
    return tuple(lax.cond(own[0, 27, 0, 0] != 0, with_whole_bricks, as_they_are, results))


def solution(mesh):
    fine = Mesh(mesh.devices.reshape(4, 2, 4, 8), AXES)
    bricks = P(AXES, None, None)
    return jax.shard_map(
        local,
        mesh=fine,
        in_specs=(bricks, P(), bricks, P(None, AXES), P(AXES)),
        out_specs=(bricks, bricks, P()),
        check_vma=False,
    )
```

```python
import functools

import jax
import jax.numpy as jnp
import numpy as np
from jax import lax
from jax.experimental import pallas as pl
from jax.experimental.pallas import tpu as pltpu
from jax.sharding import Mesh, PartitionSpec as P

BRICK = 4
TILE = 4
BZ = 2
HALO = 40
SLOTS = 8
VOXELS = 64
CHANNELS = 128
PLANE = BRICK * BRICK
PLANES = BRICK + 2
WIDE = 9 * CHANNELS
ROWS_M = 28

DIRECTIONS = ((1, 0), (-1, 0), (0, 1), (0, -1), (1, 1), (1, -1), (-1, 1), (-1, -1))
LENGTHS = (TILE * BZ,) * 4 + (BZ,) * 4
STARTS = tuple(int(start) for start in np.cumsum((0,) + LENGTHS[:-1]))
AXES = ("x", "c", "y", "z")
VMEM_LIMIT = 24 * 1024 * 1024


def where_equal(left, right):
    return jnp.where(left == right, 1.0, 0.0).astype(jnp.bfloat16)


def shift_matrix():
    row = lax.broadcasted_iota(jnp.int32, (9 * PLANE, 9 * PLANE), 0)
    column = lax.broadcasted_iota(jnp.int32, (9 * PLANE, 9 * PLANE), 1)
    number = row >> 4
    third = (number * 11) >> 5
    y = ((row >> 2) & 3) + third + 3
    z = (row & 3) + number - 3 * third + 3
    return where_equal(column, ((y >> 2) * 3 + (z >> 2)) * PLANE + (y & 3) * BRICK + (z & 3))


def layer_matrix():
    row = lax.broadcasted_iota(jnp.int32, (2 * PLANE, VOXELS), 0)
    column = lax.broadcasted_iota(jnp.int32, (2 * PLANE, VOXELS), 1)
    return where_equal(column, ((row >> 2) & 3) * PLANE + (row >> 4) * 12 + (row & 3))


def expand_matrix(side):
    row = lax.broadcasted_iota(jnp.int32, (VOXELS, PLANE), 0)
    column = lax.broadcasted_iota(jnp.int32, (VOXELS, PLANE), 1)
    return where_equal(row, (column >> 2) * PLANE + side * 12 + (column & 3))


def pack_layers_kernel(recv_slot_ref, features_ref, cotangent_ref, to_first, to_second, to_sibling, to_outer,
                       own_f, own_c, sides, slot_ref, sems):
    bricks = (own_f, own_c)
    copies = [
        pltpu.make_async_copy(ref, target, sems.at[number])
        for number, (ref, target) in enumerate((
            (features_ref, own_f.at[pl.ds(0, SLOTS)]),
            (cotangent_ref, own_c.at[pl.ds(0, SLOTS)]),
            (recv_slot_ref, slot_ref),
        ))
    ]
    for copy in copies:
        copy.start()
    for own in bricks:
        own[SLOTS] = jnp.zeros((VOXELS, CHANNELS), jnp.bfloat16)
    sides[:, SLOTS] = jnp.zeros((2, 2 * PLANE, CHANNELS), jnp.bfloat16)
    core = lax.axis_index("c")
    odd = lax.axis_index("z") & 1
    layer = layer_matrix()
    for copy in copies:
        copy.wait()
    for kind in range(2):
        beside = jnp.concatenate([bricks[kind][slot] for slot in range(SLOTS)], axis=1)
        picked = jnp.dot(layer, beside, preferred_element_type=jnp.float32).astype(jnp.bfloat16)
        for slot in range(SLOTS):
            sides[kind, slot] = picked[:, slot * CHANNELS : (slot + 1) * CHANNELS]

    def put(packet, position, halo, source, begin):
        slot = jnp.clip(slot_ref[halo], 0, SLOTS)
        rows = pl.ds(begin, PLANE)
        packet[position, :, :CHANNELS] = source[0][slot, rows]
        packet[position, :, CHANNELS:] = source[1][slot, rows]

    for packet, up in ((to_first, 1 - odd), (to_second, odd)):
        begin = pl.multiple_of(up * PLANE, PLANE)
        position = 0
        for number in (2, 4, 6):
            for halo in range(LENGTHS[number]):
                put(packet, position, STARTS[number] + up * LENGTHS[number] + halo, (sides.at[0], sides.at[1]), begin)
                position += 1
    for packet, up in ((to_sibling, 1 - core), (to_outer, core)):
        begin = pl.multiple_of(up * (VOXELS - PLANE), PLANE)
        for position in range(LENGTHS[0]):
            put(packet, position, up * LENGTHS[0] + position, bricks, begin)


def pack_layers(recv_slot, features, cotangent):
    vmem = pl.BlockSpec(memory_space=pltpu.VMEM)
    hbm = pl.BlockSpec(memory_space=pltpu.HBM)
    return pl.pallas_call(
        pack_layers_kernel,
        in_specs=[hbm, hbm, hbm],
        out_specs=[vmem] * 6,
        out_shape=[
            jax.ShapeDtypeStruct((length, PLANE, 2 * CHANNELS), jnp.bfloat16) for length in (12, 12, 8, 8)
        ] + [jax.ShapeDtypeStruct((SLOTS + 1, VOXELS, CHANNELS), jnp.bfloat16)] * 2,
        scratch_shapes=[
            pltpu.VMEM((2, SLOTS + 1, 2 * PLANE, CHANNELS), jnp.bfloat16),
            pltpu.SMEM((HALO,), jnp.int32),
            pltpu.SemaphoreType.DMA((3,)),
        ],
        compiler_params=pltpu.CompilerParams(vmem_limit_bytes=VMEM_LIMIT),
    )(recv_slot, features, cotangent)


def fill_bricks(halos, lanes, bricks):
    begin_at = SLOTS
    for halo in halos:
        bricks[begin_at : begin_at + halo.shape[0]] = halo[:, :, lanes]
        begin_at += halo.shape[0]


def expand_tiles(side, tiles, targets, bricks):
    whole = jnp.dot(
        expand_matrix(side), jnp.concatenate(tiles, axis=1), preferred_element_type=jnp.float32
    ).astype(jnp.bfloat16)
    for position, target in enumerate(targets):
        bricks[SLOTS + target] = whole[:, position * CHANNELS : (position + 1) * CHANNELS]


def fill_along_y(halos, lanes, bricks):
    odd = lax.axis_index("z") & 1
    for faces, side in ((halos[0], odd), (halos[1], 1 - odd)):
        tiles = [faces[position, :, lanes] for position in range(SLOTS)]
        targets = [STARTS[2] + side * LENGTHS[2] + position for position in range(SLOTS)]
        expand_tiles(side, tiles, targets, bricks)


def fill_along_x(halos, lanes, bricks):
    core, odd = lax.axis_index("c"), lax.axis_index("z") & 1
    both = ((halos[0], core), (halos[1], 1 - core))
    for packet, below in both:
        for position in range(SLOTS):
            tile = packet[position, :, lanes]
            target = SLOTS + below * LENGTHS[0] + position
            for begin in range(0, VOXELS, PLANE):
                bricks[target, begin : begin + PLANE] = tile
    for order, side in ((0, odd), (1, 1 - odd)):
        tiles = []
        targets = []
        for packet, below in both:
            for position in range(BZ):
                tiles.append(packet[SLOTS + BZ * order + position, :, lanes])
                targets.append(STARTS[4] + side * BZ + below * 2 * BZ + position)
        expand_tiles(side, tiles, targets, bricks)


def fill_nothing(halos, lanes, bricks):
    pass


def out_of_place(dst):
    k = lax.broadcasted_iota(jnp.int32, dst.shape, 1)
    ninth = jnp.where(k >= 18, 2, jnp.where(k >= 9, 1, 0))
    rest = k - 9 * ninth
    offset = (ninth - 1, jnp.where(rest >= 6, 2, jnp.where(rest >= 3, 1, 0)) - 1)
    wrong = jnp.zeros(dst.shape, jnp.float32)
    for number, heading in enumerate(DIRECTIONS):
        start = SLOTS + STARTS[number]
        here = (dst >= start) & (dst < start + LENGTHS[number])
        for axis in range(2):
            if heading[axis]:
                wrong = jnp.where(here & (offset[axis] != heading[axis]), 1.0, wrong)
    return jnp.max(jnp.max(wrong, axis=1, keepdims=True), axis=0, keepdims=True)


def build_taps(unroll, dst_ref, bricks, planes, taps):
    shift = shift_matrix()

    def around(slot, plane):
        side = 0 if plane == 0 else 2 if plane == PLANES - 1 else 1
        local = (plane - 1) % BRICK * PLANE
        return jnp.concatenate(
            [bricks[dst_ref[slot, side * 9 + number], local : local + PLANE] for number in range(9)], axis=0
        )

    def one_slot(slot, carry):
        for index in range(0, len(planes), 2):
            pair = jnp.concatenate((around(slot, planes[index]), around(slot, planes[index + 1])), axis=1)
            moved = jnp.dot(shift, pair, preferred_element_type=jnp.float32).astype(jnp.bfloat16)
            for number in range(9):
                rows = moved[number * PLANE : (number + 1) * PLANE]
                target = slice(number * CHANNELS, (number + 1) * CHANNELS)
                taps[slot, index, :, target] = rows[:, :CHANNELS]
                taps[slot, index + 1, :, target] = rows[:, CHANNELS:]
        return carry

    lax.fori_loop(0, SLOTS, one_slot, 0, unroll=unroll)


def taps_of(mid, edge, side):
    if side == 0:
        planes = jnp.concatenate((edge[:, :1], mid[:, :3]), axis=1)
    elif side == 1:
        planes = mid[...]
    else:
        planes = jnp.concatenate((mid[:, 1:], edge[:, 1:]), axis=1)
    return planes.reshape(SLOTS * VOXELS, WIDE)


def mid_kernel(fill, unroll, count, dst_ref, features_ref, cotangent_ref, *rest):
    halos = rest[:count]
    mid_f, mid_c, bricks_f, bricks_c = rest[count:]
    for kind, (own, bricks, mid) in enumerate(((features_ref, bricks_f, mid_f), (cotangent_ref, bricks_c, mid_c))):
        bricks[:SLOTS] = own[:SLOTS]
        for begin, end in ((SLOTS, SLOTS + STARTS[2]), (SLOTS + STARTS[4], SLOTS + HALO + 1)):
            bricks[begin:end] = jnp.zeros((end - begin, VOXELS, CHANNELS), jnp.bfloat16)
        fill(halos, slice(kind * CHANNELS, (kind + 1) * CHANNELS), bricks)
        build_taps(unroll, dst_ref, bricks, (1, 2, 3, 4), mid)


def weight_kernel(fill, unroll, count, dst_ref, table_ref, mid, _, *rest):
    halos = rest[:count]
    flipped_ref, send_ref, keep_ref, edge, bricks = rest[count:]
    fill(halos, slice(CHANNELS, 2 * CHANNELS), bricks)
    build_taps(unroll, dst_ref, bricks, (0, PLANES - 1), edge)
    core = lax.axis_index("c")
    flipped = jnp.concatenate((flipped_ref[1 - core], flipped_ref[core]), axis=0)
    half = CHANNELS // 2
    for side in (1, 0, 2):
        part = jnp.dot(flipped, taps_of(mid, edge, side), preferred_element_type=jnp.float32)
        for number in range(9):
            block = part[:, number * CHANNELS : (number + 1) * CHANNELS]
            m = side * 9 + number
            for quarter in range(4):
                rows = slice(quarter * 16, quarter * 16 + 16)
                send_ref[quarter, m] = block[:half][rows].astype(jnp.bfloat16)
                keep_ref[quarter, m] = block[half:][rows]
    flag = jnp.broadcast_to(out_of_place(table_ref[...]), (16, CHANNELS))
    for quarter in range(4):
        send_ref[quarter, 27] = flag.astype(jnp.bfloat16)
        keep_ref[quarter, 27] = flag


def grad_kernel(mid, edge, weights_ref, grad_ref):
    grad = None
    for side in range(3):
        matrix = jnp.concatenate([weights_ref[26 - side * 9 - number] for number in range(9)], axis=1)
        part = lax.dot_general(
            taps_of(mid, edge, side), matrix, (((1,), (1,)), ((), ())), preferred_element_type=jnp.float32
        )
        grad = part if grad is None else grad + part
    grad_ref[...] = grad.astype(jnp.bfloat16).reshape(SLOTS, VOXELS, CHANNELS)


def edge_kernel(fill, unroll, count, dst_ref, _, *rest):
    edge, bricks = rest[count:]
    fill(rest[:count], slice(0, CHANNELS), bricks)
    build_taps(unroll, dst_ref, bricks, (0, PLANES - 1), edge)


def output_kernel(mid, edge, weights_ref, outputs_ref):
    outputs = None
    for side in range(3):
        matrix = weights_ref[side * 9 : side * 9 + 9].reshape(WIDE, CHANNELS)
        part = jnp.dot(taps_of(mid, edge, side), matrix, preferred_element_type=jnp.float32)
        outputs = part if outputs is None else outputs + part
    outputs_ref[...] = outputs.astype(jnp.bfloat16).reshape(SLOTS, VOXELS, CHANNELS)


VMEM_SPEC = pl.BlockSpec(memory_space=pltpu.VMEM)
SMEM_SPEC = pl.BlockSpec(memory_space=pltpu.SMEM)
BRICK_SHAPE = jax.ShapeDtypeStruct((SLOTS, VOXELS, CHANNELS), jnp.bfloat16)
MID_SHAPE = jax.ShapeDtypeStruct((SLOTS, BRICK, PLANE, WIDE), jnp.bfloat16)
EDGE_SHAPE = jax.ShapeDtypeStruct((SLOTS, 2, PLANE, WIDE), jnp.bfloat16)
ALL_BRICKS = jax.ShapeDtypeStruct((SLOTS + HALO + 1, VOXELS, CHANNELS), jnp.bfloat16)
PARAMS = pltpu.CompilerParams(vmem_limit_bytes=VMEM_LIMIT)
COST = pl.CostEstimate(flops=4 * SLOTS * VOXELS * 27 * CHANNELS * CHANNELS, bytes_accessed=4_000_000, transcendentals=0)


def mid_taps(fill, unroll, dst, own_f, own_c, halos):
    return pl.pallas_call(
        functools.partial(mid_kernel, fill, unroll, len(halos)),
        in_specs=[SMEM_SPEC] + [VMEM_SPEC] * (2 + len(halos)),
        out_specs=[VMEM_SPEC] * 4,
        out_shape=[MID_SHAPE, MID_SHAPE, ALL_BRICKS, ALL_BRICKS],
        compiler_params=PARAMS,
        cost_estimate=COST,
    )(dst, own_f, own_c, *halos)


def weight_sums(fill, unroll, dst, mid, bricks, halos, flipped):
    return pl.pallas_call(
        functools.partial(weight_kernel, fill, unroll, len(halos)),
        in_specs=[SMEM_SPEC] + [VMEM_SPEC] * (4 + len(halos)),
        out_specs=[VMEM_SPEC] * 4,
        out_shape=[
            jax.ShapeDtypeStruct((4, ROWS_M, 16, CHANNELS), jnp.bfloat16),
            jax.ShapeDtypeStruct((4, ROWS_M, 16, CHANNELS), jnp.float32),
            EDGE_SHAPE,
            ALL_BRICKS,
        ],
        input_output_aliases={3: 3},
        compiler_params=PARAMS,
        cost_estimate=COST,
    )(dst, dst, mid, bricks, *halos, flipped)


def feature_edges(fill, unroll, dst, bricks, halos):
    return pl.pallas_call(
        functools.partial(edge_kernel, fill, unroll, len(halos)),
        in_specs=[SMEM_SPEC] + [VMEM_SPEC] * (1 + len(halos)),
        out_specs=[VMEM_SPEC] * 2,
        out_shape=[EDGE_SHAPE, ALL_BRICKS],
        input_output_aliases={1: 1},
        compiler_params=PARAMS,
        cost_estimate=COST,
    )(dst, bricks, *halos)[0]


def product(kernel, mid, edge, weights):
    return pl.pallas_call(
        kernel,
        in_specs=[VMEM_SPEC] * 3,
        out_specs=VMEM_SPEC,
        out_shape=BRICK_SHAPE,
        compiler_params=PARAMS,
        cost_estimate=COST,
    )(mid, edge, weights)


def convolve(fill, unroll, dst, mids, halos, flipped, weights):
    mid_f, mid_c, bricks_f, bricks_c = mids
    send, keep, edge_c, _ = weight_sums(fill, unroll, dst, mid_c, bricks_c, halos, flipped)
    arrived = lax.ppermute(send, "c", [(0, 1), (1, 0)])
    input_grad = product(grad_kernel, mid_c, edge_c, weights)
    edge_f = feature_edges(fill, unroll, dst, bricks_f, halos)
    arrived, input_grad, edge_f = lax.optimization_barrier((arrived, input_grad, edge_f))
    own = sum_everywhere(arrived, keep)
    other = lax.ppermute(own, "c", [(0, 1), (1, 0)])
    outputs = product(output_kernel, mid_f, edge_f, weights)
    return outputs, input_grad, own, other


def pack_bricks_kernel(slot_ref, features_ref, cotangent_ref, *packets):
    begin_at = 0
    for packet in packets:
        for position in range(packet.shape[0]):
            slot = slot_ref[begin_at + position]
            row = jnp.clip(slot, 0, SLOTS - 1)

            @pl.when(slot < SLOTS)
            def _():
                packet[position, :, :CHANNELS] = features_ref[row]
                packet[position, :, CHANNELS:] = cotangent_ref[row]

            @pl.when(slot >= SLOTS)
            def _():
                packet[position] = jnp.zeros((VOXELS, 2 * CHANNELS), jnp.bfloat16)

        begin_at += packet.shape[0]


def pack_bricks(recv_slot, features, cotangent):
    vmem = pl.BlockSpec(memory_space=pltpu.VMEM)
    return pl.pallas_call(
        pack_bricks_kernel,
        in_specs=[pl.BlockSpec(memory_space=pltpu.SMEM), vmem, vmem],
        out_specs=[vmem] * 8,
        out_shape=[
            jax.ShapeDtypeStruct((length, VOXELS, 2 * CHANNELS), jnp.bfloat16) for length in LENGTHS
        ],
        compiler_params=pltpu.CompilerParams(vmem_limit_bytes=VMEM_LIMIT),
    )(recv_slot, features, cotangent)


def pass_to(value, step_x, step_y):
    pairs = []
    for gx in range(8):
        for gy in range(32):
            if 0 <= gx + step_x < 8 and 0 <= gy + step_y < 32:
                pairs.append((gx * 32 + gy, (gx + step_x) * 32 + gy + step_y))
    return lax.ppermute(value, AXES, pairs)


def sum_everywhere(arrived, keep):
    chip_sum = (keep + arrived.astype(jnp.float32)).astype(jnp.bfloat16)
    parts = chip_sum.reshape(16, 7, 16, CHANNELS)
    parts = lax.all_to_all(parts, ("x", "y"), 0, 0)
    total = jnp.sum(parts.astype(jnp.float32), axis=0)
    largest = jnp.max(jnp.abs(total), axis=(0, 1))
    power = jnp.clip(jnp.ceil(jnp.log2(jnp.maximum(largest, 1e-37))), -100.0, 100.0)
    power = jnp.broadcast_to(power, (1, 16, CHANNELS))
    share = jnp.concatenate((total * jnp.exp2(14.0 - power), power), axis=0).astype(jnp.float16)
    column = lax.all_to_all(jnp.broadcast_to(share[None], (8,) + share.shape), "z", 0, 0).astype(jnp.float32)
    total = jnp.sum(column[:, :7] * jnp.exp2(column[:, 7:] - 14.0), axis=0)
    share = (total * (1.0 / (VOXELS * SLOTS))).astype(jnp.bfloat16)
    whole = jnp.broadcast_to(share[None], (16,) + share.shape)
    return lax.all_to_all(whole, ("x", "y"), 0, 0).reshape(4, ROWS_M, 16, CHANNELS)


def spread_kernel(own_ref, other_ref, outputs_ref, grad_ref, outputs_out, grad_out, out_ref, whole, sems):
    half = CHANNELS // 2
    core = lax.axis_index("c")
    copies = [
        pltpu.make_async_copy(outputs_ref, outputs_out, sems.at[9]),
        pltpu.make_async_copy(grad_ref, grad_out, sems.at[10]),
    ]
    for copy in copies:
        copy.start()
    for chunk in range(9):
        for m in range(3 * chunk, 3 * chunk + 3):
            for quarter in range(4):
                for ref, side in ((own_ref, core), (other_ref, 1 - core)):
                    begin = pl.multiple_of(side * half + quarter * 16, 16)
                    whole[26 - m, pl.ds(begin, 16)] = ref[quarter, m].astype(jnp.float32)
        rows = pl.ds(24 - 3 * chunk, 3)
        copies.append(pltpu.make_async_copy(whole.at[rows], out_ref.at[rows], sems.at[chunk]))
        copies[-1].start()
    for copy in copies:
        copy.wait()


def spread_out(outputs, input_grad, own, other):
    return pl.pallas_call(
        spread_kernel,
        in_specs=[VMEM_SPEC] * 4,
        out_specs=[pl.BlockSpec(memory_space=pltpu.HBM)] * 3,
        out_shape=[BRICK_SHAPE, BRICK_SHAPE, jax.ShapeDtypeStruct((27, CHANNELS, CHANNELS), jnp.float32)],
        scratch_shapes=[
            pltpu.VMEM((27, CHANNELS, CHANNELS), jnp.float32),
            pltpu.SemaphoreType.DMA((11,)),
        ],
        compiler_params=PARAMS,
    )(own, other, outputs, input_grad)


def local(features, weights, cotangent, dst_index, recv_slot):
    core = lax.axis_index("c")
    dst = jnp.clip(dst_index.T, 0, SLOTS + HALO)

    to_first, to_second, to_sibling, to_outer, own_f, own_c = pack_layers(recv_slot, features, cotangent)
    flipped = jnp.transpose(own_f[:SLOTS].reshape(SLOTS * VOXELS, CHANNELS))
    flipped = flipped.reshape(2, CHANNELS // 2, SLOTS * VOXELS)
    y_first = lax.ppermute(to_first, ("y", "z"), [(gy, gy ^ 1) for gy in range(32)])
    y_second = lax.ppermute(to_second, ("y", "z"), [(gy, ((gy + 1) ^ 1) - 1) for gy in range(1, 31)])

    def relayed(packet, up):
        corners = [lax.dynamic_slice_in_dim(value, SLOTS + BZ * up, BZ, axis=0) for value in (y_first, y_second)]
        return jnp.concatenate((packet, *corners), axis=0)

    x_outer = lax.ppermute(relayed(to_outer, core), ("x", "c"), [(2 * x + 1, 2 * x + 2) for x in range(3)]
                           + [(2 * x + 2, 2 * x + 1) for x in range(3)])
    x_sibling = lax.ppermute(relayed(to_sibling, 1 - core), "c", [(0, 1), (1, 0)])
    mids = mid_taps(fill_along_y, SLOTS, dst, own_f, own_c, (y_first, y_second))
    results = convolve(fill_along_x, SLOTS, dst, mids, (x_sibling, x_outer), flipped, weights)

    def with_whole_bricks(results):
        packets = pack_bricks(recv_slot, features, cotangent)
        halos = [pass_to(packet, -heading[0], -heading[1]) for packet, heading in zip(packets, DIRECTIONS)]
        mids = mid_taps(fill_bricks, 1, dst, own_f, own_c, halos)
        return spread_out(*convolve(fill_nothing, 1, dst, mids, (), flipped, weights))

    def as_they_are(results):
        return spread_out(*results)

    own = results[2]
    return tuple(lax.cond(own[0, 27, 0, 0] != 0, with_whole_bricks, as_they_are, results))


def solution(mesh):
    fine = Mesh(mesh.devices.reshape(4, 2, 4, 8), AXES)
    bricks = P(AXES, None, None)
    return jax.shard_map(
        local,
        mesh=fine,
        in_specs=(bricks, P(), bricks, P(None, AXES), P(AXES)),
        out_specs=(bricks, bricks, P()),
        check_vma=False,
    )
```

```python
import functools

import jax
import jax.numpy as jnp
import numpy as np
from jax import lax
from jax.experimental import pallas as pl
from jax.experimental.pallas import tpu as pltpu
from jax.sharding import Mesh, PartitionSpec as P

BRICK = 4
TILE = 4
BZ = 2
HALO = 40
SLOTS = 8
VOXELS = 64
CHANNELS = 128
PLANE = BRICK * BRICK
PLANES = BRICK + 2
WIDE = 9 * CHANNELS
ROWS_M = 28

DIRECTIONS = ((1, 0), (-1, 0), (0, 1), (0, -1), (1, 1), (1, -1), (-1, 1), (-1, -1))
LENGTHS = (TILE * BZ,) * 4 + (BZ,) * 4
STARTS = tuple(int(start) for start in np.cumsum((0,) + LENGTHS[:-1]))
AXES = ("x", "c", "y", "z")
VMEM_LIMIT = 24 * 1024 * 1024


def where_equal(left, right):
    return jnp.where(left == right, 1.0, 0.0).astype(jnp.bfloat16)


def shift_matrix():
    row = lax.broadcasted_iota(jnp.int32, (9 * PLANE, 9 * PLANE), 0)
    column = lax.broadcasted_iota(jnp.int32, (9 * PLANE, 9 * PLANE), 1)
    number = row >> 4
    third = (number * 11) >> 5
    y = ((row >> 2) & 3) + third + 3
    z = (row & 3) + number - 3 * third + 3
    return where_equal(column, ((y >> 2) * 3 + (z >> 2)) * PLANE + (y & 3) * BRICK + (z & 3))


def layer_matrix():
    row = lax.broadcasted_iota(jnp.int32, (4 * PLANE, VOXELS), 0)
    column = lax.broadcasted_iota(jnp.int32, (4 * PLANE, VOXELS), 1)
    quarter = (row >> 2) & 3
    vx = jnp.where(row < 2 * PLANE, quarter, (quarter >> 1) * 3)
    return where_equal(column, vx * PLANE + ((row >> 4) & 1) * 12 + (row & 3))


def expand_matrix(side):
    row = lax.broadcasted_iota(jnp.int32, (VOXELS, PLANE), 0)
    column = lax.broadcasted_iota(jnp.int32, (VOXELS, PLANE), 1)
    return where_equal(row, (column >> 2) * PLANE + side * 12 + (column & 3))


def expand_corner_matrix(order, side):
    row = lax.broadcasted_iota(jnp.int32, (2 * VOXELS, PLANE), 0)
    column = lax.broadcasted_iota(jnp.int32, (2 * VOXELS, PLANE), 1)
    vy = (row >> 2) & 3
    return where_equal(column + vy * PLANE, order * 8 + (row >> 6) * 4 + (row & 3) + side * 3 * PLANE)


def pack_layers_kernel(recv_slot_ref, features_ref, cotangent_ref, to_first, to_second, to_sibling, to_outer,
                       own_f, own_c, sides, slot_ref, sems):
    bricks = (own_f, own_c)
    copies = [
        pltpu.make_async_copy(ref, target, sems.at[number])
        for number, (ref, target) in enumerate((
            (features_ref, own_f.at[pl.ds(0, SLOTS)]),
            (cotangent_ref, own_c.at[pl.ds(0, SLOTS)]),
            (recv_slot_ref, slot_ref),
        ))
    ]
    for copy in copies:
        copy.start()
    for own in bricks:
        own[SLOTS] = jnp.zeros((VOXELS, CHANNELS), jnp.bfloat16)
    sides[:, SLOTS] = jnp.zeros((2, 4 * PLANE, CHANNELS), jnp.bfloat16)
    core = lax.axis_index("c")
    odd = lax.axis_index("z") & 1
    layer = layer_matrix()
    block = lax.broadcasted_iota(jnp.int32, (PLANE, CHANNELS), 0) >> 2
    masks = [where_equal(block, number) for number in range(4)]
    for copy in copies:
        copy.wait()
    for kind in range(2):
        beside = jnp.concatenate([bricks[kind][slot] for slot in range(SLOTS)], axis=1)
        picked = jnp.dot(layer, beside, preferred_element_type=jnp.float32).astype(jnp.bfloat16)
        for slot in range(SLOTS):
            sides[kind, slot] = picked[:, slot * CHANNELS : (slot + 1) * CHANNELS]

    def put(packet, position, halo, source, begin):
        slot = jnp.clip(slot_ref[halo], 0, SLOTS)
        rows = pl.ds(begin, PLANE)
        packet[position, :, :CHANNELS] = source[0][slot, rows]
        packet[position, :, CHANNELS:] = source[1][slot, rows]

    for packet, up in ((to_first, 1 - odd), (to_second, odd)):
        begin = pl.multiple_of(up * PLANE, PLANE)
        for position in range(SLOTS):
            put(packet, position, STARTS[2] + up * LENGTHS[2] + position, (sides.at[0], sides.at[1]), begin)
        rows = pl.ds(pl.multiple_of((up + 2) * PLANE, PLANE), PLANE)
        halos = [STARTS[number] + up * BZ + position for number in (4, 6) for position in range(BZ)]
        slots = [jnp.clip(slot_ref[halo], 0, SLOTS) for halo in halos]
        for kind in range(2):
            tile = sides[kind, slots[0], rows] * masks[0]
            for number in range(1, 4):
                tile = tile + sides[kind, slots[number], rows] * masks[number]
            packet[SLOTS, :, kind * CHANNELS : (kind + 1) * CHANNELS] = tile
    for packet, up in ((to_sibling, 1 - core), (to_outer, core)):
        begin = pl.multiple_of(up * (VOXELS - PLANE), PLANE)
        for position in range(LENGTHS[0]):
            put(packet, position, up * LENGTHS[0] + position, bricks, begin)


def pack_layers(recv_slot, features, cotangent):
    vmem = pl.BlockSpec(memory_space=pltpu.VMEM)
    hbm = pl.BlockSpec(memory_space=pltpu.HBM)
    return pl.pallas_call(
        pack_layers_kernel,
        in_specs=[hbm] * 3,
        out_specs=[vmem] * 6,
        out_shape=[
            jax.ShapeDtypeStruct((length, PLANE, 2 * CHANNELS), jnp.bfloat16) for length in (SLOTS + 1, SLOTS + 1, SLOTS, SLOTS)
        ] + [jax.ShapeDtypeStruct((SLOTS + 1, VOXELS, CHANNELS), jnp.bfloat16)] * 2,
        scratch_shapes=[
            pltpu.VMEM((2, SLOTS + 1, 4 * PLANE, CHANNELS), jnp.bfloat16),
            pltpu.SMEM((HALO,), jnp.int32),
            pltpu.SemaphoreType.DMA((3,)),
        ],
        compiler_params=pltpu.CompilerParams(vmem_limit_bytes=VMEM_LIMIT),
    )(recv_slot, features, cotangent)


def fill_bricks(halos, lanes, bricks):
    begin_at = SLOTS
    for halo in halos:
        bricks[begin_at : begin_at + halo.shape[0]] = halo[:, :, lanes]
        begin_at += halo.shape[0]


def fill_along_y(halos, lanes, bricks):
    odd = lax.axis_index("z") & 1
    for faces, side in ((halos[0], odd), (halos[1], 1 - odd)):
        tiles = jnp.concatenate([faces[position, :, lanes] for position in range(SLOTS)], axis=1)
        whole = jnp.dot(expand_matrix(side), tiles, preferred_element_type=jnp.float32).astype(jnp.bfloat16)
        for position in range(SLOTS):
            target = SLOTS + STARTS[2] + side * LENGTHS[2] + position
            bricks[target] = whole[:, position * CHANNELS : (position + 1) * CHANNELS]


def fill_along_x(halos, lanes, bricks):
    core, odd = lax.axis_index("c"), lax.axis_index("z") & 1
    both = ((halos[0], core), (halos[1], 1 - core))
    for packet, below in both:
        for position in range(SLOTS):
            tile = packet[position, :, lanes]
            target = SLOTS + below * LENGTHS[0] + position
            for begin in range(0, VOXELS, PLANE):
                bricks[target, begin : begin + PLANE] = tile
    tiles = jnp.concatenate([packet[SLOTS, :, lanes] for packet in halos], axis=1)
    for order, side in ((0, odd), (1, 1 - odd)):
        whole = jnp.dot(
            expand_corner_matrix(order, side), tiles, preferred_element_type=jnp.float32
        ).astype(jnp.bfloat16)
        for number, (_, below) in enumerate(both):
            for position in range(BZ):
                target = SLOTS + STARTS[4] + side * BZ + below * 2 * BZ + position
                bricks[target] = whole[
                    position * VOXELS : (position + 1) * VOXELS, number * CHANNELS : (number + 1) * CHANNELS
                ]


def fill_nothing(halos, lanes, bricks):
    pass


def out_of_place(dst):
    k = lax.broadcasted_iota(jnp.int32, dst.shape, 1)
    ninth = jnp.where(k >= 18, 2, jnp.where(k >= 9, 1, 0))
    rest = k - 9 * ninth
    offset = (ninth - 1, jnp.where(rest >= 6, 2, jnp.where(rest >= 3, 1, 0)) - 1)
    wrong = jnp.zeros(dst.shape, jnp.float32)
    for number, heading in enumerate(DIRECTIONS):
        start = SLOTS + STARTS[number]
        here = (dst >= start) & (dst < start + LENGTHS[number])
        for axis in range(2):
            if heading[axis]:
                wrong = jnp.where(here & (offset[axis] != heading[axis]), 1.0, wrong)
    return jnp.max(jnp.max(wrong, axis=1, keepdims=True), axis=0, keepdims=True)


def build_taps(unroll, dst_ref, bricks, planes, taps):
    shift = shift_matrix()

    def around(slot, plane):
        side = 0 if plane == 0 else 2 if plane == PLANES - 1 else 1
        local = (plane - 1) % BRICK * PLANE
        return jnp.concatenate(
            [bricks[dst_ref[slot, side * 9 + number], local : local + PLANE] for number in range(9)], axis=0
        )

    def one_slot(slot, carry):
        for index in range(0, len(planes), 2):
            pair = jnp.concatenate((around(slot, planes[index]), around(slot, planes[index + 1])), axis=1)
            moved = jnp.dot(shift, pair, preferred_element_type=jnp.float32).astype(jnp.bfloat16)
            for number in range(9):
                rows = moved[number * PLANE : (number + 1) * PLANE]
                target = slice(number * CHANNELS, (number + 1) * CHANNELS)
                taps[slot, index, :, target] = rows[:, :CHANNELS]
                taps[slot, index + 1, :, target] = rows[:, CHANNELS:]
        return carry

    lax.fori_loop(0, SLOTS, one_slot, 0, unroll=unroll)


def taps_of(mid, edge, side):
    if side == 0:
        planes = jnp.concatenate((edge[:, :1], mid[:, :3]), axis=1)
    elif side == 1:
        planes = mid[...]
    else:
        planes = jnp.concatenate((mid[:, 1:], edge[:, 1:]), axis=1)
    return planes.reshape(SLOTS * VOXELS, WIDE)


def mid_kernel(fill, unroll, count, dst_ref, features_ref, cotangent_ref, *rest):
    halos = rest[:count]
    mid_f, mid_c, bricks_f, bricks_c = rest[count:]
    for kind, (own, bricks, mid) in enumerate(((features_ref, bricks_f, mid_f), (cotangent_ref, bricks_c, mid_c))):
        bricks[:SLOTS] = own[:SLOTS]
        for begin, end in ((SLOTS, SLOTS + STARTS[2]), (SLOTS + STARTS[4], SLOTS + HALO + 1)):
            bricks[begin:end] = jnp.zeros((end - begin, VOXELS, CHANNELS), jnp.bfloat16)
        fill(halos, slice(kind * CHANNELS, (kind + 1) * CHANNELS), bricks)
        build_taps(unroll, dst_ref, bricks, (1, 2, 3, 4), mid)


def weight_kernel(fill, unroll, count, dst_ref, table_ref, mid, _, *rest):
    halos = rest[:count]
    flipped_ref, send_ref, keep_ref, edge, bricks = rest[count:]
    fill(halos, slice(CHANNELS, 2 * CHANNELS), bricks)
    build_taps(unroll, dst_ref, bricks, (0, PLANES - 1), edge)
    core = lax.axis_index("c")
    flipped = jnp.concatenate((flipped_ref[1 - core], flipped_ref[core]), axis=0)
    half = CHANNELS // 2
    for side in (1, 0, 2):
        part = jnp.dot(flipped, taps_of(mid, edge, side), preferred_element_type=jnp.float32)
        for number in range(9):
            block = part[:, number * CHANNELS : (number + 1) * CHANNELS]
            m = side * 9 + number
            for quarter in range(4):
                rows = slice(quarter * 16, quarter * 16 + 16)
                send_ref[quarter, m] = block[:half][rows].astype(jnp.bfloat16)
                keep_ref[quarter, m] = block[half:][rows]
    flag = jnp.broadcast_to(out_of_place(table_ref[...]), (16, CHANNELS))
    for quarter in range(4):
        send_ref[quarter, 27] = flag.astype(jnp.bfloat16)
        keep_ref[quarter, 27] = flag


def grad_kernel(mid, edge, weights_ref, grad_ref):
    grad = None
    for side in range(3):
        matrix = jnp.concatenate([weights_ref[26 - side * 9 - number] for number in range(9)], axis=1)
        part = lax.dot_general(
            taps_of(mid, edge, side), matrix, (((1,), (1,)), ((), ())), preferred_element_type=jnp.float32
        )
        grad = part if grad is None else grad + part
    grad_ref[...] = grad.astype(jnp.bfloat16).reshape(SLOTS, VOXELS, CHANNELS)


def edge_kernel(fill, unroll, count, dst_ref, _, *rest):
    edge, bricks = rest[count:]
    fill(rest[:count], slice(0, CHANNELS), bricks)
    build_taps(unroll, dst_ref, bricks, (0, PLANES - 1), edge)


def output_kernel(mid, edge, weights_ref, outputs_ref):
    outputs = None
    for side in range(3):
        matrix = weights_ref[side * 9 : side * 9 + 9].reshape(WIDE, CHANNELS)
        part = jnp.dot(taps_of(mid, edge, side), matrix, preferred_element_type=jnp.float32)
        outputs = part if outputs is None else outputs + part
    outputs_ref[...] = outputs.astype(jnp.bfloat16).reshape(SLOTS, VOXELS, CHANNELS)


VMEM_SPEC = pl.BlockSpec(memory_space=pltpu.VMEM)
SMEM_SPEC = pl.BlockSpec(memory_space=pltpu.SMEM)
BRICK_SHAPE = jax.ShapeDtypeStruct((SLOTS, VOXELS, CHANNELS), jnp.bfloat16)
MID_SHAPE = jax.ShapeDtypeStruct((SLOTS, BRICK, PLANE, WIDE), jnp.bfloat16)
EDGE_SHAPE = jax.ShapeDtypeStruct((SLOTS, 2, PLANE, WIDE), jnp.bfloat16)
ALL_BRICKS = jax.ShapeDtypeStruct((SLOTS + HALO + 1, VOXELS, CHANNELS), jnp.bfloat16)
PARAMS = pltpu.CompilerParams(vmem_limit_bytes=VMEM_LIMIT)
COST = pl.CostEstimate(flops=4 * SLOTS * VOXELS * 27 * CHANNELS * CHANNELS, bytes_accessed=4_000_000, transcendentals=0)


def mid_taps(fill, unroll, dst, own_f, own_c, halos):
    return pl.pallas_call(
        functools.partial(mid_kernel, fill, unroll, len(halos)),
        in_specs=[SMEM_SPEC] + [VMEM_SPEC] * (2 + len(halos)),
        out_specs=[VMEM_SPEC] * 4,
        out_shape=[MID_SHAPE, MID_SHAPE, ALL_BRICKS, ALL_BRICKS],
        compiler_params=PARAMS,
        cost_estimate=COST,
    )(dst, own_f, own_c, *halos)


def weight_sums(fill, unroll, dst, mid, bricks, halos, flipped):
    return pl.pallas_call(
        functools.partial(weight_kernel, fill, unroll, len(halos)),
        in_specs=[SMEM_SPEC] + [VMEM_SPEC] * (4 + len(halos)),
        out_specs=[VMEM_SPEC] * 4,
        out_shape=[
            jax.ShapeDtypeStruct((4, ROWS_M, 16, CHANNELS), jnp.bfloat16),
            jax.ShapeDtypeStruct((4, ROWS_M, 16, CHANNELS), jnp.float32),
            EDGE_SHAPE,
            ALL_BRICKS,
        ],
        input_output_aliases={3: 3},
        compiler_params=PARAMS,
        cost_estimate=COST,
    )(dst, dst, mid, bricks, *halos, flipped)


def feature_edges(fill, unroll, dst, bricks, halos):
    return pl.pallas_call(
        functools.partial(edge_kernel, fill, unroll, len(halos)),
        in_specs=[SMEM_SPEC] + [VMEM_SPEC] * (1 + len(halos)),
        out_specs=[VMEM_SPEC] * 2,
        out_shape=[EDGE_SHAPE, ALL_BRICKS],
        input_output_aliases={1: 1},
        compiler_params=PARAMS,
        cost_estimate=COST,
    )(dst, bricks, *halos)[0]


def product(kernel, mid, edge, weights):
    return pl.pallas_call(
        kernel,
        in_specs=[VMEM_SPEC] * 3,
        out_specs=VMEM_SPEC,
        out_shape=BRICK_SHAPE,
        compiler_params=PARAMS,
        cost_estimate=COST,
    )(mid, edge, weights)


def convolve(fill, unroll, dst, mids, halos, flipped, weights):
    mid_f, mid_c, bricks_f, bricks_c = mids
    send, keep, edge_c, _ = weight_sums(fill, unroll, dst, mid_c, bricks_c, halos, flipped)
    arrived = lax.ppermute(send, "c", [(0, 1), (1, 0)])
    input_grad = product(grad_kernel, mid_c, edge_c, weights)
    edge_f = feature_edges(fill, unroll, dst, bricks_f, halos)
    arrived, input_grad, edge_f = lax.optimization_barrier((arrived, input_grad, edge_f))
    own = sum_everywhere(arrived, keep)
    other = lax.ppermute(own, "c", [(0, 1), (1, 0)])
    outputs = product(output_kernel, mid_f, edge_f, weights)
    return outputs, input_grad, own, other


def pack_bricks_kernel(slot_ref, features_ref, cotangent_ref, *packets):
    begin_at = 0
    for packet in packets:
        for position in range(packet.shape[0]):
            slot = slot_ref[begin_at + position]
            row = jnp.clip(slot, 0, SLOTS - 1)

            @pl.when(slot < SLOTS)
            def _():
                packet[position, :, :CHANNELS] = features_ref[row]
                packet[position, :, CHANNELS:] = cotangent_ref[row]

            @pl.when(slot >= SLOTS)
            def _():
                packet[position] = jnp.zeros((VOXELS, 2 * CHANNELS), jnp.bfloat16)

        begin_at += packet.shape[0]


def pack_bricks(recv_slot, features, cotangent):
    vmem = pl.BlockSpec(memory_space=pltpu.VMEM)
    return pl.pallas_call(
        pack_bricks_kernel,
        in_specs=[pl.BlockSpec(memory_space=pltpu.SMEM), vmem, vmem],
        out_specs=[vmem] * 8,
        out_shape=[
            jax.ShapeDtypeStruct((length, VOXELS, 2 * CHANNELS), jnp.bfloat16) for length in LENGTHS
        ],
        compiler_params=pltpu.CompilerParams(vmem_limit_bytes=VMEM_LIMIT),
    )(recv_slot, features, cotangent)


def pass_to(value, step_x, step_y):
    pairs = []
    for gx in range(8):
        for gy in range(32):
            if 0 <= gx + step_x < 8 and 0 <= gy + step_y < 32:
                pairs.append((gx * 32 + gy, (gx + step_x) * 32 + gy + step_y))
    return lax.ppermute(value, AXES, pairs)


def sum_everywhere(arrived, keep):
    chip_sum = (keep + arrived.astype(jnp.float32)).astype(jnp.bfloat16)
    parts = chip_sum.reshape(16, 7, 16, CHANNELS)
    parts = lax.all_to_all(parts, ("x", "y"), 0, 0)
    total = jnp.sum(parts.astype(jnp.float32), axis=0)
    largest = jnp.max(jnp.abs(total), axis=(0, 1))
    power = jnp.clip(jnp.ceil(jnp.log2(jnp.maximum(largest, 1e-37))), -100.0, 100.0)
    power = jnp.broadcast_to(power, (1, 16, CHANNELS))
    share = jnp.concatenate((total * jnp.exp2(14.0 - power), power), axis=0).astype(jnp.float16)
    column = lax.all_to_all(jnp.broadcast_to(share[None], (8,) + share.shape), "z", 0, 0).astype(jnp.float32)
    total = jnp.sum(column[:, :7] * jnp.exp2(column[:, 7:] - 14.0), axis=0)
    share = (total * (1.0 / (VOXELS * SLOTS))).astype(jnp.bfloat16)
    whole = jnp.broadcast_to(share[None], (16,) + share.shape)
    return lax.all_to_all(whole, ("x", "y"), 0, 0).reshape(4, ROWS_M, 16, CHANNELS)


def spread_kernel(own_ref, other_ref, outputs_ref, grad_ref, outputs_out, grad_out, out_ref, whole, sems):
    half = CHANNELS // 2
    core = lax.axis_index("c")
    copies = [
        pltpu.make_async_copy(outputs_ref, outputs_out, sems.at[9]),
        pltpu.make_async_copy(grad_ref, grad_out, sems.at[10]),
    ]
    for copy in copies:
        copy.start()
    for chunk in range(9):
        for m in range(3 * chunk, 3 * chunk + 3):
            for quarter in range(4):
                for ref, side in ((own_ref, core), (other_ref, 1 - core)):
                    begin = pl.multiple_of(side * half + quarter * 16, 16)
                    whole[26 - m, pl.ds(begin, 16)] = ref[quarter, m].astype(jnp.float32)
        rows = pl.ds(24 - 3 * chunk, 3)
        copies.append(pltpu.make_async_copy(whole.at[rows], out_ref.at[rows], sems.at[chunk]))
        copies[-1].start()
    for copy in copies:
        copy.wait()


def spread_out(outputs, input_grad, own, other):
    return pl.pallas_call(
        spread_kernel,
        in_specs=[VMEM_SPEC] * 4,
        out_specs=[pl.BlockSpec(memory_space=pltpu.HBM)] * 3,
        out_shape=[BRICK_SHAPE, BRICK_SHAPE, jax.ShapeDtypeStruct((27, CHANNELS, CHANNELS), jnp.float32)],
        scratch_shapes=[
            pltpu.VMEM((27, CHANNELS, CHANNELS), jnp.float32),
            pltpu.SemaphoreType.DMA((11,)),
        ],
        compiler_params=PARAMS,
    )(own, other, outputs, input_grad)


def local(features, weights, cotangent, dst_index, recv_slot):
    core = lax.axis_index("c")
    dst = jnp.clip(dst_index.T, 0, SLOTS + HALO)

    to_first, to_second, to_sibling, to_outer, own_f, own_c = pack_layers(recv_slot, features, cotangent)
    flipped = jnp.transpose(own_f[:SLOTS].reshape(SLOTS * VOXELS, CHANNELS))
    flipped = flipped.reshape(2, CHANNELS // 2, SLOTS * VOXELS)
    y_second = lax.ppermute(to_second, ("y", "z"), [(gy, ((gy + 1) ^ 1) - 1) for gy in range(1, 31)])
    y_first = lax.ppermute(to_first, ("y", "z"), [(gy, gy ^ 1) for gy in range(32)])
    y_first, y_second, dst, flipped = lax.optimization_barrier((y_first, y_second, dst, flipped))

    def relayed(packet, up):
        corners = [lax.dynamic_slice_in_dim(value[SLOTS:], 8 * up, 8, axis=1) for value in (y_first, y_second)]
        return jnp.concatenate((packet, jnp.concatenate(corners, axis=1)), axis=0)

    x_outer = lax.ppermute(relayed(to_outer, core), ("x", "c"), [(2 * x + 1, 2 * x + 2) for x in range(3)]
                           + [(2 * x + 2, 2 * x + 1) for x in range(3)])
    x_sibling = lax.ppermute(relayed(to_sibling, 1 - core), "c", [(0, 1), (1, 0)])
    mids = mid_taps(fill_along_y, SLOTS, dst, own_f, own_c, (y_first, y_second))
    results = convolve(fill_along_x, SLOTS, dst, mids, (x_sibling, x_outer), flipped, weights)

    def with_whole_bricks(results):
        packets = pack_bricks(recv_slot, features, cotangent)
        halos = [pass_to(packet, -heading[0], -heading[1]) for packet, heading in zip(packets, DIRECTIONS)]
        mids = mid_taps(fill_bricks, 1, dst, own_f, own_c, halos)
        return spread_out(*convolve(fill_nothing, 1, dst, mids, (), flipped, weights))

    def as_they_are(results):
        return spread_out(*results)

    own = results[2]
    return tuple(lax.cond(own[0, 27, 0, 0] != 0, with_whole_bricks, as_they_are, results))


def solution(mesh):
    fine = Mesh(mesh.devices.reshape(4, 2, 4, 8), AXES)
    bricks = P(AXES, None, None)
    return jax.shard_map(
        local,
        mesh=fine,
        in_specs=(bricks, P(), bricks, P(None, AXES), P(AXES)),
        out_specs=(bricks, bricks, P()),
        check_vma=False,
    )
```

```python
import functools

import jax
import jax.numpy as jnp
import numpy as np
from jax import lax
from jax.experimental import pallas as pl
from jax.experimental.pallas import tpu as pltpu
from jax.sharding import Mesh, PartitionSpec as P

BRICK = 4
TILE = 4
BZ = 2
HALO = 40
SLOTS = 8
VOXELS = 64
CHANNELS = 128
PLANE = BRICK * BRICK
PLANES = BRICK + 2
WIDE = 9 * CHANNELS
ROWS_M = 28

DIRECTIONS = ((1, 0), (-1, 0), (0, 1), (0, -1), (1, 1), (1, -1), (-1, 1), (-1, -1))
LENGTHS = (TILE * BZ,) * 4 + (BZ,) * 4
STARTS = tuple(int(start) for start in np.cumsum((0,) + LENGTHS[:-1]))
AXES = ("x", "c", "y", "z")
VMEM_LIMIT = 24 * 1024 * 1024


def where_equal(left, right):
    return jnp.where(left == right, 1.0, 0.0).astype(jnp.bfloat16)


def shift_matrix():
    row = lax.broadcasted_iota(jnp.int32, (9 * PLANE, 9 * PLANE), 0)
    column = lax.broadcasted_iota(jnp.int32, (9 * PLANE, 9 * PLANE), 1)
    number = row >> 4
    third = (number * 11) >> 5
    y = ((row >> 2) & 3) + third + 3
    z = (row & 3) + number - 3 * third + 3
    return where_equal(column, ((y >> 2) * 3 + (z >> 2)) * PLANE + (y & 3) * BRICK + (z & 3))


def layer_matrix():
    row = lax.broadcasted_iota(jnp.int32, (4 * PLANE, VOXELS), 0)
    column = lax.broadcasted_iota(jnp.int32, (4 * PLANE, VOXELS), 1)
    quarter = (row >> 2) & 3
    vx = jnp.where(row < 2 * PLANE, quarter, (quarter >> 1) * 3)
    return where_equal(column, vx * PLANE + ((row >> 4) & 1) * 12 + (row & 3))


def expand_matrix(side):
    row = lax.broadcasted_iota(jnp.int32, (VOXELS, PLANE), 0)
    column = lax.broadcasted_iota(jnp.int32, (VOXELS, PLANE), 1)
    return where_equal(row, (column >> 2) * PLANE + side * 12 + (column & 3))


def expand_corner_matrix(order, side):
    row = lax.broadcasted_iota(jnp.int32, (2 * VOXELS, PLANE), 0)
    column = lax.broadcasted_iota(jnp.int32, (2 * VOXELS, PLANE), 1)
    vy = (row >> 2) & 3
    return where_equal(column + vy * PLANE, order * 8 + (row >> 6) * 4 + (row & 3) + side * 3 * PLANE)


def pack_layers_kernel(recv_slot_ref, features_ref, cotangent_ref, to_first, to_second, to_sibling, to_outer,
                       own_f, own_c, sides, slot_ref, sems):
    bricks = (own_f, own_c)
    copies = [
        pltpu.make_async_copy(ref, target, sems.at[number])
        for number, (ref, target) in enumerate((
            (features_ref, own_f.at[pl.ds(0, SLOTS)]),
            (cotangent_ref, own_c.at[pl.ds(0, SLOTS)]),
            (recv_slot_ref, slot_ref),
        ))
    ]
    for copy in copies:
        copy.start()
    for own in bricks:
        own[SLOTS] = jnp.zeros((VOXELS, CHANNELS), jnp.bfloat16)
    sides[:, SLOTS] = jnp.zeros((2, 4 * PLANE, CHANNELS), jnp.bfloat16)
    core = lax.axis_index("c")
    odd = lax.axis_index("z") & 1
    layer = layer_matrix()
    block = lax.broadcasted_iota(jnp.int32, (PLANE, CHANNELS), 0) >> 2
    masks = [where_equal(block, number) for number in range(4)]
    for copy in copies:
        copy.wait()
    for kind in range(2):
        beside = jnp.concatenate([bricks[kind][slot] for slot in range(SLOTS)], axis=1)
        picked = jnp.dot(layer, beside, preferred_element_type=jnp.float32).astype(jnp.bfloat16)
        for slot in range(SLOTS):
            sides[kind, slot] = picked[:, slot * CHANNELS : (slot + 1) * CHANNELS]

    def put(packet, position, halo, source, begin):
        slot = jnp.clip(slot_ref[halo], 0, SLOTS)
        rows = pl.ds(begin, PLANE)
        packet[position, :, :CHANNELS] = source[0][slot, rows]
        packet[position, :, CHANNELS:] = source[1][slot, rows]

    for packet, up in ((to_first, 1 - odd), (to_second, odd)):
        begin = pl.multiple_of(up * PLANE, PLANE)
        for position in range(SLOTS):
            put(packet, position, STARTS[2] + up * LENGTHS[2] + position, (sides.at[0], sides.at[1]), begin)
        rows = pl.ds(pl.multiple_of((up + 2) * PLANE, PLANE), PLANE)
        halos = [STARTS[number] + up * BZ + position for number in (4, 6) for position in range(BZ)]
        slots = [jnp.clip(slot_ref[halo], 0, SLOTS) for halo in halos]
        for kind in range(2):
            tile = sides[kind, slots[0], rows] * masks[0]
            for number in range(1, 4):
                tile = tile + sides[kind, slots[number], rows] * masks[number]
            packet[SLOTS, :, kind * CHANNELS : (kind + 1) * CHANNELS] = tile
    for packet, up in ((to_sibling, 1 - core), (to_outer, core)):
        begin = pl.multiple_of(up * (VOXELS - PLANE), PLANE)
        for position in range(LENGTHS[0]):
            put(packet, position, up * LENGTHS[0] + position, bricks, begin)


def pack_layers(recv_slot, features, cotangent):
    vmem = pl.BlockSpec(memory_space=pltpu.VMEM)
    hbm = pl.BlockSpec(memory_space=pltpu.HBM)
    return pl.pallas_call(
        pack_layers_kernel,
        in_specs=[hbm] * 3,
        out_specs=[vmem] * 6,
        out_shape=[
            jax.ShapeDtypeStruct((length, PLANE, 2 * CHANNELS), jnp.bfloat16) for length in (SLOTS + 1, SLOTS + 1, SLOTS, SLOTS)
        ] + [jax.ShapeDtypeStruct((SLOTS + 1, VOXELS, CHANNELS), jnp.bfloat16)] * 2,
        scratch_shapes=[
            pltpu.VMEM((2, SLOTS + 1, 4 * PLANE, CHANNELS), jnp.bfloat16),
            pltpu.SMEM((HALO,), jnp.int32),
            pltpu.SemaphoreType.DMA((3,)),
        ],
        compiler_params=pltpu.CompilerParams(vmem_limit_bytes=VMEM_LIMIT),
    )(recv_slot, features, cotangent)


def fill_bricks(halos, lanes, bricks):
    begin_at = SLOTS
    for halo in halos:
        bricks[begin_at : begin_at + halo.shape[0]] = halo[:, :, lanes]
        begin_at += halo.shape[0]


def fill_along_y(halos, lanes, bricks):
    odd = lax.axis_index("z") & 1
    for faces, side in ((halos[0], odd), (halos[1], 1 - odd)):
        tiles = jnp.concatenate([faces[position, :, lanes] for position in range(SLOTS)], axis=1)
        whole = jnp.dot(expand_matrix(side), tiles, preferred_element_type=jnp.float32).astype(jnp.bfloat16)
        for position in range(SLOTS):
            target = SLOTS + STARTS[2] + side * LENGTHS[2] + position
            bricks[target] = whole[:, position * CHANNELS : (position + 1) * CHANNELS]


def fill_along_x(halos, lanes, bricks):
    core, odd = lax.axis_index("c"), lax.axis_index("z") & 1
    both = ((halos[0], core), (halos[1], 1 - core))
    for packet, below in both:
        for position in range(SLOTS):
            tile = packet[position, :, lanes]
            target = SLOTS + below * LENGTHS[0] + position
            for begin in range(0, VOXELS, PLANE):
                bricks[target, begin : begin + PLANE] = tile
    tiles = jnp.concatenate([packet[SLOTS, :, lanes] for packet in halos], axis=1)
    for order, side in ((0, odd), (1, 1 - odd)):
        whole = jnp.dot(
            expand_corner_matrix(order, side), tiles, preferred_element_type=jnp.float32
        ).astype(jnp.bfloat16)
        for number, (_, below) in enumerate(both):
            for position in range(BZ):
                target = SLOTS + STARTS[4] + side * BZ + below * 2 * BZ + position
                bricks[target] = whole[
                    position * VOXELS : (position + 1) * VOXELS, number * CHANNELS : (number + 1) * CHANNELS
                ]


def fill_nothing(halos, lanes, bricks):
    pass


def out_of_place(dst):
    k = lax.broadcasted_iota(jnp.int32, dst.shape, 1)
    ninth = jnp.where(k >= 18, 2, jnp.where(k >= 9, 1, 0))
    rest = k - 9 * ninth
    offset = (ninth - 1, jnp.where(rest >= 6, 2, jnp.where(rest >= 3, 1, 0)) - 1)
    wrong = jnp.zeros(dst.shape, jnp.float32)
    for number, heading in enumerate(DIRECTIONS):
        start = SLOTS + STARTS[number]
        here = (dst >= start) & (dst < start + LENGTHS[number])
        for axis in range(2):
            if heading[axis]:
                wrong = jnp.where(here & (offset[axis] != heading[axis]), 1.0, wrong)
    return jnp.max(jnp.max(wrong, axis=1, keepdims=True), axis=0, keepdims=True)


def build_taps(unroll, dst_ref, bricks, planes, taps):
    shift = shift_matrix()

    def around(slot, plane):
        side = 0 if plane == 0 else 2 if plane == PLANES - 1 else 1
        local = (plane - 1) % BRICK * PLANE
        return jnp.concatenate(
            [bricks[dst_ref[slot, side * 9 + number], local : local + PLANE] for number in range(9)], axis=0
        )

    def one_slot(slot, carry):
        for index in range(0, len(planes), 2):
            pair = jnp.concatenate((around(slot, planes[index]), around(slot, planes[index + 1])), axis=1)
            moved = jnp.dot(shift, pair, preferred_element_type=jnp.float32).astype(jnp.bfloat16)
            for number in range(9):
                rows = moved[number * PLANE : (number + 1) * PLANE]
                target = slice(number * CHANNELS, (number + 1) * CHANNELS)
                taps[slot, index, :, target] = rows[:, :CHANNELS]
                taps[slot, index + 1, :, target] = rows[:, CHANNELS:]
        return carry

    lax.fori_loop(0, SLOTS, one_slot, 0, unroll=unroll)


def taps_of(mid, edge, side):
    if side == 0:
        planes = jnp.concatenate((edge[:, :1], mid[:, :3]), axis=1)
    elif side == 1:
        planes = mid[...]
    else:
        planes = jnp.concatenate((mid[:, 1:], edge[:, 1:]), axis=1)
    return planes.reshape(SLOTS * VOXELS, WIDE)


def store_products(flipped_ref, tap, first, send_ref, keep_ref):
    core = lax.axis_index("c")
    half = CHANNELS // 2
    flipped = jnp.concatenate((flipped_ref[1 - core], flipped_ref[core]), axis=0)
    part = jnp.dot(flipped, tap, preferred_element_type=jnp.float32)
    for number in range(9):
        block = part[:, number * CHANNELS : (number + 1) * CHANNELS]
        for quarter in range(4):
            rows = slice(quarter * 16, quarter * 16 + 16)
            send_ref[quarter, first + number] = block[:half][rows].astype(jnp.bfloat16)
            keep_ref[quarter, first + number] = block[half:][rows]


def grad_part(tap, weights_ref, side):
    matrix = jnp.concatenate([weights_ref[26 - side * 9 - number] for number in range(9)], axis=1)
    return lax.dot_general(tap, matrix, (((1,), (1,)), ((), ())), preferred_element_type=jnp.float32)


def mid_kernel(fill, unroll, count, dst_ref, features_ref, cotangent_ref, flipped_ref, weights_ref, *rest):
    halos = rest[:count]
    mid_f, mid_c, bricks_f, bricks_c, send_ref, keep_ref, grad_ref = rest[count:]
    for kind, (own, bricks, mid) in enumerate(((features_ref, bricks_f, mid_f), (cotangent_ref, bricks_c, mid_c))):
        bricks[:SLOTS] = own[:SLOTS]
        for begin, end in ((SLOTS, SLOTS + STARTS[2]), (SLOTS + STARTS[4], SLOTS + HALO + 1)):
            bricks[begin:end] = jnp.zeros((end - begin, VOXELS, CHANNELS), jnp.bfloat16)
        fill(halos, slice(kind * CHANNELS, (kind + 1) * CHANNELS), bricks)
        build_taps(unroll, dst_ref, bricks, (1, 2, 3, 4), mid)
    tap = mid_c[...].reshape(SLOTS * VOXELS, WIDE)
    store_products(flipped_ref, tap, 0, send_ref, keep_ref)
    grad_ref[...] = grad_part(tap, weights_ref, 1)


def weight_kernel(fill, unroll, count, dst_ref, table_ref, mid, _, *rest):
    halos = rest[:count]
    flipped_ref, send_mid, keep_mid, send_ref, keep_ref, edge, bricks = rest[count:]
    fill(halos, slice(CHANNELS, 2 * CHANNELS), bricks)
    build_taps(unroll, dst_ref, bricks, (0, PLANES - 1), edge)
    send_ref[:, 9:18] = send_mid[...]
    keep_ref[:, 9:18] = keep_mid[...]
    for side in (0, 2):
        store_products(flipped_ref, taps_of(mid, edge, side), side * 9, send_ref, keep_ref)
    flag = jnp.broadcast_to(out_of_place(table_ref[...]), (16, CHANNELS))
    for quarter in range(4):
        send_ref[quarter, 27] = flag.astype(jnp.bfloat16)
        keep_ref[quarter, 27] = flag


def grad_kernel(mid, edge, weights_ref, grad_mid, grad_ref):
    grad = grad_mid[...]
    for side in (0, 2):
        grad = grad + grad_part(taps_of(mid, edge, side), weights_ref, side)
    grad_ref[...] = grad.astype(jnp.bfloat16).reshape(SLOTS, VOXELS, CHANNELS)


def edge_kernel(fill, unroll, count, dst_ref, _, *rest):
    edge, bricks = rest[count:]
    fill(rest[:count], slice(0, CHANNELS), bricks)
    build_taps(unroll, dst_ref, bricks, (0, PLANES - 1), edge)


def output_kernel(mid, edge, weights_ref, outputs_ref):
    outputs = None
    for side in range(3):
        matrix = weights_ref[side * 9 : side * 9 + 9].reshape(WIDE, CHANNELS)
        part = jnp.dot(taps_of(mid, edge, side), matrix, preferred_element_type=jnp.float32)
        outputs = part if outputs is None else outputs + part
    outputs_ref[...] = outputs.astype(jnp.bfloat16).reshape(SLOTS, VOXELS, CHANNELS)


VMEM_SPEC = pl.BlockSpec(memory_space=pltpu.VMEM)
SMEM_SPEC = pl.BlockSpec(memory_space=pltpu.SMEM)
BRICK_SHAPE = jax.ShapeDtypeStruct((SLOTS, VOXELS, CHANNELS), jnp.bfloat16)
MID_SHAPE = jax.ShapeDtypeStruct((SLOTS, BRICK, PLANE, WIDE), jnp.bfloat16)
EDGE_SHAPE = jax.ShapeDtypeStruct((SLOTS, 2, PLANE, WIDE), jnp.bfloat16)
ALL_BRICKS = jax.ShapeDtypeStruct((SLOTS + HALO + 1, VOXELS, CHANNELS), jnp.bfloat16)
PARAMS = pltpu.CompilerParams(vmem_limit_bytes=VMEM_LIMIT)
COST = pl.CostEstimate(flops=4 * SLOTS * VOXELS * 27 * CHANNELS * CHANNELS, bytes_accessed=4_000_000, transcendentals=0)


def mid_taps(fill, unroll, dst, own_f, own_c, halos, flipped, weights):
    return pl.pallas_call(
        functools.partial(mid_kernel, fill, unroll, len(halos)),
        in_specs=[SMEM_SPEC] + [VMEM_SPEC] * (4 + len(halos)),
        out_specs=[VMEM_SPEC] * 7,
        out_shape=[
            MID_SHAPE, MID_SHAPE, ALL_BRICKS, ALL_BRICKS,
            jax.ShapeDtypeStruct((4, 9, 16, CHANNELS), jnp.bfloat16),
            jax.ShapeDtypeStruct((4, 9, 16, CHANNELS), jnp.float32),
            jax.ShapeDtypeStruct((SLOTS * VOXELS, CHANNELS), jnp.float32),
        ],
        compiler_params=PARAMS,
        cost_estimate=COST,
    )(dst, own_f, own_c, flipped, weights, *halos)


def weight_sums(fill, unroll, dst, mid, bricks, halos, flipped, send, keep):
    return pl.pallas_call(
        functools.partial(weight_kernel, fill, unroll, len(halos)),
        in_specs=[SMEM_SPEC] + [VMEM_SPEC] * (6 + len(halos)),
        out_specs=[VMEM_SPEC] * 4,
        out_shape=[
            jax.ShapeDtypeStruct((4, ROWS_M, 16, CHANNELS), jnp.bfloat16),
            jax.ShapeDtypeStruct((4, ROWS_M, 16, CHANNELS), jnp.float32),
            EDGE_SHAPE,
            ALL_BRICKS,
        ],
        input_output_aliases={3: 3},
        compiler_params=PARAMS,
        cost_estimate=COST,
    )(dst, dst, mid, bricks, *halos, flipped, send, keep)


def feature_edges(fill, unroll, dst, bricks, halos):
    return pl.pallas_call(
        functools.partial(edge_kernel, fill, unroll, len(halos)),
        in_specs=[SMEM_SPEC] + [VMEM_SPEC] * (1 + len(halos)),
        out_specs=[VMEM_SPEC] * 2,
        out_shape=[EDGE_SHAPE, ALL_BRICKS],
        input_output_aliases={1: 1},
        compiler_params=PARAMS,
        cost_estimate=COST,
    )(dst, bricks, *halos)[0]


def product(kernel, *operands):
    return pl.pallas_call(
        kernel,
        in_specs=[VMEM_SPEC] * len(operands),
        out_specs=VMEM_SPEC,
        out_shape=BRICK_SHAPE,
        compiler_params=PARAMS,
        cost_estimate=COST,
    )(*operands)


def convolve(fill, unroll, dst, mids, halos, flipped, weights):
    mid_f, mid_c, bricks_f, bricks_c, send, keep, grad_mid = mids
    send, keep, edge_c, _ = weight_sums(fill, unroll, dst, mid_c, bricks_c, halos, flipped, send, keep)
    arrived = lax.ppermute(send, "c", [(0, 1), (1, 0)])
    input_grad = product(grad_kernel, mid_c, edge_c, weights, grad_mid)
    edge_f = feature_edges(fill, unroll, dst, bricks_f, halos)
    arrived, input_grad, edge_f = lax.optimization_barrier((arrived, input_grad, edge_f))
    own = sum_everywhere(arrived, keep)
    other = lax.ppermute(own, "c", [(0, 1), (1, 0)])
    outputs = product(output_kernel, mid_f, edge_f, weights)
    return outputs, input_grad, own, other


def pack_bricks_kernel(slot_ref, features_ref, cotangent_ref, *packets):
    begin_at = 0
    for packet in packets:
        for position in range(packet.shape[0]):
            slot = slot_ref[begin_at + position]
            row = jnp.clip(slot, 0, SLOTS - 1)

            @pl.when(slot < SLOTS)
            def _():
                packet[position, :, :CHANNELS] = features_ref[row]
                packet[position, :, CHANNELS:] = cotangent_ref[row]

            @pl.when(slot >= SLOTS)
            def _():
                packet[position] = jnp.zeros((VOXELS, 2 * CHANNELS), jnp.bfloat16)

        begin_at += packet.shape[0]


def pack_bricks(recv_slot, features, cotangent):
    vmem = pl.BlockSpec(memory_space=pltpu.VMEM)
    return pl.pallas_call(
        pack_bricks_kernel,
        in_specs=[pl.BlockSpec(memory_space=pltpu.SMEM), vmem, vmem],
        out_specs=[vmem] * 8,
        out_shape=[
            jax.ShapeDtypeStruct((length, VOXELS, 2 * CHANNELS), jnp.bfloat16) for length in LENGTHS
        ],
        compiler_params=pltpu.CompilerParams(vmem_limit_bytes=VMEM_LIMIT),
    )(recv_slot, features, cotangent)


def pass_to(value, step_x, step_y):
    pairs = []
    for gx in range(8):
        for gy in range(32):
            if 0 <= gx + step_x < 8 and 0 <= gy + step_y < 32:
                pairs.append((gx * 32 + gy, (gx + step_x) * 32 + gy + step_y))
    return lax.ppermute(value, AXES, pairs)


def sum_everywhere(arrived, keep):
    chip_sum = (keep + arrived.astype(jnp.float32)).astype(jnp.bfloat16)
    parts = chip_sum.reshape(16, 7, 16, CHANNELS)
    parts = lax.all_to_all(parts, ("x", "y"), 0, 0)
    total = jnp.sum(parts.astype(jnp.float32), axis=0)
    largest = jnp.max(jnp.abs(total), axis=(0, 1))
    power = jnp.clip(jnp.ceil(jnp.log2(jnp.maximum(largest, 1e-37))), -100.0, 100.0)
    power = jnp.broadcast_to(power, (1, 16, CHANNELS))
    share = jnp.concatenate((total * jnp.exp2(14.0 - power), power), axis=0).astype(jnp.float16)
    column = lax.all_to_all(jnp.broadcast_to(share[None], (8,) + share.shape), "z", 0, 0).astype(jnp.float32)
    total = jnp.sum(column[:, :7] * jnp.exp2(column[:, 7:] - 14.0), axis=0)
    share = (total * (1.0 / (VOXELS * SLOTS))).astype(jnp.bfloat16)
    whole = jnp.broadcast_to(share[None], (16,) + share.shape)
    return lax.all_to_all(whole, ("x", "y"), 0, 0).reshape(4, ROWS_M, 16, CHANNELS)


def spread_kernel(own_ref, other_ref, outputs_ref, grad_ref, outputs_out, grad_out, out_ref, whole, sems):
    half = CHANNELS // 2
    core = lax.axis_index("c")
    copies = [
        pltpu.make_async_copy(outputs_ref, outputs_out, sems.at[9]),
        pltpu.make_async_copy(grad_ref, grad_out, sems.at[10]),
    ]
    for copy in copies:
        copy.start()
    for chunk in range(9):
        for m in range(3 * chunk, 3 * chunk + 3):
            for quarter in range(4):
                for ref, side in ((own_ref, core), (other_ref, 1 - core)):
                    begin = pl.multiple_of(side * half + quarter * 16, 16)
                    whole[26 - m, pl.ds(begin, 16)] = ref[quarter, m].astype(jnp.float32)
        rows = pl.ds(24 - 3 * chunk, 3)
        copies.append(pltpu.make_async_copy(whole.at[rows], out_ref.at[rows], sems.at[chunk]))
        copies[-1].start()
    for copy in copies:
        copy.wait()


def spread_out(outputs, input_grad, own, other):
    return pl.pallas_call(
        spread_kernel,
        in_specs=[VMEM_SPEC] * 4,
        out_specs=[pl.BlockSpec(memory_space=pltpu.HBM)] * 3,
        out_shape=[BRICK_SHAPE, BRICK_SHAPE, jax.ShapeDtypeStruct((27, CHANNELS, CHANNELS), jnp.float32)],
        scratch_shapes=[
            pltpu.VMEM((27, CHANNELS, CHANNELS), jnp.float32),
            pltpu.SemaphoreType.DMA((11,)),
        ],
        compiler_params=PARAMS,
    )(own, other, outputs, input_grad)


def local(features, weights, cotangent, dst_index, recv_slot):
    core = lax.axis_index("c")
    dst = jnp.clip(dst_index.T, 0, SLOTS + HALO)

    to_first, to_second, to_sibling, to_outer, own_f, own_c = pack_layers(recv_slot, features, cotangent)
    flipped = jnp.transpose(own_f[:SLOTS].reshape(SLOTS * VOXELS, CHANNELS))
    flipped = flipped.reshape(2, CHANNELS // 2, SLOTS * VOXELS)
    y_second = lax.ppermute(to_second, ("y", "z"), [(gy, ((gy + 1) ^ 1) - 1) for gy in range(1, 31)])
    y_first = lax.ppermute(to_first, ("y", "z"), [(gy, gy ^ 1) for gy in range(32)])
    y_first, y_second, dst, flipped = lax.optimization_barrier((y_first, y_second, dst, flipped))

    def relayed(packet, up):
        corners = [lax.dynamic_slice_in_dim(value[SLOTS:], 8 * up, 8, axis=1) for value in (y_first, y_second)]
        return jnp.concatenate((packet, jnp.concatenate(corners, axis=1)), axis=0)

    x_outer = lax.ppermute(relayed(to_outer, core), ("x", "c"), [(2 * x + 1, 2 * x + 2) for x in range(3)]
                           + [(2 * x + 2, 2 * x + 1) for x in range(3)])
    x_sibling = lax.ppermute(relayed(to_sibling, 1 - core), "c", [(0, 1), (1, 0)])
    mids = mid_taps(fill_along_y, SLOTS, dst, own_f, own_c, (y_first, y_second), flipped, weights)
    results = convolve(fill_along_x, SLOTS, dst, mids, (x_sibling, x_outer), flipped, weights)

    def with_whole_bricks(results):
        packets = pack_bricks(recv_slot, features, cotangent)
        halos = [pass_to(packet, -heading[0], -heading[1]) for packet, heading in zip(packets, DIRECTIONS)]
        mids = mid_taps(fill_bricks, 1, dst, own_f, own_c, halos, flipped, weights)
        return spread_out(*convolve(fill_nothing, 1, dst, mids, (), flipped, weights))

    def as_they_are(results):
        return spread_out(*results)

    own = results[2]
    return tuple(lax.cond(own[0, 27, 0, 0] != 0, with_whole_bricks, as_they_are, results))


def solution(mesh):
    fine = Mesh(mesh.devices.reshape(4, 2, 4, 8), AXES)
    bricks = P(AXES, None, None)
    return jax.shard_map(
        local,
        mesh=fine,
        in_specs=(bricks, P(), bricks, P(None, AXES), P(AXES)),
        out_specs=(bricks, bricks, P()),
        check_vma=False,
    )
```

```python
import functools

import jax
import jax.numpy as jnp
import numpy as np
from jax import lax
from jax.experimental import pallas as pl
from jax.experimental.pallas import tpu as pltpu
from jax.sharding import Mesh, PartitionSpec as P

BRICK = 4
TILE = 4
BZ = 2
HALO = 40
SLOTS = 8
VOXELS = 64
CHANNELS = 128
PLANE = BRICK * BRICK
PLANES = BRICK + 2
WIDE = 9 * CHANNELS
ROWS_M = 28

DIRECTIONS = ((1, 0), (-1, 0), (0, 1), (0, -1), (1, 1), (1, -1), (-1, 1), (-1, -1))
LENGTHS = (TILE * BZ,) * 4 + (BZ,) * 4
STARTS = tuple(int(start) for start in np.cumsum((0,) + LENGTHS[:-1]))
AXES = ("x", "c", "y", "z")
VMEM_LIMIT = 24 * 1024 * 1024


def where_equal(left, right):
    return jnp.where(left == right, 1.0, 0.0).astype(jnp.bfloat16)


def shift_matrix():
    row = lax.broadcasted_iota(jnp.int32, (9 * PLANE, 9 * PLANE), 0)
    column = lax.broadcasted_iota(jnp.int32, (9 * PLANE, 9 * PLANE), 1)
    number = row >> 4
    third = (number * 11) >> 5
    y = ((row >> 2) & 3) + third + 3
    z = (row & 3) + number - 3 * third + 3
    return where_equal(column, ((y >> 2) * 3 + (z >> 2)) * PLANE + (y & 3) * BRICK + (z & 3))


def layer_matrix():
    row = lax.broadcasted_iota(jnp.int32, (4 * PLANE, VOXELS), 0)
    column = lax.broadcasted_iota(jnp.int32, (4 * PLANE, VOXELS), 1)
    quarter = (row >> 2) & 3
    vx = jnp.where(row < 2 * PLANE, quarter, (quarter >> 1) * 3)
    return where_equal(column, vx * PLANE + ((row >> 4) & 1) * 12 + (row & 3))


def expand_matrix(side):
    row = lax.broadcasted_iota(jnp.int32, (VOXELS, PLANE), 0)
    column = lax.broadcasted_iota(jnp.int32, (VOXELS, PLANE), 1)
    return where_equal(row, (column >> 2) * PLANE + side * 12 + (column & 3))


def expand_corner_matrix(order, side):
    row = lax.broadcasted_iota(jnp.int32, (2 * VOXELS, PLANE), 0)
    column = lax.broadcasted_iota(jnp.int32, (2 * VOXELS, PLANE), 1)
    vy = (row >> 2) & 3
    return where_equal(column + vy * PLANE, order * 8 + (row >> 6) * 4 + (row & 3) + side * 3 * PLANE)


def pack_layers_kernel(recv_slot_ref, features_ref, cotangent_ref, mine, theirs, to_outer,
                       own_f, own_c, sides, slot_ref, sems):
    bricks = (own_f, own_c)
    copies = [
        pltpu.make_async_copy(ref, target, sems.at[number])
        for number, (ref, target) in enumerate((
            (features_ref, own_f.at[pl.ds(0, SLOTS)]),
            (cotangent_ref, own_c.at[pl.ds(0, SLOTS)]),
            (recv_slot_ref, slot_ref),
        ))
    ]
    for copy in copies:
        copy.start()
    for own in bricks:
        own[SLOTS] = jnp.zeros((VOXELS, CHANNELS), jnp.bfloat16)
    sides[:, SLOTS] = jnp.zeros((2, 4 * PLANE, CHANNELS), jnp.bfloat16)
    core = lax.axis_index("c")
    odd = lax.axis_index("z") & 1
    layer = layer_matrix()
    block = lax.broadcasted_iota(jnp.int32, (PLANE, CHANNELS), 0) >> 2
    masks = [where_equal(block, number) for number in range(4)]
    for copy in copies:
        copy.wait()
    for kind in range(2):
        beside = jnp.concatenate([bricks[kind][slot] for slot in range(SLOTS)], axis=1)
        picked = jnp.dot(layer, beside, preferred_element_type=jnp.float32).astype(jnp.bfloat16)
        for slot in range(SLOTS):
            sides[kind, slot] = picked[:, slot * CHANNELS : (slot + 1) * CHANNELS]

    def put(packet, position, halo, source, begin):
        slot = jnp.clip(slot_ref[halo], 0, SLOTS)
        rows = pl.ds(begin, PLANE)
        packet[position, :, :CHANNELS] = source[0][slot, rows]
        packet[position, :, CHANNELS:] = source[1][slot, rows]

    turn = odd ^ core
    for packet, up in ((mine, 1 - turn), (theirs, turn)):
        begin = pl.multiple_of(up * PLANE, PLANE)
        for position in range(SLOTS):
            put(packet, position, STARTS[2] + up * LENGTHS[2] + position, (sides.at[0], sides.at[1]), begin)
        rows = pl.ds(pl.multiple_of((up + 2) * PLANE, PLANE), PLANE)
        halos = [STARTS[number] + up * BZ + position for number in (4, 6) for position in range(BZ)]
        slots = [jnp.clip(slot_ref[halo], 0, SLOTS) for halo in halos]
        for kind in range(2):
            tile = sides[kind, slots[0], rows] * masks[0]
            for number in range(1, 4):
                tile = tile + sides[kind, slots[number], rows] * masks[number]
            packet[SLOTS, :, kind * CHANNELS : (kind + 1) * CHANNELS] = tile
    for packet, first, up in ((theirs, SLOTS + 1, 1 - core), (to_outer, 0, core)):
        begin = pl.multiple_of(up * (VOXELS - PLANE), PLANE)
        for position in range(LENGTHS[0]):
            put(packet, first + position, up * LENGTHS[0] + position, bricks, begin)


def pack_layers(recv_slot, features, cotangent):
    vmem = pl.BlockSpec(memory_space=pltpu.VMEM)
    hbm = pl.BlockSpec(memory_space=pltpu.HBM)
    return pl.pallas_call(
        pack_layers_kernel,
        in_specs=[hbm] * 3,
        out_specs=[vmem] * 5,
        out_shape=[
            jax.ShapeDtypeStruct((length, PLANE, 2 * CHANNELS), jnp.bfloat16) for length in (SLOTS + 1, 2 * SLOTS + 1, SLOTS)
        ] + [jax.ShapeDtypeStruct((SLOTS + 1, VOXELS, CHANNELS), jnp.bfloat16)] * 2,
        scratch_shapes=[
            pltpu.VMEM((2, SLOTS + 1, 4 * PLANE, CHANNELS), jnp.bfloat16),
            pltpu.SMEM((HALO,), jnp.int32),
            pltpu.SemaphoreType.DMA((3,)),
        ],
        compiler_params=pltpu.CompilerParams(vmem_limit_bytes=VMEM_LIMIT),
    )(recv_slot, features, cotangent)


def fill_bricks(halos, lanes, bricks):
    begin_at = SLOTS
    for halo in halos:
        bricks[begin_at : begin_at + halo.shape[0]] = halo[:, :, lanes]
        begin_at += halo.shape[0]


def fill_along_y(halos, lanes, bricks):
    turn = lax.axis_index("z") & 1 ^ lax.axis_index("c")
    for faces, side in ((halos[0], turn), (halos[1], 1 - turn)):
        tiles = jnp.concatenate([faces[position, :, lanes] for position in range(SLOTS)], axis=1)
        whole = jnp.dot(expand_matrix(side), tiles, preferred_element_type=jnp.float32).astype(jnp.bfloat16)
        for position in range(SLOTS):
            target = SLOTS + STARTS[2] + side * LENGTHS[2] + position
            bricks[target] = whole[:, position * CHANNELS : (position + 1) * CHANNELS]


def fill_along_x(halos, lanes, bricks):
    core = lax.axis_index("c")
    turn = lax.axis_index("z") & 1 ^ core
    both = ((halos[0], core), (halos[1], 1 - core))
    for packet, below in both:
        for position in range(SLOTS):
            tile = packet[position, :, lanes]
            target = SLOTS + below * LENGTHS[0] + position
            for begin in range(0, VOXELS, PLANE):
                bricks[target, begin : begin + PLANE] = tile
    tiles = jnp.concatenate([packet[SLOTS, :, lanes] for packet in halos], axis=1)
    for order, side in ((0, 1 - turn), (1, turn)):
        whole = jnp.dot(
            expand_corner_matrix(order, side), tiles, preferred_element_type=jnp.float32
        ).astype(jnp.bfloat16)
        for number, (_, below) in enumerate(both):
            for position in range(BZ):
                target = SLOTS + STARTS[4] + side * BZ + below * 2 * BZ + position
                bricks[target] = whole[
                    position * VOXELS : (position + 1) * VOXELS, number * CHANNELS : (number + 1) * CHANNELS
                ]


def fill_nothing(halos, lanes, bricks):
    pass


def out_of_place(dst):
    k = lax.broadcasted_iota(jnp.int32, dst.shape, 1)
    ninth = jnp.where(k >= 18, 2, jnp.where(k >= 9, 1, 0))
    rest = k - 9 * ninth
    offset = (ninth - 1, jnp.where(rest >= 6, 2, jnp.where(rest >= 3, 1, 0)) - 1)
    wrong = jnp.zeros(dst.shape, jnp.float32)
    for number, heading in enumerate(DIRECTIONS):
        start = SLOTS + STARTS[number]
        here = (dst >= start) & (dst < start + LENGTHS[number])
        for axis in range(2):
            if heading[axis]:
                wrong = jnp.where(here & (offset[axis] != heading[axis]), 1.0, wrong)
    return jnp.max(jnp.max(wrong, axis=1, keepdims=True), axis=0, keepdims=True)


def build_taps(unroll, dst_ref, bricks, planes, taps):
    shift = shift_matrix()

    def around(slot, plane):
        side = 0 if plane == 0 else 2 if plane == PLANES - 1 else 1
        local = (plane - 1) % BRICK * PLANE
        return jnp.concatenate(
            [bricks[dst_ref[slot, side * 9 + number], local : local + PLANE] for number in range(9)], axis=0
        )

    def one_slot(slot, carry):
        for index in range(0, len(planes), 2):
            pair = jnp.concatenate((around(slot, planes[index]), around(slot, planes[index + 1])), axis=1)
            moved = jnp.dot(shift, pair, preferred_element_type=jnp.float32).astype(jnp.bfloat16)
            for number in range(9):
                rows = moved[number * PLANE : (number + 1) * PLANE]
                target = slice(number * CHANNELS, (number + 1) * CHANNELS)
                taps[slot, index, :, target] = rows[:, :CHANNELS]
                taps[slot, index + 1, :, target] = rows[:, CHANNELS:]
        return carry

    lax.fori_loop(0, SLOTS, one_slot, 0, unroll=unroll)


def taps_of(mid, edge, side):
    if side == 0:
        planes = jnp.concatenate((edge[:, :1], mid[:, :3]), axis=1)
    elif side == 1:
        planes = mid[...]
    else:
        planes = jnp.concatenate((mid[:, 1:], edge[:, 1:]), axis=1)
    return planes.reshape(SLOTS * VOXELS, WIDE)


def store_products(flipped_ref, tap, first, send_ref, keep_ref):
    core = lax.axis_index("c")
    half = CHANNELS // 2
    flipped = jnp.concatenate((flipped_ref[1 - core], flipped_ref[core]), axis=0)
    part = jnp.dot(flipped, tap, preferred_element_type=jnp.float32)
    for number in range(9):
        block = part[:, number * CHANNELS : (number + 1) * CHANNELS]
        for quarter in range(4):
            rows = slice(quarter * 16, quarter * 16 + 16)
            send_ref[quarter, first + number] = block[:half][rows].astype(jnp.bfloat16)
            keep_ref[quarter, first + number] = block[half:][rows]


def grad_part(tap, weights_ref, side):
    matrix = jnp.concatenate([weights_ref[26 - side * 9 - number] for number in range(9)], axis=1)
    return lax.dot_general(tap, matrix, (((1,), (1,)), ((), ())), preferred_element_type=jnp.float32)


def mid_kernel(fill, unroll, count, dst_ref, features_ref, cotangent_ref, flipped_ref, weights_ref, *rest):
    halos = rest[:count]
    mid_f, mid_c, bricks_f, bricks_c, send_ref, keep_ref, grad_ref = rest[count:]
    for kind, (own, bricks, mid) in enumerate(((features_ref, bricks_f, mid_f), (cotangent_ref, bricks_c, mid_c))):
        bricks[:SLOTS] = own[:SLOTS]
        for begin, end in ((SLOTS, SLOTS + STARTS[2]), (SLOTS + STARTS[4], SLOTS + HALO + 1)):
            bricks[begin:end] = jnp.zeros((end - begin, VOXELS, CHANNELS), jnp.bfloat16)
        fill(halos, slice(kind * CHANNELS, (kind + 1) * CHANNELS), bricks)
        build_taps(unroll, dst_ref, bricks, (1, 2, 3, 4), mid)
    tap = mid_c[...].reshape(SLOTS * VOXELS, WIDE)
    store_products(flipped_ref, tap, 0, send_ref, keep_ref)
    grad_ref[...] = grad_part(tap, weights_ref, 1)


def weight_kernel(fill, unroll, count, dst_ref, table_ref, mid, _, *rest):
    halos = rest[:count]
    flipped_ref, send_mid, keep_mid, send_ref, keep_ref, edge, bricks = rest[count:]
    fill(halos, slice(CHANNELS, 2 * CHANNELS), bricks)
    build_taps(unroll, dst_ref, bricks, (0, PLANES - 1), edge)
    send_ref[:, 9:18] = send_mid[...]
    keep_ref[:, 9:18] = keep_mid[...]
    for side in (0, 2):
        store_products(flipped_ref, taps_of(mid, edge, side), side * 9, send_ref, keep_ref)
    flag = jnp.broadcast_to(out_of_place(table_ref[...]), (16, CHANNELS))
    for quarter in range(4):
        send_ref[quarter, 27] = flag.astype(jnp.bfloat16)
        keep_ref[quarter, 27] = flag


def grad_kernel(mid, edge, weights_ref, grad_mid, grad_ref):
    grad = grad_mid[...]
    for side in (0, 2):
        grad = grad + grad_part(taps_of(mid, edge, side), weights_ref, side)
    grad_ref[...] = grad.astype(jnp.bfloat16).reshape(SLOTS, VOXELS, CHANNELS)


def edge_kernel(fill, unroll, count, dst_ref, _, *rest):
    edge, bricks = rest[count:]
    fill(rest[:count], slice(0, CHANNELS), bricks)
    build_taps(unroll, dst_ref, bricks, (0, PLANES - 1), edge)


def output_kernel(mid, edge, weights_ref, outputs_ref):
    outputs = None
    for side in range(3):
        matrix = weights_ref[side * 9 : side * 9 + 9].reshape(WIDE, CHANNELS)
        part = jnp.dot(taps_of(mid, edge, side), matrix, preferred_element_type=jnp.float32)
        outputs = part if outputs is None else outputs + part
    outputs_ref[...] = outputs.astype(jnp.bfloat16).reshape(SLOTS, VOXELS, CHANNELS)


VMEM_SPEC = pl.BlockSpec(memory_space=pltpu.VMEM)
SMEM_SPEC = pl.BlockSpec(memory_space=pltpu.SMEM)
BRICK_SHAPE = jax.ShapeDtypeStruct((SLOTS, VOXELS, CHANNELS), jnp.bfloat16)
MID_SHAPE = jax.ShapeDtypeStruct((SLOTS, BRICK, PLANE, WIDE), jnp.bfloat16)
EDGE_SHAPE = jax.ShapeDtypeStruct((SLOTS, 2, PLANE, WIDE), jnp.bfloat16)
ALL_BRICKS = jax.ShapeDtypeStruct((SLOTS + HALO + 1, VOXELS, CHANNELS), jnp.bfloat16)
PARAMS = pltpu.CompilerParams(vmem_limit_bytes=VMEM_LIMIT)
COST = pl.CostEstimate(flops=4 * SLOTS * VOXELS * 27 * CHANNELS * CHANNELS, bytes_accessed=4_000_000, transcendentals=0)


def mid_taps(fill, unroll, dst, own_f, own_c, halos, flipped, weights):
    return pl.pallas_call(
        functools.partial(mid_kernel, fill, unroll, len(halos)),
        in_specs=[SMEM_SPEC] + [VMEM_SPEC] * (4 + len(halos)),
        out_specs=[VMEM_SPEC] * 7,
        out_shape=[
            MID_SHAPE, MID_SHAPE, ALL_BRICKS, ALL_BRICKS,
            jax.ShapeDtypeStruct((4, 9, 16, CHANNELS), jnp.bfloat16),
            jax.ShapeDtypeStruct((4, 9, 16, CHANNELS), jnp.float32),
            jax.ShapeDtypeStruct((SLOTS * VOXELS, CHANNELS), jnp.float32),
        ],
        compiler_params=PARAMS,
        cost_estimate=COST,
    )(dst, own_f, own_c, flipped, weights, *halos)


def weight_sums(fill, unroll, dst, mid, bricks, halos, flipped, send, keep):
    return pl.pallas_call(
        functools.partial(weight_kernel, fill, unroll, len(halos)),
        in_specs=[SMEM_SPEC] + [VMEM_SPEC] * (6 + len(halos)),
        out_specs=[VMEM_SPEC] * 4,
        out_shape=[
            jax.ShapeDtypeStruct((4, ROWS_M, 16, CHANNELS), jnp.bfloat16),
            jax.ShapeDtypeStruct((4, ROWS_M, 16, CHANNELS), jnp.float32),
            EDGE_SHAPE,
            ALL_BRICKS,
        ],
        input_output_aliases={3: 3},
        compiler_params=PARAMS,
        cost_estimate=COST,
    )(dst, dst, mid, bricks, *halos, flipped, send, keep)


def feature_edges(fill, unroll, dst, bricks, halos):
    return pl.pallas_call(
        functools.partial(edge_kernel, fill, unroll, len(halos)),
        in_specs=[SMEM_SPEC] + [VMEM_SPEC] * (1 + len(halos)),
        out_specs=[VMEM_SPEC] * 2,
        out_shape=[EDGE_SHAPE, ALL_BRICKS],
        input_output_aliases={1: 1},
        compiler_params=PARAMS,
        cost_estimate=COST,
    )(dst, bricks, *halos)[0]


def product(kernel, *operands):
    return pl.pallas_call(
        kernel,
        in_specs=[VMEM_SPEC] * len(operands),
        out_specs=VMEM_SPEC,
        out_shape=BRICK_SHAPE,
        compiler_params=PARAMS,
        cost_estimate=COST,
    )(*operands)


def convolve(fill, unroll, dst, mids, halos, flipped, weights):
    mid_f, mid_c, bricks_f, bricks_c, send, keep, grad_mid = mids
    send, keep, edge_c, _ = weight_sums(fill, unroll, dst, mid_c, bricks_c, halos, flipped, send, keep)
    arrived = lax.ppermute(send, "c", [(0, 1), (1, 0)])
    input_grad = product(grad_kernel, mid_c, edge_c, weights, grad_mid)
    edge_f = feature_edges(fill, unroll, dst, bricks_f, halos)
    arrived, input_grad, edge_f = lax.optimization_barrier((arrived, input_grad, edge_f))
    own = sum_everywhere(arrived, keep)
    other = lax.ppermute(own, "c", [(0, 1), (1, 0)])
    outputs = product(output_kernel, mid_f, edge_f, weights)
    return outputs, input_grad, own, other


def pack_bricks_kernel(slot_ref, features_ref, cotangent_ref, *packets):
    begin_at = 0
    for packet in packets:
        for position in range(packet.shape[0]):
            slot = slot_ref[begin_at + position]
            row = jnp.clip(slot, 0, SLOTS - 1)

            @pl.when(slot < SLOTS)
            def _():
                packet[position, :, :CHANNELS] = features_ref[row]
                packet[position, :, CHANNELS:] = cotangent_ref[row]

            @pl.when(slot >= SLOTS)
            def _():
                packet[position] = jnp.zeros((VOXELS, 2 * CHANNELS), jnp.bfloat16)

        begin_at += packet.shape[0]


def pack_bricks(recv_slot, features, cotangent):
    vmem = pl.BlockSpec(memory_space=pltpu.VMEM)
    return pl.pallas_call(
        pack_bricks_kernel,
        in_specs=[pl.BlockSpec(memory_space=pltpu.SMEM), vmem, vmem],
        out_specs=[vmem] * 8,
        out_shape=[
            jax.ShapeDtypeStruct((length, VOXELS, 2 * CHANNELS), jnp.bfloat16) for length in LENGTHS
        ],
        compiler_params=pltpu.CompilerParams(vmem_limit_bytes=VMEM_LIMIT),
    )(recv_slot, features, cotangent)


def pass_to(value, step_x, step_y):
    pairs = []
    for gx in range(8):
        for gy in range(32):
            if 0 <= gx + step_x < 8 and 0 <= gy + step_y < 32:
                pairs.append((gx * 32 + gy, (gx + step_x) * 32 + gy + step_y))
    return lax.ppermute(value, AXES, pairs)


def sum_everywhere(arrived, keep):
    chip_sum = (keep + arrived.astype(jnp.float32)).astype(jnp.bfloat16)
    parts = chip_sum.reshape(16, 7, 16, CHANNELS)
    parts = lax.all_to_all(parts, ("x", "y"), 0, 0)
    total = jnp.sum(parts.astype(jnp.float32), axis=0)
    largest = jnp.max(jnp.abs(total), axis=(0, 1))
    power = jnp.clip(jnp.ceil(jnp.log2(jnp.maximum(largest, 1e-37))), -100.0, 100.0)
    power = jnp.broadcast_to(power, (1, 16, CHANNELS))
    share = jnp.concatenate((total * jnp.exp2(14.0 - power), power), axis=0).astype(jnp.float16)
    column = lax.all_to_all(jnp.broadcast_to(share[None], (8,) + share.shape), "z", 0, 0).astype(jnp.float32)
    total = jnp.sum(column[:, :7] * jnp.exp2(column[:, 7:] - 14.0), axis=0)
    share = (total * (1.0 / (VOXELS * SLOTS))).astype(jnp.bfloat16)
    whole = jnp.broadcast_to(share[None], (16,) + share.shape)
    return lax.all_to_all(whole, ("x", "y"), 0, 0).reshape(4, ROWS_M, 16, CHANNELS)


def spread_kernel(own_ref, other_ref, outputs_ref, grad_ref, outputs_out, grad_out, out_ref, whole, sems):
    half = CHANNELS // 2
    core = lax.axis_index("c")
    copies = [
        pltpu.make_async_copy(outputs_ref, outputs_out, sems.at[9]),
        pltpu.make_async_copy(grad_ref, grad_out, sems.at[10]),
    ]
    for copy in copies:
        copy.start()
    for chunk in range(9):
        for m in range(3 * chunk, 3 * chunk + 3):
            for quarter in range(4):
                for ref, side in ((own_ref, core), (other_ref, 1 - core)):
                    begin = pl.multiple_of(side * half + quarter * 16, 16)
                    whole[26 - m, pl.ds(begin, 16)] = ref[quarter, m].astype(jnp.float32)
        rows = pl.ds(24 - 3 * chunk, 3)
        copies.append(pltpu.make_async_copy(whole.at[rows], out_ref.at[rows], sems.at[chunk]))
        copies[-1].start()
    for copy in copies:
        copy.wait()


def spread_out(outputs, input_grad, own, other):
    return pl.pallas_call(
        spread_kernel,
        in_specs=[VMEM_SPEC] * 4,
        out_specs=[pl.BlockSpec(memory_space=pltpu.HBM)] * 3,
        out_shape=[BRICK_SHAPE, BRICK_SHAPE, jax.ShapeDtypeStruct((27, CHANNELS, CHANNELS), jnp.float32)],
        scratch_shapes=[
            pltpu.VMEM((27, CHANNELS, CHANNELS), jnp.float32),
            pltpu.SemaphoreType.DMA((11,)),
        ],
        compiler_params=PARAMS,
    )(own, other, outputs, input_grad)


def local(features, weights, cotangent, dst_index, recv_slot):
    core = lax.axis_index("c")
    dst = jnp.clip(dst_index.T, 0, SLOTS + HALO)

    mine, theirs, to_outer, own_f, own_c = pack_layers(recv_slot, features, cotangent)
    flipped = jnp.transpose(own_f[:SLOTS].reshape(SLOTS * VOXELS, CHANNELS))
    flipped = flipped.reshape(2, CHANNELS // 2, SLOTS * VOXELS)
    count = SLOTS + 1
    from_sibling = lax.ppermute(theirs, "c", [(0, 1), (1, 0)])
    pairs = [(gy, gy ^ 1) for gy in range(32)]
    pairs += [(32 + gy, 32 + ((gy + 1) ^ 1) - 1) for gy in range(1, 31)]
    along_y = lax.ppermute(jnp.concatenate((mine, from_sibling[:count]), axis=0), ("c", "y", "z"), pairs)
    along_y, dst, flipped = lax.optimization_barrier((along_y, dst, flipped))
    handed_on = lax.ppermute(
        jnp.concatenate((along_y[count:], along_y[SLOTS:count]), axis=0), "c", [(0, 1), (1, 0)]
    )
    y_mine, y_other = along_y[:count], handed_on[:count]

    def with_corners(faces, *corners):
        rows = [lax.dynamic_slice_in_dim(value, 8 * core, 8, axis=1) for value in corners]
        return jnp.concatenate((faces, jnp.concatenate(rows, axis=1)), axis=0)

    x_outer = lax.ppermute(
        with_corners(to_outer, y_mine[SLOTS:], y_other[SLOTS:]), ("x", "c"),
        [(2 * x + 1, 2 * x + 2) for x in range(3)] + [(2 * x + 2, 2 * x + 1) for x in range(3)],
    )
    x_sibling = with_corners(from_sibling[count:], handed_on[count:], along_y[count + SLOTS :])
    mids = mid_taps(fill_along_y, SLOTS, dst, own_f, own_c, (y_mine, y_other), flipped, weights)
    results = convolve(fill_along_x, SLOTS, dst, mids, (x_sibling, x_outer), flipped, weights)

    def with_whole_bricks(results):
        packets = pack_bricks(recv_slot, features, cotangent)
        halos = [pass_to(packet, -heading[0], -heading[1]) for packet, heading in zip(packets, DIRECTIONS)]
        mids = mid_taps(fill_bricks, 1, dst, own_f, own_c, halos, flipped, weights)
        return spread_out(*convolve(fill_nothing, 1, dst, mids, (), flipped, weights))

    def as_they_are(results):
        return spread_out(*results)

    own = results[2]
    return tuple(lax.cond(own[0, 27, 0, 0] != 0, with_whole_bricks, as_they_are, results))


def solution(mesh):
    fine = Mesh(mesh.devices.reshape(4, 2, 4, 8), AXES)
    bricks = P(AXES, None, None)
    return jax.shard_map(
        local,
        mesh=fine,
        in_specs=(bricks, P(), bricks, P(None, AXES), P(AXES)),
        out_specs=(bricks, bricks, P()),
        check_vma=False,
    )
```

```python
import functools

import jax
import jax.numpy as jnp
import numpy as np
from jax import lax
from jax.experimental import pallas as pl
from jax.experimental.pallas import tpu as pltpu
from jax.sharding import Mesh, PartitionSpec as P

BRICK = 4
TILE = 4
BZ = 2
HALO = 40
SLOTS = 8
VOXELS = 64
CHANNELS = 128
PLANE = BRICK * BRICK
PLANES = BRICK + 2
WIDE = 9 * CHANNELS
ROWS_M = 28

DIRECTIONS = ((1, 0), (-1, 0), (0, 1), (0, -1), (1, 1), (1, -1), (-1, 1), (-1, -1))
LENGTHS = (TILE * BZ,) * 4 + (BZ,) * 4
STARTS = tuple(int(start) for start in np.cumsum((0,) + LENGTHS[:-1]))
AXES = ("x", "c", "y", "z")
VMEM_LIMIT = 24 * 1024 * 1024


def where_equal(left, right):
    return jnp.where(left == right, 1.0, 0.0).astype(jnp.bfloat16)


def shift_matrix():
    row = lax.broadcasted_iota(jnp.int32, (9 * PLANE, 9 * PLANE), 0)
    column = lax.broadcasted_iota(jnp.int32, (9 * PLANE, 9 * PLANE), 1)
    number = row >> 4
    third = (number * 11) >> 5
    y = ((row >> 2) & 3) + third + 3
    z = (row & 3) + number - 3 * third + 3
    return where_equal(column, ((y >> 2) * 3 + (z >> 2)) * PLANE + (y & 3) * BRICK + (z & 3))


def layer_matrix():
    row = lax.broadcasted_iota(jnp.int32, (4 * PLANE, VOXELS), 0)
    column = lax.broadcasted_iota(jnp.int32, (4 * PLANE, VOXELS), 1)
    quarter = (row >> 2) & 3
    vx = jnp.where(row < 2 * PLANE, quarter, (quarter >> 1) * 3)
    return where_equal(column, vx * PLANE + ((row >> 4) & 1) * 12 + (row & 3))


def expand_matrix(side):
    row = lax.broadcasted_iota(jnp.int32, (VOXELS, PLANE), 0)
    column = lax.broadcasted_iota(jnp.int32, (VOXELS, PLANE), 1)
    return where_equal(row, (column >> 2) * PLANE + side * 12 + (column & 3))


def expand_corner_matrix(order, side):
    row = lax.broadcasted_iota(jnp.int32, (2 * VOXELS, PLANE), 0)
    column = lax.broadcasted_iota(jnp.int32, (2 * VOXELS, PLANE), 1)
    vy = (row >> 2) & 3
    return where_equal(column + vy * PLANE, order * 8 + (row >> 6) * 4 + (row & 3) + side * 3 * PLANE)


def pack_layers_kernel(recv_slot_ref, features_ref, cotangent_ref, to_first, to_second, to_sibling, to_outer,
                       own_f, own_c, sides, slot_ref, sems):
    bricks = (own_f, own_c)
    copies = [
        pltpu.make_async_copy(ref, target, sems.at[number])
        for number, (ref, target) in enumerate((
            (features_ref, own_f.at[pl.ds(0, SLOTS)]),
            (cotangent_ref, own_c.at[pl.ds(0, SLOTS)]),
            (recv_slot_ref, slot_ref),
        ))
    ]
    for copy in copies:
        copy.start()
    for own in bricks:
        own[SLOTS] = jnp.zeros((VOXELS, CHANNELS), jnp.bfloat16)
    sides[:, SLOTS] = jnp.zeros((2, 4 * PLANE, CHANNELS), jnp.bfloat16)
    core = lax.axis_index("c")
    odd = lax.axis_index("z") & 1
    layer = layer_matrix()
    block = lax.broadcasted_iota(jnp.int32, (PLANE, CHANNELS), 0) >> 2
    masks = [where_equal(block, number) for number in range(4)]
    for copy in copies:
        copy.wait()
    for kind in range(2):
        beside = jnp.concatenate([bricks[kind][slot] for slot in range(SLOTS)], axis=1)
        picked = jnp.dot(layer, beside, preferred_element_type=jnp.float32).astype(jnp.bfloat16)
        for slot in range(SLOTS):
            sides[kind, slot] = picked[:, slot * CHANNELS : (slot + 1) * CHANNELS]

    def put(packet, position, halo, source, begin):
        slot = jnp.clip(slot_ref[halo], 0, SLOTS)
        rows = pl.ds(begin, PLANE)
        packet[position, :, :CHANNELS] = source[0][slot, rows]
        packet[position, :, CHANNELS:] = source[1][slot, rows]

    for packet, up in ((to_first, 1 - odd), (to_second, odd)):
        begin = pl.multiple_of(up * PLANE, PLANE)
        for position in range(SLOTS):
            put(packet, position, STARTS[2] + up * LENGTHS[2] + position, (sides.at[0], sides.at[1]), begin)
        rows = pl.ds(pl.multiple_of((up + 2) * PLANE, PLANE), PLANE)
        halos = [STARTS[number] + up * BZ + position for number in (4, 6) for position in range(BZ)]
        slots = [jnp.clip(slot_ref[halo], 0, SLOTS) for halo in halos]
        for kind in range(2):
            tile = sides[kind, slots[0], rows] * masks[0]
            for number in range(1, 4):
                tile = tile + sides[kind, slots[number], rows] * masks[number]
            packet[SLOTS, :, kind * CHANNELS : (kind + 1) * CHANNELS] = tile
    for packet, up in ((to_sibling, 1 - core), (to_outer, core)):
        begin = pl.multiple_of(up * (VOXELS - PLANE), PLANE)
        for position in range(LENGTHS[0]):
            put(packet, position, up * LENGTHS[0] + position, bricks, begin)


def pack_layers(recv_slot, features, cotangent):
    vmem = pl.BlockSpec(memory_space=pltpu.VMEM)
    hbm = pl.BlockSpec(memory_space=pltpu.HBM)
    return pl.pallas_call(
        pack_layers_kernel,
        in_specs=[hbm] * 3,
        out_specs=[vmem] * 6,
        out_shape=[
            jax.ShapeDtypeStruct((length, PLANE, 2 * CHANNELS), jnp.bfloat16) for length in (SLOTS + 1, SLOTS + 1, SLOTS, SLOTS)
        ] + [jax.ShapeDtypeStruct((SLOTS + 1, VOXELS, CHANNELS), jnp.bfloat16)] * 2,
        scratch_shapes=[
            pltpu.VMEM((2, SLOTS + 1, 4 * PLANE, CHANNELS), jnp.bfloat16),
            pltpu.SMEM((HALO,), jnp.int32),
            pltpu.SemaphoreType.DMA((3,)),
        ],
        compiler_params=pltpu.CompilerParams(vmem_limit_bytes=VMEM_LIMIT),
    )(recv_slot, features, cotangent)


def fill_bricks(halos, lanes, bricks):
    begin_at = SLOTS
    for halo in halos:
        bricks[begin_at : begin_at + halo.shape[0]] = halo[:, :, lanes]
        begin_at += halo.shape[0]


def fill_along_y(halos, lanes, bricks):
    odd = lax.axis_index("z") & 1
    for faces, side in ((halos[0], odd), (halos[1], 1 - odd)):
        tiles = jnp.concatenate([faces[position, :, lanes] for position in range(SLOTS)], axis=1)
        whole = jnp.dot(expand_matrix(side), tiles, preferred_element_type=jnp.float32).astype(jnp.bfloat16)
        for position in range(SLOTS):
            target = SLOTS + STARTS[2] + side * LENGTHS[2] + position
            bricks[target] = whole[:, position * CHANNELS : (position + 1) * CHANNELS]


def fill_along_x(halos, lanes, bricks):
    core, odd = lax.axis_index("c"), lax.axis_index("z") & 1
    both = ((halos[0], core), (halos[1], 1 - core))
    for packet, below in both:
        for position in range(SLOTS):
            tile = packet[position, :, lanes]
            target = SLOTS + below * LENGTHS[0] + position
            for begin in range(0, VOXELS, PLANE):
                bricks[target, begin : begin + PLANE] = tile
    tiles = jnp.concatenate([packet[SLOTS, :, lanes] for packet in halos], axis=1)
    for order, side in ((0, odd), (1, 1 - odd)):
        whole = jnp.dot(
            expand_corner_matrix(order, side), tiles, preferred_element_type=jnp.float32
        ).astype(jnp.bfloat16)
        for number, (_, below) in enumerate(both):
            for position in range(BZ):
                target = SLOTS + STARTS[4] + side * BZ + below * 2 * BZ + position
                bricks[target] = whole[
                    position * VOXELS : (position + 1) * VOXELS, number * CHANNELS : (number + 1) * CHANNELS
                ]


def fill_nothing(halos, lanes, bricks):
    pass


def out_of_place(dst):
    k = lax.broadcasted_iota(jnp.int32, dst.shape, 1)
    ninth = jnp.where(k >= 18, 2, jnp.where(k >= 9, 1, 0))
    rest = k - 9 * ninth
    offset = (ninth - 1, jnp.where(rest >= 6, 2, jnp.where(rest >= 3, 1, 0)) - 1)
    wrong = jnp.zeros(dst.shape, jnp.float32)
    for number, heading in enumerate(DIRECTIONS):
        start = SLOTS + STARTS[number]
        here = (dst >= start) & (dst < start + LENGTHS[number])
        for axis in range(2):
            if heading[axis]:
                wrong = jnp.where(here & (offset[axis] != heading[axis]), 1.0, wrong)
    return jnp.max(jnp.max(wrong, axis=1, keepdims=True), axis=0, keepdims=True)


def build_taps(unroll, dst_ref, bricks, planes, taps):
    shift = shift_matrix()

    def around(slot, plane):
        side = 0 if plane == 0 else 2 if plane == PLANES - 1 else 1
        local = (plane - 1) % BRICK * PLANE
        return jnp.concatenate(
            [bricks[dst_ref[slot, side * 9 + number], local : local + PLANE] for number in range(9)], axis=0
        )

    def one_slot(slot, carry):
        for index in range(0, len(planes), 2):
            pair = jnp.concatenate((around(slot, planes[index]), around(slot, planes[index + 1])), axis=1)
            moved = jnp.dot(shift, pair, preferred_element_type=jnp.float32).astype(jnp.bfloat16)
            for number in range(9):
                rows = moved[number * PLANE : (number + 1) * PLANE]
                target = slice(number * CHANNELS, (number + 1) * CHANNELS)
                taps[slot, index, :, target] = rows[:, :CHANNELS]
                taps[slot, index + 1, :, target] = rows[:, CHANNELS:]
        return carry

    lax.fori_loop(0, SLOTS, one_slot, 0, unroll=unroll)


def taps_of(mid, edge, side):
    if side == 0:
        planes = jnp.concatenate((edge[:, :1], mid[:, :3]), axis=1)
    elif side == 1:
        planes = mid[...]
    else:
        planes = jnp.concatenate((mid[:, 1:], edge[:, 1:]), axis=1)
    return planes.reshape(SLOTS * VOXELS, WIDE)


def store_products(flipped_ref, tap, first, send_ref, keep_ref):
    core = lax.axis_index("c")
    half = CHANNELS // 2
    flipped = jnp.concatenate((flipped_ref[1 - core], flipped_ref[core]), axis=0)
    part = jnp.dot(flipped, tap, preferred_element_type=jnp.float32)
    for number in range(9):
        block = part[:, number * CHANNELS : (number + 1) * CHANNELS]
        for quarter in range(4):
            rows = slice(quarter * 16, quarter * 16 + 16)
            send_ref[quarter, first + number] = block[:half][rows].astype(jnp.bfloat16)
            keep_ref[quarter, first + number] = block[half:][rows]


def grad_part(tap, weights_ref, side):
    matrix = jnp.concatenate([weights_ref[26 - side * 9 - number] for number in range(9)], axis=1)
    return lax.dot_general(tap, matrix, (((1,), (1,)), ((), ())), preferred_element_type=jnp.float32)


def mid_kernel(fill, unroll, count, dst_ref, features_ref, cotangent_ref, flipped_ref, weights_ref, *rest):
    halos = rest[:count]
    mid_f, mid_c, bricks_f, bricks_c, send_ref, keep_ref, grad_ref = rest[count:]
    for kind, (own, bricks, mid) in enumerate(((features_ref, bricks_f, mid_f), (cotangent_ref, bricks_c, mid_c))):
        bricks[:SLOTS] = own[:SLOTS]
        for begin, end in ((SLOTS, SLOTS + STARTS[2]), (SLOTS + STARTS[4], SLOTS + HALO + 1)):
            bricks[begin:end] = jnp.zeros((end - begin, VOXELS, CHANNELS), jnp.bfloat16)
        fill(halos, slice(kind * CHANNELS, (kind + 1) * CHANNELS), bricks)
        build_taps(unroll, dst_ref, bricks, (1, 2, 3, 4), mid)
    tap = mid_c[...].reshape(SLOTS * VOXELS, WIDE)
    store_products(flipped_ref, tap, 0, send_ref, keep_ref)
    grad_ref[...] = grad_part(tap, weights_ref, 1)


def weight_kernel(fill, unroll, count, dst_ref, table_ref, mid, _, *rest):
    halos = rest[:count]
    flipped_ref, send_mid, keep_mid, send_ref, keep_ref, edge, bricks = rest[count:]
    fill(halos, slice(CHANNELS, 2 * CHANNELS), bricks)
    build_taps(unroll, dst_ref, bricks, (0, PLANES - 1), edge)
    send_ref[:, 9:18] = send_mid[...]
    keep_ref[:, 9:18] = keep_mid[...]
    for side in (0, 2):
        store_products(flipped_ref, taps_of(mid, edge, side), side * 9, send_ref, keep_ref)
    flag = jnp.broadcast_to(out_of_place(table_ref[...]), (16, CHANNELS))
    for quarter in range(4):
        send_ref[quarter, 27] = flag.astype(jnp.bfloat16)
        keep_ref[quarter, 27] = flag


def grad_kernel(mid, edge, weights_ref, grad_mid, grad_ref):
    grad = grad_mid[...]
    for side in (0, 2):
        grad = grad + grad_part(taps_of(mid, edge, side), weights_ref, side)
    grad_ref[...] = grad.astype(jnp.bfloat16).reshape(SLOTS, VOXELS, CHANNELS)


def edge_kernel(fill, unroll, count, dst_ref, _, *rest):
    edge, bricks = rest[count:]
    fill(rest[:count], slice(0, CHANNELS), bricks)
    build_taps(unroll, dst_ref, bricks, (0, PLANES - 1), edge)


def output_kernel(mid, edge, weights_ref, outputs_ref):
    outputs = None
    for side in range(3):
        matrix = weights_ref[side * 9 : side * 9 + 9].reshape(WIDE, CHANNELS)
        part = jnp.dot(taps_of(mid, edge, side), matrix, preferred_element_type=jnp.float32)
        outputs = part if outputs is None else outputs + part
    outputs_ref[...] = outputs.astype(jnp.bfloat16).reshape(SLOTS, VOXELS, CHANNELS)


VMEM_SPEC = pl.BlockSpec(memory_space=pltpu.VMEM)
SMEM_SPEC = pl.BlockSpec(memory_space=pltpu.SMEM)
BRICK_SHAPE = jax.ShapeDtypeStruct((SLOTS, VOXELS, CHANNELS), jnp.bfloat16)
MID_SHAPE = jax.ShapeDtypeStruct((SLOTS, BRICK, PLANE, WIDE), jnp.bfloat16)
EDGE_SHAPE = jax.ShapeDtypeStruct((SLOTS, 2, PLANE, WIDE), jnp.bfloat16)
ALL_BRICKS = jax.ShapeDtypeStruct((SLOTS + HALO + 1, VOXELS, CHANNELS), jnp.bfloat16)
PARAMS = pltpu.CompilerParams(vmem_limit_bytes=VMEM_LIMIT)
COST = pl.CostEstimate(flops=4 * SLOTS * VOXELS * 27 * CHANNELS * CHANNELS, bytes_accessed=4_000_000, transcendentals=0)


def mid_taps(fill, unroll, dst, own_f, own_c, halos, flipped, weights):
    return pl.pallas_call(
        functools.partial(mid_kernel, fill, unroll, len(halos)),
        in_specs=[SMEM_SPEC] + [VMEM_SPEC] * (4 + len(halos)),
        out_specs=[VMEM_SPEC] * 7,
        out_shape=[
            MID_SHAPE, MID_SHAPE, ALL_BRICKS, ALL_BRICKS,
            jax.ShapeDtypeStruct((4, 9, 16, CHANNELS), jnp.bfloat16),
            jax.ShapeDtypeStruct((4, 9, 16, CHANNELS), jnp.float32),
            jax.ShapeDtypeStruct((SLOTS * VOXELS, CHANNELS), jnp.float32),
        ],
        compiler_params=PARAMS,
        cost_estimate=COST,
    )(dst, own_f, own_c, flipped, weights, *halos)


def weight_sums(fill, unroll, dst, mid, bricks, halos, flipped, send, keep):
    return pl.pallas_call(
        functools.partial(weight_kernel, fill, unroll, len(halos)),
        in_specs=[SMEM_SPEC] + [VMEM_SPEC] * (6 + len(halos)),
        out_specs=[VMEM_SPEC] * 4,
        out_shape=[
            jax.ShapeDtypeStruct((4, ROWS_M, 16, CHANNELS), jnp.bfloat16),
            jax.ShapeDtypeStruct((4, ROWS_M, 16, CHANNELS), jnp.float32),
            EDGE_SHAPE,
            ALL_BRICKS,
        ],
        input_output_aliases={3: 3},
        compiler_params=PARAMS,
        cost_estimate=COST,
    )(dst, dst, mid, bricks, *halos, flipped, send, keep)


def feature_edges(fill, unroll, dst, bricks, halos):
    return pl.pallas_call(
        functools.partial(edge_kernel, fill, unroll, len(halos)),
        in_specs=[SMEM_SPEC] + [VMEM_SPEC] * (1 + len(halos)),
        out_specs=[VMEM_SPEC] * 2,
        out_shape=[EDGE_SHAPE, ALL_BRICKS],
        input_output_aliases={1: 1},
        compiler_params=PARAMS,
        cost_estimate=COST,
    )(dst, bricks, *halos)[0]


def product(kernel, *operands):
    return pl.pallas_call(
        kernel,
        in_specs=[VMEM_SPEC] * len(operands),
        out_specs=VMEM_SPEC,
        out_shape=BRICK_SHAPE,
        compiler_params=PARAMS,
        cost_estimate=COST,
    )(*operands)


def convolve(fill, unroll, dst, mids, halos, flipped, weights):
    mid_f, mid_c, bricks_f, bricks_c, send, keep, grad_mid = mids
    send, keep, edge_c, _ = weight_sums(fill, unroll, dst, mid_c, bricks_c, halos, flipped, send, keep)
    arrived = lax.ppermute(send, "c", [(0, 1), (1, 0)])
    input_grad = product(grad_kernel, mid_c, edge_c, weights, grad_mid)
    edge_f = feature_edges(fill, unroll, dst, bricks_f, halos)
    arrived, input_grad, edge_f = lax.optimization_barrier((arrived, input_grad, edge_f))
    own = sum_everywhere(arrived, keep)
    other = lax.ppermute(own, "c", [(0, 1), (1, 0)])
    outputs = product(output_kernel, mid_f, edge_f, weights)
    return outputs, input_grad, own, other


def pack_bricks_kernel(slot_ref, features_ref, cotangent_ref, *packets):
    begin_at = 0
    for packet in packets:
        for position in range(packet.shape[0]):
            slot = slot_ref[begin_at + position]
            row = jnp.clip(slot, 0, SLOTS - 1)

            @pl.when(slot < SLOTS)
            def _():
                packet[position, :, :CHANNELS] = features_ref[row]
                packet[position, :, CHANNELS:] = cotangent_ref[row]

            @pl.when(slot >= SLOTS)
            def _():
                packet[position] = jnp.zeros((VOXELS, 2 * CHANNELS), jnp.bfloat16)

        begin_at += packet.shape[0]


def pack_bricks(recv_slot, features, cotangent):
    vmem = pl.BlockSpec(memory_space=pltpu.VMEM)
    return pl.pallas_call(
        pack_bricks_kernel,
        in_specs=[pl.BlockSpec(memory_space=pltpu.SMEM), vmem, vmem],
        out_specs=[vmem] * 8,
        out_shape=[
            jax.ShapeDtypeStruct((length, VOXELS, 2 * CHANNELS), jnp.bfloat16) for length in LENGTHS
        ],
        compiler_params=pltpu.CompilerParams(vmem_limit_bytes=VMEM_LIMIT),
    )(recv_slot, features, cotangent)


def pass_to(value, step_x, step_y):
    pairs = []
    for gx in range(8):
        for gy in range(32):
            if 0 <= gx + step_x < 8 and 0 <= gy + step_y < 32:
                pairs.append((gx * 32 + gy, (gx + step_x) * 32 + gy + step_y))
    return lax.ppermute(value, AXES, pairs)


def sum_everywhere(arrived, keep):
    chip_sum = (keep + arrived.astype(jnp.float32)).astype(jnp.bfloat16)
    parts = chip_sum.reshape(16, 7, 16, CHANNELS)
    parts = lax.all_to_all(parts, ("x", "y"), 0, 0)
    total = jnp.sum(parts.astype(jnp.float32), axis=0)
    largest = jnp.max(jnp.abs(total), axis=(0, 1))
    power = jnp.clip(jnp.ceil(jnp.log2(jnp.maximum(largest, 1e-37))), -100.0, 100.0)
    power = jnp.broadcast_to(power, (1, 16, CHANNELS))
    share = jnp.concatenate((total * jnp.exp2(14.0 - power), power), axis=0).astype(jnp.float16)
    column = lax.all_to_all(jnp.broadcast_to(share[None], (8,) + share.shape), "z", 0, 0).astype(jnp.float32)
    total = jnp.sum(column[:, :7] * jnp.exp2(column[:, 7:] - 14.0), axis=0)
    share = (total * (1.0 / (VOXELS * SLOTS))).astype(jnp.bfloat16)
    whole = jnp.broadcast_to(share[None], (16,) + share.shape)
    return lax.all_to_all(whole, ("x", "y"), 0, 0).reshape(4, ROWS_M, 16, CHANNELS)


def spread_kernel(own_ref, other_ref, outputs_ref, grad_ref, outputs_out, grad_out, out_ref, whole, sems):
    half = CHANNELS // 2
    core = lax.axis_index("c")
    copies = [
        pltpu.make_async_copy(outputs_ref, outputs_out, sems.at[9]),
        pltpu.make_async_copy(grad_ref, grad_out, sems.at[10]),
    ]
    for copy in copies:
        copy.start()
    for chunk in range(9):
        for m in range(3 * chunk, 3 * chunk + 3):
            for quarter in range(4):
                for ref, side in ((own_ref, core), (other_ref, 1 - core)):
                    begin = pl.multiple_of(side * half + quarter * 16, 16)
                    whole[26 - m, pl.ds(begin, 16)] = ref[quarter, m].astype(jnp.float32)
        rows = pl.ds(24 - 3 * chunk, 3)
        copies.append(pltpu.make_async_copy(whole.at[rows], out_ref.at[rows], sems.at[chunk]))
        copies[-1].start()
    for copy in copies:
        copy.wait()


def spread_out(outputs, input_grad, own, other):
    return pl.pallas_call(
        spread_kernel,
        in_specs=[VMEM_SPEC] * 4,
        out_specs=[pl.BlockSpec(memory_space=pltpu.HBM)] * 3,
        out_shape=[BRICK_SHAPE, BRICK_SHAPE, jax.ShapeDtypeStruct((27, CHANNELS, CHANNELS), jnp.float32)],
        scratch_shapes=[
            pltpu.VMEM((27, CHANNELS, CHANNELS), jnp.float32),
            pltpu.SemaphoreType.DMA((11,)),
        ],
        compiler_params=PARAMS,
    )(own, other, outputs, input_grad)


def local(features, weights, cotangent, dst_index, recv_slot):
    core = lax.axis_index("c")
    dst = jnp.clip(dst_index.T, 0, SLOTS + HALO)

    to_first, to_second, to_sibling, to_outer, own_f, own_c = pack_layers(recv_slot, features, cotangent)
    flipped = jnp.transpose(own_f[:SLOTS].reshape(SLOTS * VOXELS, CHANNELS))
    flipped = flipped.reshape(2, CHANNELS // 2, SLOTS * VOXELS)
    y_second = lax.ppermute(to_second, ("y", "z"), [(gy, ((gy + 1) ^ 1) - 1) for gy in range(1, 31)])
    y_first = lax.ppermute(to_first, ("y", "z"), [(gy, gy ^ 1) for gy in range(32)])
    y_second, y_first, dst, flipped = lax.optimization_barrier((y_second, y_first, dst, flipped))

    def relayed(packet, up):
        corners = [lax.dynamic_slice_in_dim(value[SLOTS:], 8 * up, 8, axis=1) for value in (y_first, y_second)]
        return jnp.concatenate((packet, jnp.concatenate(corners, axis=1)), axis=0)

    x_sibling = lax.ppermute(relayed(to_sibling, 1 - core), "c", [(0, 1), (1, 0)])
    x_outer = lax.ppermute(relayed(to_outer, core), ("x", "c"), [(2 * x + 1, 2 * x + 2) for x in range(3)]
                           + [(2 * x + 2, 2 * x + 1) for x in range(3)])
    mids = mid_taps(fill_along_y, SLOTS, dst, own_f, own_c, (y_first, y_second), flipped, weights)
    results = convolve(fill_along_x, SLOTS, dst, mids, (x_sibling, x_outer), flipped, weights)

    def with_whole_bricks(results):
        packets = pack_bricks(recv_slot, features, cotangent)
        halos = [pass_to(packet, -heading[0], -heading[1]) for packet, heading in zip(packets, DIRECTIONS)]
        mids = mid_taps(fill_bricks, 1, dst, own_f, own_c, halos, flipped, weights)
        return spread_out(*convolve(fill_nothing, 1, dst, mids, (), flipped, weights))

    def as_they_are(results):
        return spread_out(*results)

    own = results[2]
    return tuple(lax.cond(own[0, 27, 0, 0] != 0, with_whole_bricks, as_they_are, results))


def solution(mesh):
    fine = Mesh(mesh.devices.reshape(4, 2, 4, 8), AXES)
    bricks = P(AXES, None, None)
    return jax.shard_map(
        local,
        mesh=fine,
        in_specs=(bricks, P(), bricks, P(None, AXES), P(AXES)),
        out_specs=(bricks, bricks, P()),
        check_vma=False,
    )
```

```python
import functools

import jax
import jax.numpy as jnp
import numpy as np
from jax import lax
from jax.experimental import pallas as pl
from jax.experimental.pallas import tpu as pltpu
from jax.sharding import Mesh, PartitionSpec as P

BRICK = 4
TILE = 4
BZ = 2
HALO = 40
SLOTS = 8
VOXELS = 64
CHANNELS = 128
PLANE = BRICK * BRICK
PLANES = BRICK + 2
WIDE = 9 * CHANNELS
ROWS_M = 28

DIRECTIONS = ((1, 0), (-1, 0), (0, 1), (0, -1), (1, 1), (1, -1), (-1, 1), (-1, -1))
LENGTHS = (TILE * BZ,) * 4 + (BZ,) * 4
STARTS = tuple(int(start) for start in np.cumsum((0,) + LENGTHS[:-1]))
AXES = ("x", "c", "y", "z")
VMEM_LIMIT = 24 * 1024 * 1024


def where_equal(left, right):
    return jnp.where(left == right, 1.0, 0.0).astype(jnp.bfloat16)


def shift_matrix():
    row = lax.broadcasted_iota(jnp.int32, (9 * PLANE, 9 * PLANE), 0)
    column = lax.broadcasted_iota(jnp.int32, (9 * PLANE, 9 * PLANE), 1)
    number = row >> 4
    third = (number * 11) >> 5
    y = ((row >> 2) & 3) + third + 3
    z = (row & 3) + number - 3 * third + 3
    return where_equal(column, ((y >> 2) * 3 + (z >> 2)) * PLANE + (y & 3) * BRICK + (z & 3))


def layer_matrix():
    row = lax.broadcasted_iota(jnp.int32, (4 * PLANE, VOXELS), 0)
    column = lax.broadcasted_iota(jnp.int32, (4 * PLANE, VOXELS), 1)
    quarter = (row >> 2) & 3
    vx = jnp.where(row < 2 * PLANE, quarter, (quarter >> 1) * 3)
    return where_equal(column, vx * PLANE + ((row >> 4) & 1) * 12 + (row & 3))


def expand_matrix(side):
    row = lax.broadcasted_iota(jnp.int32, (VOXELS, PLANE), 0)
    column = lax.broadcasted_iota(jnp.int32, (VOXELS, PLANE), 1)
    return where_equal(row, (column >> 2) * PLANE + side * 12 + (column & 3))


def expand_corner_matrix(order, side):
    row = lax.broadcasted_iota(jnp.int32, (2 * VOXELS, PLANE), 0)
    column = lax.broadcasted_iota(jnp.int32, (2 * VOXELS, PLANE), 1)
    vy = (row >> 2) & 3
    return where_equal(column + vy * PLANE, order * 8 + (row >> 6) * 4 + (row & 3) + side * 3 * PLANE)


def pack_layers_kernel(recv_slot_ref, features_ref, cotangent_ref, to_first, to_second, to_sibling, to_outer,
                       own_f, own_c, sides, slot_ref, sems):
    bricks = (own_f, own_c)
    copies = [
        pltpu.make_async_copy(ref, target, sems.at[number])
        for number, (ref, target) in enumerate((
            (features_ref, own_f.at[pl.ds(0, SLOTS)]),
            (cotangent_ref, own_c.at[pl.ds(0, SLOTS)]),
            (recv_slot_ref, slot_ref),
        ))
    ]
    for copy in copies:
        copy.start()
    for own in bricks:
        own[SLOTS] = jnp.zeros((VOXELS, CHANNELS), jnp.bfloat16)
    sides[:, SLOTS] = jnp.zeros((2, 4 * PLANE, CHANNELS), jnp.bfloat16)
    core = lax.axis_index("c")
    odd = lax.axis_index("z") & 1
    layer = layer_matrix()
    block = lax.broadcasted_iota(jnp.int32, (PLANE, CHANNELS), 0) >> 2
    masks = [where_equal(block, number) for number in range(4)]
    for copy in copies:
        copy.wait()
    for kind in range(2):
        beside = jnp.concatenate([bricks[kind][slot] for slot in range(SLOTS)], axis=1)
        picked = jnp.dot(layer, beside, preferred_element_type=jnp.float32).astype(jnp.bfloat16)
        for slot in range(SLOTS):
            sides[kind, slot] = picked[:, slot * CHANNELS : (slot + 1) * CHANNELS]

    def put(packet, position, halo, source, begin):
        slot = jnp.clip(slot_ref[halo], 0, SLOTS)
        rows = pl.ds(begin, PLANE)
        packet[position, :, :CHANNELS] = source[0][slot, rows]
        packet[position, :, CHANNELS:] = source[1][slot, rows]

    for packet, up in ((to_first, 1 - odd), (to_second, odd)):
        begin = pl.multiple_of(up * PLANE, PLANE)
        for position in range(SLOTS):
            put(packet, position, STARTS[2] + up * LENGTHS[2] + position, (sides.at[0], sides.at[1]), begin)
        rows = pl.ds(pl.multiple_of((up + 2) * PLANE, PLANE), PLANE)
        halos = [STARTS[number] + up * BZ + position for number in (4, 6) for position in range(BZ)]
        slots = [jnp.clip(slot_ref[halo], 0, SLOTS) for halo in halos]
        for kind in range(2):
            tile = sides[kind, slots[0], rows] * masks[0]
            for number in range(1, 4):
                tile = tile + sides[kind, slots[number], rows] * masks[number]
            packet[SLOTS, :, kind * CHANNELS : (kind + 1) * CHANNELS] = tile
    for packet, up in ((to_sibling, 1 - core), (to_outer, core)):
        begin = pl.multiple_of(up * (VOXELS - PLANE), PLANE)
        for position in range(LENGTHS[0]):
            put(packet, position, up * LENGTHS[0] + position, bricks, begin)


def pack_layers(recv_slot, features, cotangent):
    vmem = pl.BlockSpec(memory_space=pltpu.VMEM)
    hbm = pl.BlockSpec(memory_space=pltpu.HBM)
    return pl.pallas_call(
        pack_layers_kernel,
        in_specs=[hbm] * 3,
        out_specs=[vmem] * 6,
        out_shape=[
            jax.ShapeDtypeStruct((length, PLANE, 2 * CHANNELS), jnp.bfloat16) for length in (SLOTS + 1, SLOTS + 1, SLOTS, SLOTS)
        ] + [jax.ShapeDtypeStruct((SLOTS + 1, VOXELS, CHANNELS), jnp.bfloat16)] * 2,
        scratch_shapes=[
            pltpu.VMEM((2, SLOTS + 1, 4 * PLANE, CHANNELS), jnp.bfloat16),
            pltpu.SMEM((HALO,), jnp.int32),
            pltpu.SemaphoreType.DMA((3,)),
        ],
        compiler_params=pltpu.CompilerParams(vmem_limit_bytes=VMEM_LIMIT),
    )(recv_slot, features, cotangent)


def fill_bricks(halos, lanes, bricks):
    begin_at = SLOTS
    for halo in halos:
        bricks[begin_at : begin_at + halo.shape[0]] = halo[:, :, lanes]
        begin_at += halo.shape[0]


def fill_along_y(halos, lanes, bricks):
    odd = lax.axis_index("z") & 1
    for faces, side in ((halos[0], odd), (halos[1], 1 - odd)):
        tiles = jnp.concatenate([faces[position, :, lanes] for position in range(SLOTS)], axis=1)
        whole = jnp.dot(expand_matrix(side), tiles, preferred_element_type=jnp.float32).astype(jnp.bfloat16)
        for position in range(SLOTS):
            target = SLOTS + STARTS[2] + side * LENGTHS[2] + position
            bricks[target] = whole[:, position * CHANNELS : (position + 1) * CHANNELS]


def fill_along_x(halos, lanes, bricks):
    core, odd = lax.axis_index("c"), lax.axis_index("z") & 1
    both = ((halos[0], core), (halos[1], 1 - core))
    for packet, below in both:
        for position in range(SLOTS):
            tile = packet[position, :, lanes]
            target = SLOTS + below * LENGTHS[0] + position
            bricks[target, :PLANE] = tile
            bricks[target, VOXELS - PLANE :] = tile
    tiles = jnp.concatenate([packet[SLOTS, :, lanes] for packet in halos], axis=1)
    for order, side in ((0, odd), (1, 1 - odd)):
        whole = jnp.dot(
            expand_corner_matrix(order, side), tiles, preferred_element_type=jnp.float32
        ).astype(jnp.bfloat16)
        for number, (_, below) in enumerate(both):
            for position in range(BZ):
                target = SLOTS + STARTS[4] + side * BZ + below * 2 * BZ + position
                bricks[target] = whole[
                    position * VOXELS : (position + 1) * VOXELS, number * CHANNELS : (number + 1) * CHANNELS
                ]


def fill_nothing(halos, lanes, bricks):
    pass


def out_of_place(dst):
    k = lax.broadcasted_iota(jnp.int32, dst.shape, 1)
    ninth = jnp.where(k >= 18, 2, jnp.where(k >= 9, 1, 0))
    rest = k - 9 * ninth
    offset = (ninth - 1, jnp.where(rest >= 6, 2, jnp.where(rest >= 3, 1, 0)) - 1)
    wrong = jnp.zeros(dst.shape, jnp.float32)
    for number, heading in enumerate(DIRECTIONS):
        start = SLOTS + STARTS[number]
        here = (dst >= start) & (dst < start + LENGTHS[number])
        for axis in range(2):
            if heading[axis]:
                wrong = jnp.where(here & (offset[axis] != heading[axis]), 1.0, wrong)
    return jnp.max(jnp.max(wrong, axis=1, keepdims=True), axis=0, keepdims=True)


def build_taps(unroll, dst_ref, bricks, planes, taps):
    shift = shift_matrix()

    def around(slot, plane):
        side = 0 if plane == 0 else 2 if plane == PLANES - 1 else 1
        local = (plane - 1) % BRICK * PLANE
        return jnp.concatenate(
            [bricks[dst_ref[slot, side * 9 + number], local : local + PLANE] for number in range(9)], axis=0
        )

    def one_slot(slot, carry):
        for index in range(0, len(planes), 2):
            pair = jnp.concatenate((around(slot, planes[index]), around(slot, planes[index + 1])), axis=1)
            moved = jnp.dot(shift, pair, preferred_element_type=jnp.float32).astype(jnp.bfloat16)
            for number in range(9):
                rows = moved[number * PLANE : (number + 1) * PLANE]
                target = slice(number * CHANNELS, (number + 1) * CHANNELS)
                taps[slot, index, :, target] = rows[:, :CHANNELS]
                taps[slot, index + 1, :, target] = rows[:, CHANNELS:]
        return carry

    lax.fori_loop(0, SLOTS, one_slot, 0, unroll=unroll)


def taps_of(mid, edge, side):
    if side == 0:
        planes = jnp.concatenate((edge[:, :1], mid[:, :3]), axis=1)
    elif side == 1:
        planes = mid[...]
    else:
        planes = jnp.concatenate((mid[:, 1:], edge[:, 1:]), axis=1)
    return planes.reshape(SLOTS * VOXELS, WIDE)


def store_products(flipped_ref, tap, first, send_ref, keep_ref):
    core = lax.axis_index("c")
    half = CHANNELS // 2
    flipped = jnp.concatenate((flipped_ref[1 - core], flipped_ref[core]), axis=0)
    part = jnp.dot(flipped, tap, preferred_element_type=jnp.float32)
    for number in range(9):
        block = part[:, number * CHANNELS : (number + 1) * CHANNELS]
        for quarter in range(4):
            rows = slice(quarter * 16, quarter * 16 + 16)
            send_ref[quarter, first + number] = block[:half][rows].astype(jnp.bfloat16)
            keep_ref[quarter, first + number] = block[half:][rows]


def grad_part(tap, matrices):
    matrix = jnp.concatenate(matrices, axis=1)
    return lax.dot_general(tap, matrix, (((1,), (1,)), ((), ())), preferred_element_type=jnp.float32)


def mid_kernel(fill, unroll, count, dst_ref, features_ref, cotangent_ref, flipped_ref, weights_ref, *rest):
    halos = rest[:count]
    mid_f, mid_c, bricks_f, bricks_c, send_ref, keep_ref, grad_ref, middle, sem = rest[count:]
    copy = pltpu.make_async_copy(weights_ref.at[pl.ds(9, 9)], middle, sem)
    copy.start()
    for kind, (own, bricks, mid) in enumerate(((features_ref, bricks_f, mid_f), (cotangent_ref, bricks_c, mid_c))):
        bricks[:SLOTS] = own[:SLOTS]
        for begin, end in ((SLOTS, SLOTS + STARTS[2]), (SLOTS + STARTS[4], SLOTS + HALO + 1)):
            bricks[begin:end] = jnp.zeros((end - begin, VOXELS, CHANNELS), jnp.bfloat16)
        fill(halos, slice(kind * CHANNELS, (kind + 1) * CHANNELS), bricks)
        build_taps(unroll, dst_ref, bricks, (1, 2, 3, 4), mid)
    tap = mid_c[...].reshape(SLOTS * VOXELS, WIDE)
    store_products(flipped_ref, tap, 0, send_ref, keep_ref)
    copy.wait()
    grad_ref[...] = grad_part(tap, [middle[8 - number] for number in range(9)])


def weight_kernel(fill, unroll, count, dst_ref, table_ref, mid, _, *rest):
    halos = rest[:count]
    flipped_ref, send_mid, keep_mid, send_ref, keep_ref, edge, bricks = rest[count:]
    fill(halos, slice(CHANNELS, 2 * CHANNELS), bricks)
    build_taps(unroll, dst_ref, bricks, (0, PLANES - 1), edge)
    send_ref[:, 9:18] = send_mid[...]
    keep_ref[:, 9:18] = keep_mid[...]
    for side in (0, 2):
        store_products(flipped_ref, taps_of(mid, edge, side), side * 9, send_ref, keep_ref)
    flag = jnp.broadcast_to(out_of_place(table_ref[...]), (16, CHANNELS))
    for quarter in range(4):
        send_ref[quarter, 27] = flag.astype(jnp.bfloat16)
        keep_ref[quarter, 27] = flag


def grad_kernel(mid, edge, weights_ref, grad_mid, grad_ref):
    grad = grad_mid[...]
    for side in (0, 2):
        matrices = [weights_ref[26 - side * 9 - number] for number in range(9)]
        grad = grad + grad_part(taps_of(mid, edge, side), matrices)
    grad_ref[...] = grad.astype(jnp.bfloat16).reshape(SLOTS, VOXELS, CHANNELS)


def edge_kernel(fill, unroll, count, dst_ref, _, *rest):
    edge, bricks = rest[count:]
    fill(rest[:count], slice(0, CHANNELS), bricks)
    build_taps(unroll, dst_ref, bricks, (0, PLANES - 1), edge)


def spread_half(half_ref, whole, out_ref, core, sem):
    for m in range(27):
        for quarter in range(4):
            whole[26 - m, quarter * 16 : quarter * 16 + 16] = half_ref[quarter, m].astype(jnp.float32)
    half = CHANNELS // 2
    copy = pltpu.make_async_copy(whole, out_ref.at[:, pl.ds(pl.multiple_of(core * half, half), half)], sem)
    copy.start()
    return copy


def output_kernel(mid, edge, weights_ref, own_ref, outputs_ref, out_ref, whole, sem):
    copy = spread_half(own_ref, whole, out_ref, lax.axis_index("c"), sem)
    outputs = None
    for side in range(3):
        matrix = weights_ref[side * 9 : side * 9 + 9].reshape(WIDE, CHANNELS)
        part = jnp.dot(taps_of(mid, edge, side), matrix, preferred_element_type=jnp.float32)
        outputs = part if outputs is None else outputs + part
    outputs_ref[...] = outputs.astype(jnp.bfloat16).reshape(SLOTS, VOXELS, CHANNELS)
    copy.wait()


def last_kernel(other_ref, outputs_ref, grad_ref, _, outputs_out, grad_out, out_ref, whole, sem, sems):
    copies = [
        pltpu.make_async_copy(outputs_ref, outputs_out, sems.at[0]),
        pltpu.make_async_copy(grad_ref, grad_out, sems.at[1]),
    ]
    for copy in copies:
        copy.start()
    copies.append(spread_half(other_ref, whole, out_ref, 1 - lax.axis_index("c"), sem))
    for copy in copies:
        copy.wait()


VMEM_SPEC = pl.BlockSpec(memory_space=pltpu.VMEM)
HBM_SPEC = pl.BlockSpec(memory_space=pltpu.HBM)
SMEM_SPEC = pl.BlockSpec(memory_space=pltpu.SMEM)
BRICK_SHAPE = jax.ShapeDtypeStruct((SLOTS, VOXELS, CHANNELS), jnp.bfloat16)
MID_SHAPE = jax.ShapeDtypeStruct((SLOTS, BRICK, PLANE, WIDE), jnp.bfloat16)
EDGE_SHAPE = jax.ShapeDtypeStruct((SLOTS, 2, PLANE, WIDE), jnp.bfloat16)
WHOLE_SHAPE = jax.ShapeDtypeStruct((27, CHANNELS, CHANNELS), jnp.float32)
ALL_BRICKS = jax.ShapeDtypeStruct((SLOTS + HALO + 1, VOXELS, CHANNELS), jnp.bfloat16)
PARAMS = pltpu.CompilerParams(vmem_limit_bytes=VMEM_LIMIT)
COST = pl.CostEstimate(flops=4 * SLOTS * VOXELS * 27 * CHANNELS * CHANNELS, bytes_accessed=4_000_000, transcendentals=0)


def mid_taps(fill, unroll, dst, own_f, own_c, halos, flipped, weights):
    return pl.pallas_call(
        functools.partial(mid_kernel, fill, unroll, len(halos)),
        in_specs=[SMEM_SPEC] + [VMEM_SPEC] * 3 + [HBM_SPEC] + [VMEM_SPEC] * len(halos),
        out_specs=[VMEM_SPEC] * 7,
        out_shape=[
            MID_SHAPE, MID_SHAPE, ALL_BRICKS, ALL_BRICKS,
            jax.ShapeDtypeStruct((4, 9, 16, CHANNELS), jnp.bfloat16),
            jax.ShapeDtypeStruct((4, 9, 16, CHANNELS), jnp.float32),
            jax.ShapeDtypeStruct((SLOTS * VOXELS, CHANNELS), jnp.float32),
        ],
        scratch_shapes=[pltpu.VMEM((9, CHANNELS, CHANNELS), jnp.bfloat16), pltpu.SemaphoreType.DMA(())],
        compiler_params=PARAMS,
        cost_estimate=COST,
    )(dst, own_f, own_c, flipped, weights, *halos)


def weight_sums(fill, unroll, dst, mid, bricks, halos, flipped, send, keep):
    return pl.pallas_call(
        functools.partial(weight_kernel, fill, unroll, len(halos)),
        in_specs=[SMEM_SPEC] + [VMEM_SPEC] * (6 + len(halos)),
        out_specs=[VMEM_SPEC] * 4,
        out_shape=[
            jax.ShapeDtypeStruct((4, ROWS_M, 16, CHANNELS), jnp.bfloat16),
            jax.ShapeDtypeStruct((4, ROWS_M, 16, CHANNELS), jnp.float32),
            EDGE_SHAPE,
            ALL_BRICKS,
        ],
        input_output_aliases={3: 3},
        compiler_params=PARAMS,
        cost_estimate=COST,
    )(dst, dst, mid, bricks, *halos, flipped, send, keep)


def feature_edges(fill, unroll, dst, bricks, halos):
    return pl.pallas_call(
        functools.partial(edge_kernel, fill, unroll, len(halos)),
        in_specs=[SMEM_SPEC] + [VMEM_SPEC] * (1 + len(halos)),
        out_specs=[VMEM_SPEC] * 2,
        out_shape=[EDGE_SHAPE, ALL_BRICKS],
        input_output_aliases={1: 1},
        compiler_params=PARAMS,
        cost_estimate=COST,
    )(dst, bricks, *halos)[0]


def input_gradient(mid, edge, weights, grad_mid):
    return pl.pallas_call(
        grad_kernel,
        in_specs=[VMEM_SPEC] * 4,
        out_specs=VMEM_SPEC,
        out_shape=BRICK_SHAPE,
        compiler_params=PARAMS,
        cost_estimate=COST,
    )(mid, edge, weights, grad_mid)


def outputs_and_half(mid, edge, weights, own):
    return pl.pallas_call(
        output_kernel,
        in_specs=[VMEM_SPEC] * 4,
        out_specs=[VMEM_SPEC, HBM_SPEC],
        out_shape=[BRICK_SHAPE, WHOLE_SHAPE],
        scratch_shapes=[pltpu.VMEM((27, CHANNELS // 2, CHANNELS), jnp.float32), pltpu.SemaphoreType.DMA(())],
        compiler_params=PARAMS,
        cost_estimate=COST,
    )(mid, edge, weights, own)


def write_rest(other, outputs, grad, whole):
    return pl.pallas_call(
        last_kernel,
        in_specs=[VMEM_SPEC] * 3 + [HBM_SPEC],
        out_specs=[HBM_SPEC] * 3,
        out_shape=[BRICK_SHAPE, BRICK_SHAPE, WHOLE_SHAPE],
        scratch_shapes=[
            pltpu.VMEM((27, CHANNELS // 2, CHANNELS), jnp.float32),
            pltpu.SemaphoreType.DMA(()),
            pltpu.SemaphoreType.DMA((2,)),
        ],
        input_output_aliases={3: 2},
        compiler_params=PARAMS,
    )(other, outputs, grad, whole)


def convolve(fill, unroll, dst, mids, halos, flipped, weights):
    mid_f, mid_c, bricks_f, bricks_c, send, keep, grad_mid = mids
    send, keep, edge_c, _ = weight_sums(fill, unroll, dst, mid_c, bricks_c, halos, flipped, send, keep)
    arrived = lax.ppermute(send, "c", [(0, 1), (1, 0)])
    input_grad = input_gradient(mid_c, edge_c, weights, grad_mid)
    edge_f = feature_edges(fill, unroll, dst, bricks_f, halos)
    arrived, input_grad, edge_f = lax.optimization_barrier((arrived, input_grad, edge_f))
    own = sum_everywhere(arrived, keep)
    other = lax.ppermute(own, "c", [(0, 1), (1, 0)])
    outputs, whole = outputs_and_half(mid_f, edge_f, weights, own)
    return write_rest(other, outputs, input_grad, whole), own


def pack_bricks_kernel(slot_ref, features_ref, cotangent_ref, *packets):
    begin_at = 0
    for packet in packets:
        for position in range(packet.shape[0]):
            slot = slot_ref[begin_at + position]
            row = jnp.clip(slot, 0, SLOTS - 1)

            @pl.when(slot < SLOTS)
            def _():
                packet[position, :, :CHANNELS] = features_ref[row]
                packet[position, :, CHANNELS:] = cotangent_ref[row]

            @pl.when(slot >= SLOTS)
            def _():
                packet[position] = jnp.zeros((VOXELS, 2 * CHANNELS), jnp.bfloat16)

        begin_at += packet.shape[0]


def pack_bricks(recv_slot, features, cotangent):
    vmem = pl.BlockSpec(memory_space=pltpu.VMEM)
    return pl.pallas_call(
        pack_bricks_kernel,
        in_specs=[pl.BlockSpec(memory_space=pltpu.SMEM), vmem, vmem],
        out_specs=[vmem] * 8,
        out_shape=[
            jax.ShapeDtypeStruct((length, VOXELS, 2 * CHANNELS), jnp.bfloat16) for length in LENGTHS
        ],
        compiler_params=pltpu.CompilerParams(vmem_limit_bytes=VMEM_LIMIT),
    )(recv_slot, features, cotangent)


def pass_to(value, step_x, step_y):
    pairs = []
    for gx in range(8):
        for gy in range(32):
            if 0 <= gx + step_x < 8 and 0 <= gy + step_y < 32:
                pairs.append((gx * 32 + gy, (gx + step_x) * 32 + gy + step_y))
    return lax.ppermute(value, AXES, pairs)


def sum_everywhere(arrived, keep):
    chip_sum = (keep + arrived.astype(jnp.float32)).astype(jnp.bfloat16)
    parts = chip_sum.reshape(16, 7, 16, CHANNELS)
    parts = lax.all_to_all(parts, ("x", "y"), 0, 0)
    total = jnp.sum(parts.astype(jnp.float32), axis=0)
    largest = jnp.max(jnp.abs(total), axis=(0, 1))
    power = jnp.clip(jnp.ceil(jnp.log2(jnp.maximum(largest, 1e-37))), -100.0, 100.0)
    power = jnp.broadcast_to(power, (8, CHANNELS))
    scaled = (total * jnp.exp2(14.0 - power[0])).reshape(7 * 16, CHANNELS)
    share = jnp.concatenate((scaled, power), axis=0).astype(jnp.float16)
    column = lax.all_to_all(jnp.broadcast_to(share[None], (8,) + share.shape), "z", 0, 0).astype(jnp.float32)
    total = jnp.sum(column[:, : 7 * 16] * jnp.exp2(column[:, 7 * 16 : 7 * 16 + 1] - 14.0), axis=0)
    share = (total * (1.0 / (VOXELS * SLOTS))).astype(jnp.bfloat16).reshape(7, 16, CHANNELS)
    whole = jnp.broadcast_to(share[None], (16,) + share.shape)
    return lax.all_to_all(whole, ("x", "y"), 0, 0).reshape(4, ROWS_M, 16, CHANNELS)


def local(features, weights, cotangent, dst_index, recv_slot):
    core = lax.axis_index("c")
    dst = jnp.clip(dst_index.T, 0, SLOTS + HALO)

    to_first, to_second, to_sibling, to_outer, own_f, own_c = pack_layers(recv_slot, features, cotangent)
    flipped = jnp.transpose(own_f[:SLOTS].reshape(SLOTS * VOXELS, CHANNELS))
    flipped = flipped.reshape(2, CHANNELS // 2, SLOTS * VOXELS)
    y_second = lax.ppermute(to_second, ("y", "z"), [(gy, ((gy + 1) ^ 1) - 1) for gy in range(1, 31)])
    y_first = lax.ppermute(to_first, ("y", "z"), [(gy, gy ^ 1) for gy in range(32)])
    y_second, y_first, dst, flipped = lax.optimization_barrier((y_second, y_first, dst, flipped))

    def relayed(packet, up):
        corners = [lax.dynamic_slice_in_dim(value[SLOTS:], 8 * up, 8, axis=1) for value in (y_first, y_second)]
        return jnp.concatenate((packet, jnp.concatenate(corners, axis=1)), axis=0)

    x_sibling = lax.ppermute(relayed(to_sibling, 1 - core), "c", [(0, 1), (1, 0)])
    x_outer = lax.ppermute(relayed(to_outer, core), ("x", "c"), [(2 * x + 1, 2 * x + 2) for x in range(3)]
                           + [(2 * x + 2, 2 * x + 1) for x in range(3)])
    mids = mid_taps(fill_along_y, SLOTS, dst, own_f, own_c, (y_first, y_second), flipped, weights)
    results, own = convolve(fill_along_x, SLOTS, dst, mids, (x_sibling, x_outer), flipped, weights)

    def with_whole_bricks(results):
        packets = pack_bricks(recv_slot, features, cotangent)
        halos = [pass_to(packet, -heading[0], -heading[1]) for packet, heading in zip(packets, DIRECTIONS)]
        mids = mid_taps(fill_bricks, 1, dst, own_f, own_c, halos, flipped, weights)
        return convolve(fill_nothing, 1, dst, mids, (), flipped, weights)[0]

    return tuple(lax.cond(own[0, 27, 0, 0] != 0, with_whole_bricks, lambda results: results, results))


def solution(mesh):
    fine = Mesh(mesh.devices.reshape(4, 2, 4, 8), AXES)
    bricks = P(AXES, None, None)
    return jax.shard_map(
        local,
        mesh=fine,
        in_specs=(bricks, P(), bricks, P(None, AXES), P(AXES)),
        out_specs=(bricks, bricks, P()),
        check_vma=False,
    )
```

```python
import functools

import jax
import jax.numpy as jnp
import numpy as np
from jax import lax
from jax.experimental import pallas as pl
from jax.experimental.pallas import tpu as pltpu
from jax.sharding import Mesh, PartitionSpec as P

BRICK = 4
TILE = 4
BZ = 2
HALO = 40
SLOTS = 8
VOXELS = 64
CHANNELS = 128
PLANE = BRICK * BRICK
PLANES = BRICK + 2
WIDE = 9 * CHANNELS
ROWS_M = 28

DIRECTIONS = ((1, 0), (-1, 0), (0, 1), (0, -1), (1, 1), (1, -1), (-1, 1), (-1, -1))
LENGTHS = (TILE * BZ,) * 4 + (BZ,) * 4
STARTS = tuple(int(start) for start in np.cumsum((0,) + LENGTHS[:-1]))
AXES = ("x", "c", "y", "z")
VMEM_LIMIT = 24 * 1024 * 1024


def where_equal(left, right):
    return jnp.where(left == right, 1.0, 0.0).astype(jnp.bfloat16)


def shift_matrix():
    row = lax.broadcasted_iota(jnp.int32, (9 * PLANE, 9 * PLANE), 0)
    column = lax.broadcasted_iota(jnp.int32, (9 * PLANE, 9 * PLANE), 1)
    number = row >> 4
    third = (number * 11) >> 5
    y = ((row >> 2) & 3) + third + 3
    z = (row & 3) + number - 3 * third + 3
    return where_equal(column, ((y >> 2) * 3 + (z >> 2)) * PLANE + (y & 3) * BRICK + (z & 3))


def layer_matrix():
    row = lax.broadcasted_iota(jnp.int32, (4 * PLANE, VOXELS), 0)
    column = lax.broadcasted_iota(jnp.int32, (4 * PLANE, VOXELS), 1)
    quarter = (row >> 2) & 3
    vx = jnp.where(row < 2 * PLANE, quarter, (quarter >> 1) * 3)
    return where_equal(column, vx * PLANE + ((row >> 4) & 1) * 12 + (row & 3))


def expand_matrix(side):
    row = lax.broadcasted_iota(jnp.int32, (VOXELS, PLANE), 0)
    column = lax.broadcasted_iota(jnp.int32, (VOXELS, PLANE), 1)
    return where_equal(row, (column >> 2) * PLANE + side * 12 + (column & 3))


def expand_corner_matrix(order, side):
    row = lax.broadcasted_iota(jnp.int32, (2 * VOXELS, PLANE), 0)
    column = lax.broadcasted_iota(jnp.int32, (2 * VOXELS, PLANE), 1)
    vy = (row >> 2) & 3
    return where_equal(column + vy * PLANE, order * 8 + (row >> 6) * 4 + (row & 3) + side * 3 * PLANE)


def pack_layers_kernel(recv_slot_ref, features_ref, cotangent_ref, to_first, to_second, to_sibling, to_outer,
                       own_f, own_c, sides, slot_ref, sems):
    bricks = (own_f, own_c)
    copies = [
        pltpu.make_async_copy(ref, target, sems.at[number])
        for number, (ref, target) in enumerate((
            (features_ref, own_f.at[pl.ds(0, SLOTS)]),
            (cotangent_ref, own_c.at[pl.ds(0, SLOTS)]),
            (recv_slot_ref, slot_ref),
        ))
    ]
    for copy in copies:
        copy.start()
    for own in bricks:
        own[SLOTS] = jnp.zeros((VOXELS, CHANNELS), jnp.bfloat16)
    sides[:, SLOTS] = jnp.zeros((2, 4 * PLANE, CHANNELS), jnp.bfloat16)
    core = lax.axis_index("c")
    odd = lax.axis_index("z") & 1
    layer = layer_matrix()
    block = lax.broadcasted_iota(jnp.int32, (PLANE, CHANNELS), 0) >> 2
    masks = [where_equal(block, number) for number in range(4)]
    for copy in copies:
        copy.wait()
    for kind in range(2):
        beside = jnp.concatenate([bricks[kind][slot] for slot in range(SLOTS)], axis=1)
        picked = jnp.dot(layer, beside, preferred_element_type=jnp.float32).astype(jnp.bfloat16)
        for slot in range(SLOTS):
            sides[kind, slot] = picked[:, slot * CHANNELS : (slot + 1) * CHANNELS]

    def put(packet, position, halo, source, begin):
        slot = jnp.clip(slot_ref[halo], 0, SLOTS)
        rows = pl.ds(begin, PLANE)
        packet[position, :, :CHANNELS] = source[0][slot, rows]
        packet[position, :, CHANNELS:] = source[1][slot, rows]

    for packet, up in ((to_first, 1 - odd), (to_second, odd)):
        begin = pl.multiple_of(up * PLANE, PLANE)
        for position in range(SLOTS):
            put(packet, position, STARTS[2] + up * LENGTHS[2] + position, (sides.at[0], sides.at[1]), begin)
        rows = pl.ds(pl.multiple_of((up + 2) * PLANE, PLANE), PLANE)
        halos = [STARTS[number] + up * BZ + position for number in (4, 6) for position in range(BZ)]
        slots = [jnp.clip(slot_ref[halo], 0, SLOTS) for halo in halos]
        for kind in range(2):
            tile = sides[kind, slots[0], rows] * masks[0]
            for number in range(1, 4):
                tile = tile + sides[kind, slots[number], rows] * masks[number]
            packet[SLOTS, :, kind * CHANNELS : (kind + 1) * CHANNELS] = tile
    for packet, up in ((to_sibling, 1 - core), (to_outer, core)):
        begin = pl.multiple_of(up * (VOXELS - PLANE), PLANE)
        for position in range(LENGTHS[0]):
            put(packet, position, up * LENGTHS[0] + position, bricks, begin)


def pack_layers(recv_slot, features, cotangent):
    vmem = pl.BlockSpec(memory_space=pltpu.VMEM)
    hbm = pl.BlockSpec(memory_space=pltpu.HBM)
    return pl.pallas_call(
        pack_layers_kernel,
        in_specs=[hbm] * 3,
        out_specs=[vmem] * 6,
        out_shape=[
            jax.ShapeDtypeStruct((length, PLANE, 2 * CHANNELS), jnp.bfloat16) for length in (SLOTS + 1, SLOTS + 1, SLOTS, SLOTS)
        ] + [jax.ShapeDtypeStruct((SLOTS + 1, VOXELS, CHANNELS), jnp.bfloat16)] * 2,
        scratch_shapes=[
            pltpu.VMEM((2, SLOTS + 1, 4 * PLANE, CHANNELS), jnp.bfloat16),
            pltpu.SMEM((HALO,), jnp.int32),
            pltpu.SemaphoreType.DMA((3,)),
        ],
        compiler_params=pltpu.CompilerParams(vmem_limit_bytes=VMEM_LIMIT),
    )(recv_slot, features, cotangent)


def fill_bricks(halos, lanes, bricks):
    begin_at = SLOTS
    for halo in halos:
        bricks[begin_at : begin_at + halo.shape[0]] = halo[:, :, lanes]
        begin_at += halo.shape[0]


def fill_along_y(halos, lanes, bricks):
    odd = lax.axis_index("z") & 1
    for faces, side in ((halos[0], odd), (halos[1], 1 - odd)):
        tiles = jnp.concatenate([faces[position, :, lanes] for position in range(SLOTS)], axis=1)
        whole = jnp.dot(expand_matrix(side), tiles, preferred_element_type=jnp.float32).astype(jnp.bfloat16)
        for position in range(SLOTS):
            target = SLOTS + STARTS[2] + side * LENGTHS[2] + position
            bricks[target] = whole[:, position * CHANNELS : (position + 1) * CHANNELS]


def fill_along_x(halos, lanes, bricks):
    core, odd = lax.axis_index("c"), lax.axis_index("z") & 1
    both = ((halos[0], core), (halos[1], 1 - core))
    for packet, below in both:
        for position in range(SLOTS):
            tile = packet[position, :, lanes]
            target = SLOTS + below * LENGTHS[0] + position
            bricks[target, :PLANE] = tile
            bricks[target, VOXELS - PLANE :] = tile
    tiles = jnp.concatenate([packet[SLOTS, :, lanes] for packet in halos], axis=1)
    for order, side in ((0, odd), (1, 1 - odd)):
        whole = jnp.dot(
            expand_corner_matrix(order, side), tiles, preferred_element_type=jnp.float32
        ).astype(jnp.bfloat16)
        for number, (_, below) in enumerate(both):
            for position in range(BZ):
                target = SLOTS + STARTS[4] + side * BZ + below * 2 * BZ + position
                bricks[target] = whole[
                    position * VOXELS : (position + 1) * VOXELS, number * CHANNELS : (number + 1) * CHANNELS
                ]


def fill_nothing(halos, lanes, bricks):
    pass


def out_of_place(dst):
    k = lax.broadcasted_iota(jnp.int32, dst.shape, 1)
    ninth = jnp.where(k >= 18, 2, jnp.where(k >= 9, 1, 0))
    rest = k - 9 * ninth
    offset = (ninth - 1, jnp.where(rest >= 6, 2, jnp.where(rest >= 3, 1, 0)) - 1)
    wrong = jnp.zeros(dst.shape, jnp.float32)
    for number, heading in enumerate(DIRECTIONS):
        start = SLOTS + STARTS[number]
        here = (dst >= start) & (dst < start + LENGTHS[number])
        for axis in range(2):
            if heading[axis]:
                wrong = jnp.where(here & (offset[axis] != heading[axis]), 1.0, wrong)
    return jnp.max(jnp.max(wrong, axis=1, keepdims=True), axis=0, keepdims=True)


def build_taps(unroll, dst_ref, bricks, planes, taps):
    shift = shift_matrix()

    def around(slot, plane):
        side = 0 if plane == 0 else 2 if plane == PLANES - 1 else 1
        local = (plane - 1) % BRICK * PLANE
        return jnp.concatenate(
            [bricks[dst_ref[slot, side * 9 + number], local : local + PLANE] for number in range(9)], axis=0
        )

    def one_slot(slot, carry):
        for index in range(0, len(planes), 2):
            pair = jnp.concatenate((around(slot, planes[index]), around(slot, planes[index + 1])), axis=1)
            moved = jnp.dot(shift, pair, preferred_element_type=jnp.float32).astype(jnp.bfloat16)
            for number in range(9):
                rows = moved[number * PLANE : (number + 1) * PLANE]
                target = slice(number * CHANNELS, (number + 1) * CHANNELS)
                taps[slot, index, :, target] = rows[:, :CHANNELS]
                taps[slot, index + 1, :, target] = rows[:, CHANNELS:]
        return carry

    lax.fori_loop(0, SLOTS, one_slot, 0, unroll=unroll)


def taps_of(mid, edge, side):
    if side == 0:
        planes = jnp.concatenate((edge[:, :1], mid[:, :3]), axis=1)
    elif side == 1:
        planes = mid[...]
    else:
        planes = jnp.concatenate((mid[:, 1:], edge[:, 1:]), axis=1)
    return planes.reshape(SLOTS * VOXELS, WIDE)


def store_products(flipped_ref, tap, first, send_ref, keep_ref):
    core = lax.axis_index("c")
    half = CHANNELS // 2
    flipped = jnp.concatenate((flipped_ref[1 - core], flipped_ref[core]), axis=0)
    part = jnp.dot(flipped, tap, preferred_element_type=jnp.float32)
    for number in range(9):
        block = part[:, number * CHANNELS : (number + 1) * CHANNELS]
        for quarter in range(4):
            rows = slice(quarter * 16, quarter * 16 + 16)
            send_ref[quarter, first + number] = block[:half][rows].astype(jnp.bfloat16)
            keep_ref[quarter, first + number] = block[half:][rows]


def grad_part(tap, weights_ref, side):
    matrix = jnp.concatenate([weights_ref[26 - side * 9 - number] for number in range(9)], axis=1)
    return lax.dot_general(tap, matrix, (((1,), (1,)), ((), ())), preferred_element_type=jnp.float32)


def mid_kernel(fill, unroll, count, dst_ref, features_ref, cotangent_ref, flipped_ref, weights_ref, *rest):
    halos = rest[:count]
    mid_f, mid_c, bricks_f, bricks_c, send_ref, keep_ref, grad_ref = rest[count:]
    for kind, (own, bricks, mid) in enumerate(((features_ref, bricks_f, mid_f), (cotangent_ref, bricks_c, mid_c))):
        bricks[:SLOTS] = own[:SLOTS]
        for begin, end in ((SLOTS, SLOTS + STARTS[2]), (SLOTS + STARTS[4], SLOTS + HALO + 1)):
            bricks[begin:end] = jnp.zeros((end - begin, VOXELS, CHANNELS), jnp.bfloat16)
        fill(halos, slice(kind * CHANNELS, (kind + 1) * CHANNELS), bricks)
        build_taps(unroll, dst_ref, bricks, (1, 2, 3, 4), mid)
    tap = mid_c[...].reshape(SLOTS * VOXELS, WIDE)
    store_products(flipped_ref, tap, 0, send_ref, keep_ref)
    grad_ref[...] = grad_part(tap, weights_ref, 1)


def weight_kernel(fill, unroll, count, dst_ref, table_ref, mid, _, *rest):
    halos = rest[:count]
    flipped_ref, send_mid, keep_mid, send_ref, keep_ref, edge, bricks = rest[count:]
    fill(halos, slice(CHANNELS, 2 * CHANNELS), bricks)
    build_taps(unroll, dst_ref, bricks, (0, PLANES - 1), edge)
    send_ref[:, 9:18] = send_mid[...]
    keep_ref[:, 9:18] = keep_mid[...]
    for side in (0, 2):
        store_products(flipped_ref, taps_of(mid, edge, side), side * 9, send_ref, keep_ref)
    flag = jnp.broadcast_to(out_of_place(table_ref[...]), (16, CHANNELS))
    for quarter in range(4):
        send_ref[quarter, 27] = flag.astype(jnp.bfloat16)
        keep_ref[quarter, 27] = flag


def grad_kernel(mid, edge, weights_ref, grad_mid, grad_ref):
    grad = grad_mid[...]
    for side in (0, 2):
        grad = grad + grad_part(taps_of(mid, edge, side), weights_ref, side)
    grad_ref[...] = grad.astype(jnp.bfloat16).reshape(SLOTS, VOXELS, CHANNELS)


def edge_kernel(fill, unroll, count, dst_ref, _, *rest):
    edge, bricks = rest[count:]
    fill(rest[:count], slice(0, CHANNELS), bricks)
    build_taps(unroll, dst_ref, bricks, (0, PLANES - 1), edge)


def output_kernel(mid, edge, weights_ref, outputs_ref):
    outputs = None
    for side in range(3):
        matrix = weights_ref[side * 9 : side * 9 + 9].reshape(WIDE, CHANNELS)
        part = jnp.dot(taps_of(mid, edge, side), matrix, preferred_element_type=jnp.float32)
        outputs = part if outputs is None else outputs + part
    outputs_ref[...] = outputs.astype(jnp.bfloat16).reshape(SLOTS, VOXELS, CHANNELS)


VMEM_SPEC = pl.BlockSpec(memory_space=pltpu.VMEM)
SMEM_SPEC = pl.BlockSpec(memory_space=pltpu.SMEM)
BRICK_SHAPE = jax.ShapeDtypeStruct((SLOTS, VOXELS, CHANNELS), jnp.bfloat16)
MID_SHAPE = jax.ShapeDtypeStruct((SLOTS, BRICK, PLANE, WIDE), jnp.bfloat16)
EDGE_SHAPE = jax.ShapeDtypeStruct((SLOTS, 2, PLANE, WIDE), jnp.bfloat16)
ALL_BRICKS = jax.ShapeDtypeStruct((SLOTS + HALO + 1, VOXELS, CHANNELS), jnp.bfloat16)
PARAMS = pltpu.CompilerParams(vmem_limit_bytes=VMEM_LIMIT)
COST = pl.CostEstimate(flops=4 * SLOTS * VOXELS * 27 * CHANNELS * CHANNELS, bytes_accessed=4_000_000, transcendentals=0)


def mid_taps(fill, unroll, dst, own_f, own_c, halos, flipped, weights):
    return pl.pallas_call(
        functools.partial(mid_kernel, fill, unroll, len(halos)),
        in_specs=[SMEM_SPEC] + [VMEM_SPEC] * (4 + len(halos)),
        out_specs=[VMEM_SPEC] * 7,
        out_shape=[
            MID_SHAPE, MID_SHAPE, ALL_BRICKS, ALL_BRICKS,
            jax.ShapeDtypeStruct((4, 9, 16, CHANNELS), jnp.bfloat16),
            jax.ShapeDtypeStruct((4, 9, 16, CHANNELS), jnp.float32),
            jax.ShapeDtypeStruct((SLOTS * VOXELS, CHANNELS), jnp.float32),
        ],
        compiler_params=PARAMS,
        cost_estimate=COST,
    )(dst, own_f, own_c, flipped, weights, *halos)


def weight_sums(fill, unroll, dst, mid, bricks, halos, flipped, send, keep):
    return pl.pallas_call(
        functools.partial(weight_kernel, fill, unroll, len(halos)),
        in_specs=[SMEM_SPEC] + [VMEM_SPEC] * (6 + len(halos)),
        out_specs=[VMEM_SPEC] * 4,
        out_shape=[
            jax.ShapeDtypeStruct((4, ROWS_M, 16, CHANNELS), jnp.bfloat16),
            jax.ShapeDtypeStruct((4, ROWS_M, 16, CHANNELS), jnp.float32),
            EDGE_SHAPE,
            ALL_BRICKS,
        ],
        input_output_aliases={3: 3},
        compiler_params=PARAMS,
        cost_estimate=COST,
    )(dst, dst, mid, bricks, *halos, flipped, send, keep)


def feature_edges(fill, unroll, dst, bricks, halos):
    return pl.pallas_call(
        functools.partial(edge_kernel, fill, unroll, len(halos)),
        in_specs=[SMEM_SPEC] + [VMEM_SPEC] * (1 + len(halos)),
        out_specs=[VMEM_SPEC] * 2,
        out_shape=[EDGE_SHAPE, ALL_BRICKS],
        input_output_aliases={1: 1},
        compiler_params=PARAMS,
        cost_estimate=COST,
    )(dst, bricks, *halos)[0]


def product(kernel, *operands):
    return pl.pallas_call(
        kernel,
        in_specs=[VMEM_SPEC] * len(operands),
        out_specs=VMEM_SPEC,
        out_shape=BRICK_SHAPE,
        compiler_params=PARAMS,
        cost_estimate=COST,
    )(*operands)


def convolve(fill, unroll, dst, mids, halos, flipped, weights):
    mid_f, mid_c, bricks_f, bricks_c, send, keep, grad_mid = mids
    send, keep, edge_c, _ = weight_sums(fill, unroll, dst, mid_c, bricks_c, halos, flipped, send, keep)
    arrived = lax.ppermute(send, "c", [(0, 1), (1, 0)])
    input_grad = product(grad_kernel, mid_c, edge_c, weights, grad_mid)
    edge_f = feature_edges(fill, unroll, dst, bricks_f, halos)
    arrived, input_grad, edge_f = lax.optimization_barrier((arrived, input_grad, edge_f))
    own = sum_everywhere(arrived, keep)
    other = lax.ppermute(own, "c", [(0, 1), (1, 0)])
    outputs = product(output_kernel, mid_f, edge_f, weights)
    return outputs, input_grad, own, other


def pack_bricks_kernel(slot_ref, features_ref, cotangent_ref, *packets):
    begin_at = 0
    for packet in packets:
        for position in range(packet.shape[0]):
            slot = slot_ref[begin_at + position]
            row = jnp.clip(slot, 0, SLOTS - 1)

            @pl.when(slot < SLOTS)
            def _():
                packet[position, :, :CHANNELS] = features_ref[row]
                packet[position, :, CHANNELS:] = cotangent_ref[row]

            @pl.when(slot >= SLOTS)
            def _():
                packet[position] = jnp.zeros((VOXELS, 2 * CHANNELS), jnp.bfloat16)

        begin_at += packet.shape[0]


def pack_bricks(recv_slot, features, cotangent):
    vmem = pl.BlockSpec(memory_space=pltpu.VMEM)
    return pl.pallas_call(
        pack_bricks_kernel,
        in_specs=[pl.BlockSpec(memory_space=pltpu.SMEM), vmem, vmem],
        out_specs=[vmem] * 8,
        out_shape=[
            jax.ShapeDtypeStruct((length, VOXELS, 2 * CHANNELS), jnp.bfloat16) for length in LENGTHS
        ],
        compiler_params=pltpu.CompilerParams(vmem_limit_bytes=VMEM_LIMIT),
    )(recv_slot, features, cotangent)


def pass_to(value, step_x, step_y):
    pairs = []
    for gx in range(8):
        for gy in range(32):
            if 0 <= gx + step_x < 8 and 0 <= gy + step_y < 32:
                pairs.append((gx * 32 + gy, (gx + step_x) * 32 + gy + step_y))
    return lax.ppermute(value, AXES, pairs)


def sum_everywhere(arrived, keep):
    chip_sum = (keep + arrived.astype(jnp.float32)).astype(jnp.bfloat16)
    parts = chip_sum.reshape(16, 7, 16, CHANNELS)
    parts = lax.all_to_all(parts, ("x", "y"), 0, 0)
    total = jnp.sum(parts.astype(jnp.float32), axis=0)
    largest = jnp.max(jnp.abs(total), axis=(0, 1))
    power = jnp.clip(jnp.ceil(jnp.log2(jnp.maximum(largest, 1e-37))), -100.0, 100.0)
    power = jnp.broadcast_to(power, (8, CHANNELS))
    scaled = (total * jnp.exp2(14.0 - power[0])).reshape(7 * 16, CHANNELS)
    share = jnp.concatenate((scaled, power), axis=0).astype(jnp.float16)
    column = lax.all_to_all(jnp.broadcast_to(share[None], (8,) + share.shape), "z", 0, 0).astype(jnp.float32)
    total = jnp.sum(column[:, : 7 * 16] * jnp.exp2(column[:, 7 * 16 : 7 * 16 + 1] - 14.0), axis=0)
    share = (total * (1.0 / (VOXELS * SLOTS))).astype(jnp.bfloat16).reshape(7, 16, CHANNELS)
    whole = jnp.broadcast_to(share[None], (16,) + share.shape)
    return lax.all_to_all(whole, ("x", "y"), 0, 0).reshape(4, ROWS_M, 16, CHANNELS)


def spread_kernel(own_ref, other_ref, outputs_ref, grad_ref, outputs_out, grad_out, out_ref, whole, sems):
    half = CHANNELS // 2
    core = lax.axis_index("c")
    copies = [
        pltpu.make_async_copy(outputs_ref, outputs_out, sems.at[9]),
        pltpu.make_async_copy(grad_ref, grad_out, sems.at[10]),
    ]
    for copy in copies:
        copy.start()
    for chunk in range(9):
        for m in range(3 * chunk, 3 * chunk + 3):
            for quarter in range(4):
                for ref, side in ((own_ref, core), (other_ref, 1 - core)):
                    begin = pl.multiple_of(side * half + quarter * 16, 16)
                    whole[26 - m, pl.ds(begin, 16)] = ref[quarter, m].astype(jnp.float32)
        rows = pl.ds(24 - 3 * chunk, 3)
        copies.append(pltpu.make_async_copy(whole.at[rows], out_ref.at[rows], sems.at[chunk]))
        copies[-1].start()
    for copy in copies:
        copy.wait()


def spread_out(outputs, input_grad, own, other):
    return pl.pallas_call(
        spread_kernel,
        in_specs=[VMEM_SPEC] * 4,
        out_specs=[pl.BlockSpec(memory_space=pltpu.HBM)] * 3,
        out_shape=[BRICK_SHAPE, BRICK_SHAPE, jax.ShapeDtypeStruct((27, CHANNELS, CHANNELS), jnp.float32)],
        scratch_shapes=[
            pltpu.VMEM((27, CHANNELS, CHANNELS), jnp.float32),
            pltpu.SemaphoreType.DMA((11,)),
        ],
        compiler_params=PARAMS,
    )(own, other, outputs, input_grad)


def local(features, weights, cotangent, dst_index, recv_slot):
    core = lax.axis_index("c")
    dst = jnp.clip(dst_index.T, 0, SLOTS + HALO)

    to_first, to_second, to_sibling, to_outer, own_f, own_c = pack_layers(recv_slot, features, cotangent)
    flipped = jnp.transpose(own_f[:SLOTS].reshape(SLOTS * VOXELS, CHANNELS))
    flipped = flipped.reshape(2, CHANNELS // 2, SLOTS * VOXELS)
    y_second = lax.ppermute(to_second, ("y", "z"), [(gy, ((gy + 1) ^ 1) - 1) for gy in range(1, 31)])
    y_first = lax.ppermute(to_first, ("y", "z"), [(gy, gy ^ 1) for gy in range(32)])
    y_second, y_first, dst, flipped = lax.optimization_barrier((y_second, y_first, dst, flipped))

    def relayed(packet, up):
        corners = [lax.dynamic_slice_in_dim(value[SLOTS:], 8 * up, 8, axis=1) for value in (y_first, y_second)]
        return jnp.concatenate((packet, jnp.concatenate(corners, axis=1)), axis=0)

    x_sibling = lax.ppermute(relayed(to_sibling, 1 - core), "c", [(0, 1), (1, 0)])
    x_outer = lax.ppermute(relayed(to_outer, core), ("x", "c"), [(2 * x + 1, 2 * x + 2) for x in range(3)]
                           + [(2 * x + 2, 2 * x + 1) for x in range(3)])
    mids = mid_taps(fill_along_y, SLOTS, dst, own_f, own_c, (y_first, y_second), flipped, weights)
    results = convolve(fill_along_x, SLOTS, dst, mids, (x_sibling, x_outer), flipped, weights)

    def with_whole_bricks(results):
        packets = pack_bricks(recv_slot, features, cotangent)
        halos = [pass_to(packet, -heading[0], -heading[1]) for packet, heading in zip(packets, DIRECTIONS)]
        mids = mid_taps(fill_bricks, 1, dst, own_f, own_c, halos, flipped, weights)
        return spread_out(*convolve(fill_nothing, 1, dst, mids, (), flipped, weights))

    def as_they_are(results):
        return spread_out(*results)

    own = results[2]
    return tuple(lax.cond(own[0, 27, 0, 0] != 0, with_whole_bricks, as_they_are, results))


def solution(mesh):
    fine = Mesh(mesh.devices.reshape(4, 2, 4, 8), AXES)
    bricks = P(AXES, None, None)
    return jax.shard_map(
        local,
        mesh=fine,
        in_specs=(bricks, P(), bricks, P(None, AXES), P(AXES)),
        out_specs=(bricks, bricks, P()),
        check_vma=False,
    )
```

```python
import functools

import jax
import jax.numpy as jnp
import numpy as np
from jax import lax
from jax.experimental import pallas as pl
from jax.experimental.pallas import tpu as pltpu
from jax.sharding import Mesh, PartitionSpec as P

BRICK = 4
TILE = 4
BZ = 2
HALO = 40
SLOTS = 8
VOXELS = 64
CHANNELS = 128
PLANE = BRICK * BRICK
PLANES = BRICK + 2
WIDE = 9 * CHANNELS
ROWS_M = 28

DIRECTIONS = ((1, 0), (-1, 0), (0, 1), (0, -1), (1, 1), (1, -1), (-1, 1), (-1, -1))
LENGTHS = (TILE * BZ,) * 4 + (BZ,) * 4
STARTS = tuple(int(start) for start in np.cumsum((0,) + LENGTHS[:-1]))
AXES = ("x", "c", "y", "z")
VMEM_LIMIT = 24 * 1024 * 1024


def where_equal(left, right):
    return jnp.where(left == right, 1.0, 0.0).astype(jnp.bfloat16)


def shift_matrix():
    row = lax.broadcasted_iota(jnp.int32, (9 * PLANE, 9 * PLANE), 0)
    column = lax.broadcasted_iota(jnp.int32, (9 * PLANE, 9 * PLANE), 1)
    number = row >> 4
    third = (number * 11) >> 5
    y = ((row >> 2) & 3) + third + 3
    z = (row & 3) + number - 3 * third + 3
    return where_equal(column, ((y >> 2) * 3 + (z >> 2)) * PLANE + (y & 3) * BRICK + (z & 3))


def layer_matrix():
    row = lax.broadcasted_iota(jnp.int32, (4 * PLANE, VOXELS), 0)
    column = lax.broadcasted_iota(jnp.int32, (4 * PLANE, VOXELS), 1)
    quarter = (row >> 2) & 3
    vx = jnp.where(row < 2 * PLANE, quarter, (quarter >> 1) * 3)
    return where_equal(column, vx * PLANE + ((row >> 4) & 1) * 12 + (row & 3))


def expand_matrix(side):
    row = lax.broadcasted_iota(jnp.int32, (VOXELS, PLANE), 0)
    column = lax.broadcasted_iota(jnp.int32, (VOXELS, PLANE), 1)
    return where_equal(row, (column >> 2) * PLANE + side * 12 + (column & 3))


def expand_corner_matrix(order, side):
    row = lax.broadcasted_iota(jnp.int32, (2 * VOXELS, PLANE), 0)
    column = lax.broadcasted_iota(jnp.int32, (2 * VOXELS, PLANE), 1)
    vy = (row >> 2) & 3
    return where_equal(column + vy * PLANE, order * 8 + (row >> 6) * 4 + (row & 3) + side * 3 * PLANE)


def pack_layers_kernel(recv_slot_ref, features_ref, cotangent_ref, to_first, to_second, to_sibling, to_outer,
                       own_f, own_c, sides, slot_ref, sems):
    bricks = (own_f, own_c)
    copies = [
        pltpu.make_async_copy(ref, target, sems.at[number])
        for number, (ref, target) in enumerate((
            (features_ref, own_f.at[pl.ds(0, SLOTS)]),
            (cotangent_ref, own_c.at[pl.ds(0, SLOTS)]),
            (recv_slot_ref, slot_ref),
        ))
    ]
    for copy in copies:
        copy.start()
    for own in bricks:
        own[SLOTS] = jnp.zeros((VOXELS, CHANNELS), jnp.bfloat16)
    sides[:, SLOTS] = jnp.zeros((2, 4 * PLANE, CHANNELS), jnp.bfloat16)
    core = lax.axis_index("c")
    odd = lax.axis_index("z") & 1
    layer = layer_matrix()
    block = lax.broadcasted_iota(jnp.int32, (PLANE, CHANNELS), 0) >> 2
    masks = [where_equal(block, number) for number in range(4)]
    for copy in copies:
        copy.wait()
    for kind in range(2):
        beside = jnp.concatenate([bricks[kind][slot] for slot in range(SLOTS)], axis=1)
        picked = jnp.dot(layer, beside, preferred_element_type=jnp.float32).astype(jnp.bfloat16)
        for slot in range(SLOTS):
            sides[kind, slot] = picked[:, slot * CHANNELS : (slot + 1) * CHANNELS]

    def put(packet, position, halo, source, begin):
        slot = jnp.clip(slot_ref[halo], 0, SLOTS)
        rows = pl.ds(begin, PLANE)
        packet[position, :, :CHANNELS] = source[0][slot, rows]
        packet[position, :, CHANNELS:] = source[1][slot, rows]

    for packet, up in ((to_first, 1 - odd), (to_second, odd)):
        begin = pl.multiple_of(up * PLANE, PLANE)
        for position in range(SLOTS):
            put(packet, position, STARTS[2] + up * LENGTHS[2] + position, (sides.at[0], sides.at[1]), begin)
        rows = pl.ds(pl.multiple_of((up + 2) * PLANE, PLANE), PLANE)
        halos = [STARTS[number] + up * BZ + position for number in (4, 6) for position in range(BZ)]
        slots = [jnp.clip(slot_ref[halo], 0, SLOTS) for halo in halos]
        for kind in range(2):
            tile = sides[kind, slots[0], rows] * masks[0]
            for number in range(1, 4):
                tile = tile + sides[kind, slots[number], rows] * masks[number]
            packet[SLOTS, :, kind * CHANNELS : (kind + 1) * CHANNELS] = tile
    for packet, up in ((to_sibling, 1 - core), (to_outer, core)):
        begin = pl.multiple_of(up * (VOXELS - PLANE), PLANE)
        for position in range(LENGTHS[0]):
            put(packet, position, up * LENGTHS[0] + position, bricks, begin)


def pack_layers(recv_slot, features, cotangent):
    vmem = pl.BlockSpec(memory_space=pltpu.VMEM)
    hbm = pl.BlockSpec(memory_space=pltpu.HBM)
    return pl.pallas_call(
        pack_layers_kernel,
        in_specs=[hbm] * 3,
        out_specs=[vmem] * 6,
        out_shape=[
            jax.ShapeDtypeStruct((length, PLANE, 2 * CHANNELS), jnp.bfloat16) for length in (SLOTS + 1, SLOTS + 1, SLOTS, SLOTS)
        ] + [jax.ShapeDtypeStruct((SLOTS + 1, VOXELS, CHANNELS), jnp.bfloat16)] * 2,
        scratch_shapes=[
            pltpu.VMEM((2, SLOTS + 1, 4 * PLANE, CHANNELS), jnp.bfloat16),
            pltpu.SMEM((HALO,), jnp.int32),
            pltpu.SemaphoreType.DMA((3,)),
        ],
        compiler_params=pltpu.CompilerParams(vmem_limit_bytes=VMEM_LIMIT),
    )(recv_slot, features, cotangent)


def fill_bricks(halos, lanes, bricks):
    begin_at = SLOTS
    for halo in halos:
        bricks[begin_at : begin_at + halo.shape[0]] = halo[:, :, lanes]
        begin_at += halo.shape[0]


def fill_along_y(halos, lanes, bricks):
    odd = lax.axis_index("z") & 1
    for faces, side in ((halos[0], odd), (halos[1], 1 - odd)):
        tiles = jnp.concatenate([faces[position, :, lanes] for position in range(SLOTS)], axis=1)
        whole = jnp.dot(expand_matrix(side), tiles, preferred_element_type=jnp.float32).astype(jnp.bfloat16)
        for position in range(SLOTS):
            target = SLOTS + STARTS[2] + side * LENGTHS[2] + position
            bricks[target] = whole[:, position * CHANNELS : (position + 1) * CHANNELS]


def fill_along_x(halos, lanes, bricks):
    core, odd = lax.axis_index("c"), lax.axis_index("z") & 1
    both = ((halos[0], core), (halos[1], 1 - core))
    for packet, below in both:
        for position in range(SLOTS):
            tile = packet[position, :, lanes]
            target = SLOTS + below * LENGTHS[0] + position
            bricks[target, :PLANE] = tile
            bricks[target, VOXELS - PLANE :] = tile
    tiles = jnp.concatenate([packet[SLOTS, :, lanes] for packet in halos], axis=1)
    for order, side in ((0, odd), (1, 1 - odd)):
        whole = jnp.dot(
            expand_corner_matrix(order, side), tiles, preferred_element_type=jnp.float32
        ).astype(jnp.bfloat16)
        for number, (_, below) in enumerate(both):
            for position in range(BZ):
                target = SLOTS + STARTS[4] + side * BZ + below * 2 * BZ + position
                bricks[target] = whole[
                    position * VOXELS : (position + 1) * VOXELS, number * CHANNELS : (number + 1) * CHANNELS
                ]


def fill_nothing(halos, lanes, bricks):
    pass


def out_of_place(dst):
    k = lax.broadcasted_iota(jnp.int32, dst.shape, 1)
    ninth = jnp.where(k >= 18, 2, jnp.where(k >= 9, 1, 0))
    rest = k - 9 * ninth
    offset = (ninth - 1, jnp.where(rest >= 6, 2, jnp.where(rest >= 3, 1, 0)) - 1)
    wrong = jnp.zeros(dst.shape, jnp.float32)
    for number, heading in enumerate(DIRECTIONS):
        start = SLOTS + STARTS[number]
        here = (dst >= start) & (dst < start + LENGTHS[number])
        for axis in range(2):
            if heading[axis]:
                wrong = jnp.where(here & (offset[axis] != heading[axis]), 1.0, wrong)
    return jnp.max(jnp.max(wrong, axis=1, keepdims=True), axis=0, keepdims=True)


def build_taps(unroll, dst_ref, bricks, planes, taps):
    shift = shift_matrix()

    def around(slot, plane):
        side = 0 if plane == 0 else 2 if plane == PLANES - 1 else 1
        local = (plane - 1) % BRICK * PLANE
        return jnp.concatenate(
            [bricks[dst_ref[slot, side * 9 + number], local : local + PLANE] for number in range(9)], axis=0
        )

    def one_slot(slot, carry):
        for index in range(0, len(planes), 2):
            pair = jnp.concatenate((around(slot, planes[index]), around(slot, planes[index + 1])), axis=1)
            moved = jnp.dot(shift, pair, preferred_element_type=jnp.float32).astype(jnp.bfloat16)
            for number in range(9):
                rows = moved[number * PLANE : (number + 1) * PLANE]
                target = slice(number * CHANNELS, (number + 1) * CHANNELS)
                taps[slot, index, :, target] = rows[:, :CHANNELS]
                taps[slot, index + 1, :, target] = rows[:, CHANNELS:]
        return carry

    lax.fori_loop(0, SLOTS, one_slot, 0, unroll=unroll)


def taps_of(mid, edge, side):
    if side == 0:
        planes = jnp.concatenate((edge[:, :1], mid[:, :3]), axis=1)
    elif side == 1:
        planes = mid[...]
    else:
        planes = jnp.concatenate((mid[:, 1:], edge[:, 1:]), axis=1)
    return planes.reshape(SLOTS * VOXELS, WIDE)


def own_half():
    return lax.axis_index("c") ^ (lax.axis_index("x") >> 1) ^ (lax.axis_index("z") >> 2)


def exchange_groups(fixed, spread):
    sizes = {"x": 4, "y": 4, "z": 8}
    groups = []
    for half in range(2):
        for kept in np.ndindex(*[sizes[axis] for axis in fixed]):
            group = []
            for free in np.ndindex(*[sizes[axis] for axis in spread]):
                at = dict(zip(fixed + spread, kept + free))
                core = half ^ (at["x"] >> 1) ^ (at["z"] >> 2)
                group.append(((at["x"] * 2 + core) * 4 + at["y"]) * 8 + at["z"])
            groups.append([int(device) for device in group])
    return groups


def store_products(flipped_ref, tap, first, send_ref, keep_ref):
    mine = own_half()
    half = CHANNELS // 2
    flipped = jnp.concatenate((flipped_ref[1 - mine], flipped_ref[mine]), axis=0)
    part = jnp.dot(flipped, tap, preferred_element_type=jnp.float32)
    for number in range(9):
        block = part[:, number * CHANNELS : (number + 1) * CHANNELS]
        for quarter in range(4):
            rows = slice(quarter * 16, quarter * 16 + 16)
            send_ref[quarter, first + number] = block[:half][rows].astype(jnp.bfloat16)
            keep_ref[quarter, first + number] = block[half:][rows]


def grad_part(tap, weights_ref, side):
    matrix = jnp.concatenate([weights_ref[26 - side * 9 - number] for number in range(9)], axis=1)
    return lax.dot_general(tap, matrix, (((1,), (1,)), ((), ())), preferred_element_type=jnp.float32)


def mid_kernel(fill, unroll, count, dst_ref, features_ref, cotangent_ref, flipped_ref, weights_ref, *rest):
    halos = rest[:count]
    mid_f, mid_c, bricks_f, bricks_c, send_ref, keep_ref, grad_ref = rest[count:]
    for kind, (own, bricks, mid) in enumerate(((features_ref, bricks_f, mid_f), (cotangent_ref, bricks_c, mid_c))):
        bricks[:SLOTS] = own[:SLOTS]
        for begin, end in ((SLOTS, SLOTS + STARTS[2]), (SLOTS + STARTS[4], SLOTS + HALO + 1)):
            bricks[begin:end] = jnp.zeros((end - begin, VOXELS, CHANNELS), jnp.bfloat16)
        fill(halos, slice(kind * CHANNELS, (kind + 1) * CHANNELS), bricks)
        build_taps(unroll, dst_ref, bricks, (1, 2, 3, 4), mid)
    tap = mid_c[...].reshape(SLOTS * VOXELS, WIDE)
    store_products(flipped_ref, tap, 0, send_ref, keep_ref)
    grad_ref[...] = grad_part(tap, weights_ref, 1)


def weight_kernel(fill, unroll, count, dst_ref, table_ref, mid, _, *rest):
    halos = rest[:count]
    flipped_ref, send_mid, keep_mid, send_ref, keep_ref, edge, bricks = rest[count:]
    fill(halos, slice(CHANNELS, 2 * CHANNELS), bricks)
    build_taps(unroll, dst_ref, bricks, (0, PLANES - 1), edge)
    send_ref[:, 9:18] = send_mid[...]
    keep_ref[:, 9:18] = keep_mid[...]
    for side in (0, 2):
        store_products(flipped_ref, taps_of(mid, edge, side), side * 9, send_ref, keep_ref)
    flag = jnp.broadcast_to(out_of_place(table_ref[...]), (16, CHANNELS))
    for quarter in range(4):
        send_ref[quarter, 27] = flag.astype(jnp.bfloat16)
        keep_ref[quarter, 27] = flag


def grad_kernel(mid, edge, weights_ref, grad_mid, grad_ref):
    grad = grad_mid[...]
    for side in (0, 2):
        grad = grad + grad_part(taps_of(mid, edge, side), weights_ref, side)
    grad_ref[...] = grad.astype(jnp.bfloat16).reshape(SLOTS, VOXELS, CHANNELS)


def edge_kernel(fill, unroll, count, dst_ref, _, *rest):
    edge, bricks = rest[count:]
    fill(rest[:count], slice(0, CHANNELS), bricks)
    build_taps(unroll, dst_ref, bricks, (0, PLANES - 1), edge)


def output_kernel(mid, edge, weights_ref, outputs_ref):
    outputs = None
    for side in range(3):
        matrix = weights_ref[side * 9 : side * 9 + 9].reshape(WIDE, CHANNELS)
        part = jnp.dot(taps_of(mid, edge, side), matrix, preferred_element_type=jnp.float32)
        outputs = part if outputs is None else outputs + part
    outputs_ref[...] = outputs.astype(jnp.bfloat16).reshape(SLOTS, VOXELS, CHANNELS)


VMEM_SPEC = pl.BlockSpec(memory_space=pltpu.VMEM)
SMEM_SPEC = pl.BlockSpec(memory_space=pltpu.SMEM)
BRICK_SHAPE = jax.ShapeDtypeStruct((SLOTS, VOXELS, CHANNELS), jnp.bfloat16)
MID_SHAPE = jax.ShapeDtypeStruct((SLOTS, BRICK, PLANE, WIDE), jnp.bfloat16)
EDGE_SHAPE = jax.ShapeDtypeStruct((SLOTS, 2, PLANE, WIDE), jnp.bfloat16)
ALL_BRICKS = jax.ShapeDtypeStruct((SLOTS + HALO + 1, VOXELS, CHANNELS), jnp.bfloat16)
PARAMS = pltpu.CompilerParams(vmem_limit_bytes=VMEM_LIMIT)
COST = pl.CostEstimate(flops=4 * SLOTS * VOXELS * 27 * CHANNELS * CHANNELS, bytes_accessed=4_000_000, transcendentals=0)


def mid_taps(fill, unroll, dst, own_f, own_c, halos, flipped, weights):
    return pl.pallas_call(
        functools.partial(mid_kernel, fill, unroll, len(halos)),
        in_specs=[SMEM_SPEC] + [VMEM_SPEC] * (4 + len(halos)),
        out_specs=[VMEM_SPEC] * 7,
        out_shape=[
            MID_SHAPE, MID_SHAPE, ALL_BRICKS, ALL_BRICKS,
            jax.ShapeDtypeStruct((4, 9, 16, CHANNELS), jnp.bfloat16),
            jax.ShapeDtypeStruct((4, 9, 16, CHANNELS), jnp.float32),
            jax.ShapeDtypeStruct((SLOTS * VOXELS, CHANNELS), jnp.float32),
        ],
        compiler_params=PARAMS,
        cost_estimate=COST,
    )(dst, own_f, own_c, flipped, weights, *halos)


def weight_sums(fill, unroll, dst, mid, bricks, halos, flipped, send, keep):
    return pl.pallas_call(
        functools.partial(weight_kernel, fill, unroll, len(halos)),
        in_specs=[SMEM_SPEC] + [VMEM_SPEC] * (6 + len(halos)),
        out_specs=[VMEM_SPEC] * 4,
        out_shape=[
            jax.ShapeDtypeStruct((4, ROWS_M, 16, CHANNELS), jnp.bfloat16),
            jax.ShapeDtypeStruct((4, ROWS_M, 16, CHANNELS), jnp.float32),
            EDGE_SHAPE,
            ALL_BRICKS,
        ],
        input_output_aliases={3: 3},
        compiler_params=PARAMS,
        cost_estimate=COST,
    )(dst, dst, mid, bricks, *halos, flipped, send, keep)


def feature_edges(fill, unroll, dst, bricks, halos):
    return pl.pallas_call(
        functools.partial(edge_kernel, fill, unroll, len(halos)),
        in_specs=[SMEM_SPEC] + [VMEM_SPEC] * (1 + len(halos)),
        out_specs=[VMEM_SPEC] * 2,
        out_shape=[EDGE_SHAPE, ALL_BRICKS],
        input_output_aliases={1: 1},
        compiler_params=PARAMS,
        cost_estimate=COST,
    )(dst, bricks, *halos)[0]


def product(kernel, *operands):
    return pl.pallas_call(
        kernel,
        in_specs=[VMEM_SPEC] * len(operands),
        out_specs=VMEM_SPEC,
        out_shape=BRICK_SHAPE,
        compiler_params=PARAMS,
        cost_estimate=COST,
    )(*operands)


def convolve(fill, unroll, dst, mids, halos, flipped, weights):
    mid_f, mid_c, bricks_f, bricks_c, send, keep, grad_mid = mids
    send, keep, edge_c, _ = weight_sums(fill, unroll, dst, mid_c, bricks_c, halos, flipped, send, keep)
    arrived = lax.ppermute(send, "c", [(0, 1), (1, 0)])
    input_grad = product(grad_kernel, mid_c, edge_c, weights, grad_mid)
    edge_f = feature_edges(fill, unroll, dst, bricks_f, halos)
    arrived, input_grad, edge_f = lax.optimization_barrier((arrived, input_grad, edge_f))
    own = sum_everywhere(arrived, keep)
    other = lax.ppermute(own, "c", [(0, 1), (1, 0)])
    outputs = product(output_kernel, mid_f, edge_f, weights)
    return outputs, input_grad, own, other


def pack_bricks_kernel(slot_ref, features_ref, cotangent_ref, *packets):
    begin_at = 0
    for packet in packets:
        for position in range(packet.shape[0]):
            slot = slot_ref[begin_at + position]
            row = jnp.clip(slot, 0, SLOTS - 1)

            @pl.when(slot < SLOTS)
            def _():
                packet[position, :, :CHANNELS] = features_ref[row]
                packet[position, :, CHANNELS:] = cotangent_ref[row]

            @pl.when(slot >= SLOTS)
            def _():
                packet[position] = jnp.zeros((VOXELS, 2 * CHANNELS), jnp.bfloat16)

        begin_at += packet.shape[0]


def pack_bricks(recv_slot, features, cotangent):
    vmem = pl.BlockSpec(memory_space=pltpu.VMEM)
    return pl.pallas_call(
        pack_bricks_kernel,
        in_specs=[pl.BlockSpec(memory_space=pltpu.SMEM), vmem, vmem],
        out_specs=[vmem] * 8,
        out_shape=[
            jax.ShapeDtypeStruct((length, VOXELS, 2 * CHANNELS), jnp.bfloat16) for length in LENGTHS
        ],
        compiler_params=pltpu.CompilerParams(vmem_limit_bytes=VMEM_LIMIT),
    )(recv_slot, features, cotangent)


def pass_to(value, step_x, step_y):
    pairs = []
    for gx in range(8):
        for gy in range(32):
            if 0 <= gx + step_x < 8 and 0 <= gy + step_y < 32:
                pairs.append((gx * 32 + gy, (gx + step_x) * 32 + gy + step_y))
    return lax.ppermute(value, AXES, pairs)


def sum_everywhere(arrived, keep):
    chip_sum = (keep + arrived.astype(jnp.float32)).astype(jnp.bfloat16)
    parts = chip_sum.reshape(16, 7, 16, CHANNELS)
    parts = lax.all_to_all(parts, AXES, 0, 0, axis_index_groups=exchange_groups(("z",), ("x", "y")))
    total = jnp.sum(parts.astype(jnp.float32), axis=0)
    largest = jnp.max(jnp.abs(total), axis=(0, 1))
    power = jnp.clip(jnp.ceil(jnp.log2(jnp.maximum(largest, 1e-37))), -100.0, 100.0)
    power = jnp.broadcast_to(power, (8, CHANNELS))
    scaled = (total * jnp.exp2(14.0 - power[0])).reshape(7 * 16, CHANNELS)
    share = jnp.concatenate((scaled, power), axis=0).astype(jnp.float16)
    column = lax.all_to_all(jnp.broadcast_to(share[None], (8,) + share.shape), AXES, 0, 0,
                            axis_index_groups=exchange_groups(("x", "y"), ("z",))).astype(jnp.float32)
    total = jnp.sum(column[:, : 7 * 16] * jnp.exp2(column[:, 7 * 16 : 7 * 16 + 1] - 14.0), axis=0)
    share = (total * (1.0 / (VOXELS * SLOTS))).astype(jnp.bfloat16).reshape(7, 16, CHANNELS)
    whole = jnp.broadcast_to(share[None], (16,) + share.shape)
    return lax.all_to_all(whole, AXES, 0, 0, axis_index_groups=exchange_groups(("z",), ("x", "y"))).reshape(4, ROWS_M, 16, CHANNELS)


def spread_kernel(own_ref, other_ref, outputs_ref, grad_ref, outputs_out, grad_out, out_ref, whole, sems):
    half = CHANNELS // 2
    core = own_half()
    copies = [
        pltpu.make_async_copy(outputs_ref, outputs_out, sems.at[9]),
        pltpu.make_async_copy(grad_ref, grad_out, sems.at[10]),
    ]
    for copy in copies:
        copy.start()
    for chunk in range(9):
        for m in range(3 * chunk, 3 * chunk + 3):
            for quarter in range(4):
                for ref, side in ((own_ref, core), (other_ref, 1 - core)):
                    begin = pl.multiple_of(side * half + quarter * 16, 16)
                    whole[26 - m, pl.ds(begin, 16)] = ref[quarter, m].astype(jnp.float32)
        rows = pl.ds(24 - 3 * chunk, 3)
        copies.append(pltpu.make_async_copy(whole.at[rows], out_ref.at[rows], sems.at[chunk]))
        copies[-1].start()
    for copy in copies:
        copy.wait()


def spread_out(outputs, input_grad, own, other):
    return pl.pallas_call(
        spread_kernel,
        in_specs=[VMEM_SPEC] * 4,
        out_specs=[pl.BlockSpec(memory_space=pltpu.HBM)] * 3,
        out_shape=[BRICK_SHAPE, BRICK_SHAPE, jax.ShapeDtypeStruct((27, CHANNELS, CHANNELS), jnp.float32)],
        scratch_shapes=[
            pltpu.VMEM((27, CHANNELS, CHANNELS), jnp.float32),
            pltpu.SemaphoreType.DMA((11,)),
        ],
        compiler_params=PARAMS,
    )(own, other, outputs, input_grad)


def local(features, weights, cotangent, dst_index, recv_slot):
    core = lax.axis_index("c")
    dst = jnp.clip(dst_index.T, 0, SLOTS + HALO)

    to_first, to_second, to_sibling, to_outer, own_f, own_c = pack_layers(recv_slot, features, cotangent)
    flipped = jnp.transpose(own_f[:SLOTS].reshape(SLOTS * VOXELS, CHANNELS))
    flipped = flipped.reshape(2, CHANNELS // 2, SLOTS * VOXELS)
    y_second = lax.ppermute(to_second, ("y", "z"), [(gy, ((gy + 1) ^ 1) - 1) for gy in range(1, 31)])
    y_first = lax.ppermute(to_first, ("y", "z"), [(gy, gy ^ 1) for gy in range(32)])
    y_second, y_first, dst, flipped = lax.optimization_barrier((y_second, y_first, dst, flipped))

    def relayed(packet, up):
        corners = [lax.dynamic_slice_in_dim(value[SLOTS:], 8 * up, 8, axis=1) for value in (y_first, y_second)]
        return jnp.concatenate((packet, jnp.concatenate(corners, axis=1)), axis=0)

    x_sibling = lax.ppermute(relayed(to_sibling, 1 - core), "c", [(0, 1), (1, 0)])
    x_outer = lax.ppermute(relayed(to_outer, core), ("x", "c"), [(2 * x + 1, 2 * x + 2) for x in range(3)]
                           + [(2 * x + 2, 2 * x + 1) for x in range(3)])
    mids = mid_taps(fill_along_y, SLOTS, dst, own_f, own_c, (y_first, y_second), flipped, weights)
    results = convolve(fill_along_x, SLOTS, dst, mids, (x_sibling, x_outer), flipped, weights)

    def with_whole_bricks(results):
        packets = pack_bricks(recv_slot, features, cotangent)
        halos = [pass_to(packet, -heading[0], -heading[1]) for packet, heading in zip(packets, DIRECTIONS)]
        mids = mid_taps(fill_bricks, 1, dst, own_f, own_c, halos, flipped, weights)
        return spread_out(*convolve(fill_nothing, 1, dst, mids, (), flipped, weights))

    def as_they_are(results):
        return spread_out(*results)

    own = results[2]
    return tuple(lax.cond(own[0, 27, 0, 0] != 0, with_whole_bricks, as_they_are, results))


def solution(mesh):
    fine = Mesh(mesh.devices.reshape(4, 2, 4, 8), AXES)
    bricks = P(AXES, None, None)
    return jax.shard_map(
        local,
        mesh=fine,
        in_specs=(bricks, P(), bricks, P(None, AXES), P(AXES)),
        out_specs=(bricks, bricks, P()),
        check_vma=False,
    )
```

```python
import functools

import jax
import jax.numpy as jnp
import numpy as np
from jax import lax
from jax.experimental import pallas as pl
from jax.experimental.pallas import tpu as pltpu
from jax.sharding import Mesh, PartitionSpec as P

BRICK = 4
TILE = 4
BZ = 2
HALO = 40
SLOTS = 8
VOXELS = 64
CHANNELS = 128
PLANE = BRICK * BRICK
PLANES = BRICK + 2
WIDE = 9 * CHANNELS
ROWS_M = 28

DIRECTIONS = ((1, 0), (-1, 0), (0, 1), (0, -1), (1, 1), (1, -1), (-1, 1), (-1, -1))
LENGTHS = (TILE * BZ,) * 4 + (BZ,) * 4
STARTS = tuple(int(start) for start in np.cumsum((0,) + LENGTHS[:-1]))
AXES = ("x", "c", "y", "z")
VMEM_LIMIT = 24 * 1024 * 1024


def where_equal(left, right):
    return jnp.where(left == right, 1.0, 0.0).astype(jnp.bfloat16)


def shift_matrix():
    row = lax.broadcasted_iota(jnp.int32, (9 * PLANE, 9 * PLANE), 0)
    column = lax.broadcasted_iota(jnp.int32, (9 * PLANE, 9 * PLANE), 1)
    number = row >> 4
    third = (number * 11) >> 5
    y = ((row >> 2) & 3) + third + 3
    z = (row & 3) + number - 3 * third + 3
    return where_equal(column, ((y >> 2) * 3 + (z >> 2)) * PLANE + (y & 3) * BRICK + (z & 3))


def layer_matrix():
    row = lax.broadcasted_iota(jnp.int32, (4 * PLANE, VOXELS), 0)
    column = lax.broadcasted_iota(jnp.int32, (4 * PLANE, VOXELS), 1)
    quarter = (row >> 2) & 3
    vx = jnp.where(row < 2 * PLANE, quarter, (quarter >> 1) * 3)
    return where_equal(column, vx * PLANE + ((row >> 4) & 1) * 12 + (row & 3))


def expand_matrix(side):
    row = lax.broadcasted_iota(jnp.int32, (VOXELS, PLANE), 0)
    column = lax.broadcasted_iota(jnp.int32, (VOXELS, PLANE), 1)
    return where_equal(row, (column >> 2) * PLANE + side * 12 + (column & 3))


def expand_corner_matrix(order, side):
    row = lax.broadcasted_iota(jnp.int32, (2 * VOXELS, PLANE), 0)
    column = lax.broadcasted_iota(jnp.int32, (2 * VOXELS, PLANE), 1)
    vy = (row >> 2) & 3
    return where_equal(column + vy * PLANE, order * 8 + (row >> 6) * 4 + (row & 3) + side * 3 * PLANE)


def pack_layers_kernel(recv_slot_ref, features_ref, cotangent_ref, to_first, to_second, to_sibling, to_outer,
                       own_f, own_c, sides, slot_ref, sems):
    bricks = (own_f, own_c)
    copies = [
        pltpu.make_async_copy(ref, target, sems.at[number])
        for number, (ref, target) in enumerate((
            (features_ref, own_f.at[pl.ds(0, SLOTS)]),
            (cotangent_ref, own_c.at[pl.ds(0, SLOTS)]),
            (recv_slot_ref, slot_ref),
        ))
    ]
    for copy in copies:
        copy.start()
    for own in bricks:
        own[SLOTS] = jnp.zeros((VOXELS, CHANNELS), jnp.bfloat16)
    sides[:, SLOTS] = jnp.zeros((2, 4 * PLANE, CHANNELS), jnp.bfloat16)
    core = lax.axis_index("c")
    odd = lax.axis_index("z") & 1
    layer = layer_matrix()
    block = lax.broadcasted_iota(jnp.int32, (PLANE, CHANNELS), 0) >> 2
    masks = [where_equal(block, number) for number in range(4)]
    for copy in copies:
        copy.wait()
    for kind in range(2):
        beside = jnp.concatenate([bricks[kind][slot] for slot in range(SLOTS)], axis=1)
        picked = jnp.dot(layer, beside, preferred_element_type=jnp.float32).astype(jnp.bfloat16)
        for slot in range(SLOTS):
            sides[kind, slot] = picked[:, slot * CHANNELS : (slot + 1) * CHANNELS]

    def put(packet, position, halo, source, begin):
        slot = jnp.clip(slot_ref[halo], 0, SLOTS)
        rows = pl.ds(begin, PLANE)
        packet[position, :, :CHANNELS] = source[0][slot, rows]
        packet[position, :, CHANNELS:] = source[1][slot, rows]

    for packet, up in ((to_first, 1 - odd), (to_second, odd)):
        begin = pl.multiple_of(up * PLANE, PLANE)
        for position in range(SLOTS):
            put(packet, position, STARTS[2] + up * LENGTHS[2] + position, (sides.at[0], sides.at[1]), begin)
        rows = pl.ds(pl.multiple_of((up + 2) * PLANE, PLANE), PLANE)
        halos = [STARTS[number] + up * BZ + position for number in (4, 6) for position in range(BZ)]
        slots = [jnp.clip(slot_ref[halo], 0, SLOTS) for halo in halos]
        for kind in range(2):
            tile = sides[kind, slots[0], rows] * masks[0]
            for number in range(1, 4):
                tile = tile + sides[kind, slots[number], rows] * masks[number]
            packet[SLOTS, :, kind * CHANNELS : (kind + 1) * CHANNELS] = tile
    for packet, up in ((to_sibling, 1 - core), (to_outer, core)):
        begin = pl.multiple_of(up * (VOXELS - PLANE), PLANE)
        for position in range(LENGTHS[0]):
            put(packet, position, up * LENGTHS[0] + position, bricks, begin)


def pack_layers(recv_slot, features, cotangent):
    vmem = pl.BlockSpec(memory_space=pltpu.VMEM)
    hbm = pl.BlockSpec(memory_space=pltpu.HBM)
    return pl.pallas_call(
        pack_layers_kernel,
        in_specs=[hbm] * 3,
        out_specs=[vmem] * 6,
        out_shape=[
            jax.ShapeDtypeStruct((length, PLANE, 2 * CHANNELS), jnp.bfloat16) for length in (SLOTS + 1, SLOTS + 1, SLOTS, SLOTS)
        ] + [jax.ShapeDtypeStruct((SLOTS + 1, VOXELS, CHANNELS), jnp.bfloat16)] * 2,
        scratch_shapes=[
            pltpu.VMEM((2, SLOTS + 1, 4 * PLANE, CHANNELS), jnp.bfloat16),
            pltpu.SMEM((HALO,), jnp.int32),
            pltpu.SemaphoreType.DMA((3,)),
        ],
        compiler_params=pltpu.CompilerParams(vmem_limit_bytes=VMEM_LIMIT),
    )(recv_slot, features, cotangent)


def fill_bricks(halos, lanes, bricks):
    begin_at = SLOTS
    for halo in halos:
        bricks[begin_at : begin_at + halo.shape[0]] = halo[:, :, lanes]
        begin_at += halo.shape[0]


def fill_along_y(halos, lanes, bricks):
    odd = lax.axis_index("z") & 1
    for faces, side in ((halos[0], odd), (halos[1], 1 - odd)):
        tiles = jnp.concatenate([faces[position, :, lanes] for position in range(SLOTS)], axis=1)
        whole = jnp.dot(expand_matrix(side), tiles, preferred_element_type=jnp.float32).astype(jnp.bfloat16)
        for position in range(SLOTS):
            target = SLOTS + STARTS[2] + side * LENGTHS[2] + position
            bricks[target] = whole[:, position * CHANNELS : (position + 1) * CHANNELS]


def fill_along_x(halos, lanes, bricks):
    core, odd = lax.axis_index("c"), lax.axis_index("z") & 1
    both = ((halos[0], core), (halos[1], 1 - core))
    for packet, below in both:
        for position in range(SLOTS):
            tile = packet[position, :, lanes]
            target = SLOTS + below * LENGTHS[0] + position
            bricks[target, :PLANE] = tile
            bricks[target, VOXELS - PLANE :] = tile
    tiles = jnp.concatenate([packet[SLOTS, :, lanes] for packet in halos], axis=1)
    for order, side in ((0, odd), (1, 1 - odd)):
        whole = jnp.dot(
            expand_corner_matrix(order, side), tiles, preferred_element_type=jnp.float32
        ).astype(jnp.bfloat16)
        for number, (_, below) in enumerate(both):
            for position in range(BZ):
                target = SLOTS + STARTS[4] + side * BZ + below * 2 * BZ + position
                bricks[target] = whole[
                    position * VOXELS : (position + 1) * VOXELS, number * CHANNELS : (number + 1) * CHANNELS
                ]


def fill_nothing(halos, lanes, bricks):
    pass


def out_of_place(dst):
    k = lax.broadcasted_iota(jnp.int32, dst.shape, 1)
    ninth = jnp.where(k >= 18, 2, jnp.where(k >= 9, 1, 0))
    rest = k - 9 * ninth
    offset = (ninth - 1, jnp.where(rest >= 6, 2, jnp.where(rest >= 3, 1, 0)) - 1)
    wrong = jnp.zeros(dst.shape, jnp.float32)
    for number, heading in enumerate(DIRECTIONS):
        start = SLOTS + STARTS[number]
        here = (dst >= start) & (dst < start + LENGTHS[number])
        for axis in range(2):
            if heading[axis]:
                wrong = jnp.where(here & (offset[axis] != heading[axis]), 1.0, wrong)
    return jnp.max(jnp.max(wrong, axis=1, keepdims=True), axis=0, keepdims=True)


def build_taps(unroll, dst_ref, bricks, planes, taps):
    shift = shift_matrix()

    def around(slot, plane):
        side = 0 if plane == 0 else 2 if plane == PLANES - 1 else 1
        local = (plane - 1) % BRICK * PLANE
        return jnp.concatenate(
            [bricks[dst_ref[slot, side * 9 + number], local : local + PLANE] for number in range(9)], axis=0
        )

    def one_slot(slot, carry):
        for index in range(0, len(planes), 2):
            pair = jnp.concatenate((around(slot, planes[index]), around(slot, planes[index + 1])), axis=1)
            moved = jnp.dot(shift, pair, preferred_element_type=jnp.float32).astype(jnp.bfloat16)
            for number in range(9):
                rows = moved[number * PLANE : (number + 1) * PLANE]
                target = slice(number * CHANNELS, (number + 1) * CHANNELS)
                taps[slot, index, :, target] = rows[:, :CHANNELS]
                taps[slot, index + 1, :, target] = rows[:, CHANNELS:]
        return carry

    lax.fori_loop(0, SLOTS, one_slot, 0, unroll=unroll)


def taps_of(mid, edge, side):
    if side == 0:
        planes = jnp.concatenate((edge[:, :1], mid[:, :3]), axis=1)
    elif side == 1:
        planes = mid[...]
    else:
        planes = jnp.concatenate((mid[:, 1:], edge[:, 1:]), axis=1)
    return planes.reshape(SLOTS * VOXELS, WIDE)


def store_products(flipped_ref, tap, first, send_ref, keep_ref):
    core = lax.axis_index("c")
    half = CHANNELS // 2
    flipped = jnp.concatenate((flipped_ref[1 - core], flipped_ref[core]), axis=0)
    part = jnp.dot(flipped, tap, preferred_element_type=jnp.float32)
    for number in range(9):
        block = part[:, number * CHANNELS : (number + 1) * CHANNELS]
        for quarter in range(4):
            rows = slice(quarter * 16, quarter * 16 + 16)
            send_ref[quarter, first + number] = block[:half][rows].astype(jnp.bfloat16)
            keep_ref[quarter, first + number] = block[half:][rows]


def grad_part(tap, weights_ref, side):
    matrix = jnp.concatenate([weights_ref[26 - side * 9 - number] for number in range(9)], axis=1)
    return lax.dot_general(tap, matrix, (((1,), (1,)), ((), ())), preferred_element_type=jnp.float32)


def mid_kernel(fill, unroll, count, dst_ref, features_ref, cotangent_ref, flipped_ref, weights_ref, *rest):
    halos = rest[:count]
    mid_f, mid_c, bricks_f, bricks_c, send_ref, keep_ref, grad_ref = rest[count:]
    for kind, (own, bricks, mid) in enumerate(((features_ref, bricks_f, mid_f), (cotangent_ref, bricks_c, mid_c))):
        bricks[:SLOTS] = own[:SLOTS]
        for begin, end in ((SLOTS, SLOTS + STARTS[2]), (SLOTS + STARTS[4], SLOTS + HALO + 1)):
            bricks[begin:end] = jnp.zeros((end - begin, VOXELS, CHANNELS), jnp.bfloat16)
        fill(halos, slice(kind * CHANNELS, (kind + 1) * CHANNELS), bricks)
        build_taps(unroll, dst_ref, bricks, (1, 2, 3, 4), mid)
    tap = mid_c[...].reshape(SLOTS * VOXELS, WIDE)
    store_products(flipped_ref, tap, 0, send_ref, keep_ref)
    grad_ref[...] = grad_part(tap, weights_ref, 1)


def weight_kernel(fill, unroll, count, dst_ref, table_ref, mid, _, *rest):
    halos = rest[:count]
    flipped_ref, send_mid, keep_mid, send_ref, keep_ref, edge, bricks = rest[count:]
    fill(halos, slice(CHANNELS, 2 * CHANNELS), bricks)
    build_taps(unroll, dst_ref, bricks, (0, PLANES - 1), edge)
    send_ref[:, 9:18] = send_mid[...]
    keep_ref[:, 9:18] = keep_mid[...]
    for side in (0, 2):
        store_products(flipped_ref, taps_of(mid, edge, side), side * 9, send_ref, keep_ref)
    flag = jnp.broadcast_to(out_of_place(table_ref[...]), (16, CHANNELS))
    for quarter in range(4):
        send_ref[quarter, 27] = flag.astype(jnp.bfloat16)
        keep_ref[quarter, 27] = flag


def grad_kernel(mid, edge, weights_ref, grad_mid, grad_ref):
    grad = grad_mid[...]
    for side in (0, 2):
        grad = grad + grad_part(taps_of(mid, edge, side), weights_ref, side)
    grad_ref[...] = grad.astype(jnp.bfloat16).reshape(SLOTS, VOXELS, CHANNELS)


def edge_kernel(fill, unroll, count, dst_ref, _, *rest):
    edge, bricks = rest[count:]
    fill(rest[:count], slice(0, CHANNELS), bricks)
    build_taps(unroll, dst_ref, bricks, (0, PLANES - 1), edge)


def output_kernel(mid, edge, weights_ref, outputs_ref):
    outputs = None
    for side in range(3):
        matrix = weights_ref[side * 9 : side * 9 + 9].reshape(WIDE, CHANNELS)
        part = jnp.dot(taps_of(mid, edge, side), matrix, preferred_element_type=jnp.float32)
        outputs = part if outputs is None else outputs + part
    outputs_ref[...] = outputs.astype(jnp.bfloat16).reshape(SLOTS, VOXELS, CHANNELS)


VMEM_SPEC = pl.BlockSpec(memory_space=pltpu.VMEM)
SMEM_SPEC = pl.BlockSpec(memory_space=pltpu.SMEM)
BRICK_SHAPE = jax.ShapeDtypeStruct((SLOTS, VOXELS, CHANNELS), jnp.bfloat16)
MID_SHAPE = jax.ShapeDtypeStruct((SLOTS, BRICK, PLANE, WIDE), jnp.bfloat16)
EDGE_SHAPE = jax.ShapeDtypeStruct((SLOTS, 2, PLANE, WIDE), jnp.bfloat16)
ALL_BRICKS = jax.ShapeDtypeStruct((SLOTS + HALO + 1, VOXELS, CHANNELS), jnp.bfloat16)
PARAMS = pltpu.CompilerParams(vmem_limit_bytes=VMEM_LIMIT)
COST = pl.CostEstimate(flops=4 * SLOTS * VOXELS * 27 * CHANNELS * CHANNELS, bytes_accessed=4_000_000, transcendentals=0)


def mid_taps(fill, unroll, dst, own_f, own_c, halos, flipped, weights):
    return pl.pallas_call(
        functools.partial(mid_kernel, fill, unroll, len(halos)),
        in_specs=[SMEM_SPEC] + [VMEM_SPEC] * (4 + len(halos)),
        out_specs=[VMEM_SPEC] * 7,
        out_shape=[
            MID_SHAPE, MID_SHAPE, ALL_BRICKS, ALL_BRICKS,
            jax.ShapeDtypeStruct((4, 9, 16, CHANNELS), jnp.bfloat16),
            jax.ShapeDtypeStruct((4, 9, 16, CHANNELS), jnp.float32),
            jax.ShapeDtypeStruct((SLOTS * VOXELS, CHANNELS), jnp.float32),
        ],
        compiler_params=PARAMS,
        cost_estimate=COST,
    )(dst, own_f, own_c, flipped, weights, *halos)


def weight_sums(fill, unroll, dst, mid, bricks, halos, flipped, send, keep):
    return pl.pallas_call(
        functools.partial(weight_kernel, fill, unroll, len(halos)),
        in_specs=[SMEM_SPEC] + [VMEM_SPEC] * (6 + len(halos)),
        out_specs=[VMEM_SPEC] * 4,
        out_shape=[
            jax.ShapeDtypeStruct((4, ROWS_M, 16, CHANNELS), jnp.bfloat16),
            jax.ShapeDtypeStruct((4, ROWS_M, 16, CHANNELS), jnp.float32),
            EDGE_SHAPE,
            ALL_BRICKS,
        ],
        input_output_aliases={3: 3},
        compiler_params=PARAMS,
        cost_estimate=COST,
    )(dst, dst, mid, bricks, *halos, flipped, send, keep)


def feature_edges(fill, unroll, dst, bricks, halos):
    return pl.pallas_call(
        functools.partial(edge_kernel, fill, unroll, len(halos)),
        in_specs=[SMEM_SPEC] + [VMEM_SPEC] * (1 + len(halos)),
        out_specs=[VMEM_SPEC] * 2,
        out_shape=[EDGE_SHAPE, ALL_BRICKS],
        input_output_aliases={1: 1},
        compiler_params=PARAMS,
        cost_estimate=COST,
    )(dst, bricks, *halos)[0]


def product(kernel, *operands):
    return pl.pallas_call(
        kernel,
        in_specs=[VMEM_SPEC] * len(operands),
        out_specs=VMEM_SPEC,
        out_shape=BRICK_SHAPE,
        compiler_params=PARAMS,
        cost_estimate=COST,
    )(*operands)


def convolve(fill, unroll, dst, mids, halos, flipped, weights):
    mid_f, mid_c, bricks_f, bricks_c, send, keep, grad_mid = mids
    send, keep, edge_c, _ = weight_sums(fill, unroll, dst, mid_c, bricks_c, halos, flipped, send, keep)
    arrived = lax.ppermute(send, "c", [(0, 1), (1, 0)])
    input_grad = product(grad_kernel, mid_c, edge_c, weights, grad_mid)
    edge_f = feature_edges(fill, unroll, dst, bricks_f, halos)
    arrived, input_grad, edge_f = lax.optimization_barrier((arrived, input_grad, edge_f))
    own = sum_everywhere(arrived, keep)
    other = lax.ppermute(own, "c", [(0, 1), (1, 0)])
    outputs = product(output_kernel, mid_f, edge_f, weights)
    return outputs, input_grad, own, other


def pack_bricks_kernel(slot_ref, features_ref, cotangent_ref, *packets):
    begin_at = 0
    for packet in packets:
        for position in range(packet.shape[0]):
            slot = slot_ref[begin_at + position]
            row = jnp.clip(slot, 0, SLOTS - 1)

            @pl.when(slot < SLOTS)
            def _():
                packet[position, :, :CHANNELS] = features_ref[row]
                packet[position, :, CHANNELS:] = cotangent_ref[row]

            @pl.when(slot >= SLOTS)
            def _():
                packet[position] = jnp.zeros((VOXELS, 2 * CHANNELS), jnp.bfloat16)

        begin_at += packet.shape[0]


def pack_bricks(recv_slot, features, cotangent):
    vmem = pl.BlockSpec(memory_space=pltpu.VMEM)
    return pl.pallas_call(
        pack_bricks_kernel,
        in_specs=[pl.BlockSpec(memory_space=pltpu.SMEM), vmem, vmem],
        out_specs=[vmem] * 8,
        out_shape=[
            jax.ShapeDtypeStruct((length, VOXELS, 2 * CHANNELS), jnp.bfloat16) for length in LENGTHS
        ],
        compiler_params=pltpu.CompilerParams(vmem_limit_bytes=VMEM_LIMIT),
    )(recv_slot, features, cotangent)


def pass_to(value, step_x, step_y):
    pairs = []
    for gx in range(8):
        for gy in range(32):
            if 0 <= gx + step_x < 8 and 0 <= gy + step_y < 32:
                pairs.append((gx * 32 + gy, (gx + step_x) * 32 + gy + step_y))
    return lax.ppermute(value, AXES, pairs)


def sum_everywhere(arrived, keep):
    chip_sum = (keep + arrived.astype(jnp.float32)).astype(jnp.bfloat16)
    parts = chip_sum.reshape(16, 7, 16, CHANNELS)
    parts = lax.all_to_all(parts, ("x", "y"), 0, 0)
    total = jnp.sum(parts.astype(jnp.float32), axis=0)
    largest = jnp.max(jnp.abs(total), axis=(0, 1))
    power = jnp.clip(jnp.ceil(jnp.log2(jnp.maximum(largest, 1e-37))), -100.0, 100.0)
    power = jnp.broadcast_to(power, (8, CHANNELS))
    scaled = (total * jnp.exp2(14.0 - power[0])).reshape(7 * 16, CHANNELS)
    share = jnp.concatenate((scaled, power), axis=0).astype(jnp.float16)
    column = lax.all_to_all(jnp.broadcast_to(share[None], (8,) + share.shape), "z", 0, 0).astype(jnp.float32)
    total = jnp.sum(column[:, : 7 * 16] * jnp.exp2(column[:, 7 * 16 : 7 * 16 + 1] - 14.0), axis=0)
    share = (total * (1.0 / (VOXELS * SLOTS))).astype(jnp.bfloat16).reshape(7, 16, CHANNELS)
    whole = jnp.broadcast_to(share[None], (16,) + share.shape)
    return lax.all_to_all(whole, ("x", "y"), 0, 0).reshape(4, ROWS_M, 16, CHANNELS)


def spread_kernel(own_ref, other_ref, outputs_ref, grad_ref, outputs_out, grad_out, out_ref, whole, sems):
    half = CHANNELS // 2
    core = lax.axis_index("c")
    copies = [
        pltpu.make_async_copy(outputs_ref, outputs_out, sems.at[9]),
        pltpu.make_async_copy(grad_ref, grad_out, sems.at[10]),
    ]
    for copy in copies:
        copy.start()
    for chunk in range(9):
        for m in range(3 * chunk, 3 * chunk + 3):
            for quarter in range(4):
                for ref, side in ((own_ref, core), (other_ref, 1 - core)):
                    begin = pl.multiple_of(side * half + quarter * 16, 16)
                    whole[26 - m, pl.ds(begin, 16)] = ref[quarter, m].astype(jnp.float32)
        rows = pl.ds(24 - 3 * chunk, 3)
        copies.append(pltpu.make_async_copy(whole.at[rows], out_ref.at[rows], sems.at[chunk]))
        copies[-1].start()
    for copy in copies:
        copy.wait()


def spread_out(outputs, input_grad, own, other):
    return pl.pallas_call(
        spread_kernel,
        in_specs=[VMEM_SPEC] * 4,
        out_specs=[pl.BlockSpec(memory_space=pltpu.HBM)] * 3,
        out_shape=[BRICK_SHAPE, BRICK_SHAPE, jax.ShapeDtypeStruct((27, CHANNELS, CHANNELS), jnp.float32)],
        scratch_shapes=[
            pltpu.VMEM((27, CHANNELS, CHANNELS), jnp.float32),
            pltpu.SemaphoreType.DMA((11,)),
        ],
        compiler_params=PARAMS,
    )(own, other, outputs, input_grad)


def local(features, weights, cotangent, dst_index, recv_slot):
    core = lax.axis_index("c")
    dst = jnp.clip(dst_index.T, 0, SLOTS + HALO)

    to_first, to_second, to_sibling, to_outer, own_f, own_c = pack_layers(recv_slot, features, cotangent)
    flipped = jnp.transpose(own_f[:SLOTS].reshape(SLOTS * VOXELS, CHANNELS))
    flipped = flipped.reshape(2, CHANNELS // 2, SLOTS * VOXELS)
    y_second = lax.ppermute(to_second, ("y", "z"), [(gy, ((gy + 1) ^ 1) - 1) for gy in range(1, 31)])
    y_first = lax.ppermute(to_first, ("y", "z"), [(gy, gy ^ 1) for gy in range(32)])
    y_first, y_second, dst, flipped = lax.optimization_barrier((y_first, y_second, dst, flipped))

    def relayed(packet, up):
        corners = [lax.dynamic_slice_in_dim(value[SLOTS:], 8 * up, 8, axis=1) for value in (y_first, y_second)]
        return jnp.concatenate((packet, jnp.concatenate(corners, axis=1)), axis=0)

    x_sibling = lax.ppermute(relayed(to_sibling, 1 - core), "c", [(0, 1), (1, 0)])
    x_outer = lax.ppermute(relayed(to_outer, core), ("x", "c"), [(2 * x + 1, 2 * x + 2) for x in range(3)]
                           + [(2 * x + 2, 2 * x + 1) for x in range(3)])
    mids = mid_taps(fill_along_y, SLOTS, dst, own_f, own_c, (y_first, y_second), flipped, weights)
    results = convolve(fill_along_x, SLOTS, dst, mids, (x_sibling, x_outer), flipped, weights)

    def with_whole_bricks(results):
        packets = pack_bricks(recv_slot, features, cotangent)
        halos = [pass_to(packet, -heading[0], -heading[1]) for packet, heading in zip(packets, DIRECTIONS)]
        mids = mid_taps(fill_bricks, 1, dst, own_f, own_c, halos, flipped, weights)
        return spread_out(*convolve(fill_nothing, 1, dst, mids, (), flipped, weights))

    def as_they_are(results):
        return spread_out(*results)

    own = results[2]
    return tuple(lax.cond(own[0, 27, 0, 0] != 0, with_whole_bricks, as_they_are, results))


def solution(mesh):
    fine = Mesh(mesh.devices.reshape(4, 2, 4, 8), AXES)
    bricks = P(AXES, None, None)
    return jax.shard_map(
        local,
        mesh=fine,
        in_specs=(bricks, P(), bricks, P(None, AXES), P(AXES)),
        out_specs=(bricks, bricks, P()),
        check_vma=False,
    )
```

```python
import functools

import jax
import jax.numpy as jnp
import numpy as np
from jax import lax
from jax.experimental import pallas as pl
from jax.experimental.pallas import tpu as pltpu
from jax.sharding import Mesh, PartitionSpec as P

BRICK = 4
TILE = 4
BZ = 2
HALO = 40
SLOTS = 8
VOXELS = 64
CHANNELS = 128
PLANE = BRICK * BRICK
PLANES = BRICK + 2
WIDE = 9 * CHANNELS
ROWS_M = 28

DIRECTIONS = ((1, 0), (-1, 0), (0, 1), (0, -1), (1, 1), (1, -1), (-1, 1), (-1, -1))
LENGTHS = (TILE * BZ,) * 4 + (BZ,) * 4
STARTS = tuple(int(start) for start in np.cumsum((0,) + LENGTHS[:-1]))
AXES = ("x", "c", "y", "z")
VMEM_LIMIT = 24 * 1024 * 1024


def where_equal(left, right):
    return jnp.where(left == right, 1.0, 0.0).astype(jnp.bfloat16)


def shift_matrix():
    row = lax.broadcasted_iota(jnp.int32, (9 * PLANE, 9 * PLANE), 0)
    column = lax.broadcasted_iota(jnp.int32, (9 * PLANE, 9 * PLANE), 1)
    number = row >> 4
    third = (number * 11) >> 5
    y = ((row >> 2) & 3) + third + 3
    z = (row & 3) + number - 3 * third + 3
    return where_equal(column, ((y >> 2) * 3 + (z >> 2)) * PLANE + (y & 3) * BRICK + (z & 3))


def layer_matrix():
    row = lax.broadcasted_iota(jnp.int32, (4 * PLANE, VOXELS), 0)
    column = lax.broadcasted_iota(jnp.int32, (4 * PLANE, VOXELS), 1)
    quarter = (row >> 2) & 3
    vx = jnp.where(row < 2 * PLANE, quarter, (quarter >> 1) * 3)
    return where_equal(column, vx * PLANE + ((row >> 4) & 1) * 12 + (row & 3))


def expand_matrix(side):
    row = lax.broadcasted_iota(jnp.int32, (VOXELS, PLANE), 0)
    column = lax.broadcasted_iota(jnp.int32, (VOXELS, PLANE), 1)
    return where_equal(row, (column >> 2) * PLANE + side * 12 + (column & 3))


def expand_corner_matrix(order, side):
    row = lax.broadcasted_iota(jnp.int32, (2 * VOXELS, PLANE), 0)
    column = lax.broadcasted_iota(jnp.int32, (2 * VOXELS, PLANE), 1)
    vy = (row >> 2) & 3
    return where_equal(column + vy * PLANE, order * 8 + (row >> 6) * 4 + (row & 3) + side * 3 * PLANE)


def pack_layers_kernel(recv_slot_ref, features_ref, cotangent_ref, to_first, to_second, to_sibling, to_outer,
                       own_f, own_c, sides, slot_ref, sems):
    bricks = (own_f, own_c)
    copies = [
        pltpu.make_async_copy(ref, target, sems.at[number])
        for number, (ref, target) in enumerate((
            (features_ref, own_f.at[pl.ds(0, SLOTS)]),
            (cotangent_ref, own_c.at[pl.ds(0, SLOTS)]),
            (recv_slot_ref, slot_ref),
        ))
    ]
    for copy in copies:
        copy.start()
    for own in bricks:
        own[SLOTS] = jnp.zeros((VOXELS, CHANNELS), jnp.bfloat16)
    sides[:, SLOTS] = jnp.zeros((2, 4 * PLANE, CHANNELS), jnp.bfloat16)
    core = lax.axis_index("c")
    odd = lax.axis_index("z") & 1
    layer = layer_matrix()
    block = lax.broadcasted_iota(jnp.int32, (PLANE, CHANNELS), 0) >> 2
    masks = [where_equal(block, number) for number in range(4)]
    for copy in copies:
        copy.wait()
    for kind in range(2):
        beside = jnp.concatenate([bricks[kind][slot] for slot in range(SLOTS)], axis=1)
        picked = jnp.dot(layer, beside, preferred_element_type=jnp.float32).astype(jnp.bfloat16)
        for slot in range(SLOTS):
            sides[kind, slot] = picked[:, slot * CHANNELS : (slot + 1) * CHANNELS]

    def put(packet, position, halo, source, begin):
        slot = jnp.clip(slot_ref[halo], 0, SLOTS)
        rows = pl.ds(begin, PLANE)
        packet[position, :, :CHANNELS] = source[0][slot, rows]
        packet[position, :, CHANNELS:] = source[1][slot, rows]

    for packet, up in ((to_first, 1 - odd), (to_second, odd)):
        begin = pl.multiple_of(up * PLANE, PLANE)
        for position in range(SLOTS):
            put(packet, position, STARTS[2] + up * LENGTHS[2] + position, (sides.at[0], sides.at[1]), begin)
        rows = pl.ds(pl.multiple_of((up + 2) * PLANE, PLANE), PLANE)
        halos = [STARTS[number] + up * BZ + position for number in (4, 6) for position in range(BZ)]
        slots = [jnp.clip(slot_ref[halo], 0, SLOTS) for halo in halos]
        for kind in range(2):
            tile = sides[kind, slots[0], rows] * masks[0]
            for number in range(1, 4):
                tile = tile + sides[kind, slots[number], rows] * masks[number]
            packet[SLOTS, :, kind * CHANNELS : (kind + 1) * CHANNELS] = tile
    for packet, up in ((to_sibling, 1 - core), (to_outer, core)):
        begin = pl.multiple_of(up * (VOXELS - PLANE), PLANE)
        for position in range(LENGTHS[0]):
            put(packet, position, up * LENGTHS[0] + position, bricks, begin)


def pack_layers(recv_slot, features, cotangent):
    vmem = pl.BlockSpec(memory_space=pltpu.VMEM)
    hbm = pl.BlockSpec(memory_space=pltpu.HBM)
    return pl.pallas_call(
        pack_layers_kernel,
        in_specs=[hbm] * 3,
        out_specs=[vmem] * 6,
        out_shape=[
            jax.ShapeDtypeStruct((length, PLANE, 2 * CHANNELS), jnp.bfloat16) for length in (SLOTS + 1, SLOTS + 1, SLOTS, SLOTS)
        ] + [jax.ShapeDtypeStruct((SLOTS + 1, VOXELS, CHANNELS), jnp.bfloat16)] * 2,
        scratch_shapes=[
            pltpu.VMEM((2, SLOTS + 1, 4 * PLANE, CHANNELS), jnp.bfloat16),
            pltpu.SMEM((HALO,), jnp.int32),
            pltpu.SemaphoreType.DMA((3,)),
        ],
        compiler_params=pltpu.CompilerParams(vmem_limit_bytes=VMEM_LIMIT),
    )(recv_slot, features, cotangent)


def fill_bricks(halos, lanes, bricks):
    begin_at = SLOTS
    for halo in halos:
        bricks[begin_at : begin_at + halo.shape[0]] = halo[:, :, lanes]
        begin_at += halo.shape[0]


def fill_along_y(halos, lanes, bricks):
    odd = lax.axis_index("z") & 1
    for faces, side in ((halos[0], odd), (halos[1], 1 - odd)):
        tiles = jnp.concatenate([faces[position, :, lanes] for position in range(SLOTS)], axis=1)
        whole = jnp.dot(expand_matrix(side), tiles, preferred_element_type=jnp.float32).astype(jnp.bfloat16)
        for position in range(SLOTS):
            target = SLOTS + STARTS[2] + side * LENGTHS[2] + position
            bricks[target] = whole[:, position * CHANNELS : (position + 1) * CHANNELS]


def fill_along_x(halos, lanes, bricks):
    core, odd = lax.axis_index("c"), lax.axis_index("z") & 1
    both = ((halos[0], core), (halos[1], 1 - core))
    for packet, below in both:
        for position in range(SLOTS):
            tile = packet[position, :, lanes]
            target = SLOTS + below * LENGTHS[0] + position
            bricks[target, :PLANE] = tile
            bricks[target, VOXELS - PLANE :] = tile
    tiles = jnp.concatenate([packet[SLOTS, :, lanes] for packet in halos], axis=1)
    for order, side in ((0, odd), (1, 1 - odd)):
        whole = jnp.dot(
            expand_corner_matrix(order, side), tiles, preferred_element_type=jnp.float32
        ).astype(jnp.bfloat16)
        for number, (_, below) in enumerate(both):
            for position in range(BZ):
                target = SLOTS + STARTS[4] + side * BZ + below * 2 * BZ + position
                bricks[target] = whole[
                    position * VOXELS : (position + 1) * VOXELS, number * CHANNELS : (number + 1) * CHANNELS
                ]


def fill_nothing(halos, lanes, bricks):
    pass


def out_of_place(dst):
    k = lax.broadcasted_iota(jnp.int32, dst.shape, 1)
    ninth = jnp.where(k >= 18, 2, jnp.where(k >= 9, 1, 0))
    rest = k - 9 * ninth
    offset = (ninth - 1, jnp.where(rest >= 6, 2, jnp.where(rest >= 3, 1, 0)) - 1)
    wrong = jnp.zeros(dst.shape, jnp.float32)
    for number, heading in enumerate(DIRECTIONS):
        start = SLOTS + STARTS[number]
        here = (dst >= start) & (dst < start + LENGTHS[number])
        for axis in range(2):
            if heading[axis]:
                wrong = jnp.where(here & (offset[axis] != heading[axis]), 1.0, wrong)
    return jnp.max(jnp.max(wrong, axis=1, keepdims=True), axis=0, keepdims=True)


def build_taps(unroll, dst_ref, bricks, planes, taps):
    shift = shift_matrix()

    def around(slot, plane):
        side = 0 if plane == 0 else 2 if plane == PLANES - 1 else 1
        local = (plane - 1) % BRICK * PLANE
        return jnp.concatenate(
            [bricks[dst_ref[slot, side * 9 + number], local : local + PLANE] for number in range(9)], axis=0
        )

    def one_slot(slot, carry):
        for index in range(0, len(planes), 2):
            pair = jnp.concatenate((around(slot, planes[index]), around(slot, planes[index + 1])), axis=1)
            moved = jnp.dot(shift, pair, preferred_element_type=jnp.float32).astype(jnp.bfloat16)
            for number in range(9):
                rows = moved[number * PLANE : (number + 1) * PLANE]
                target = slice(number * CHANNELS, (number + 1) * CHANNELS)
                taps[slot, index, :, target] = rows[:, :CHANNELS]
                taps[slot, index + 1, :, target] = rows[:, CHANNELS:]
        return carry

    lax.fori_loop(0, SLOTS, one_slot, 0, unroll=unroll)


def taps_of(mid, edge, side):
    if side == 0:
        planes = jnp.concatenate((edge[:, :1], mid[:, :3]), axis=1)
    elif side == 1:
        planes = mid[...]
    else:
        planes = jnp.concatenate((mid[:, 1:], edge[:, 1:]), axis=1)
    return planes.reshape(SLOTS * VOXELS, WIDE)


def store_products(flipped_ref, tap, first, send_ref, keep_ref):
    core = lax.axis_index("c")
    half = CHANNELS // 2
    flipped = jnp.concatenate((flipped_ref[1 - core], flipped_ref[core]), axis=0)
    part = jnp.dot(flipped, tap, preferred_element_type=jnp.float32)
    for number in range(9):
        block = part[:, number * CHANNELS : (number + 1) * CHANNELS]
        for quarter in range(4):
            rows = slice(quarter * 16, quarter * 16 + 16)
            send_ref[quarter, first + number] = block[:half][rows].astype(jnp.bfloat16)
            keep_ref[quarter, first + number] = block[half:][rows]


def grad_part(tap, weights_ref, side):
    matrix = jnp.concatenate([weights_ref[26 - side * 9 - number] for number in range(9)], axis=1)
    return lax.dot_general(tap, matrix, (((1,), (1,)), ((), ())), preferred_element_type=jnp.float32)


def mid_kernel(fill, unroll, count, dst_ref, features_ref, cotangent_ref, flipped_ref, weights_ref, *rest):
    halos = rest[:count]
    mid_f, mid_c, bricks_f, bricks_c, send_ref, keep_ref, grad_ref = rest[count:]
    for kind, (own, bricks, mid) in enumerate(((features_ref, bricks_f, mid_f), (cotangent_ref, bricks_c, mid_c))):
        bricks[:SLOTS] = own[:SLOTS]
        for begin, end in ((SLOTS, SLOTS + STARTS[2]), (SLOTS + STARTS[4], SLOTS + HALO + 1)):
            bricks[begin:end] = jnp.zeros((end - begin, VOXELS, CHANNELS), jnp.bfloat16)
        fill(halos, slice(kind * CHANNELS, (kind + 1) * CHANNELS), bricks)
        build_taps(unroll, dst_ref, bricks, (1, 2, 3, 4), mid)
    tap = mid_c[...].reshape(SLOTS * VOXELS, WIDE)
    store_products(flipped_ref, tap, 0, send_ref, keep_ref)
    grad_ref[...] = grad_part(tap, weights_ref, 1)


def weight_kernel(fill, unroll, count, dst_ref, table_ref, mid, _, *rest):
    halos = rest[:count]
    flipped_ref, send_mid, keep_mid, send_ref, keep_ref, edge, bricks = rest[count:]
    fill(halos, slice(CHANNELS, 2 * CHANNELS), bricks)
    build_taps(unroll, dst_ref, bricks, (0, PLANES - 1), edge)
    send_ref[:, 9:18] = send_mid[...]
    keep_ref[:, 9:18] = keep_mid[...]
    for side in (0, 2):
        store_products(flipped_ref, taps_of(mid, edge, side), side * 9, send_ref, keep_ref)
    flag = jnp.broadcast_to(out_of_place(table_ref[...]), (16, CHANNELS))
    for quarter in range(4):
        send_ref[quarter, 27] = flag.astype(jnp.bfloat16)
        keep_ref[quarter, 27] = flag


def grad_kernel(mid, edge, weights_ref, grad_mid, grad_ref):
    grad = grad_mid[...]
    for side in (0, 2):
        grad = grad + grad_part(taps_of(mid, edge, side), weights_ref, side)
    grad_ref[...] = grad.astype(jnp.bfloat16).reshape(SLOTS, VOXELS, CHANNELS)


def edge_kernel(fill, unroll, count, dst_ref, _, *rest):
    edge, bricks = rest[count:]
    fill(rest[:count], slice(0, CHANNELS), bricks)
    build_taps(unroll, dst_ref, bricks, (0, PLANES - 1), edge)


def output_kernel(mid, edge, weights_ref, outputs_ref):
    outputs = None
    for side in range(3):
        matrix = weights_ref[side * 9 : side * 9 + 9].reshape(WIDE, CHANNELS)
        part = jnp.dot(taps_of(mid, edge, side), matrix, preferred_element_type=jnp.float32)
        outputs = part if outputs is None else outputs + part
    outputs_ref[...] = outputs.astype(jnp.bfloat16).reshape(SLOTS, VOXELS, CHANNELS)


VMEM_SPEC = pl.BlockSpec(memory_space=pltpu.VMEM)
SMEM_SPEC = pl.BlockSpec(memory_space=pltpu.SMEM)
BRICK_SHAPE = jax.ShapeDtypeStruct((SLOTS, VOXELS, CHANNELS), jnp.bfloat16)
MID_SHAPE = jax.ShapeDtypeStruct((SLOTS, BRICK, PLANE, WIDE), jnp.bfloat16)
EDGE_SHAPE = jax.ShapeDtypeStruct((SLOTS, 2, PLANE, WIDE), jnp.bfloat16)
ALL_BRICKS = jax.ShapeDtypeStruct((SLOTS + HALO + 1, VOXELS, CHANNELS), jnp.bfloat16)
PARAMS = pltpu.CompilerParams(vmem_limit_bytes=VMEM_LIMIT)
COST = pl.CostEstimate(flops=4 * SLOTS * VOXELS * 27 * CHANNELS * CHANNELS, bytes_accessed=4_000_000, transcendentals=0)


def mid_taps(fill, unroll, dst, own_f, own_c, halos, flipped, weights):
    return pl.pallas_call(
        functools.partial(mid_kernel, fill, unroll, len(halos)),
        in_specs=[SMEM_SPEC] + [VMEM_SPEC] * (4 + len(halos)),
        out_specs=[VMEM_SPEC] * 7,
        out_shape=[
            MID_SHAPE, MID_SHAPE, ALL_BRICKS, ALL_BRICKS,
            jax.ShapeDtypeStruct((4, 9, 16, CHANNELS), jnp.bfloat16),
            jax.ShapeDtypeStruct((4, 9, 16, CHANNELS), jnp.float32),
            jax.ShapeDtypeStruct((SLOTS * VOXELS, CHANNELS), jnp.float32),
        ],
        compiler_params=PARAMS,
        cost_estimate=COST,
    )(dst, own_f, own_c, flipped, weights, *halos)


def weight_sums(fill, unroll, dst, mid, bricks, halos, flipped, send, keep):
    return pl.pallas_call(
        functools.partial(weight_kernel, fill, unroll, len(halos)),
        in_specs=[SMEM_SPEC] + [VMEM_SPEC] * (6 + len(halos)),
        out_specs=[VMEM_SPEC] * 4,
        out_shape=[
            jax.ShapeDtypeStruct((4, ROWS_M, 16, CHANNELS), jnp.bfloat16),
            jax.ShapeDtypeStruct((4, ROWS_M, 16, CHANNELS), jnp.float32),
            EDGE_SHAPE,
            ALL_BRICKS,
        ],
        input_output_aliases={3: 3},
        compiler_params=PARAMS,
        cost_estimate=COST,
    )(dst, dst, mid, bricks, *halos, flipped, send, keep)


def feature_edges(fill, unroll, dst, bricks, halos):
    return pl.pallas_call(
        functools.partial(edge_kernel, fill, unroll, len(halos)),
        in_specs=[SMEM_SPEC] + [VMEM_SPEC] * (1 + len(halos)),
        out_specs=[VMEM_SPEC] * 2,
        out_shape=[EDGE_SHAPE, ALL_BRICKS],
        input_output_aliases={1: 1},
        compiler_params=PARAMS,
        cost_estimate=COST,
    )(dst, bricks, *halos)[0]


def product(kernel, *operands):
    return pl.pallas_call(
        kernel,
        in_specs=[VMEM_SPEC] * len(operands),
        out_specs=VMEM_SPEC,
        out_shape=BRICK_SHAPE,
        compiler_params=PARAMS,
        cost_estimate=COST,
    )(*operands)


def convolve(fill, unroll, dst, mids, halos, flipped, weights):
    mid_f, mid_c, bricks_f, bricks_c, send, keep, grad_mid = mids
    send, keep, edge_c, _ = weight_sums(fill, unroll, dst, mid_c, bricks_c, halos, flipped, send, keep)
    arrived = lax.ppermute(send, "c", [(0, 1), (1, 0)])
    input_grad = product(grad_kernel, mid_c, edge_c, weights, grad_mid)
    edge_f = feature_edges(fill, unroll, dst, bricks_f, halos)
    arrived, input_grad, edge_f = lax.optimization_barrier((arrived, input_grad, edge_f))
    own = sum_everywhere(arrived, keep)
    other = lax.ppermute(own, "c", [(0, 1), (1, 0)])
    outputs = product(output_kernel, mid_f, edge_f, weights)
    return outputs, input_grad, own, other


def pack_bricks_kernel(slot_ref, features_ref, cotangent_ref, *packets):
    begin_at = 0
    for packet in packets:
        for position in range(packet.shape[0]):
            slot = slot_ref[begin_at + position]
            row = jnp.clip(slot, 0, SLOTS - 1)

            @pl.when(slot < SLOTS)
            def _():
                packet[position, :, :CHANNELS] = features_ref[row]
                packet[position, :, CHANNELS:] = cotangent_ref[row]

            @pl.when(slot >= SLOTS)
            def _():
                packet[position] = jnp.zeros((VOXELS, 2 * CHANNELS), jnp.bfloat16)

        begin_at += packet.shape[0]


def pack_bricks(recv_slot, features, cotangent):
    vmem = pl.BlockSpec(memory_space=pltpu.VMEM)
    return pl.pallas_call(
        pack_bricks_kernel,
        in_specs=[pl.BlockSpec(memory_space=pltpu.SMEM), vmem, vmem],
        out_specs=[vmem] * 8,
        out_shape=[
            jax.ShapeDtypeStruct((length, VOXELS, 2 * CHANNELS), jnp.bfloat16) for length in LENGTHS
        ],
        compiler_params=pltpu.CompilerParams(vmem_limit_bytes=VMEM_LIMIT),
    )(recv_slot, features, cotangent)


def pass_to(value, step_x, step_y):
    pairs = []
    for gx in range(8):
        for gy in range(32):
            if 0 <= gx + step_x < 8 and 0 <= gy + step_y < 32:
                pairs.append((gx * 32 + gy, (gx + step_x) * 32 + gy + step_y))
    return lax.ppermute(value, AXES, pairs)


def sum_everywhere(arrived, keep):
    chip_sum = (keep + arrived.astype(jnp.float32)).astype(jnp.bfloat16)
    parts = chip_sum.reshape(16, 7, 16, CHANNELS)
    parts = lax.all_to_all(parts, ("x", "y"), 0, 0)
    total = jnp.sum(parts.astype(jnp.float32), axis=0)
    largest = jnp.max(jnp.abs(total), axis=(0, 1))
    power = jnp.clip(jnp.ceil(jnp.log2(jnp.maximum(largest, 1e-37))), -100.0, 100.0)
    power = jnp.broadcast_to(power, (8, CHANNELS))
    scaled = (total * jnp.exp2(14.0 - power[0])).reshape(7 * 16, CHANNELS)
    share = jnp.concatenate((scaled, power), axis=0).astype(jnp.float16)
    column = lax.all_to_all(jnp.broadcast_to(share[None], (8,) + share.shape), "z", 0, 0).astype(jnp.float32)
    total = jnp.sum(column[:, : 7 * 16] * jnp.exp2(column[:, 7 * 16 : 7 * 16 + 1] - 14.0), axis=0)
    share = (total * (1.0 / (VOXELS * SLOTS))).astype(jnp.bfloat16).reshape(7, 16, CHANNELS)
    whole = jnp.broadcast_to(share[None], (16,) + share.shape)
    return lax.all_to_all(whole, ("x", "y"), 0, 0).reshape(4, ROWS_M, 16, CHANNELS)


def spread_kernel(own_ref, other_ref, outputs_ref, grad_ref, outputs_out, grad_out, out_ref, whole, sems):
    half = CHANNELS // 2
    core = lax.axis_index("c")
    copies = [
        pltpu.make_async_copy(outputs_ref, outputs_out, sems.at[9]),
        pltpu.make_async_copy(grad_ref, grad_out, sems.at[10]),
    ]
    for copy in copies:
        copy.start()
    for chunk in range(9):
        for m in range(3 * chunk, 3 * chunk + 3):
            for quarter in range(4):
                for ref, side in ((own_ref, core), (other_ref, 1 - core)):
                    begin = pl.multiple_of(side * half + quarter * 16, 16)
                    whole[26 - m, pl.ds(begin, 16)] = ref[quarter, m].astype(jnp.float32)
        rows = pl.ds(24 - 3 * chunk, 3)
        copies.append(pltpu.make_async_copy(whole.at[rows], out_ref.at[rows], sems.at[chunk]))
        copies[-1].start()
    for copy in copies:
        copy.wait()


def spread_out(outputs, input_grad, own, other):
    return pl.pallas_call(
        spread_kernel,
        in_specs=[VMEM_SPEC] * 4,
        out_specs=[pl.BlockSpec(memory_space=pltpu.HBM)] * 3,
        out_shape=[BRICK_SHAPE, BRICK_SHAPE, jax.ShapeDtypeStruct((27, CHANNELS, CHANNELS), jnp.float32)],
        scratch_shapes=[
            pltpu.VMEM((27, CHANNELS, CHANNELS), jnp.float32),
            pltpu.SemaphoreType.DMA((11,)),
        ],
        compiler_params=PARAMS,
    )(own, other, outputs, input_grad)


def local(features, weights, cotangent, dst_index, recv_slot):
    core = lax.axis_index("c")
    dst = jnp.clip(dst_index.T, 0, SLOTS + HALO)

    to_first, to_second, to_sibling, to_outer, own_f, own_c = pack_layers(recv_slot, features, cotangent)
    flipped = jnp.transpose(own_f[:SLOTS].reshape(SLOTS * VOXELS, CHANNELS))
    flipped = flipped.reshape(2, CHANNELS // 2, SLOTS * VOXELS)
    y_second = lax.ppermute(to_second, ("y", "z"), [(gy, ((gy + 1) ^ 1) - 1) for gy in range(1, 31)])
    y_first = lax.ppermute(to_first, ("y", "z"), [(gy, gy ^ 1) for gy in range(32)])
    y_second, y_first, dst, flipped = lax.optimization_barrier((y_second, y_first, dst, flipped))

    def relayed(packet, up):
        corners = [lax.dynamic_slice_in_dim(value[SLOTS:], 8 * up, 8, axis=1) for value in (y_first, y_second)]
        return jnp.concatenate((packet, jnp.concatenate(corners, axis=1)), axis=0)

    x_outer = lax.ppermute(relayed(to_outer, core), ("x", "c"), [(2 * x + 1, 2 * x + 2) for x in range(3)]
                           + [(2 * x + 2, 2 * x + 1) for x in range(3)])
    x_sibling = lax.ppermute(relayed(to_sibling, 1 - core), "c", [(0, 1), (1, 0)])
    mids = mid_taps(fill_along_y, SLOTS, dst, own_f, own_c, (y_first, y_second), flipped, weights)
    results = convolve(fill_along_x, SLOTS, dst, mids, (x_sibling, x_outer), flipped, weights)

    def with_whole_bricks(results):
        packets = pack_bricks(recv_slot, features, cotangent)
        halos = [pass_to(packet, -heading[0], -heading[1]) for packet, heading in zip(packets, DIRECTIONS)]
        mids = mid_taps(fill_bricks, 1, dst, own_f, own_c, halos, flipped, weights)
        return spread_out(*convolve(fill_nothing, 1, dst, mids, (), flipped, weights))

    def as_they_are(results):
        return spread_out(*results)

    own = results[2]
    return tuple(lax.cond(own[0, 27, 0, 0] != 0, with_whole_bricks, as_they_are, results))


def solution(mesh):
    fine = Mesh(mesh.devices.reshape(4, 2, 4, 8), AXES)
    bricks = P(AXES, None, None)
    return jax.shard_map(
        local,
        mesh=fine,
        in_specs=(bricks, P(), bricks, P(None, AXES), P(AXES)),
        out_specs=(bricks, bricks, P()),
        check_vma=False,
    )
```

```python
import functools

import jax
import jax.numpy as jnp
import numpy as np
from jax import lax
from jax.experimental import pallas as pl
from jax.experimental.pallas import tpu as pltpu
from jax.sharding import Mesh, PartitionSpec as P

BRICK = 4
TILE = 4
BZ = 2
HALO = 40
SLOTS = 8
VOXELS = 64
CHANNELS = 128
PLANE = BRICK * BRICK
PLANES = BRICK + 2
WIDE = 9 * CHANNELS
ROWS_M = 28

DIRECTIONS = ((1, 0), (-1, 0), (0, 1), (0, -1), (1, 1), (1, -1), (-1, 1), (-1, -1))
LENGTHS = (TILE * BZ,) * 4 + (BZ,) * 4
STARTS = tuple(int(start) for start in np.cumsum((0,) + LENGTHS[:-1]))
AXES = ("x", "c", "y", "z")
VMEM_LIMIT = 24 * 1024 * 1024


def where_equal(left, right):
    return jnp.where(left == right, 1.0, 0.0).astype(jnp.bfloat16)


def shift_matrix():
    row = lax.broadcasted_iota(jnp.int32, (9 * PLANE, 9 * PLANE), 0)
    column = lax.broadcasted_iota(jnp.int32, (9 * PLANE, 9 * PLANE), 1)
    number = row >> 4
    third = (number * 11) >> 5
    y = ((row >> 2) & 3) + third + 3
    z = (row & 3) + number - 3 * third + 3
    return where_equal(column, ((y >> 2) * 3 + (z >> 2)) * PLANE + (y & 3) * BRICK + (z & 3))


def layer_matrix():
    row = lax.broadcasted_iota(jnp.int32, (4 * PLANE, VOXELS), 0)
    column = lax.broadcasted_iota(jnp.int32, (4 * PLANE, VOXELS), 1)
    quarter = (row >> 2) & 3
    vx = jnp.where(row < 2 * PLANE, quarter, (quarter >> 1) * 3)
    return where_equal(column, vx * PLANE + ((row >> 4) & 1) * 12 + (row & 3))


def expand_matrix(side):
    row = lax.broadcasted_iota(jnp.int32, (VOXELS, PLANE), 0)
    column = lax.broadcasted_iota(jnp.int32, (VOXELS, PLANE), 1)
    return where_equal(row, (column >> 2) * PLANE + side * 12 + (column & 3))


def expand_corner_matrix(order, side):
    row = lax.broadcasted_iota(jnp.int32, (2 * VOXELS, PLANE), 0)
    column = lax.broadcasted_iota(jnp.int32, (2 * VOXELS, PLANE), 1)
    vy = (row >> 2) & 3
    return where_equal(column + vy * PLANE, order * 8 + (row >> 6) * 4 + (row & 3) + side * 3 * PLANE)


def pack_layers_kernel(recv_slot_ref, features_ref, cotangent_ref, to_first, to_second, to_sibling, to_outer,
                       own_f, own_c, sides, slot_ref, sems):
    bricks = (own_f, own_c)
    copies = [
        pltpu.make_async_copy(ref, target, sems.at[number])
        for number, (ref, target) in enumerate((
            (features_ref, own_f.at[pl.ds(0, SLOTS)]),
            (cotangent_ref, own_c.at[pl.ds(0, SLOTS)]),
            (recv_slot_ref, slot_ref),
        ))
    ]
    for copy in copies:
        copy.start()
    for own in bricks:
        own[SLOTS] = jnp.zeros((VOXELS, CHANNELS), jnp.bfloat16)
    sides[:, SLOTS] = jnp.zeros((2, 4 * PLANE, CHANNELS), jnp.bfloat16)
    core = lax.axis_index("c")
    odd = lax.axis_index("z") & 1
    layer = layer_matrix()
    block = lax.broadcasted_iota(jnp.int32, (PLANE, CHANNELS), 0) >> 2
    masks = [where_equal(block, number) for number in range(4)]
    for copy in copies:
        copy.wait()
    for kind in range(2):
        beside = jnp.concatenate([bricks[kind][slot] for slot in range(SLOTS)], axis=1)
        picked = jnp.dot(layer, beside, preferred_element_type=jnp.float32).astype(jnp.bfloat16)
        for slot in range(SLOTS):
            sides[kind, slot] = picked[:, slot * CHANNELS : (slot + 1) * CHANNELS]

    def put(packet, position, halo, source, begin):
        slot = jnp.clip(slot_ref[halo], 0, SLOTS)
        rows = pl.ds(begin, PLANE)
        packet[position, :, :CHANNELS] = source[0][slot, rows]
        packet[position, :, CHANNELS:] = source[1][slot, rows]

    for packet, up in ((to_first, 1 - odd), (to_second, odd)):
        begin = pl.multiple_of(up * PLANE, PLANE)
        for position in range(SLOTS):
            put(packet, position, STARTS[2] + up * LENGTHS[2] + position, (sides.at[0], sides.at[1]), begin)
        rows = pl.ds(pl.multiple_of((up + 2) * PLANE, PLANE), PLANE)
        halos = [STARTS[number] + up * BZ + position for number in (4, 6) for position in range(BZ)]
        slots = [jnp.clip(slot_ref[halo], 0, SLOTS) for halo in halos]
        for kind in range(2):
            tile = sides[kind, slots[0], rows] * masks[0]
            for number in range(1, 4):
                tile = tile + sides[kind, slots[number], rows] * masks[number]
            packet[SLOTS, :, kind * CHANNELS : (kind + 1) * CHANNELS] = tile
    for packet, up in ((to_sibling, 1 - core), (to_outer, core)):
        begin = pl.multiple_of(up * (VOXELS - PLANE), PLANE)
        for position in range(LENGTHS[0]):
            put(packet, position, up * LENGTHS[0] + position, bricks, begin)


def pack_layers(recv_slot, features, cotangent):
    vmem = pl.BlockSpec(memory_space=pltpu.VMEM)
    hbm = pl.BlockSpec(memory_space=pltpu.HBM)
    return pl.pallas_call(
        pack_layers_kernel,
        in_specs=[hbm] * 3,
        out_specs=[vmem] * 6,
        out_shape=[
            jax.ShapeDtypeStruct((length, PLANE, 2 * CHANNELS), jnp.bfloat16) for length in (SLOTS + 1, SLOTS + 1, SLOTS, SLOTS)
        ] + [jax.ShapeDtypeStruct((SLOTS + 1, VOXELS, CHANNELS), jnp.bfloat16)] * 2,
        scratch_shapes=[
            pltpu.VMEM((2, SLOTS + 1, 4 * PLANE, CHANNELS), jnp.bfloat16),
            pltpu.SMEM((HALO,), jnp.int32),
            pltpu.SemaphoreType.DMA((3,)),
        ],
        compiler_params=pltpu.CompilerParams(vmem_limit_bytes=VMEM_LIMIT),
    )(recv_slot, features, cotangent)


def fill_bricks(halos, lanes, bricks):
    begin_at = SLOTS
    for halo in halos:
        bricks[begin_at : begin_at + halo.shape[0]] = halo[:, :, lanes]
        begin_at += halo.shape[0]


def fill_along_y(halos, lanes, bricks):
    odd = lax.axis_index("z") & 1
    for faces, side in ((halos[0], odd), (halos[1], 1 - odd)):
        tiles = jnp.concatenate([faces[position, :, lanes] for position in range(SLOTS)], axis=1)
        whole = jnp.dot(expand_matrix(side), tiles, preferred_element_type=jnp.float32).astype(jnp.bfloat16)
        for position in range(SLOTS):
            target = SLOTS + STARTS[2] + side * LENGTHS[2] + position
            bricks[target] = whole[:, position * CHANNELS : (position + 1) * CHANNELS]


def fill_along_x(halos, lanes, bricks):
    core, odd = lax.axis_index("c"), lax.axis_index("z") & 1
    both = ((halos[0], core), (halos[1], 1 - core))
    for packet, below in both:
        for position in range(SLOTS):
            tile = packet[position, :, lanes]
            target = SLOTS + below * LENGTHS[0] + position
            bricks[target, :PLANE] = tile
            bricks[target, VOXELS - PLANE :] = tile
    tiles = jnp.concatenate([packet[SLOTS, :, lanes] for packet in halos], axis=1)
    for order, side in ((0, odd), (1, 1 - odd)):
        whole = jnp.dot(
            expand_corner_matrix(order, side), tiles, preferred_element_type=jnp.float32
        ).astype(jnp.bfloat16)
        for number, (_, below) in enumerate(both):
            for position in range(BZ):
                target = SLOTS + STARTS[4] + side * BZ + below * 2 * BZ + position
                bricks[target] = whole[
                    position * VOXELS : (position + 1) * VOXELS, number * CHANNELS : (number + 1) * CHANNELS
                ]


def fill_nothing(halos, lanes, bricks):
    pass


def out_of_place(dst):
    k = lax.broadcasted_iota(jnp.int32, dst.shape, 1)
    ninth = jnp.where(k >= 18, 2, jnp.where(k >= 9, 1, 0))
    rest = k - 9 * ninth
    offset = (ninth - 1, jnp.where(rest >= 6, 2, jnp.where(rest >= 3, 1, 0)) - 1)
    wrong = jnp.zeros(dst.shape, jnp.float32)
    for number, heading in enumerate(DIRECTIONS):
        start = SLOTS + STARTS[number]
        here = (dst >= start) & (dst < start + LENGTHS[number])
        for axis in range(2):
            if heading[axis]:
                wrong = jnp.where(here & (offset[axis] != heading[axis]), 1.0, wrong)
    return jnp.max(jnp.max(wrong, axis=1, keepdims=True), axis=0, keepdims=True)


def build_taps(unroll, dst_ref, bricks, planes, taps):
    shift = shift_matrix()

    def around(slot, plane):
        side = 0 if plane == 0 else 2 if plane == PLANES - 1 else 1
        local = (plane - 1) % BRICK * PLANE
        return jnp.concatenate(
            [bricks[dst_ref[slot, side * 9 + number], local : local + PLANE] for number in range(9)], axis=0
        )

    def one_slot(slot, carry):
        for index in range(0, len(planes), 2):
            pair = jnp.concatenate((around(slot, planes[index]), around(slot, planes[index + 1])), axis=1)
            moved = jnp.dot(shift, pair, preferred_element_type=jnp.float32).astype(jnp.bfloat16)
            for number in range(9):
                rows = moved[number * PLANE : (number + 1) * PLANE]
                target = slice(number * CHANNELS, (number + 1) * CHANNELS)
                taps[slot, index, :, target] = rows[:, :CHANNELS]
                taps[slot, index + 1, :, target] = rows[:, CHANNELS:]
        return carry

    lax.fori_loop(0, SLOTS, one_slot, 0, unroll=unroll)


def taps_of(mid, edge, side):
    if side == 0:
        planes = jnp.concatenate((edge[:, :1], mid[:, :3]), axis=1)
    elif side == 1:
        planes = mid[...]
    else:
        planes = jnp.concatenate((mid[:, 1:], edge[:, 1:]), axis=1)
    return planes.reshape(SLOTS * VOXELS, WIDE)


def store_products(flipped_ref, tap, first, send_ref, keep_ref):
    core = lax.axis_index("c")
    half = CHANNELS // 2
    flipped = jnp.concatenate((flipped_ref[1 - core], flipped_ref[core]), axis=0)
    part = jnp.dot(flipped, tap, preferred_element_type=jnp.float32)
    for number in range(9):
        block = part[:, number * CHANNELS : (number + 1) * CHANNELS]
        for quarter in range(4):
            rows = slice(quarter * 16, quarter * 16 + 16)
            send_ref[quarter, first + number] = block[:half][rows].astype(jnp.bfloat16)
            keep_ref[quarter, first + number] = block[half:][rows]


def grad_part(tap, weights_ref, side):
    matrix = jnp.concatenate([weights_ref[26 - side * 9 - number] for number in range(9)], axis=1)
    return lax.dot_general(tap, matrix, (((1,), (1,)), ((), ())), preferred_element_type=jnp.float32)


def output_part(tap, weights_ref, side):
    matrix = weights_ref[side * 9 : side * 9 + 9].reshape(WIDE, CHANNELS)
    return jnp.dot(tap, matrix, preferred_element_type=jnp.float32)


def mid_kernel(fill, unroll, count, dst_ref, features_ref, cotangent_ref, flipped_ref, weights_ref, *rest):
    halos = rest[:count]
    mid_f, mid_c, bricks_f, bricks_c, send_ref, keep_ref, grad_ref, outputs_ref = rest[count:]
    for kind, (own, bricks, mid) in enumerate(((features_ref, bricks_f, mid_f), (cotangent_ref, bricks_c, mid_c))):
        bricks[:SLOTS] = own[:SLOTS]
        for begin, end in ((SLOTS, SLOTS + STARTS[2]), (SLOTS + STARTS[4], SLOTS + HALO + 1)):
            bricks[begin:end] = jnp.zeros((end - begin, VOXELS, CHANNELS), jnp.bfloat16)
        fill(halos, slice(kind * CHANNELS, (kind + 1) * CHANNELS), bricks)
        build_taps(unroll, dst_ref, bricks, (1, 2, 3, 4), mid)
    tap = mid_c[...].reshape(SLOTS * VOXELS, WIDE)
    store_products(flipped_ref, tap, 0, send_ref, keep_ref)
    grad_ref[...] = grad_part(tap, weights_ref, 1)
    outputs_ref[...] = output_part(mid_f[...].reshape(SLOTS * VOXELS, WIDE), weights_ref, 1)


def weight_kernel(fill, unroll, count, dst_ref, table_ref, mid, _, *rest):
    halos = rest[:count]
    flipped_ref, send_mid, keep_mid, send_ref, keep_ref, edge, bricks = rest[count:]
    fill(halos, slice(CHANNELS, 2 * CHANNELS), bricks)
    build_taps(unroll, dst_ref, bricks, (0, PLANES - 1), edge)
    send_ref[:, 9:18] = send_mid[...]
    keep_ref[:, 9:18] = keep_mid[...]
    for side in (0, 2):
        store_products(flipped_ref, taps_of(mid, edge, side), side * 9, send_ref, keep_ref)
    flag = jnp.broadcast_to(out_of_place(table_ref[...]), (16, CHANNELS))
    for quarter in range(4):
        send_ref[quarter, 27] = flag.astype(jnp.bfloat16)
        keep_ref[quarter, 27] = flag


def grad_kernel(mid, edge, weights_ref, grad_mid, grad_ref):
    grad = grad_mid[...]
    for side in (0, 2):
        grad = grad + grad_part(taps_of(mid, edge, side), weights_ref, side)
    grad_ref[...] = grad.astype(jnp.bfloat16).reshape(SLOTS, VOXELS, CHANNELS)


def edge_kernel(fill, unroll, count, dst_ref, _, *rest):
    edge, bricks = rest[count:]
    fill(rest[:count], slice(0, CHANNELS), bricks)
    build_taps(unroll, dst_ref, bricks, (0, PLANES - 1), edge)


def output_kernel(mid, edge, weights_ref, outputs_mid, outputs_ref):
    outputs = outputs_mid[...]
    for side in (0, 2):
        outputs = outputs + output_part(taps_of(mid, edge, side), weights_ref, side)
    outputs_ref[...] = outputs.astype(jnp.bfloat16).reshape(SLOTS, VOXELS, CHANNELS)


VMEM_SPEC = pl.BlockSpec(memory_space=pltpu.VMEM)
SMEM_SPEC = pl.BlockSpec(memory_space=pltpu.SMEM)
BRICK_SHAPE = jax.ShapeDtypeStruct((SLOTS, VOXELS, CHANNELS), jnp.bfloat16)
MID_SHAPE = jax.ShapeDtypeStruct((SLOTS, BRICK, PLANE, WIDE), jnp.bfloat16)
EDGE_SHAPE = jax.ShapeDtypeStruct((SLOTS, 2, PLANE, WIDE), jnp.bfloat16)
ALL_BRICKS = jax.ShapeDtypeStruct((SLOTS + HALO + 1, VOXELS, CHANNELS), jnp.bfloat16)
PARAMS = pltpu.CompilerParams(vmem_limit_bytes=VMEM_LIMIT)
COST = pl.CostEstimate(flops=4 * SLOTS * VOXELS * 27 * CHANNELS * CHANNELS, bytes_accessed=4_000_000, transcendentals=0)


def mid_taps(fill, unroll, dst, own_f, own_c, halos, flipped, weights):
    return pl.pallas_call(
        functools.partial(mid_kernel, fill, unroll, len(halos)),
        in_specs=[SMEM_SPEC] + [VMEM_SPEC] * (4 + len(halos)),
        out_specs=[VMEM_SPEC] * 8,
        out_shape=[
            MID_SHAPE, MID_SHAPE, ALL_BRICKS, ALL_BRICKS,
            jax.ShapeDtypeStruct((4, 9, 16, CHANNELS), jnp.bfloat16),
            jax.ShapeDtypeStruct((4, 9, 16, CHANNELS), jnp.float32),
            jax.ShapeDtypeStruct((SLOTS * VOXELS, CHANNELS), jnp.float32),
            jax.ShapeDtypeStruct((SLOTS * VOXELS, CHANNELS), jnp.float32),
        ],
        compiler_params=PARAMS,
        cost_estimate=COST,
    )(dst, own_f, own_c, flipped, weights, *halos)


def weight_sums(fill, unroll, dst, mid, bricks, halos, flipped, send, keep):
    return pl.pallas_call(
        functools.partial(weight_kernel, fill, unroll, len(halos)),
        in_specs=[SMEM_SPEC] + [VMEM_SPEC] * (6 + len(halos)),
        out_specs=[VMEM_SPEC] * 4,
        out_shape=[
            jax.ShapeDtypeStruct((4, ROWS_M, 16, CHANNELS), jnp.bfloat16),
            jax.ShapeDtypeStruct((4, ROWS_M, 16, CHANNELS), jnp.float32),
            EDGE_SHAPE,
            ALL_BRICKS,
        ],
        input_output_aliases={3: 3},
        compiler_params=PARAMS,
        cost_estimate=COST,
    )(dst, dst, mid, bricks, *halos, flipped, send, keep)


def feature_edges(fill, unroll, dst, bricks, halos):
    return pl.pallas_call(
        functools.partial(edge_kernel, fill, unroll, len(halos)),
        in_specs=[SMEM_SPEC] + [VMEM_SPEC] * (1 + len(halos)),
        out_specs=[VMEM_SPEC] * 2,
        out_shape=[EDGE_SHAPE, ALL_BRICKS],
        input_output_aliases={1: 1},
        compiler_params=PARAMS,
        cost_estimate=COST,
    )(dst, bricks, *halos)[0]


def product(kernel, *operands):
    return pl.pallas_call(
        kernel,
        in_specs=[VMEM_SPEC] * len(operands),
        out_specs=VMEM_SPEC,
        out_shape=BRICK_SHAPE,
        compiler_params=PARAMS,
        cost_estimate=COST,
    )(*operands)


def convolve(fill, unroll, dst, mids, halos, flipped, weights):
    mid_f, mid_c, bricks_f, bricks_c, send, keep, grad_mid, outputs_mid = mids
    send, keep, edge_c, _ = weight_sums(fill, unroll, dst, mid_c, bricks_c, halos, flipped, send, keep)
    arrived = lax.ppermute(send, "c", [(0, 1), (1, 0)])
    input_grad = product(grad_kernel, mid_c, edge_c, weights, grad_mid)
    edge_f = feature_edges(fill, unroll, dst, bricks_f, halos)
    arrived, input_grad, edge_f = lax.optimization_barrier((arrived, input_grad, edge_f))
    own = sum_everywhere(arrived, keep)
    other = lax.ppermute(own, "c", [(0, 1), (1, 0)])
    outputs = product(output_kernel, mid_f, edge_f, weights, outputs_mid)
    return outputs, input_grad, own, other


def pack_bricks_kernel(slot_ref, features_ref, cotangent_ref, *packets):
    begin_at = 0
    for packet in packets:
        for position in range(packet.shape[0]):
            slot = slot_ref[begin_at + position]
            row = jnp.clip(slot, 0, SLOTS - 1)

            @pl.when(slot < SLOTS)
            def _():
                packet[position, :, :CHANNELS] = features_ref[row]
                packet[position, :, CHANNELS:] = cotangent_ref[row]

            @pl.when(slot >= SLOTS)
            def _():
                packet[position] = jnp.zeros((VOXELS, 2 * CHANNELS), jnp.bfloat16)

        begin_at += packet.shape[0]


def pack_bricks(recv_slot, features, cotangent):
    vmem = pl.BlockSpec(memory_space=pltpu.VMEM)
    return pl.pallas_call(
        pack_bricks_kernel,
        in_specs=[pl.BlockSpec(memory_space=pltpu.SMEM), vmem, vmem],
        out_specs=[vmem] * 8,
        out_shape=[
            jax.ShapeDtypeStruct((length, VOXELS, 2 * CHANNELS), jnp.bfloat16) for length in LENGTHS
        ],
        compiler_params=pltpu.CompilerParams(vmem_limit_bytes=VMEM_LIMIT),
    )(recv_slot, features, cotangent)


def pass_to(value, step_x, step_y):
    pairs = []
    for gx in range(8):
        for gy in range(32):
            if 0 <= gx + step_x < 8 and 0 <= gy + step_y < 32:
                pairs.append((gx * 32 + gy, (gx + step_x) * 32 + gy + step_y))
    return lax.ppermute(value, AXES, pairs)


def sum_everywhere(arrived, keep):
    chip_sum = (keep + arrived.astype(jnp.float32)).astype(jnp.bfloat16)
    parts = chip_sum.reshape(16, 7, 16, CHANNELS)
    parts = lax.all_to_all(parts, ("x", "y"), 0, 0)
    total = jnp.sum(parts.astype(jnp.float32), axis=0)
    largest = jnp.max(jnp.abs(total), axis=(0, 1))
    power = jnp.clip(jnp.ceil(jnp.log2(jnp.maximum(largest, 1e-37))), -100.0, 100.0)
    power = jnp.broadcast_to(power, (8, CHANNELS))
    scaled = (total * jnp.exp2(14.0 - power[0])).reshape(7 * 16, CHANNELS)
    share = jnp.concatenate((scaled, power), axis=0).astype(jnp.float16)
    column = lax.all_to_all(jnp.broadcast_to(share[None], (8,) + share.shape), "z", 0, 0).astype(jnp.float32)
    total = jnp.sum(column[:, : 7 * 16] * jnp.exp2(column[:, 7 * 16 : 7 * 16 + 1] - 14.0), axis=0)
    share = (total * (1.0 / (VOXELS * SLOTS))).astype(jnp.bfloat16).reshape(7, 16, CHANNELS)
    whole = jnp.broadcast_to(share[None], (16,) + share.shape)
    return lax.all_to_all(whole, ("x", "y"), 0, 0).reshape(4, ROWS_M, 16, CHANNELS)


def spread_kernel(own_ref, other_ref, outputs_ref, grad_ref, outputs_out, grad_out, out_ref, whole, sems):
    half = CHANNELS // 2
    core = lax.axis_index("c")
    copies = [
        pltpu.make_async_copy(outputs_ref, outputs_out, sems.at[9]),
        pltpu.make_async_copy(grad_ref, grad_out, sems.at[10]),
    ]
    for copy in copies:
        copy.start()
    for chunk in range(9):
        for m in range(3 * chunk, 3 * chunk + 3):
            for quarter in range(4):
                for ref, side in ((own_ref, core), (other_ref, 1 - core)):
                    begin = pl.multiple_of(side * half + quarter * 16, 16)
                    whole[26 - m, pl.ds(begin, 16)] = ref[quarter, m].astype(jnp.float32)
        rows = pl.ds(24 - 3 * chunk, 3)
        copies.append(pltpu.make_async_copy(whole.at[rows], out_ref.at[rows], sems.at[chunk]))
        copies[-1].start()
    for copy in copies:
        copy.wait()


def spread_out(outputs, input_grad, own, other):
    return pl.pallas_call(
        spread_kernel,
        in_specs=[VMEM_SPEC] * 4,
        out_specs=[pl.BlockSpec(memory_space=pltpu.HBM)] * 3,
        out_shape=[BRICK_SHAPE, BRICK_SHAPE, jax.ShapeDtypeStruct((27, CHANNELS, CHANNELS), jnp.float32)],
        scratch_shapes=[
            pltpu.VMEM((27, CHANNELS, CHANNELS), jnp.float32),
            pltpu.SemaphoreType.DMA((11,)),
        ],
        compiler_params=PARAMS,
    )(own, other, outputs, input_grad)


def local(features, weights, cotangent, dst_index, recv_slot):
    core = lax.axis_index("c")
    dst = jnp.clip(dst_index.T, 0, SLOTS + HALO)

    to_first, to_second, to_sibling, to_outer, own_f, own_c = pack_layers(recv_slot, features, cotangent)
    flipped = jnp.transpose(own_f[:SLOTS].reshape(SLOTS * VOXELS, CHANNELS))
    flipped = flipped.reshape(2, CHANNELS // 2, SLOTS * VOXELS)
    y_second = lax.ppermute(to_second, ("y", "z"), [(gy, ((gy + 1) ^ 1) - 1) for gy in range(1, 31)])
    y_first = lax.ppermute(to_first, ("y", "z"), [(gy, gy ^ 1) for gy in range(32)])
    y_second, y_first, dst, flipped = lax.optimization_barrier((y_second, y_first, dst, flipped))

    def relayed(packet, up):
        corners = [lax.dynamic_slice_in_dim(value[SLOTS:], 8 * up, 8, axis=1) for value in (y_first, y_second)]
        return jnp.concatenate((packet, jnp.concatenate(corners, axis=1)), axis=0)

    x_sibling = lax.ppermute(relayed(to_sibling, 1 - core), "c", [(0, 1), (1, 0)])
    x_outer = lax.ppermute(relayed(to_outer, core), ("x", "c"), [(2 * x + 1, 2 * x + 2) for x in range(3)]
                           + [(2 * x + 2, 2 * x + 1) for x in range(3)])
    mids = mid_taps(fill_along_y, SLOTS, dst, own_f, own_c, (y_first, y_second), flipped, weights)
    results = convolve(fill_along_x, SLOTS, dst, mids, (x_sibling, x_outer), flipped, weights)

    def with_whole_bricks(results):
        packets = pack_bricks(recv_slot, features, cotangent)
        halos = [pass_to(packet, -heading[0], -heading[1]) for packet, heading in zip(packets, DIRECTIONS)]
        mids = mid_taps(fill_bricks, 1, dst, own_f, own_c, halos, flipped, weights)
        return spread_out(*convolve(fill_nothing, 1, dst, mids, (), flipped, weights))

    def as_they_are(results):
        return spread_out(*results)

    own = results[2]
    return tuple(lax.cond(own[0, 27, 0, 0] != 0, with_whole_bricks, as_they_are, results))


def solution(mesh):
    fine = Mesh(mesh.devices.reshape(4, 2, 4, 8), AXES)
    bricks = P(AXES, None, None)
    return jax.shard_map(
        local,
        mesh=fine,
        in_specs=(bricks, P(), bricks, P(None, AXES), P(AXES)),
        out_specs=(bricks, bricks, P()),
        check_vma=False,
    )
```
